32 devices in a mesh: parts: 2 (over x), replica: 16 (over z, y, core).
Axes of the slice: x: 2, y: 2, z: 4, core: 2. Of those that a mesh axis runs over, the one named last changes fastest.
Arguments:
- kv_pages: bfloat16 [8192, 2, 64, 128], P(('parts', 'replica')), parts along dimension 0, may hold values from -6 to 6
- page_scale: bfloat16 [8192, 2], P(('parts', 'replica')), parts along dimension 0, may hold values from 0.25 to 2
- page_table: int32 [256, 32], P(('parts', 'replica')), parts along dimension 0, may hold values from 0 to 255, as said below
- lengths: int32 [32], P('parts'), parts along dimension 0, may hold values from 1 to 2048, as said below
- request_moves: int32 [32], P('parts'), parts along dimension 0, may hold values from 0 to 15, as said below
- queries: bfloat16 [256, 768], P(('parts', 'replica')), parts along dimension 0, may hold values from -32 to 32
- new_kv: bfloat16 [256, 256], P(('parts', 'replica')), parts along dimension 0, may hold values from -32 to 32
- output_proj: bfloat16 [12288, 6144], P('replica'), as said below
- residual: bfloat16 [256, 768], P(('parts', 'replica')), parts along dimension 0, may hold values from -4 to 4
Outputs:
- layer_out: bfloat16 [256, 768], P(('parts', 'replica')), parts along dimension 0
The draws below stay inside these ranges and needn't reach their ends.
There are 2 independent parts, one for each index of `parts`. The reference program is written for one: setup_inputs(seed, part) draws one part's arguments, and reference() takes and returns one part's arrays. A program takes and returns all parts, laid end to end along the dimension named above; an argument that names none is the same for every part. Nothing has to cross between parts.
Inputs may be any that keep to these rules, and one draw needn't show every extreme that they name: `page_table`: the 8 rows of one device name each of its 256 pool pages once. `lengths`: some slot has exactly 2048 tokens. `request_moves`: a permutation of the slots; every replica sends exactly one request to each other replica, and each arriving request takes a slot that one of the replica's own departing requests left; all other slots keep their request. `output_proj`: the blocks of all replicas for one head group are equal.
All inputs are finite; a program needn't handle non-finite values.
Results may differ from the reference program's by a relative error of at most 0.0039.
Values may be sent and summed in bfloat16 or wider, within the bound.
No kernel may reach another device: no remote copies, remote signals or barrier semaphores. Data moves between devices by JAX's collectives and lax.ppermute only.
A program may use at most 128 MiB of HBM per device.

```python
import math
import jax
import jax.numpy as jnp
from jax import lax

D = 6144
QH = 48
KVH = 8
HD = 128
PAGE = 64
MAXP = 32
REQ = 8
NREP = 2
QPK = 6
POOL = 256
SLOTS = 16
DB = 768
N_REPLICA = 16


def draw_queries(key, part):
    key = jax.random.fold_in(key, 1)
    gaussian = jax.random.normal(key, (N_REPLICA * REQ, QPK, HD), jnp.float32)
    head_values = gaussian
    return jnp.clip(head_values, -32.0, 32.0).reshape(N_REPLICA * REQ, QPK * HD).astype(jnp.bfloat16)


def draw_new_kv(key, part):
    key = jax.random.fold_in(key, 2)
    gaussian = jax.random.normal(key, (N_REPLICA * REQ, 2, HD), jnp.float32)
    keys_part = gaussian[:, 0]
    stacked = jnp.stack([keys_part, gaussian[:, 1]], axis=1)
    return jnp.clip(stacked, -32.0, 32.0).reshape(N_REPLICA * REQ, 2 * HD).astype(jnp.bfloat16)


def draw_output_proj(key, part):
    key = jax.random.fold_in(key, 3)
    single = jax.random.normal(key, (KVH * QPK * HD, D), jnp.float32) * (QH * HD) ** (-0.5)
    return jnp.tile(single, (NREP, 1)).astype(jnp.bfloat16)


def pool_order(subkey):
    return jax.random.permutation(subkey, POOL)


def draw_page_table(key, part):
    key = jax.random.fold_in(key, 4)
    orders = jax.vmap(pool_order)(jax.random.split(key, N_REPLICA))
    return orders.astype(jnp.int32).reshape(N_REPLICA * REQ, MAXP)


def draw_lengths(key, part):
    key = jax.random.fold_in(key, 5)
    context = jax.random.randint(key, (SLOTS,), 1, MAXP * PAGE + 1, dtype=jnp.int32)
    longest = jax.random.randint(jax.random.fold_in(key, 6), (), 0, SLOTS, dtype=jnp.int32)
    return context.at[longest].set(MAXP * PAGE)


def slot_order(subkey):
    return jax.random.permutation(subkey, REQ)


def draw_request_moves(key, part):
    key = jax.random.fold_in(key, 7)
    orders = jax.vmap(slot_order)(jax.random.split(key, NREP)).astype(jnp.int32)
    moved = jnp.arange(SLOTS, dtype=jnp.int32)
    replicas_at = jnp.arange(NREP, dtype=jnp.int32)
    for column in range(NREP - 1):
        sources = (replicas_at - (column + 1)) % NREP
        moved = moved.at[replicas_at * REQ + orders[:, column]].set(sources * REQ + orders[sources, column])
    return moved


def steps_of(stream_key, shape, cuts, low, high):
    loudness = 1.0
    for dim, shards_of in cuts:
        steps = jax.random.uniform(jax.random.fold_in(jax.random.fold_in(stream_key, 6), dim), (shards_of,), jnp.float32, low / len(cuts), high / len(cuts))
        loudness = loudness * jnp.repeat(jnp.exp(steps), shape[dim] // shards_of).reshape((-1,) + (1,) * (len(shape) - 1 - dim))
    return loudness


def bell_draw(key, extent, deviation, most, cuts=(), kind=jnp.bfloat16):
    array = deviation * jax.random.normal(key, extent, jnp.float32)
    if cuts:
        array = array * steps_of(key, extent, cuts, -0.22, 0.18)
    return jnp.clip(array, -most, most).astype(kind)


def setup_inputs(seed: int = 0, part: int = 0) -> dict:
    arg_keys = jax.random.split(jax.random.key(seed), 10)
    part_splits = jax.random.split(jax.random.fold_in(arg_keys[9], part), 10)
    kv_pages = bell_draw(part_splits[0], (N_REPLICA * POOL, 2, PAGE, HD), 1.0, 6.0, ((0, 16),))
    page_scale = jnp.clip(jnp.exp(math.log(2.0) - 2.0794415 * jax.random.uniform(part_splits[1], (N_REPLICA * POOL, 2), jnp.float32) ** steps_of(part_splits[1], (N_REPLICA * POOL, 2), ((0, 16),), -0.2, 0.2)), 0.25, 2.0).astype(jnp.bfloat16)
    page_table = draw_page_table(jax.random.fold_in(jax.random.fold_in(arg_keys[9], part), 71), part)
    lengths = draw_lengths(jax.random.fold_in(jax.random.fold_in(arg_keys[9], part), 71), part)
    request_moves = draw_request_moves(jax.random.fold_in(jax.random.fold_in(arg_keys[9], part), 71), part)
    queries = draw_queries(jax.random.fold_in(jax.random.fold_in(arg_keys[9], part), 71), part)
    new_kv = draw_new_kv(jax.random.fold_in(jax.random.fold_in(arg_keys[9], part), 71), part)
    output_proj = draw_output_proj(jax.random.fold_in(arg_keys[9], 71), part)
    residual = bell_draw(part_splits[8], (N_REPLICA * REQ, DB), 0.25, 4.0, ((0, 16),))
    return dict(kv_pages=kv_pages, page_scale=page_scale, page_table=page_table, lengths=lengths, request_moves=request_moves, queries=queries, new_kv=new_kv, output_proj=output_proj, residual=residual)


def attend_device(position, kv_pages, page_scale, tables, lengths, request_moves, query_blocks, token_blocks):
    replica = position // KVH
    tensor_shard = position % KVH
    source = lax.dynamic_slice_in_dim(request_moves, replica * REQ, REQ)
    source_dev = source // REQ * KVH + tensor_shard
    rows_used = tables[source_dev, source % REQ]
    page_ids = source_dev[:, None] * POOL + rows_used
    kv_cache = kv_pages[page_ids].astype(jnp.float32)
    scales = page_scale[page_ids].astype(jnp.float32)
    context = lengths[source]
    query_heads = lax.dynamic_index_in_dim(query_blocks, position, 0, False).astype(jnp.float32)
    new_tokens = lax.dynamic_index_in_dim(token_blocks, position, 0, False).astype(jnp.float32)
    factor = 1.0 / math.sqrt(HD)
    scores = jnp.einsum('jhe,jpne->jhpn', query_heads, kv_cache[:, :, 0]) * scales[:, None, :, 0, None] * factor
    scores = scores.reshape(REQ, QPK, MAXP * PAGE)
    places = jnp.arange(MAXP * PAGE, dtype=jnp.int32)
    visible = places[None, :] < context[:, None]
    scores = jnp.where(visible[:, None, :], scores, -jnp.inf)
    own_score = jnp.einsum('jhe,je->jh', query_heads, new_tokens[:, 0]) * factor
    highest = jnp.maximum(lax.optimization_barrier(jnp.max(scores, axis=2)), own_score)
    weights = jnp.exp(scores - highest[:, :, None])
    own_weight = jnp.exp(own_score - highest)
    denominator = lax.optimization_barrier(jnp.sum(weights, axis=2)) + own_weight
    weights = lax.optimization_barrier((weights / denominator[:, :, None]).astype(jnp.bfloat16)).astype(jnp.float32)
    own_weight = lax.optimization_barrier((own_weight / denominator).astype(jnp.bfloat16)).astype(jnp.float32)
    weights = weights.reshape(REQ, QPK, MAXP, PAGE)
    mixture = jnp.einsum('jhpn,jpne->jhpe', weights, kv_cache[:, :, 1]) * scales[:, None, :, 1, None]
    attended = lax.optimization_barrier(jnp.sum(mixture, axis=2)) + own_weight[:, :, None] * new_tokens[:, None, 1]
    return attended.astype(jnp.bfloat16).reshape(REQ, QPK * HD)

def reference(kv_pages, page_scale, page_table, lengths, request_moves, queries, new_kv, output_proj, residual):
    devices = N_REPLICA
    tables = page_table.reshape(devices, REQ, MAXP)
    query_blocks = queries.reshape(devices, REQ, QPK, HD)
    token_blocks = new_kv.reshape(devices, REQ, 2, HD)

    def per_device(position):
        return attend_device(position, kv_pages, page_scale, tables, lengths, request_moves, query_blocks, token_blocks)
    attended = lax.map(per_device, jnp.arange(devices, dtype=jnp.int32))
    attended = attended.reshape(NREP, KVH, REQ, QPK * HD)
    projection = output_proj.reshape(NREP, KVH, QPK * HD, D)

    def project(operands):
        return jnp.einsum('tjf,tfd->jd', operands[0].astype(jnp.float32), operands[1].astype(jnp.float32))
    projected = lax.map(project, (attended, projection))
    projected = projected.reshape(NREP, REQ, KVH, DB).transpose(0, 2, 1, 3)
    combined = projected + residual.reshape(NREP, KVH, REQ, DB).astype(jnp.float32)
    return combined.astype(jnp.bfloat16).reshape(N_REPLICA * REQ, DB)
```

```python
import functools
import math

import jax
import jax.numpy as jnp
from jax import lax
from jax.experimental import pallas as pl
from jax.experimental.pallas import tpu as pltpu
from jax.sharding import PartitionSpec as P

KVH = 8
ROWS = 8
GROUP = 4
F32 = jnp.float32
BF16 = jnp.bfloat16


def attend_project(replicas, per_kv, *refs):
    lengths, moves, table_s, table_v, page_scale = refs[:5]
    q_refs = refs[5 : 5 + replicas]
    nk_refs = refs[5 + replicas : 5 + 2 * replicas]
    kv_pages, proj = refs[5 + 2 * replicas : 7 + 2 * replicas]
    rest = refs[7 + 2 * replicas :]
    blocks = rest[:KVH]
    leaving = rest[KVH : KVH + (replicas - 1) * KVH]
    (target, kv_buf, w_buf, q_all, nk_all, q_stage, q_rows, nk_rows, scales, attended, part, kv_sem, w_sem) = rest[
        KVH + (replicas - 1) * KVH :
    ]

    requests, max_pages = table_v.shape
    page_len, head_dim = kv_pages.shape[2:]
    pool = page_scale.shape[0]
    tokens = max_pages * page_len
    width = blocks[0].shape[1]
    slots = moves.shape[0]
    factor = 1.0 / math.sqrt(head_dim)
    position = lax.axis_index("replica")
    replica = position // KVH
    shard = position % KVH

    def groups_of(j):
        count = (lengths[replica * requests + j] + page_len - 1) // page_len
        return (count + GROUP - 1) // GROUP

    for j in range(requests):
        groups = groups_of(j)

        def start(g, carry, j=j):
            for i in range(GROUP):
                p = g * GROUP + i
                pltpu.make_async_copy(kv_pages.at[table_s[j, p]], kv_buf.at[j, p], kv_sem.at[j]).start()
            return carry

        def clear(g, carry, j=j):
            for i in range(GROUP):
                kv_buf[j, g * GROUP + i, 1] = jnp.zeros((page_len, head_dim), BF16)
            return carry

        lax.fori_loop(0, groups, start, 0)
        lax.fori_loop(groups, max_pages // GROUP, clear, 0)

    def w_copy(k):
        column = pl.multiple_of((shard ^ k) * width, 128)
        return pltpu.make_async_copy(proj.at[:, pl.ds(column, width)], w_buf.at[k], w_sem.at[k])

    for k in range(KVH):
        w_copy(k).start()

    def place(g, carry):
        slot = moves[g]

        @pl.when(slot // requests == replica)
        def _():
            target[slot % requests] = g

        return carry

    lax.fori_loop(0, slots, place, 0)

    for d in range(replicas):
        q_all[d * requests : (d + 1) * requests, :] = q_refs[d][...].astype(F32)
        nk_all[d * requests : (d + 1) * requests, :] = nk_refs[d][...].astype(F32)
    for j in range(requests):
        goal = target[j]
        away = lax.rem(goal // requests - replica + replicas, replicas)
        row = away * requests + lax.rem(goal, requests)
        q_stage[j : j + 1, :] = q_all[pl.ds(row, 1), :]
        nk_rows[j : j + 1, :] = nk_all[pl.ds(row, 1), :]
    q_rows[...] = jnp.zeros_like(q_rows)
    for h in range(per_kv):
        q_rows[pl.ds(h, requests, stride=ROWS), :] = q_stage[:, h * head_dim : (h + 1) * head_dim]

    scale_t = page_scale[...].astype(F32).T.astype(BF16)
    page_ids = lax.broadcasted_iota(jnp.int32, (pool, max_pages), 0)
    for j in range(requests):
        chosen = (page_ids == table_v[j : j + 1, :]).astype(F32).astype(BF16)
        scales[:, j : j + 1, :] = jnp.dot(scale_t, chosen, preferred_element_type=F32)[:, None, :]
    spread = (
        lax.broadcasted_iota(jnp.int32, (max_pages, tokens), 1) // page_len
        == lax.broadcasted_iota(jnp.int32, (max_pages, tokens), 0)
    ).astype(F32).astype(BF16)
    key_scale = jnp.dot(scales[0].astype(BF16), spread, preferred_element_type=F32) * factor
    value_scale = jnp.dot(scales[1].astype(BF16), spread, preferred_element_type=F32)
    places = lax.broadcasted_iota(jnp.int32, (1, tokens), 1)

    def wait_pages(j):
        groups = groups_of(j)
        size = max_pages // GROUP
        while size:

            @pl.when((groups & size) != 0)
            def _(size=size):
                pages = size * GROUP
                pltpu.make_async_copy(kv_pages.at[pl.ds(0, pages)], kv_buf.at[j, pl.ds(0, pages)], kv_sem.at[j]).wait()

            size //= 2

    def score(j):
        queries = q_rows[j * ROWS : (j + 1) * ROWS, :]
        keys = kv_buf[j, :, 0].reshape(tokens, head_dim)
        raw = lax.dot_general(queries.astype(BF16), keys, (((1,), (1,)), ((), ())), preferred_element_type=F32)
        context = lengths[replica * requests + j]
        return jnp.where(places < context, raw * key_scale[j : j + 1], -jnp.inf)

    def finish(j, scores):
        queries = q_rows[j * ROWS : (j + 1) * ROWS, :]
        new_key = nk_rows[j : j + 1, :head_dim]
        new_value = nk_rows[j : j + 1, head_dim:]
        own = jnp.sum(queries * new_key, axis=1, keepdims=True) * factor
        highest = jnp.maximum(jnp.max(scores, axis=1, keepdims=True), own)
        weights = jnp.exp(scores - highest)
        own_weight = jnp.exp(own - highest)
        inverse = 1.0 / (jnp.sum(weights, axis=1, keepdims=True) + own_weight)
        weights = (weights * inverse).astype(BF16).astype(F32)
        own_weight = (own_weight * inverse).astype(BF16).astype(F32)
        scaled = weights * value_scale[j : j + 1]
        high = scaled.astype(BF16)
        low = (scaled - high.astype(F32)).astype(BF16)
        values = kv_buf[j, :, 1].reshape(tokens, head_dim)
        mixed = jnp.dot(jnp.concatenate([high, low], axis=0), values, preferred_element_type=F32)
        attended[j * ROWS : (j + 1) * ROWS, :] = mixed[:ROWS] + mixed[ROWS:] + own_weight * new_value

    wait_pages(0)
    scores = score(0)
    for j in range(requests):
        following = None
        if j + 1 < requests:
            wait_pages(j + 1)
            following = score(j + 1)
        finish(j, scores)
        scores = following

    heads = [attended[pl.ds(h, requests, stride=ROWS), :] for h in range(per_kv)]
    mixture = jnp.concatenate(heads, axis=1).astype(BF16)
    for k in range(KVH):
        w_copy(k).wait()
        part[...] = jnp.dot(mixture, w_buf[k], preferred_element_type=F32)
        blocks[k][...] = part[...]
        for j in range(requests):
            away = lax.rem(target[j] // requests - replica + replicas, replicas)
            for d in range(1, replicas):

                @pl.when(away == d)
                def _(j=j, d=d):
                    leaving[(d - 1) * KVH + k][...] = part[j : j + 1, :]


def combine(replicas, *refs):
    moves, residual = refs[:2]
    blocks = refs[2 : 2 + KVH]
    arrived = refs[2 + KVH : 2 + KVH + (replicas - 1) * KVH]
    out = refs[-1]
    requests = residual.shape[0]
    replica = lax.axis_index("replica") // KVH
    total = blocks[0][...].astype(F32)
    for block in blocks[1:]:
        total = total + block[...].astype(F32)
    slots = lax.broadcasted_iota(jnp.int32, total.shape, 0)
    for d in range(1, replicas):
        row = arrived[(d - 1) * KVH][...]
        for k in range(1, KVH):
            row = row + arrived[(d - 1) * KVH + k][...]
        here = jnp.int32(0)
        for j in range(requests):
            away = lax.rem(replica - moves[replica * requests + j] // requests + replicas, replicas)
            here = jnp.where(away == d, j, here)
        total = jnp.where(slots == here, row, total)
    out[...] = (residual[...].astype(F32) + total).astype(out.dtype)


def on_device(
    kv_pages, page_scale, page_table, lengths, request_moves, queries, new_kv, output_proj, residual
):
    devices = lax.axis_size("replica")
    replicas = devices // KVH
    requests, max_pages = page_table.shape
    page_len, head_dim = kv_pages.shape[2:]
    per_kv = queries.shape[1] // head_dim
    width = output_proj.shape[1] // KVH
    tokens = max_pages * page_len

    def toward(value, replica_steps, head_mask):
        pairs = [
            (i, (i // KVH + replica_steps) % replicas * KVH + ((i % KVH) ^ head_mask)) for i in range(devices)
        ]
        return lax.ppermute(value, "replica", pairs)

    q_parts = [queries] + [toward(queries, -d, 0) for d in range(1, replicas)]
    nk_parts = [new_kv] + [toward(new_kv, -d, 0) for d in range(1, replicas)]

    smem = pl.BlockSpec(memory_space=pltpu.SMEM)
    vmem = pl.BlockSpec(memory_space=pltpu.VMEM)
    hbm = pl.BlockSpec(memory_space=pl.ANY)
    leaving = (replicas - 1) * KVH
    parts = pl.pallas_call(
        functools.partial(attend_project, replicas, per_kv),
        out_shape=[jax.ShapeDtypeStruct((requests, width), F32)] * KVH
        + [jax.ShapeDtypeStruct((1, width), F32)] * leaving,
        in_specs=[smem, smem, smem, vmem, vmem] + [vmem] * (2 * replicas) + [hbm, hbm],
        out_specs=[vmem] * (KVH + leaving),
        scratch_shapes=[
            pltpu.SMEM((requests,), jnp.int32),
            pltpu.VMEM((requests, max_pages, 2, page_len, head_dim), BF16),
            pltpu.VMEM((KVH, per_kv * head_dim, width), BF16),
            pltpu.VMEM((replicas * requests, per_kv * head_dim), F32),
            pltpu.VMEM((replicas * requests, 2 * head_dim), F32),
            pltpu.VMEM((requests, per_kv * head_dim), F32),
            pltpu.VMEM((requests * ROWS, head_dim), F32),
            pltpu.VMEM((requests, 2 * head_dim), F32),
            pltpu.VMEM((2, requests, max_pages), F32),
            pltpu.VMEM((requests * ROWS, head_dim), F32),
            pltpu.VMEM((requests, width), F32),
            pltpu.SemaphoreType.DMA((requests,)),
            pltpu.SemaphoreType.DMA((KVH,)),
        ],
        compiler_params=pltpu.CompilerParams(vmem_limit_bytes=40 * 2**20),
        cost_estimate=pl.CostEstimate(
            flops=4 * per_kv * requests * tokens * head_dim + 2 * requests * per_kv * head_dim * KVH * width,
            bytes_accessed=2 * (kv_pages.size + output_proj.size),
            transcendentals=requests * ROWS * tokens,
        ),
        name="attend_project",
    )(lengths, request_moves, page_table, page_table, page_scale, *q_parts, *nk_parts, kv_pages, output_proj)

    blocks = [parts[0]] + [toward(parts[k], 0, k) for k in range(1, KVH)]
    arrived = [
        toward(parts[KVH + (d - 1) * KVH + k], d, k) for d in range(1, replicas) for k in range(KVH)
    ]
    return pl.pallas_call(
        functools.partial(combine, replicas),
        out_shape=jax.ShapeDtypeStruct(residual.shape, residual.dtype),
        in_specs=[smem] + [vmem] * (1 + KVH + leaving),
        out_specs=vmem,
        name="combine",
    )(request_moves, residual, *blocks, *arrived)


def solution(mesh):
    return jax.shard_map(
        on_device,
        mesh=mesh,
        in_specs=(
            P(("parts", "replica"), None, None, None),
            P(("parts", "replica"), None),
            P(("parts", "replica"), None),
            P("parts"),
            P("parts"),
            P(("parts", "replica"), None),
            P(("parts", "replica"), None),
            P("replica", None),
            P(("parts", "replica"), None),
        ),
        out_specs=P(("parts", "replica"), None),
        check_vma=False,
    )
```

```python
import functools
import math

import jax
import jax.numpy as jnp
from jax import lax
from jax.experimental import pallas as pl
from jax.experimental.pallas import tpu as pltpu
from jax.sharding import PartitionSpec as P

KVH = 8
ROWS = 8
CHUNK = 4
LOADS = 8
F32 = jnp.float32
BF16 = jnp.bfloat16
VMEM = pl.BlockSpec(memory_space=pltpu.VMEM)
HBM = pl.BlockSpec(memory_space=pltpu.HBM)


def softmax_parts(scores, own):
    highest = jnp.maximum(jnp.max(scores, axis=1, keepdims=True), own)
    weights = jnp.exp(scores - highest)
    own_weight = jnp.exp(own - highest)
    return weights, own_weight, 1.0 / (jnp.sum(weights, axis=1, keepdims=True) + own_weight)


def split_scaled(weights, inverse, value_scale):
    scaled = (weights * inverse).astype(BF16).astype(F32) * value_scale
    high = scaled.astype(BF16)
    low = (scaled - high.astype(F32)).astype(BF16)
    return jnp.concatenate([high, low], axis=0)


def dot_keys(queries, keys):
    return lax.dot_general(queries, keys, (((1,), (1,)), ((), ())), preferred_element_type=F32)


def attend_resident(
    replicas,
    per_kv,
    lengths_h,
    moves_h,
    table_h,
    scale_h,
    queries_h,
    new_kv_h,
    kv_pages,
    proj,
    attended,
    weights_out,
    away_kv,
    away_info,
    goal_mask,
    here_mask,
    lengths,
    moves,
    table_s,
    table_v,
    scale_v,
    queries,
    new_kv,
    pool,
    target,
    q_rows,
    page_scales,
    key_scale,
    value_scale,
    scores,
    mixed,
    small_sem,
    kv_sem,
    w_sem,
):
    requests, max_pages = table_h.shape
    pages, _, page_len, head_dim = kv_pages.shape
    tokens = max_pages * page_len
    slots = moves_h.shape[0]
    factor = 1.0 / math.sqrt(head_dim)
    replica = lax.axis_index("replica") // KVH

    small = [
        pltpu.make_async_copy(src, dst, small_sem.at[i])
        for i, (src, dst) in enumerate(
            [
                (moves_h, moves),
                (lengths_h, lengths),
                (table_h, table_s),
                (table_h, table_v),
                (scale_h, scale_v),
                (queries_h, queries),
                (new_kv_h, new_kv),
            ]
        )
    ]
    for copy in small:
        copy.start()
    step = pages // LOADS
    kv_copies = [
        pltpu.make_async_copy(kv_pages.at[pl.ds(i * step, step)], pool.at[pl.ds(i * step, step)], kv_sem.at[i])
        for i in range(LOADS)
    ]
    for copy in kv_copies:
        copy.start()
    step = proj.shape[0] // LOADS
    w_copies = [
        pltpu.make_async_copy(proj.at[pl.ds(i * step, step)], weights_out.at[pl.ds(i * step, step)], w_sem.at[i])
        for i in range(LOADS)
    ]
    for copy in w_copies:
        copy.start()
    for copy in small:
        copy.wait()

    def place(g, carry):
        slot = moves[g]

        @pl.when(slot // requests == replica)
        def _():
            target[slot % requests] = g

        return carry

    lax.fori_loop(0, slots, place, 0)
    row_ids = lax.broadcasted_iota(jnp.int32, (requests, head_dim), 0)
    leaver = []
    for d in range(1, replicas):
        out_slot = jnp.int32(0)
        here = jnp.int32(0)
        for j in range(requests):
            away = lax.rem(target[j] // requests - replica + replicas, replicas)
            out_slot = jnp.where(away == d, j, out_slot)
            behind = lax.rem(replica - moves[replica * requests + j] // requests + replicas, replicas)
            here = jnp.where(behind == d, j, here)
        leaver.append(out_slot)
        goal_mask[d - 1] = (row_ids == lax.rem(target[out_slot], requests)).astype(F32)
        here_mask[d - 1] = (row_ids == here).astype(F32)

    q_all = queries[...].astype(F32)
    nk_all = new_kv[...].astype(F32)
    q_rows[...] = jnp.zeros_like(q_rows)
    for h in range(per_kv):
        q_rows[pl.ds(h, requests, stride=ROWS), :] = q_all[:, h * head_dim : (h + 1) * head_dim]

    page_ids = lax.broadcasted_iota(jnp.int32, (pages, max_pages), 0)
    scale_rows = scale_v[...]
    for j in range(requests):
        chosen = (page_ids == table_v[j : j + 1, :]).astype(F32).astype(BF16)
        page_scales[:, j : j + 1, :] = jnp.dot(scale_rows, chosen, preferred_element_type=F32)[:, None, :]
    spread = (
        lax.broadcasted_iota(jnp.int32, (max_pages, tokens), 1) // page_len
        == lax.broadcasted_iota(jnp.int32, (max_pages, tokens), 0)
    ).astype(F32).astype(BF16)
    key_scale[...] = jnp.dot(page_scales[0].astype(BF16), spread, preferred_element_type=F32) * factor
    value_scale[...] = jnp.dot(page_scales[1].astype(BF16), spread, preferred_element_type=F32)
    places = lax.broadcasted_iota(jnp.int32, (1, tokens), 1)
    for d in range(1, replicas):
        out_slot = leaver[d - 1]
        away_info[d - 1, 0:1, :] = key_scale[pl.ds(out_slot, 1), :]
        away_info[d - 1, 1:2, :] = value_scale[pl.ds(out_slot, 1), :]
        away_info[d - 1, 2:3, :] = (places < lengths[replica * requests + out_slot]).astype(F32)

    for copy in kv_copies:
        copy.wait()

    for d in range(1, replicas):

        def hand_on(p, carry, d=d):
            away_kv[d - 1, p] = pool[table_s[leaver[d - 1], p]]
            return carry

        lax.fori_loop(0, max_pages, hand_on, 0, unroll=4)

    def gather(j, c, which):
        return jnp.concatenate([pool[table_s[j, c * CHUNK + i], which] for i in range(CHUNK)], axis=0)

    span = CHUNK * page_len
    own = []
    for j in range(requests):
        rows = slice(j * ROWS, (j + 1) * ROWS)
        q = q_rows[rows, :]
        own.append(jnp.sum(q * nk_all[j : j + 1, :head_dim], axis=1, keepdims=True) * factor)
        q = q.astype(BF16)
        context = lengths[replica * requests + j]
        for c in range(max_pages // CHUNK):
            columns = slice(c * span, (c + 1) * span)
            raw = dot_keys(q, gather(j, c, 0)) * key_scale[j : j + 1, columns]
            scores[rows, columns] = jnp.where(places[:, columns] < context, raw, -jnp.inf)
    stats = []
    for j in range(requests):
        rows = slice(j * ROWS, (j + 1) * ROWS)
        weights, own_weight, inverse = softmax_parts(scores[rows, :], own[j])
        scores[rows, :] = weights
        stats.append((own_weight, inverse))
    for j in range(requests):
        rows = slice(j * ROWS, (j + 1) * ROWS)
        own_weight, inverse = stats[j]
        total = jnp.zeros((2 * ROWS, head_dim), F32)
        for c in range(max_pages // CHUNK):
            columns = slice(c * span, (c + 1) * span)
            both = split_scaled(scores[rows, columns], inverse, value_scale[j : j + 1, columns])
            total = total + jnp.dot(both, gather(j, c, 1), preferred_element_type=F32)
        own_weight = (own_weight * inverse).astype(BF16).astype(F32)
        mixed[rows, :] = total[:ROWS] + total[ROWS:] + own_weight * nk_all[j : j + 1, head_dim:]
    for h in range(per_kv):
        attended[:, h * head_dim : (h + 1) * head_dim] = mixed[pl.ds(h, requests, stride=ROWS), :]
    for copy in w_copies:
        copy.wait()


def attend_away(replicas, per_kv, *refs):
    count = replicas - 1
    away_kv, away_info, goal_mask = refs[:3]
    queries = refs[3 : 3 + count]
    new_kv = refs[3 + count : 3 + 2 * count]
    outs = refs[3 + 2 * count : 3 + 3 * count]
    q_rows, scores = refs[3 + 3 * count :]
    max_pages, _, page_len, head_dim = away_kv.shape[1:]
    factor = 1.0 / math.sqrt(head_dim)
    span = CHUNK * page_len
    for d in range(count):
        pick = goal_mask[d]
        q_all = queries[d][...].astype(F32)
        q_rows[...] = jnp.zeros_like(q_rows)
        for h in range(per_kv):
            q_rows[h : h + 1, :] = jnp.sum(q_all[:, h * head_dim : (h + 1) * head_dim] * pick, axis=0, keepdims=True)
        nk_all = new_kv[d][...].astype(F32)
        new_key = jnp.sum(nk_all[:, :head_dim] * pick, axis=0, keepdims=True)
        new_value = jnp.sum(nk_all[:, head_dim:] * pick, axis=0, keepdims=True)
        q = q_rows[...]
        own = jnp.sum(q * new_key, axis=1, keepdims=True) * factor
        q = q.astype(BF16)
        for c in range(max_pages // CHUNK):
            columns = slice(c * span, (c + 1) * span)
            keys = away_kv[d, c * CHUNK : (c + 1) * CHUNK, 0].reshape(span, head_dim)
            raw = dot_keys(q, keys) * away_info[d, 0:1, columns]
            scores[:, columns] = jnp.where(away_info[d, 2:3, columns] > 0, raw, -jnp.inf)
        weights, own_weight, inverse = softmax_parts(scores[...], own)
        total = jnp.zeros((2 * ROWS, head_dim), F32)
        for c in range(max_pages // CHUNK):
            columns = slice(c * span, (c + 1) * span)
            values = away_kv[d, c * CHUNK : (c + 1) * CHUNK, 1].reshape(span, head_dim)
            both = split_scaled(weights[:, columns], inverse, away_info[d, 1:2, columns])
            total = total + jnp.dot(both, values, preferred_element_type=F32)
        own_weight = (own_weight * inverse).astype(BF16).astype(F32)
        mixed = total[:ROWS] + total[ROWS:] + own_weight * new_value
        for h in range(per_kv):
            outs[d][:, h * head_dim : (h + 1) * head_dim] = mixed[h : h + 1, :]


def project(replicas, per_kv, attended, proj, here_mask, *refs):
    arrived = refs[: replicas - 1]
    out = refs[-1]
    head_dim = here_mask.shape[2]
    pieces = []
    for h in range(per_kv):
        columns = slice(h * head_dim, (h + 1) * head_dim)
        piece = attended[:, columns]
        for d in range(replicas - 1):
            piece = jnp.where(here_mask[d] > 0, arrived[d][:, columns], piece)
        pieces.append(piece)
    mixture = jnp.concatenate(pieces, axis=1).astype(BF16)
    width = out.shape[2]
    for k in range(out.shape[0]):
        part = jnp.dot(mixture, proj[:, k * width : (k + 1) * width], preferred_element_type=F32)
        out[k] = part.astype(out.dtype)


def on_device(
    kv_pages, page_scale, page_table, lengths, request_moves, queries, new_kv, output_proj, residual
):
    devices = lax.axis_size("replica")
    replicas = devices // KVH
    requests, max_pages = page_table.shape
    pages, _, page_len, head_dim = kv_pages.shape
    per_kv = queries.shape[1] // head_dim
    width = output_proj.shape[1] // KVH
    tokens = max_pages * page_len
    count = replicas - 1

    def toward(value, steps):
        pairs = [(i, (i + steps * KVH) % devices) for i in range(devices)]
        return lax.ppermute(value, "replica", pairs)

    came_q = [toward(queries, -d) for d in range(1, replicas)]
    came_nk = [toward(new_kv, -d) for d in range(1, replicas)]

    def shape(*dims, dtype=F32):
        return jax.ShapeDtypeStruct(dims, dtype)

    attended, proj, away_kv, away_info, goal_mask, here_mask = pl.pallas_call(
        functools.partial(attend_resident, replicas, per_kv),
        out_shape=[
            shape(requests, per_kv * head_dim),
            shape(*output_proj.shape, dtype=BF16),
            shape(count, max_pages, 2, page_len, head_dim, dtype=BF16),
            shape(count, 8, tokens),
            shape(count, requests, head_dim),
            shape(count, requests, head_dim),
        ],
        in_specs=[HBM] * 8,
        out_specs=[VMEM] * 6,
        scratch_shapes=[
            pltpu.SMEM(lengths.shape, jnp.int32),
            pltpu.SMEM(request_moves.shape, jnp.int32),
            pltpu.SMEM(page_table.shape, jnp.int32),
            pltpu.VMEM(page_table.shape, jnp.int32),
            pltpu.VMEM((2, pages), BF16),
            pltpu.VMEM(queries.shape, BF16),
            pltpu.VMEM(new_kv.shape, BF16),
            pltpu.VMEM(kv_pages.shape, BF16),
            pltpu.SMEM((requests,), jnp.int32),
            pltpu.VMEM((requests * ROWS, head_dim), F32),
            pltpu.VMEM((2, requests, max_pages), F32),
            pltpu.VMEM((requests, tokens), F32),
            pltpu.VMEM((requests, tokens), F32),
            pltpu.VMEM((requests * ROWS, tokens), F32),
            pltpu.VMEM((requests * ROWS, head_dim), F32),
            pltpu.SemaphoreType.DMA((7,)),
            pltpu.SemaphoreType.DMA((LOADS,)),
            pltpu.SemaphoreType.DMA((LOADS,)),
        ],
        compiler_params=pltpu.CompilerParams(vmem_limit_bytes=16 * 2**20),
        cost_estimate=pl.CostEstimate(
            flops=4 * per_kv * requests * tokens * head_dim,
            bytes_accessed=2 * (kv_pages.size + output_proj.size),
            transcendentals=requests * ROWS * tokens,
        ),
        name="attend_resident",
    )(
        *(
            pltpu.with_memory_space_constraint(x, pltpu.HBM)
            for x in (lengths, request_moves, page_table, page_scale.T, queries, new_kv, kv_pages, output_proj)
        )
    )

    rows = pl.pallas_call(
        functools.partial(attend_away, replicas, per_kv),
        out_shape=[shape(1, per_kv * head_dim)] * count,
        in_specs=[VMEM] * (3 + 2 * count),
        out_specs=[VMEM] * count,
        scratch_shapes=[pltpu.VMEM((ROWS, head_dim), F32), pltpu.VMEM((ROWS, tokens), F32)],
        name="attend_away",
    )(away_kv, away_info, goal_mask, *came_q, *came_nk)
    arrived = [toward(rows[d - 1], d) for d in range(1, replicas)]

    parts = pl.pallas_call(
        functools.partial(project, replicas, per_kv),
        out_shape=shape(KVH, requests, width),
        in_specs=[VMEM] * (3 + count),
        out_specs=VMEM,
        name="project",
    )(attended, proj, here_mask, *arrived)

    groups = [list(range(r * KVH, (r + 1) * KVH)) for r in range(replicas)]
    parts = lax.all_to_all(parts, "replica", 0, 0, axis_index_groups=groups, tiled=True)
    return (residual.astype(F32) + jnp.sum(parts, axis=0)).astype(BF16)


def solution(mesh):
    return jax.shard_map(
        on_device,
        mesh=mesh,
        in_specs=(
            P(("parts", "replica"), None, None, None),
            P(("parts", "replica"), None),
            P(("parts", "replica"), None),
            P("parts"),
            P("parts"),
            P(("parts", "replica"), None),
            P(("parts", "replica"), None),
            P("replica", None),
            P(("parts", "replica"), None),
        ),
        out_specs=P(("parts", "replica"), None),
        check_vma=False,
    )
```

```python
import functools
import math

import jax
import jax.numpy as jnp
from jax import lax
from jax.experimental import pallas as pl
from jax.experimental.pallas import tpu as pltpu
from jax.sharding import PartitionSpec as P

KVH = 8
ROWS = 8
CHUNK = 4
LOADS = 8
F32 = jnp.float32
BF16 = jnp.bfloat16
VMEM = pl.BlockSpec(memory_space=pltpu.VMEM)
HBM = pl.BlockSpec(memory_space=pltpu.HBM)


def softmax_parts(scores, own):
    highest = jnp.maximum(jnp.max(scores, axis=1, keepdims=True), own)
    weights = jnp.exp(scores - highest)
    own_weight = jnp.exp(own - highest)
    return weights, own_weight, 1.0 / (jnp.sum(weights, axis=1, keepdims=True) + own_weight)


def split_scaled(weights, inverse, value_scale):
    scaled = (weights * inverse).astype(BF16).astype(F32) * value_scale
    high = scaled.astype(BF16)
    low = (scaled - high.astype(F32)).astype(BF16)
    return jnp.concatenate([high, low], axis=0)


def dot_keys(queries, keys):
    return lax.dot_general(queries, keys, (((1,), (1,)), ((), ())), preferred_element_type=F32)


def attend_resident(
    replicas,
    per_kv,
    lengths_h,
    moves_h,
    table_h,
    scale_h,
    queries_h,
    new_kv_h,
    kv_pages,
    proj,
    attended,
    weights_out,
    away_kv,
    away_info,
    goal_mask,
    here_mask,
    lengths,
    moves,
    table_s,
    table_v,
    scale_v,
    queries,
    new_kv,
    pool,
    target,
    q_rows,
    page_scales,
    key_scale,
    value_scale,
    scores,
    mixed,
    small_sem,
    kv_sem,
    w_sem,
):
    requests, max_pages = table_h.shape
    pages, _, page_len, head_dim = kv_pages.shape
    tokens = max_pages * page_len
    slots = moves_h.shape[0]
    factor = 1.0 / math.sqrt(head_dim)
    replica = lax.axis_index("replica") // KVH

    small = [
        pltpu.make_async_copy(src, dst, small_sem.at[i])
        for i, (src, dst) in enumerate(
            [
                (moves_h, moves),
                (lengths_h, lengths),
                (table_h, table_s),
                (table_h, table_v),
                (scale_h, scale_v),
                (queries_h, queries),
                (new_kv_h, new_kv),
            ]
        )
    ]
    for copy in small:
        copy.start()
    step = pages // LOADS
    kv_copies = [
        pltpu.make_async_copy(kv_pages.at[pl.ds(i * step, step)], pool.at[pl.ds(i * step, step)], kv_sem.at[i])
        for i in range(LOADS)
    ]
    for copy in kv_copies:
        copy.start()
    step = proj.shape[0] // LOADS
    w_copies = [
        pltpu.make_async_copy(proj.at[pl.ds(i * step, step)], weights_out.at[pl.ds(i * step, step)], w_sem.at[i])
        for i in range(LOADS)
    ]
    for copy in w_copies:
        copy.start()
    for copy in small:
        copy.wait()

    def place(g, carry):
        slot = moves[g]

        @pl.when(slot // requests == replica)
        def _():
            target[slot % requests] = g

        return carry

    lax.fori_loop(0, slots, place, 0)
    row_ids = lax.broadcasted_iota(jnp.int32, (requests, head_dim), 0)
    leaver = []
    for d in range(1, replicas):
        out_slot = jnp.int32(0)
        here = jnp.int32(0)
        for j in range(requests):
            away = lax.rem(target[j] // requests - replica + replicas, replicas)
            out_slot = jnp.where(away == d, j, out_slot)
            behind = lax.rem(replica - moves[replica * requests + j] // requests + replicas, replicas)
            here = jnp.where(behind == d, j, here)
        leaver.append(out_slot)
        goal_mask[d - 1] = (row_ids == lax.rem(target[out_slot], requests)).astype(F32)
        here_mask[d - 1] = (row_ids == here).astype(F32)

    q_all = queries[...].astype(F32)
    nk_all = new_kv[...].astype(F32)
    q_rows[...] = jnp.zeros_like(q_rows)
    for h in range(per_kv):
        q_rows[pl.ds(h, requests, stride=ROWS), :] = q_all[:, h * head_dim : (h + 1) * head_dim]

    page_ids = lax.broadcasted_iota(jnp.int32, (pages, max_pages), 0)
    scale_rows = scale_v[...]
    for j in range(requests):
        chosen = (page_ids == table_v[j : j + 1, :]).astype(F32).astype(BF16)
        page_scales[:, j : j + 1, :] = jnp.dot(scale_rows, chosen, preferred_element_type=F32)[:, None, :]
    spread = (
        lax.broadcasted_iota(jnp.int32, (max_pages, tokens), 1) // page_len
        == lax.broadcasted_iota(jnp.int32, (max_pages, tokens), 0)
    ).astype(F32).astype(BF16)
    key_scale[...] = jnp.dot(page_scales[0].astype(BF16), spread, preferred_element_type=F32) * factor
    value_scale[...] = jnp.dot(page_scales[1].astype(BF16), spread, preferred_element_type=F32)
    places = lax.broadcasted_iota(jnp.int32, (1, tokens), 1)
    for d in range(1, replicas):
        out_slot = leaver[d - 1]
        away_info[d - 1, 0:1, :] = key_scale[pl.ds(out_slot, 1), :]
        away_info[d - 1, 1:2, :] = value_scale[pl.ds(out_slot, 1), :]
        away_info[d - 1, 2:3, :] = (places < lengths[replica * requests + out_slot]).astype(F32)

    for copy in kv_copies:
        copy.wait()

    for d in range(1, replicas):

        def hand_on(p, carry, d=d):
            away_kv[d - 1, p] = pool[table_s[leaver[d - 1], p]]
            return carry

        lax.fori_loop(0, max_pages, hand_on, 0, unroll=4)

    def gather(j, c, which):
        return jnp.concatenate([pool[table_s[j, c * CHUNK + i], which] for i in range(CHUNK)], axis=0)

    span = CHUNK * page_len
    own = []
    for j in range(requests):
        rows = slice(j * ROWS, (j + 1) * ROWS)
        q = q_rows[rows, :]
        own.append(jnp.sum(q * nk_all[j : j + 1, :head_dim], axis=1, keepdims=True) * factor)
        q = q.astype(BF16)
        context = lengths[replica * requests + j]
        for c in range(max_pages // CHUNK):
            columns = slice(c * span, (c + 1) * span)
            raw = dot_keys(q, gather(j, c, 0)) * key_scale[j : j + 1, columns]
            scores[rows, columns] = jnp.where(places[:, columns] < context, raw, -jnp.inf)
    stats = []
    for j in range(requests):
        rows = slice(j * ROWS, (j + 1) * ROWS)
        weights, own_weight, inverse = softmax_parts(scores[rows, :], own[j])
        scores[rows, :] = weights
        stats.append((own_weight, inverse))
    for j in range(requests):
        rows = slice(j * ROWS, (j + 1) * ROWS)
        own_weight, inverse = stats[j]
        total = jnp.zeros((2 * ROWS, head_dim), F32)
        for c in range(max_pages // CHUNK):
            columns = slice(c * span, (c + 1) * span)
            both = split_scaled(scores[rows, columns], inverse, value_scale[j : j + 1, columns])
            total = total + jnp.dot(both, gather(j, c, 1), preferred_element_type=F32)
        own_weight = (own_weight * inverse).astype(BF16).astype(F32)
        mixed[rows, :] = total[:ROWS] + total[ROWS:] + own_weight * nk_all[j : j + 1, head_dim:]
    for h in range(per_kv):
        attended[:, h * head_dim : (h + 1) * head_dim] = mixed[pl.ds(h, requests, stride=ROWS), :]
    for copy in w_copies:
        copy.wait()


def attend_away(replicas, per_kv, *refs):
    count = replicas - 1
    away_kv, away_info, goal_mask = refs[:3]
    queries = refs[3 : 3 + count]
    new_kv = refs[3 + count : 3 + 2 * count]
    outs = refs[3 + 2 * count : 3 + 3 * count]
    q_rows, scores = refs[3 + 3 * count :]
    max_pages, _, page_len, head_dim = away_kv.shape[1:]
    factor = 1.0 / math.sqrt(head_dim)
    span = CHUNK * page_len
    for d in range(count):
        pick = goal_mask[d]
        q_all = queries[d][...].astype(F32)
        q_rows[...] = jnp.zeros_like(q_rows)
        for h in range(per_kv):
            q_rows[h : h + 1, :] = jnp.sum(q_all[:, h * head_dim : (h + 1) * head_dim] * pick, axis=0, keepdims=True)
        nk_all = new_kv[d][...].astype(F32)
        new_key = jnp.sum(nk_all[:, :head_dim] * pick, axis=0, keepdims=True)
        new_value = jnp.sum(nk_all[:, head_dim:] * pick, axis=0, keepdims=True)
        q = q_rows[...]
        own = jnp.sum(q * new_key, axis=1, keepdims=True) * factor
        q = q.astype(BF16)
        for c in range(max_pages // CHUNK):
            columns = slice(c * span, (c + 1) * span)
            keys = away_kv[d, c * CHUNK : (c + 1) * CHUNK, 0].reshape(span, head_dim)
            raw = dot_keys(q, keys) * away_info[d, 0:1, columns]
            scores[:, columns] = jnp.where(away_info[d, 2:3, columns] > 0, raw, -jnp.inf)
        weights, own_weight, inverse = softmax_parts(scores[...], own)
        total = jnp.zeros((2 * ROWS, head_dim), F32)
        for c in range(max_pages // CHUNK):
            columns = slice(c * span, (c + 1) * span)
            values = away_kv[d, c * CHUNK : (c + 1) * CHUNK, 1].reshape(span, head_dim)
            both = split_scaled(weights[:, columns], inverse, away_info[d, 1:2, columns])
            total = total + jnp.dot(both, values, preferred_element_type=F32)
        own_weight = (own_weight * inverse).astype(BF16).astype(F32)
        mixed = total[:ROWS] + total[ROWS:] + own_weight * new_value
        for h in range(per_kv):
            outs[d][:, h * head_dim : (h + 1) * head_dim] = mixed[h : h + 1, :]


def on_device(
    kv_pages, page_scale, page_table, lengths, request_moves, queries, new_kv, output_proj, residual
):
    devices = lax.axis_size("replica")
    replicas = devices // KVH
    requests, max_pages = page_table.shape
    pages, _, page_len, head_dim = kv_pages.shape
    per_kv = queries.shape[1] // head_dim
    width = output_proj.shape[1] // KVH
    tokens = max_pages * page_len
    count = replicas - 1

    def toward(value, steps):
        pairs = [(i, (i + steps * KVH) % devices) for i in range(devices)]
        return lax.ppermute(value, "replica", pairs)

    came_q = [toward(queries, -d) for d in range(1, replicas)]
    came_nk = [toward(new_kv, -d) for d in range(1, replicas)]

    def shape(*dims, dtype=F32):
        return jax.ShapeDtypeStruct(dims, dtype)

    attended, proj, away_kv, away_info, goal_mask, here_mask = pl.pallas_call(
        functools.partial(attend_resident, replicas, per_kv),
        out_shape=[
            shape(requests, per_kv * head_dim),
            shape(*output_proj.shape, dtype=BF16),
            shape(count, max_pages, 2, page_len, head_dim, dtype=BF16),
            shape(count, 8, tokens),
            shape(count, requests, head_dim),
            shape(count, requests, head_dim),
        ],
        in_specs=[HBM] * 8,
        out_specs=[VMEM] * 6,
        scratch_shapes=[
            pltpu.SMEM(lengths.shape, jnp.int32),
            pltpu.SMEM(request_moves.shape, jnp.int32),
            pltpu.SMEM(page_table.shape, jnp.int32),
            pltpu.VMEM(page_table.shape, jnp.int32),
            pltpu.VMEM((2, pages), BF16),
            pltpu.VMEM(queries.shape, BF16),
            pltpu.VMEM(new_kv.shape, BF16),
            pltpu.VMEM(kv_pages.shape, BF16),
            pltpu.SMEM((requests,), jnp.int32),
            pltpu.VMEM((requests * ROWS, head_dim), F32),
            pltpu.VMEM((2, requests, max_pages), F32),
            pltpu.VMEM((requests, tokens), F32),
            pltpu.VMEM((requests, tokens), F32),
            pltpu.VMEM((requests * ROWS, tokens), F32),
            pltpu.VMEM((requests * ROWS, head_dim), F32),
            pltpu.SemaphoreType.DMA((7,)),
            pltpu.SemaphoreType.DMA((LOADS,)),
            pltpu.SemaphoreType.DMA((LOADS,)),
        ],
        compiler_params=pltpu.CompilerParams(vmem_limit_bytes=16 * 2**20),
        cost_estimate=pl.CostEstimate(
            flops=4 * per_kv * requests * tokens * head_dim,
            bytes_accessed=2 * (kv_pages.size + output_proj.size),
            transcendentals=requests * ROWS * tokens,
        ),
        name="attend_resident",
    )(
        *(
            pltpu.with_memory_space_constraint(x, pltpu.HBM)
            for x in (lengths, request_moves, page_table, page_scale.T, queries, new_kv, kv_pages, output_proj)
        )
    )

    rows = pl.pallas_call(
        functools.partial(attend_away, replicas, per_kv),
        out_shape=[shape(1, per_kv * head_dim)] * count,
        in_specs=[VMEM] * (3 + 2 * count),
        out_specs=[VMEM] * count,
        scratch_shapes=[pltpu.VMEM((ROWS, head_dim), F32), pltpu.VMEM((ROWS, tokens), F32)],
        compiler_params=pltpu.CompilerParams(vmem_limit_bytes=4 * 2**20),
        name="attend_away",
    )(away_kv, away_info, goal_mask, *came_q, *came_nk)
    arrived = [toward(rows[d - 1], d) for d in range(1, replicas)]

    for d in range(count):
        attended = jnp.where(here_mask[d][:, :1] > 0, arrived[d], attended)
    parts = jnp.dot(attended.astype(BF16), proj, preferred_element_type=F32)
    parts = parts.reshape(requests, KVH, width).transpose(1, 0, 2).astype(BF16)

    groups = [list(range(r * KVH, (r + 1) * KVH)) for r in range(replicas)]
    parts = lax.all_to_all(parts, "replica", 0, 0, axis_index_groups=groups, tiled=True).astype(F32)
    return (residual.astype(F32) + jnp.sum(parts, axis=0)).astype(BF16)


def solution(mesh):
    return jax.shard_map(
        on_device,
        mesh=mesh,
        in_specs=(
            P(("parts", "replica"), None, None, None),
            P(("parts", "replica"), None),
            P(("parts", "replica"), None),
            P("parts"),
            P("parts"),
            P(("parts", "replica"), None),
            P(("parts", "replica"), None),
            P("replica", None),
            P(("parts", "replica"), None),
        ),
        out_specs=P(("parts", "replica"), None),
        check_vma=False,
    )
```

```python
import functools
import math

import jax
import jax.numpy as jnp
from jax import lax
from jax.experimental import pallas as pl
from jax.experimental.pallas import tpu as pltpu
from jax.sharding import PartitionSpec as P

KVH = 8
ROWS = 8
CHUNK = 4
LOADS = 8
F32 = jnp.float32
BF16 = jnp.bfloat16
VMEM = pl.BlockSpec(memory_space=pltpu.VMEM)
HBM = pl.BlockSpec(memory_space=pltpu.HBM)


def softmax_parts(scores, own):
    highest = jnp.maximum(jnp.max(scores, axis=1, keepdims=True), own)
    weights = jnp.exp(scores - highest)
    own_weight = jnp.exp(own - highest)
    return weights, own_weight, 1.0 / (jnp.sum(weights, axis=1, keepdims=True) + own_weight)


def split_scaled(weights, inverse, value_scale):
    scaled = (weights * inverse).astype(BF16).astype(F32) * value_scale
    high = scaled.astype(BF16)
    low = (scaled - high.astype(F32)).astype(BF16)
    return jnp.concatenate([high, low], axis=0)


def dot_keys(queries, keys):
    return lax.dot_general(queries, keys, (((1,), (1,)), ((), ())), preferred_element_type=F32)


def attend_resident(
    replicas,
    per_kv,
    lengths_h,
    moves_h,
    table_h,
    scale_h,
    queries_h,
    new_kv_h,
    kv_pages,
    attended,
    away_kv,
    away_info,
    goal_mask,
    here_mask,
    lengths,
    moves,
    table_s,
    table_v,
    scale_v,
    queries,
    new_kv,
    pool,
    target,
    q_rows,
    page_scales,
    key_scale,
    value_scale,
    scores,
    mixed,
    small_sem,
    kv_sem,
):
    requests, max_pages = table_h.shape
    pages, _, page_len, head_dim = kv_pages.shape
    tokens = max_pages * page_len
    slots = moves_h.shape[0]
    factor = 1.0 / math.sqrt(head_dim)
    replica = lax.axis_index("replica") // KVH

    small = [
        pltpu.make_async_copy(src, dst, small_sem.at[i])
        for i, (src, dst) in enumerate(
            [
                (moves_h, moves),
                (lengths_h, lengths),
                (table_h, table_s),
                (table_h, table_v),
                (scale_h, scale_v),
                (queries_h, queries),
                (new_kv_h, new_kv),
            ]
        )
    ]
    for copy in small:
        copy.start()
    step = pages // LOADS
    kv_copies = [
        pltpu.make_async_copy(kv_pages.at[pl.ds(i * step, step)], pool.at[pl.ds(i * step, step)], kv_sem.at[i])
        for i in range(LOADS)
    ]
    for copy in kv_copies:
        copy.start()
    for copy in small:
        copy.wait()

    def place(g, carry):
        slot = moves[g]

        @pl.when(slot // requests == replica)
        def _():
            target[slot % requests] = g

        return carry

    lax.fori_loop(0, slots, place, 0)
    row_ids = lax.broadcasted_iota(jnp.int32, (requests, head_dim), 0)
    leaver = []
    for d in range(1, replicas):
        out_slot = jnp.int32(0)
        here = jnp.int32(0)
        for j in range(requests):
            away = lax.rem(target[j] // requests - replica + replicas, replicas)
            out_slot = jnp.where(away == d, j, out_slot)
            behind = lax.rem(replica - moves[replica * requests + j] // requests + replicas, replicas)
            here = jnp.where(behind == d, j, here)
        leaver.append(out_slot)
        goal_mask[d - 1] = (row_ids == lax.rem(target[out_slot], requests)).astype(F32)
        here_mask[d - 1] = (row_ids == here).astype(F32)

    q_all = queries[...].astype(F32)
    nk_all = new_kv[...].astype(F32)
    q_rows[...] = jnp.zeros_like(q_rows)
    for h in range(per_kv):
        q_rows[pl.ds(h, requests, stride=ROWS), :] = q_all[:, h * head_dim : (h + 1) * head_dim]

    page_ids = lax.broadcasted_iota(jnp.int32, (pages, max_pages), 0)
    scale_rows = scale_v[...]
    for j in range(requests):
        chosen = (page_ids == table_v[j : j + 1, :]).astype(F32).astype(BF16)
        page_scales[:, j : j + 1, :] = jnp.dot(scale_rows, chosen, preferred_element_type=F32)[:, None, :]
    spread = (
        lax.broadcasted_iota(jnp.int32, (max_pages, tokens), 1) // page_len
        == lax.broadcasted_iota(jnp.int32, (max_pages, tokens), 0)
    ).astype(F32).astype(BF16)
    key_scale[...] = jnp.dot(page_scales[0].astype(BF16), spread, preferred_element_type=F32) * factor
    value_scale[...] = jnp.dot(page_scales[1].astype(BF16), spread, preferred_element_type=F32)
    places = lax.broadcasted_iota(jnp.int32, (1, tokens), 1)
    for d in range(1, replicas):
        out_slot = leaver[d - 1]
        away_info[d - 1, 0:1, :] = key_scale[pl.ds(out_slot, 1), :]
        away_info[d - 1, 1:2, :] = value_scale[pl.ds(out_slot, 1), :]
        away_info[d - 1, 2:3, :] = (places < lengths[replica * requests + out_slot]).astype(F32)

    for copy in kv_copies:
        copy.wait()

    for d in range(1, replicas):

        def hand_on(p, carry, d=d):
            away_kv[d - 1, p] = pool[table_s[leaver[d - 1], p]]
            return carry

        lax.fori_loop(0, max_pages, hand_on, 0, unroll=4)

    def gather(j, c, which):
        return jnp.concatenate([pool[table_s[j, c * CHUNK + i], which] for i in range(CHUNK)], axis=0)

    span = CHUNK * page_len
    own = []
    for j in range(requests):
        rows = slice(j * ROWS, (j + 1) * ROWS)
        q = q_rows[rows, :]
        own.append(jnp.sum(q * nk_all[j : j + 1, :head_dim], axis=1, keepdims=True) * factor)
        q = q.astype(BF16)
        context = lengths[replica * requests + j]
        for c in range(max_pages // CHUNK):
            columns = slice(c * span, (c + 1) * span)
            raw = dot_keys(q, gather(j, c, 0)) * key_scale[j : j + 1, columns]
            scores[rows, columns] = jnp.where(places[:, columns] < context, raw, -jnp.inf)
    stats = []
    for j in range(requests):
        rows = slice(j * ROWS, (j + 1) * ROWS)
        weights, own_weight, inverse = softmax_parts(scores[rows, :], own[j])
        scores[rows, :] = weights
        stats.append((own_weight, inverse))
    for j in range(requests):
        rows = slice(j * ROWS, (j + 1) * ROWS)
        own_weight, inverse = stats[j]
        total = jnp.zeros((2 * ROWS, head_dim), F32)
        for c in range(max_pages // CHUNK):
            columns = slice(c * span, (c + 1) * span)
            both = split_scaled(scores[rows, columns], inverse, value_scale[j : j + 1, columns])
            total = total + jnp.dot(both, gather(j, c, 1), preferred_element_type=F32)
        own_weight = (own_weight * inverse).astype(BF16).astype(F32)
        mixed[rows, :] = total[:ROWS] + total[ROWS:] + own_weight * nk_all[j : j + 1, head_dim:]
    for h in range(per_kv):
        attended[:, h * head_dim : (h + 1) * head_dim] = mixed[pl.ds(h, requests, stride=ROWS), :]


def attend_away(replicas, per_kv, *refs):
    count = replicas - 1
    away_kv, away_info, goal_mask = refs[:3]
    queries = refs[3 : 3 + count]
    new_kv = refs[3 + count : 3 + 2 * count]
    outs = refs[3 + 2 * count : 3 + 3 * count]
    q_rows, scores = refs[3 + 3 * count :]
    max_pages, _, page_len, head_dim = away_kv.shape[1:]
    factor = 1.0 / math.sqrt(head_dim)
    span = CHUNK * page_len
    for d in range(count):
        pick = goal_mask[d]
        q_all = queries[d][...].astype(F32)
        q_rows[...] = jnp.zeros_like(q_rows)
        for h in range(per_kv):
            q_rows[h : h + 1, :] = jnp.sum(q_all[:, h * head_dim : (h + 1) * head_dim] * pick, axis=0, keepdims=True)
        nk_all = new_kv[d][...].astype(F32)
        new_key = jnp.sum(nk_all[:, :head_dim] * pick, axis=0, keepdims=True)
        new_value = jnp.sum(nk_all[:, head_dim:] * pick, axis=0, keepdims=True)
        q = q_rows[...]
        own = jnp.sum(q * new_key, axis=1, keepdims=True) * factor
        q = q.astype(BF16)
        for c in range(max_pages // CHUNK):
            columns = slice(c * span, (c + 1) * span)
            keys = away_kv[d, c * CHUNK : (c + 1) * CHUNK, 0].reshape(span, head_dim)
            raw = dot_keys(q, keys) * away_info[d, 0:1, columns]
            scores[:, columns] = jnp.where(away_info[d, 2:3, columns] > 0, raw, -jnp.inf)
        weights, own_weight, inverse = softmax_parts(scores[...], own)
        total = jnp.zeros((2 * ROWS, head_dim), F32)
        for c in range(max_pages // CHUNK):
            columns = slice(c * span, (c + 1) * span)
            values = away_kv[d, c * CHUNK : (c + 1) * CHUNK, 1].reshape(span, head_dim)
            both = split_scaled(weights[:, columns], inverse, away_info[d, 1:2, columns])
            total = total + jnp.dot(both, values, preferred_element_type=F32)
        own_weight = (own_weight * inverse).astype(BF16).astype(F32)
        mixed = total[:ROWS] + total[ROWS:] + own_weight * new_value
        for h in range(per_kv):
            outs[d][:, h * head_dim : (h + 1) * head_dim] = mixed[h : h + 1, :]


def on_device(
    kv_pages, page_scale, page_table, lengths, request_moves, queries, new_kv, output_proj, residual
):
    devices = lax.axis_size("replica")
    replicas = devices // KVH
    requests, max_pages = page_table.shape
    pages, _, page_len, head_dim = kv_pages.shape
    per_kv = queries.shape[1] // head_dim
    width = output_proj.shape[1] // KVH
    tokens = max_pages * page_len
    count = replicas - 1

    def toward(value, steps):
        pairs = [(i, (i + steps * KVH) % devices) for i in range(devices)]
        return lax.ppermute(value, "replica", pairs)

    came_q = [toward(queries, -d) for d in range(1, replicas)]
    came_nk = [toward(new_kv, -d) for d in range(1, replicas)]

    def shape(*dims, dtype=F32):
        return jax.ShapeDtypeStruct(dims, dtype)

    attended, away_kv, away_info, goal_mask, here_mask = pl.pallas_call(
        functools.partial(attend_resident, replicas, per_kv),
        out_shape=[
            shape(requests, per_kv * head_dim),
            shape(count, max_pages, 2, page_len, head_dim, dtype=BF16),
            shape(count, 8, tokens),
            shape(count, requests, head_dim),
            shape(count, requests, head_dim),
        ],
        in_specs=[HBM] * 7,
        out_specs=[VMEM] * 5,
        scratch_shapes=[
            pltpu.SMEM(lengths.shape, jnp.int32),
            pltpu.SMEM(request_moves.shape, jnp.int32),
            pltpu.SMEM(page_table.shape, jnp.int32),
            pltpu.VMEM(page_table.shape, jnp.int32),
            pltpu.VMEM((2, pages), BF16),
            pltpu.VMEM(queries.shape, BF16),
            pltpu.VMEM(new_kv.shape, BF16),
            pltpu.VMEM(kv_pages.shape, BF16),
            pltpu.SMEM((requests,), jnp.int32),
            pltpu.VMEM((requests * ROWS, head_dim), F32),
            pltpu.VMEM((2, requests, max_pages), F32),
            pltpu.VMEM((requests, tokens), F32),
            pltpu.VMEM((requests, tokens), F32),
            pltpu.VMEM((requests * ROWS, tokens), F32),
            pltpu.VMEM((requests * ROWS, head_dim), F32),
            pltpu.SemaphoreType.DMA((7,)),
            pltpu.SemaphoreType.DMA((LOADS,)),
        ],
        compiler_params=pltpu.CompilerParams(vmem_limit_bytes=16 * 2**20),
        cost_estimate=pl.CostEstimate(
            flops=4 * per_kv * requests * tokens * head_dim,
            bytes_accessed=2 * kv_pages.size,
            transcendentals=requests * ROWS * tokens,
        ),
        name="attend_resident",
    )(
        *(
            pltpu.with_memory_space_constraint(x, pltpu.HBM)
            for x in (lengths, request_moves, page_table, page_scale.T, queries, new_kv, kv_pages)
        )
    )

    rows = pl.pallas_call(
        functools.partial(attend_away, replicas, per_kv),
        out_shape=[shape(1, per_kv * head_dim)] * count,
        in_specs=[VMEM] * (3 + 2 * count),
        out_specs=[VMEM] * count,
        scratch_shapes=[pltpu.VMEM((ROWS, head_dim), F32), pltpu.VMEM((ROWS, tokens), F32)],
        compiler_params=pltpu.CompilerParams(vmem_limit_bytes=4 * 2**20),
        name="attend_away",
    )(away_kv, away_info, goal_mask, *came_q, *came_nk)
    arrived = [toward(rows[d - 1], d) for d in range(1, replicas)]

    for d in range(count):
        attended = jnp.where(here_mask[d][:, :1] > 0, arrived[d], attended)
    parts = jnp.dot(attended.astype(BF16), output_proj, preferred_element_type=F32)
    parts = parts.reshape(requests, KVH, width).transpose(1, 0, 2)

    groups = [list(range(r * KVH, (r + 1) * KVH)) for r in range(replicas)]
    total = lax.psum_scatter(parts, "replica", scatter_dimension=0, axis_index_groups=groups)
    return (residual.astype(F32) + total).astype(BF16)


def solution(mesh):
    return jax.shard_map(
        on_device,
        mesh=mesh,
        in_specs=(
            P(("parts", "replica"), None, None, None),
            P(("parts", "replica"), None),
            P(("parts", "replica"), None),
            P("parts"),
            P("parts"),
            P(("parts", "replica"), None),
            P(("parts", "replica"), None),
            P("replica", None),
            P(("parts", "replica"), None),
        ),
        out_specs=P(("parts", "replica"), None),
        check_vma=False,
    )
```

```python
import functools
import math

import jax
import jax.numpy as jnp
from jax import lax
from jax.experimental import pallas as pl
from jax.experimental.pallas import tpu as pltpu
from jax.sharding import PartitionSpec as P

KVH = 8
ORDER = (0, 2, 4, 6)
ROWS = 8
CHUNK = 4
LOADS = 8
F32 = jnp.float32
BF16 = jnp.bfloat16
VMEM = pl.BlockSpec(memory_space=pltpu.VMEM)
HBM = pl.BlockSpec(memory_space=pltpu.HBM)


def softmax_parts(scores, own):
    highest = jnp.maximum(jnp.max(scores, axis=1, keepdims=True), own)
    weights = jnp.exp(scores - highest)
    own_weight = jnp.exp(own - highest)
    return weights, own_weight, 1.0 / (jnp.sum(weights, axis=1, keepdims=True) + own_weight)


def split_scaled(weights, inverse, value_scale):
    scaled = (weights * inverse).astype(BF16).astype(F32) * value_scale
    high = scaled.astype(BF16)
    low = (scaled - high.astype(F32)).astype(BF16)
    return jnp.concatenate([high, low], axis=0)


def dot_keys(queries, keys):
    return lax.dot_general(queries, keys, (((1,), (1,)), ((), ())), preferred_element_type=F32)


def attend_resident(
    replicas,
    per_kv,
    lengths_h,
    moves_h,
    table_h,
    scale_h,
    queries_h,
    new_kv_h,
    kv_pages,
    attended,
    away_kv,
    away_info,
    goal_mask,
    here_mask,
    lengths,
    moves,
    table_s,
    table_v,
    scale_v,
    queries,
    new_kv,
    pool,
    target,
    q_rows,
    page_scales,
    key_scale,
    value_scale,
    scores,
    mixed,
    small_sem,
    kv_sem,
):
    requests, max_pages = table_h.shape
    pages, _, page_len, head_dim = kv_pages.shape
    tokens = max_pages * page_len
    slots = moves_h.shape[0]
    factor = 1.0 / math.sqrt(head_dim)
    replica = lax.axis_index("replica") // KVH

    small = [
        pltpu.make_async_copy(src, dst, small_sem.at[i])
        for i, (src, dst) in enumerate(
            [
                (moves_h, moves),
                (lengths_h, lengths),
                (table_h, table_s),
                (table_h, table_v),
                (scale_h, scale_v),
                (queries_h, queries),
                (new_kv_h, new_kv),
            ]
        )
    ]
    for copy in small:
        copy.start()
    step = pages // LOADS
    kv_copies = [
        pltpu.make_async_copy(kv_pages.at[pl.ds(i * step, step)], pool.at[pl.ds(i * step, step)], kv_sem.at[i])
        for i in range(LOADS)
    ]
    for copy in kv_copies:
        copy.start()
    for copy in small:
        copy.wait()

    def place(g, carry):
        slot = moves[g]

        @pl.when(slot // requests == replica)
        def _():
            target[slot % requests] = g

        return carry

    lax.fori_loop(0, slots, place, 0)
    row_ids = lax.broadcasted_iota(jnp.int32, (requests, head_dim), 0)
    leaver = []
    for d in range(1, replicas):
        out_slot = jnp.int32(0)
        here = jnp.int32(0)
        for j in range(requests):
            away = lax.rem(target[j] // requests - replica + replicas, replicas)
            out_slot = jnp.where(away == d, j, out_slot)
            behind = lax.rem(replica - moves[replica * requests + j] // requests + replicas, replicas)
            here = jnp.where(behind == d, j, here)
        leaver.append(out_slot)
        goal_mask[d - 1] = (row_ids == lax.rem(target[out_slot], requests)).astype(F32)
        here_mask[d - 1] = (row_ids == here).astype(F32)

    q_all = queries[...].astype(F32)
    nk_all = new_kv[...].astype(F32)
    q_rows[...] = jnp.zeros_like(q_rows)
    for h in range(per_kv):
        q_rows[pl.ds(h, requests, stride=ROWS), :] = q_all[:, h * head_dim : (h + 1) * head_dim]

    page_ids = lax.broadcasted_iota(jnp.int32, (pages, max_pages), 0)
    scale_rows = scale_v[...]
    for j in range(requests):
        chosen = (page_ids == table_v[j : j + 1, :]).astype(F32).astype(BF16)
        page_scales[:, j : j + 1, :] = jnp.dot(scale_rows, chosen, preferred_element_type=F32)[:, None, :]
    spread = (
        lax.broadcasted_iota(jnp.int32, (max_pages, tokens), 1) // page_len
        == lax.broadcasted_iota(jnp.int32, (max_pages, tokens), 0)
    ).astype(F32).astype(BF16)
    key_scale[...] = jnp.dot(page_scales[0].astype(BF16), spread, preferred_element_type=F32) * factor
    value_scale[...] = jnp.dot(page_scales[1].astype(BF16), spread, preferred_element_type=F32)
    places = lax.broadcasted_iota(jnp.int32, (1, tokens), 1)
    for d in range(1, replicas):
        out_slot = leaver[d - 1]
        away_info[d - 1, 0:1, :] = key_scale[pl.ds(out_slot, 1), :]
        away_info[d - 1, 1:2, :] = value_scale[pl.ds(out_slot, 1), :]
        away_info[d - 1, 2:3, :] = (places < lengths[replica * requests + out_slot]).astype(F32)

    for copy in kv_copies:
        copy.wait()

    for d in range(1, replicas):

        def hand_on(p, carry, d=d):
            away_kv[d - 1, p] = pool[table_s[leaver[d - 1], p]]
            return carry

        lax.fori_loop(0, max_pages, hand_on, 0, unroll=4)

    def gather(j, c, which):
        return jnp.concatenate([pool[table_s[j, c * CHUNK + i], which] for i in range(CHUNK)], axis=0)

    span = CHUNK * page_len
    own = []
    for j in range(requests):
        rows = slice(j * ROWS, (j + 1) * ROWS)
        q = q_rows[rows, :]
        own.append(jnp.sum(q * nk_all[j : j + 1, :head_dim], axis=1, keepdims=True) * factor)
        q = q.astype(BF16)
        context = lengths[replica * requests + j]
        for c in range(max_pages // CHUNK):
            columns = slice(c * span, (c + 1) * span)
            raw = dot_keys(q, gather(j, c, 0)) * key_scale[j : j + 1, columns]
            scores[rows, columns] = jnp.where(places[:, columns] < context, raw, -jnp.inf)
    stats = []
    for j in range(requests):
        rows = slice(j * ROWS, (j + 1) * ROWS)
        weights, own_weight, inverse = softmax_parts(scores[rows, :], own[j])
        scores[rows, :] = weights
        stats.append((own_weight, inverse))
    for j in range(requests):
        rows = slice(j * ROWS, (j + 1) * ROWS)
        own_weight, inverse = stats[j]
        total = jnp.zeros((2 * ROWS, head_dim), F32)
        for c in range(max_pages // CHUNK):
            columns = slice(c * span, (c + 1) * span)
            both = split_scaled(scores[rows, columns], inverse, value_scale[j : j + 1, columns])
            total = total + jnp.dot(both, gather(j, c, 1), preferred_element_type=F32)
        own_weight = (own_weight * inverse).astype(BF16).astype(F32)
        mixed[rows, :] = total[:ROWS] + total[ROWS:] + own_weight * nk_all[j : j + 1, head_dim:]
    for h in range(per_kv):
        attended[:, h * head_dim : (h + 1) * head_dim] = mixed[pl.ds(h, requests, stride=ROWS), :]


def attend_away(replicas, per_kv, *refs):
    count = replicas - 1
    away_kv, away_info, goal_mask = refs[:3]
    came = refs[3 : 3 + count]
    outs = refs[3 + count : 3 + 2 * count]
    q_rows, scores = refs[3 + 2 * count :]
    max_pages, _, page_len, head_dim = away_kv.shape[1:]
    factor = 1.0 / math.sqrt(head_dim)
    span = CHUNK * page_len
    for d in range(count):
        pick = goal_mask[d]
        came_all = came[d][...].astype(F32)
        q_rows[...] = jnp.zeros_like(q_rows)
        for h in range(per_kv):
            q_rows[h : h + 1, :] = jnp.sum(
                came_all[:, h * head_dim : (h + 1) * head_dim] * pick, axis=0, keepdims=True
            )
        nk_all = came_all[:, per_kv * head_dim :]
        new_key = jnp.sum(nk_all[:, :head_dim] * pick, axis=0, keepdims=True)
        new_value = jnp.sum(nk_all[:, head_dim:] * pick, axis=0, keepdims=True)
        q = q_rows[...]
        own = jnp.sum(q * new_key, axis=1, keepdims=True) * factor
        q = q.astype(BF16)
        for c in range(max_pages // CHUNK):
            columns = slice(c * span, (c + 1) * span)
            keys = away_kv[d, c * CHUNK : (c + 1) * CHUNK, 0].reshape(span, head_dim)
            raw = dot_keys(q, keys) * away_info[d, 0:1, columns]
            scores[:, columns] = jnp.where(away_info[d, 2:3, columns] > 0, raw, -jnp.inf)
        weights, own_weight, inverse = softmax_parts(scores[...], own)
        total = jnp.zeros((2 * ROWS, head_dim), F32)
        for c in range(max_pages // CHUNK):
            columns = slice(c * span, (c + 1) * span)
            values = away_kv[d, c * CHUNK : (c + 1) * CHUNK, 1].reshape(span, head_dim)
            both = split_scaled(weights[:, columns], inverse, away_info[d, 1:2, columns])
            total = total + jnp.dot(both, values, preferred_element_type=F32)
        own_weight = (own_weight * inverse).astype(BF16).astype(F32)
        mixed = total[:ROWS] + total[ROWS:] + own_weight * new_value
        for h in range(per_kv):
            outs[d][:, h * head_dim : (h + 1) * head_dim] = mixed[h : h + 1, :]


def load_weights(proj, after, near, far, sem):
    del after
    width = proj.shape[1] // KVH
    shard = lax.axis_index("replica") % KVH
    copies = []
    for i, k in enumerate(ORDER):
        for out, head in ((far, shard ^ k ^ 1), (near, shard ^ k)):
            column = pl.multiple_of(head * width, 128)
            copies.append(
                pltpu.make_async_copy(
                    proj.at[:, pl.ds(column, width)], out.at[:, pl.ds(i * width, width)], sem.at[len(copies)]
                )
            )
    for copy in copies:
        copy.start()
    for copy in copies:
        copy.wait()


def merge(replicas, attended, here_mask, *refs):
    arrived, out = refs[: replicas - 1], refs[-1]
    head_dim = here_mask.shape[2]
    for h in range(attended.shape[1] // head_dim):
        columns = slice(h * head_dim, (h + 1) * head_dim)
        piece = attended[:, columns]
        for d in range(replicas - 1):
            piece = jnp.where(here_mask[d] > 0, arrived[d][:, columns], piece)
        out[:, columns] = piece.astype(out.dtype)


def on_device(
    kv_pages, page_scale, page_table, lengths, request_moves, queries, new_kv, output_proj, residual
):
    devices = lax.axis_size("replica")
    replicas = devices // KVH
    requests, max_pages = page_table.shape
    pages, _, page_len, head_dim = kv_pages.shape
    per_kv = queries.shape[1] // head_dim
    width = output_proj.shape[1] // KVH
    tokens = max_pages * page_len
    count = replicas - 1

    def toward(value, steps):
        pairs = [(i, (i + steps * KVH) % devices) for i in range(devices)]
        return lax.ppermute(value, "replica", pairs)

    def partner(value, mask):
        return lax.ppermute(value, "replica", [(i, i ^ mask) for i in range(devices)])

    asked = jnp.concatenate([queries, new_kv], axis=1)
    came = [toward(asked, -d) for d in range(1, replicas)]

    def shape(*dims, dtype=F32):
        return jax.ShapeDtypeStruct(dims, dtype)

    attended, away_kv, away_info, goal_mask, here_mask = pl.pallas_call(
        functools.partial(attend_resident, replicas, per_kv),
        out_shape=[
            shape(requests, per_kv * head_dim),
            shape(count, max_pages, 2, page_len, head_dim, dtype=BF16),
            shape(count, 8, tokens),
            shape(count, requests, head_dim),
            shape(count, requests, head_dim),
        ],
        in_specs=[HBM] * 7,
        out_specs=[VMEM] * 5,
        scratch_shapes=[
            pltpu.SMEM(lengths.shape, jnp.int32),
            pltpu.SMEM(request_moves.shape, jnp.int32),
            pltpu.SMEM(page_table.shape, jnp.int32),
            pltpu.VMEM(page_table.shape, jnp.int32),
            pltpu.VMEM((2, pages), BF16),
            pltpu.VMEM(queries.shape, BF16),
            pltpu.VMEM(new_kv.shape, BF16),
            pltpu.VMEM(kv_pages.shape, BF16),
            pltpu.SMEM((requests,), jnp.int32),
            pltpu.VMEM((requests * ROWS, head_dim), F32),
            pltpu.VMEM((2, requests, max_pages), F32),
            pltpu.VMEM((requests, tokens), F32),
            pltpu.VMEM((requests, tokens), F32),
            pltpu.VMEM((requests * ROWS, tokens), F32),
            pltpu.VMEM((requests * ROWS, head_dim), F32),
            pltpu.SemaphoreType.DMA((7,)),
            pltpu.SemaphoreType.DMA((LOADS,)),
        ],
        compiler_params=pltpu.CompilerParams(vmem_limit_bytes=16 * 2**20),
        cost_estimate=pl.CostEstimate(
            flops=4 * per_kv * requests * tokens * head_dim,
            bytes_accessed=2 * kv_pages.size,
            transcendentals=requests * ROWS * tokens,
        ),
        name="attend_resident",
    )(
        *(
            pltpu.with_memory_space_constraint(x, pltpu.HBM)
            for x in (lengths, request_moves, page_table, page_scale.T, queries, new_kv, kv_pages)
        )
    )

    rows = pl.pallas_call(
        functools.partial(attend_away, replicas, per_kv),
        out_shape=[shape(1, per_kv * head_dim)] * count,
        in_specs=[VMEM] * (3 + count),
        out_specs=[VMEM] * count,
        scratch_shapes=[pltpu.VMEM((ROWS, head_dim), F32), pltpu.VMEM((ROWS, tokens), F32)],
        compiler_params=pltpu.CompilerParams(vmem_limit_bytes=4 * 2**20),
        name="attend_away",
    )(away_kv, away_info, goal_mask, *came)
    arrived = [toward(rows[d - 1], d) for d in range(1, replicas)]

    half = output_proj.shape[1] // 2
    near, far = pl.pallas_call(
        load_weights,
        out_shape=[shape(output_proj.shape[0], half, dtype=BF16)] * 2,
        in_specs=[HBM] * 2,
        out_specs=[VMEM] * 2,
        scratch_shapes=[pltpu.SemaphoreType.DMA((KVH,))],
        compiler_params=pltpu.CompilerParams(vmem_limit_bytes=2**20),
        cost_estimate=pl.CostEstimate(flops=0, bytes_accessed=4 * output_proj.size, transcendentals=0),
        name="load_weights",
    )(pltpu.with_memory_space_constraint(output_proj, pltpu.HBM), rows[0])
    mixture = pl.pallas_call(
        functools.partial(merge, replicas),
        out_shape=shape(*attended.shape, dtype=BF16),
        in_specs=[VMEM] * (2 + count),
        out_specs=VMEM,
        compiler_params=pltpu.CompilerParams(vmem_limit_bytes=2**20),
        name="merge",
    )(attended, here_mask, *arrived)

    other = partner(jnp.dot(mixture, far, preferred_element_type=F32), 1)
    chip = lax.optimization_barrier(jnp.dot(mixture, near, preferred_element_type=F32)) + other
    total = chip[:, :width]
    for i in range(1, KVH // 2):
        total = total + partner(chip[:, i * width : (i + 1) * width], ORDER[i])
    return (residual.astype(F32) + total).astype(BF16)


def solution(mesh):
    return jax.shard_map(
        on_device,
        mesh=mesh,
        in_specs=(
            P(("parts", "replica"), None, None, None),
            P(("parts", "replica"), None),
            P(("parts", "replica"), None),
            P("parts"),
            P("parts"),
            P(("parts", "replica"), None),
            P(("parts", "replica"), None),
            P("replica", None),
            P(("parts", "replica"), None),
        ),
        out_specs=P(("parts", "replica"), None),
        check_vma=False,
    )
```

```python
import functools
import math

import jax
import jax.numpy as jnp
from jax import lax
from jax.experimental import pallas as pl
from jax.experimental.pallas import tpu as pltpu
from jax.sharding import PartitionSpec as P

KVH = 8
ORDER = (0, 4, 2, 6)
ROWS = 8
CHUNK = 4
LOADS = 8
F32 = jnp.float32
BF16 = jnp.bfloat16
VMEM = pl.BlockSpec(memory_space=pltpu.VMEM)
HBM = pl.BlockSpec(memory_space=pltpu.HBM)


def softmax_parts(scores, own):
    highest = jnp.maximum(jnp.max(scores, axis=1, keepdims=True), own)
    weights = jnp.exp(scores - highest)
    own_weight = jnp.exp(own - highest)
    return weights, own_weight, 1.0 / (jnp.sum(weights, axis=1, keepdims=True) + own_weight)


def split_scaled(weights, inverse, value_scale):
    scaled = (weights * inverse).astype(BF16).astype(F32) * value_scale
    high = scaled.astype(BF16)
    low = (scaled - high.astype(F32)).astype(BF16)
    return jnp.concatenate([high, low], axis=0)


def dot_keys(queries, keys):
    return lax.dot_general(queries, keys, (((1,), (1,)), ((), ())), preferred_element_type=F32)


def bring_pool(
    replicas,
    per_kv,
    lengths_h,
    moves_h,
    table_h,
    scale_h,
    queries_h,
    new_kv_h,
    kv_pages,
    pool,
    q_rows,
    nk_rows,
    key_scale,
    value_scale,
    away_kv,
    away_info,
    goal_mask,
    here_mask,
    lengths,
    moves,
    table_s,
    table_v,
    scale_v,
    queries,
    new_kv,
    target,
    page_scales,
    small_sem,
    kv_sem,
):
    requests, max_pages = table_h.shape
    pages, _, page_len, head_dim = kv_pages.shape
    tokens = max_pages * page_len
    slots = moves_h.shape[0]
    factor = 1.0 / math.sqrt(head_dim)
    replica = lax.axis_index("replica") // KVH

    small = [
        pltpu.make_async_copy(src, dst, small_sem.at[i])
        for i, (src, dst) in enumerate(
            [
                (moves_h, moves),
                (lengths_h, lengths),
                (table_h, table_s),
                (table_h, table_v),
                (scale_h, scale_v),
                (queries_h, queries),
                (new_kv_h, new_kv),
            ]
        )
    ]
    for copy in small:
        copy.start()
    step = pages // LOADS
    kv_copies = [
        pltpu.make_async_copy(kv_pages.at[pl.ds(i * step, step)], pool.at[pl.ds(i * step, step)], kv_sem.at[i])
        for i in range(LOADS)
    ]
    for copy in kv_copies:
        copy.start()
    for copy in small:
        copy.wait()

    def place(g, carry):
        slot = moves[g]

        @pl.when(slot // requests == replica)
        def _():
            target[slot % requests] = g

        return carry

    lax.fori_loop(0, slots, place, 0)
    row_ids = lax.broadcasted_iota(jnp.int32, (requests, head_dim), 0)
    leaver = []
    for d in range(1, replicas):
        out_slot = jnp.int32(0)
        here = jnp.int32(0)
        for j in range(requests):
            away = lax.rem(target[j] // requests - replica + replicas, replicas)
            out_slot = jnp.where(away == d, j, out_slot)
            behind = lax.rem(replica - moves[replica * requests + j] // requests + replicas, replicas)
            here = jnp.where(behind == d, j, here)
        leaver.append(out_slot)
        goal_mask[d - 1] = (row_ids == lax.rem(target[out_slot], requests)).astype(F32)
        here_mask[d - 1] = (row_ids == here).astype(F32)

    q_all = queries[...].astype(F32)
    nk_rows[...] = new_kv[...].astype(F32)
    q_rows[...] = jnp.zeros_like(q_rows)
    for h in range(per_kv):
        q_rows[pl.ds(h, requests, stride=ROWS), :] = q_all[:, h * head_dim : (h + 1) * head_dim]

    page_ids = lax.broadcasted_iota(jnp.int32, (pages, max_pages), 0)
    scale_rows = scale_v[...]
    for j in range(requests):
        chosen = (page_ids == table_v[j : j + 1, :]).astype(F32).astype(BF16)
        page_scales[:, j : j + 1, :] = jnp.dot(scale_rows, chosen, preferred_element_type=F32)[:, None, :]
    spread = (
        lax.broadcasted_iota(jnp.int32, (max_pages, tokens), 1) // page_len
        == lax.broadcasted_iota(jnp.int32, (max_pages, tokens), 0)
    ).astype(F32).astype(BF16)
    key_scale[...] = jnp.dot(page_scales[0].astype(BF16), spread, preferred_element_type=F32) * factor
    value_scale[...] = jnp.dot(page_scales[1].astype(BF16), spread, preferred_element_type=F32)
    places = lax.broadcasted_iota(jnp.int32, (1, tokens), 1)
    for d in range(1, replicas):
        out_slot = leaver[d - 1]
        away_info[d - 1, 0:1, :] = key_scale[pl.ds(out_slot, 1), :]
        away_info[d - 1, 1:2, :] = value_scale[pl.ds(out_slot, 1), :]
        away_info[d - 1, 2:3, :] = (places < lengths[replica * requests + out_slot]).astype(F32)

    for copy in kv_copies:
        copy.wait()

    for d in range(1, replicas):

        def hand_on(p, carry, d=d):
            away_kv[d - 1, p] = pool[table_s[leaver[d - 1], p]]
            return carry

        lax.fori_loop(0, max_pages, hand_on, 0, unroll=4)


def attend_resident(
    per_kv,
    lengths_h,
    table_h,
    proj,
    after,
    pool,
    q_rows,
    nk_rows,
    key_scale,
    value_scale,
    attended,
    near,
    far,
    lengths,
    table_s,
    scores,
    mixed,
    small_sem,
    w_sem,
):
    del after
    requests, max_pages = table_h.shape
    _, _, page_len, head_dim = pool.shape
    tokens = max_pages * page_len
    factor = 1.0 / math.sqrt(head_dim)
    position = lax.axis_index("replica")
    replica = position // KVH
    shard = position % KVH

    small = [
        pltpu.make_async_copy(lengths_h, lengths, small_sem.at[0]),
        pltpu.make_async_copy(table_h, table_s, small_sem.at[1]),
    ]
    for copy in small:
        copy.start()
    width = proj.shape[1] // KVH
    w_copies = []
    for out, mask in ((far, 1), (near, 0)):
        for i, k in enumerate(ORDER):
            column = pl.multiple_of((shard ^ k ^ mask) * width, 128)
            w_copies.append(
                pltpu.make_async_copy(
                    proj.at[:, pl.ds(column, width)], out.at[:, pl.ds(i * width, width)], w_sem.at[len(w_copies)]
                )
            )
    for copy in w_copies:
        copy.start()
    for copy in small:
        copy.wait()

    def gather(j, c, which):
        return jnp.concatenate([pool[table_s[j, c * CHUNK + i], which] for i in range(CHUNK)], axis=0)

    places = lax.broadcasted_iota(jnp.int32, (1, tokens), 1)
    span = CHUNK * page_len
    own = []
    for j in range(requests):
        rows = slice(j * ROWS, (j + 1) * ROWS)
        q = q_rows[rows, :]
        own.append(jnp.sum(q * nk_rows[j : j + 1, :head_dim], axis=1, keepdims=True) * factor)
        q = q.astype(BF16)
        context = lengths[replica * requests + j]
        for c in range(max_pages // CHUNK):
            columns = slice(c * span, (c + 1) * span)
            raw = dot_keys(q, gather(j, c, 0)) * key_scale[j : j + 1, columns]
            scores[rows, columns] = jnp.where(places[:, columns] < context, raw, -jnp.inf)
    stats = []
    for j in range(requests):
        rows = slice(j * ROWS, (j + 1) * ROWS)
        weights, own_weight, inverse = softmax_parts(scores[rows, :], own[j])
        scores[rows, :] = weights
        stats.append((own_weight, inverse))
    for j in range(requests):
        rows = slice(j * ROWS, (j + 1) * ROWS)
        own_weight, inverse = stats[j]
        total = jnp.zeros((2 * ROWS, head_dim), F32)
        for c in range(max_pages // CHUNK):
            columns = slice(c * span, (c + 1) * span)
            both = split_scaled(scores[rows, columns], inverse, value_scale[j : j + 1, columns])
            total = total + jnp.dot(both, gather(j, c, 1), preferred_element_type=F32)
        own_weight = (own_weight * inverse).astype(BF16).astype(F32)
        mixed[rows, :] = total[:ROWS] + total[ROWS:] + own_weight * nk_rows[j : j + 1, head_dim:]
    for h in range(per_kv):
        attended[:, h * head_dim : (h + 1) * head_dim] = mixed[pl.ds(h, requests, stride=ROWS), :]
    for copy in w_copies:
        copy.wait()


def attend_away(replicas, per_kv, *refs):
    count = replicas - 1
    away_kv, away_info, goal_mask = refs[:3]
    came = refs[3 : 3 + count]
    outs = refs[3 + count : 3 + 2 * count]
    q_rows, scores = refs[3 + 2 * count :]
    max_pages, _, page_len, head_dim = away_kv.shape[1:]
    factor = 1.0 / math.sqrt(head_dim)
    span = CHUNK * page_len
    for d in range(count):
        pick = goal_mask[d]
        came_all = came[d][...].astype(F32)
        q_rows[...] = jnp.zeros_like(q_rows)
        for h in range(per_kv):
            q_rows[h : h + 1, :] = jnp.sum(
                came_all[:, h * head_dim : (h + 1) * head_dim] * pick, axis=0, keepdims=True
            )
        nk_all = came_all[:, per_kv * head_dim :]
        new_key = jnp.sum(nk_all[:, :head_dim] * pick, axis=0, keepdims=True)
        new_value = jnp.sum(nk_all[:, head_dim:] * pick, axis=0, keepdims=True)
        q = q_rows[...]
        own = jnp.sum(q * new_key, axis=1, keepdims=True) * factor
        q = q.astype(BF16)
        for c in range(max_pages // CHUNK):
            columns = slice(c * span, (c + 1) * span)
            keys = away_kv[d, c * CHUNK : (c + 1) * CHUNK, 0].reshape(span, head_dim)
            raw = dot_keys(q, keys) * away_info[d, 0:1, columns]
            scores[:, columns] = jnp.where(away_info[d, 2:3, columns] > 0, raw, -jnp.inf)
        weights, own_weight, inverse = softmax_parts(scores[...], own)
        total = jnp.zeros((2 * ROWS, head_dim), F32)
        for c in range(max_pages // CHUNK):
            columns = slice(c * span, (c + 1) * span)
            values = away_kv[d, c * CHUNK : (c + 1) * CHUNK, 1].reshape(span, head_dim)
            both = split_scaled(weights[:, columns], inverse, away_info[d, 1:2, columns])
            total = total + jnp.dot(both, values, preferred_element_type=F32)
        own_weight = (own_weight * inverse).astype(BF16).astype(F32)
        mixed = total[:ROWS] + total[ROWS:] + own_weight * new_value
        for h in range(per_kv):
            outs[d][:, h * head_dim : (h + 1) * head_dim] = mixed[h : h + 1, :]


def merge(replicas, attended, here_mask, *refs):
    arrived, out = refs[: replicas - 1], refs[-1]
    head_dim = here_mask.shape[2]
    for h in range(attended.shape[1] // head_dim):
        columns = slice(h * head_dim, (h + 1) * head_dim)
        piece = attended[:, columns]
        for d in range(replicas - 1):
            piece = jnp.where(here_mask[d] > 0, arrived[d][:, columns], piece)
        out[:, columns] = piece.astype(out.dtype)


def on_device(
    kv_pages, page_scale, page_table, lengths, request_moves, queries, new_kv, output_proj, residual
):
    devices = lax.axis_size("replica")
    replicas = devices // KVH
    requests, max_pages = page_table.shape
    pages, _, page_len, head_dim = kv_pages.shape
    per_kv = queries.shape[1] // head_dim
    width = output_proj.shape[1] // KVH
    tokens = max_pages * page_len
    count = replicas - 1

    def toward(value, steps):
        pairs = [(i, (i + steps * KVH) % devices) for i in range(devices)]
        return lax.ppermute(value, "replica", pairs)

    def partner(value, mask):
        return lax.ppermute(value, "replica", [(i, i ^ mask) for i in range(devices)])

    asked = jnp.concatenate([queries, new_kv], axis=1)
    came = [toward(asked, -d) for d in range(1, replicas)]

    def shape(*dims, dtype=F32):
        return jax.ShapeDtypeStruct(dims, dtype)

    in_hbm = functools.partial(pltpu.with_memory_space_constraint, memory_space=pltpu.HBM)
    pool, q_rows, nk_rows, key_scale, value_scale, away_kv, away_info, goal_mask, here_mask = pl.pallas_call(
        functools.partial(bring_pool, replicas, per_kv),
        out_shape=[
            shape(*kv_pages.shape, dtype=BF16),
            shape(requests * ROWS, head_dim),
            shape(requests, 2 * head_dim),
            shape(requests, tokens),
            shape(requests, tokens),
            shape(count, max_pages, 2, page_len, head_dim, dtype=BF16),
            shape(count, 8, tokens),
            shape(count, requests, head_dim),
            shape(count, requests, head_dim),
        ],
        in_specs=[HBM] * 7,
        out_specs=[VMEM] * 9,
        scratch_shapes=[
            pltpu.SMEM(lengths.shape, jnp.int32),
            pltpu.SMEM(request_moves.shape, jnp.int32),
            pltpu.SMEM(page_table.shape, jnp.int32),
            pltpu.VMEM(page_table.shape, jnp.int32),
            pltpu.VMEM((2, pages), BF16),
            pltpu.VMEM(queries.shape, BF16),
            pltpu.VMEM(new_kv.shape, BF16),
            pltpu.SMEM((requests,), jnp.int32),
            pltpu.VMEM((2, requests, max_pages), F32),
            pltpu.SemaphoreType.DMA((7,)),
            pltpu.SemaphoreType.DMA((LOADS,)),
        ],
        compiler_params=pltpu.CompilerParams(vmem_limit_bytes=4 * 2**20),
        cost_estimate=pl.CostEstimate(flops=0, bytes_accessed=4 * kv_pages.size, transcendentals=0),
        name="bring_pool",
    )(*(in_hbm(x) for x in (lengths, request_moves, page_table, page_scale.T, queries, new_kv, kv_pages)))

    rows = pl.pallas_call(
        functools.partial(attend_away, replicas, per_kv),
        out_shape=[shape(1, per_kv * head_dim)] * count,
        in_specs=[VMEM] * (3 + count),
        out_specs=[VMEM] * count,
        scratch_shapes=[pltpu.VMEM((ROWS, head_dim), F32), pltpu.VMEM((ROWS, tokens), F32)],
        compiler_params=pltpu.CompilerParams(vmem_limit_bytes=4 * 2**20),
        name="attend_away",
    )(away_kv, away_info, goal_mask, *came)
    arrived = [toward(rows[d - 1], d) for d in range(1, replicas)]

    half = output_proj.shape[1] // 2
    attended, near, far = pl.pallas_call(
        functools.partial(attend_resident, per_kv),
        out_shape=[shape(requests, per_kv * head_dim)] + [shape(output_proj.shape[0], half, dtype=BF16)] * 2,
        in_specs=[HBM] * 4 + [VMEM] * 5,
        out_specs=[VMEM] * 3,
        scratch_shapes=[
            pltpu.SMEM(lengths.shape, jnp.int32),
            pltpu.SMEM(page_table.shape, jnp.int32),
            pltpu.VMEM((requests * ROWS, tokens), F32),
            pltpu.VMEM((requests * ROWS, head_dim), F32),
            pltpu.SemaphoreType.DMA((2,)),
            pltpu.SemaphoreType.DMA((KVH,)),
        ],
        compiler_params=pltpu.CompilerParams(vmem_limit_bytes=8 * 2**20),
        cost_estimate=pl.CostEstimate(
            flops=4 * per_kv * requests * tokens * head_dim,
            bytes_accessed=4 * output_proj.size,
            transcendentals=requests * ROWS * tokens,
        ),
        name="attend_resident",
    )(
        in_hbm(lengths), in_hbm(page_table), in_hbm(output_proj), rows[0], pool, q_rows, nk_rows, key_scale, value_scale
    )
    mixture = pl.pallas_call(
        functools.partial(merge, replicas),
        out_shape=shape(*attended.shape, dtype=BF16),
        in_specs=[VMEM] * (2 + count),
        out_specs=VMEM,
        compiler_params=pltpu.CompilerParams(vmem_limit_bytes=2**20),
        name="merge",
    )(attended, here_mask, *arrived)

    other = partner(jnp.dot(mixture, far, preferred_element_type=F32), 1)
    chip = lax.optimization_barrier(jnp.dot(mixture, near, preferred_element_type=F32)) + other
    came_y = partner(chip[:, 2 * width :].astype(BF16), ORDER[2]).astype(F32)
    pair = chip[:, : 2 * width] + came_y
    came_z = partner(pair[:, width:].astype(BF16), ORDER[1]).astype(F32)
    return (residual.astype(F32) + pair[:, :width] + came_z).astype(BF16)


def solution(mesh):
    return jax.shard_map(
        on_device,
        mesh=mesh,
        in_specs=(
            P(("parts", "replica"), None, None, None),
            P(("parts", "replica"), None),
            P(("parts", "replica"), None),
            P("parts"),
            P("parts"),
            P(("parts", "replica"), None),
            P(("parts", "replica"), None),
            P("replica", None),
            P(("parts", "replica"), None),
        ),
        out_specs=P(("parts", "replica"), None),
        check_vma=False,
    )
```

```python
import functools
import math

import jax
import jax.numpy as jnp
from jax import lax
from jax.experimental import pallas as pl
from jax.experimental.pallas import tpu as pltpu
from jax.sharding import PartitionSpec as P

KVH = 8
CORES = 2
ROWS = 8
CHUNK = 4
LOADS = 8
F32 = jnp.float32
BF16 = jnp.bfloat16
VMEM = pl.BlockSpec(memory_space=pltpu.VMEM)
HBM = pl.BlockSpec(memory_space=pltpu.HBM)


def softmax_parts(scores, own):
    highest = jnp.maximum(jnp.max(scores, axis=1, keepdims=True), own)
    weights = jnp.exp(scores - highest)
    own_weight = jnp.exp(own - highest)
    return weights, own_weight, 1.0 / (jnp.sum(weights, axis=1, keepdims=True) + own_weight)


def split_scaled(weights, inverse, value_scale):
    scaled = (weights * inverse).astype(BF16).astype(F32) * value_scale
    high = scaled.astype(BF16)
    low = (scaled - high.astype(F32)).astype(BF16)
    return jnp.concatenate([high, low], axis=0)


def dot_keys(queries, keys):
    return lax.dot_general(queries, keys, (((1,), (1,)), ((), ())), preferred_element_type=F32)


def bring_pool(
    replicas,
    per_kv,
    lengths_h,
    moves_h,
    table_h,
    scale_h,
    queries_h,
    new_kv_h,
    kv_pages,
    pool,
    q_rows,
    nk_rows,
    key_scale,
    value_scale,
    away_kv,
    away_info,
    goal_mask,
    here_mask,
    lengths,
    moves,
    table_s,
    table_v,
    scale_v,
    queries,
    new_kv,
    target,
    page_scales,
    small_sem,
    kv_sem,
):
    requests, max_pages = table_h.shape
    pages, _, page_len, head_dim = kv_pages.shape
    tokens = max_pages * page_len
    slots = moves_h.shape[0]
    factor = 1.0 / math.sqrt(head_dim)
    replica = lax.axis_index("replica") // KVH

    small = [
        pltpu.make_async_copy(src, dst, small_sem.at[i])
        for i, (src, dst) in enumerate(
            [
                (moves_h, moves),
                (lengths_h, lengths),
                (table_h, table_s),
                (table_h, table_v),
                (scale_h, scale_v),
                (queries_h, queries),
                (new_kv_h, new_kv),
            ]
        )
    ]
    for copy in small:
        copy.start()
    step = pages // LOADS
    kv_copies = [
        pltpu.make_async_copy(kv_pages.at[pl.ds(i * step, step)], pool.at[pl.ds(i * step, step)], kv_sem.at[i])
        for i in range(LOADS)
    ]
    for copy in kv_copies:
        copy.start()
    for copy in small:
        copy.wait()

    def place(g, carry):
        slot = moves[g]

        @pl.when(slot // requests == replica)
        def _():
            target[slot % requests] = g

        return carry

    lax.fori_loop(0, slots, place, 0)
    row_ids = lax.broadcasted_iota(jnp.int32, (requests, head_dim), 0)
    leaver = []
    for d in range(1, replicas):
        out_slot = jnp.int32(0)
        here = jnp.int32(0)
        for j in range(requests):
            away = lax.rem(target[j] // requests - replica + replicas, replicas)
            out_slot = jnp.where(away == d, j, out_slot)
            behind = lax.rem(replica - moves[replica * requests + j] // requests + replicas, replicas)
            here = jnp.where(behind == d, j, here)
        leaver.append(out_slot)
        goal_mask[d - 1] = (row_ids == lax.rem(target[out_slot], requests)).astype(F32)
        here_mask[d - 1] = (row_ids == here).astype(F32)

    q_all = queries[...].astype(F32)
    nk_rows[...] = new_kv[...].astype(F32)
    q_rows[...] = jnp.zeros_like(q_rows)
    for h in range(per_kv):
        q_rows[pl.ds(h, requests, stride=ROWS), :] = q_all[:, h * head_dim : (h + 1) * head_dim]

    page_ids = lax.broadcasted_iota(jnp.int32, (pages, max_pages), 0)
    scale_rows = scale_v[...]
    for j in range(requests):
        chosen = (page_ids == table_v[j : j + 1, :]).astype(F32).astype(BF16)
        page_scales[:, j : j + 1, :] = jnp.dot(scale_rows, chosen, preferred_element_type=F32)[:, None, :]
    spread = (
        lax.broadcasted_iota(jnp.int32, (max_pages, tokens), 1) // page_len
        == lax.broadcasted_iota(jnp.int32, (max_pages, tokens), 0)
    ).astype(F32).astype(BF16)
    key_scale[...] = jnp.dot(page_scales[0].astype(BF16), spread, preferred_element_type=F32) * factor
    value_scale[...] = jnp.dot(page_scales[1].astype(BF16), spread, preferred_element_type=F32)
    places = lax.broadcasted_iota(jnp.int32, (1, tokens), 1)
    for d in range(1, replicas):
        out_slot = leaver[d - 1]
        away_info[d - 1, 0:1, :] = key_scale[pl.ds(out_slot, 1), :]
        away_info[d - 1, 1:2, :] = value_scale[pl.ds(out_slot, 1), :]
        away_info[d - 1, 2:3, :] = (places < lengths[replica * requests + out_slot]).astype(F32)

    for copy in kv_copies:
        copy.wait()

    for d in range(1, replicas):

        def hand_on(p, carry, d=d):
            away_kv[d - 1, p] = pool[table_s[leaver[d - 1], p]]
            return carry

        lax.fori_loop(0, max_pages, hand_on, 0, unroll=4)


def attend_resident(
    per_kv,
    lengths_h,
    table_h,
    proj,
    after,
    pool,
    q_rows,
    nk_rows,
    key_scale,
    value_scale,
    attended,
    near,
    far,
    lengths,
    table_s,
    scores,
    mixed,
    small_sem,
    w_sem,
):
    del after
    requests, max_pages = table_h.shape
    _, _, page_len, head_dim = pool.shape
    tokens = max_pages * page_len
    factor = 1.0 / math.sqrt(head_dim)
    position = lax.axis_index("replica")
    replica = position // KVH
    core = position % CORES

    small = [
        pltpu.make_async_copy(lengths_h, lengths, small_sem.at[0]),
        pltpu.make_async_copy(table_h, table_s, small_sem.at[1]),
    ]
    for copy in small:
        copy.start()
    width = proj.shape[1] // KVH
    w_copies = []
    for out, mask in ((far, 1), (near, 0)):
        for i in range(KVH // CORES):
            column = pl.multiple_of((i * CORES + (core ^ mask)) * width, 128)
            w_copies.append(
                pltpu.make_async_copy(
                    proj.at[:, pl.ds(column, width)], out.at[:, pl.ds(i * width, width)], w_sem.at[len(w_copies)]
                )
            )
    for copy in w_copies:
        copy.start()
    for copy in small:
        copy.wait()

    def gather(j, c, which):
        return jnp.concatenate([pool[table_s[j, c * CHUNK + i], which] for i in range(CHUNK)], axis=0)

    places = lax.broadcasted_iota(jnp.int32, (1, tokens), 1)
    span = CHUNK * page_len
    own = []
    for j in range(requests):
        rows = slice(j * ROWS, (j + 1) * ROWS)
        q = q_rows[rows, :]
        own.append(jnp.sum(q * nk_rows[j : j + 1, :head_dim], axis=1, keepdims=True) * factor)
        q = q.astype(BF16)
        context = lengths[replica * requests + j]
        for c in range(max_pages // CHUNK):
            columns = slice(c * span, (c + 1) * span)
            raw = dot_keys(q, gather(j, c, 0)) * key_scale[j : j + 1, columns]
            scores[rows, columns] = jnp.where(places[:, columns] < context, raw, -jnp.inf)
    stats = []
    for j in range(requests):
        rows = slice(j * ROWS, (j + 1) * ROWS)
        weights, own_weight, inverse = softmax_parts(scores[rows, :], own[j])
        scores[rows, :] = weights
        stats.append((own_weight, inverse))
    for j in range(requests):
        rows = slice(j * ROWS, (j + 1) * ROWS)
        own_weight, inverse = stats[j]
        total = jnp.zeros((2 * ROWS, head_dim), F32)
        for c in range(max_pages // CHUNK):
            columns = slice(c * span, (c + 1) * span)
            both = split_scaled(scores[rows, columns], inverse, value_scale[j : j + 1, columns])
            total = total + jnp.dot(both, gather(j, c, 1), preferred_element_type=F32)
        own_weight = (own_weight * inverse).astype(BF16).astype(F32)
        mixed[rows, :] = total[:ROWS] + total[ROWS:] + own_weight * nk_rows[j : j + 1, head_dim:]
    for h in range(per_kv):
        attended[:, h * head_dim : (h + 1) * head_dim] = mixed[pl.ds(h, requests, stride=ROWS), :]
    for copy in w_copies:
        copy.wait()


def attend_away(replicas, per_kv, *refs):
    count = replicas - 1
    away_kv, away_info, goal_mask = refs[:3]
    came = refs[3 : 3 + count]
    outs = refs[3 + count : 3 + 2 * count]
    q_rows, scores = refs[3 + 2 * count :]
    max_pages, _, page_len, head_dim = away_kv.shape[1:]
    factor = 1.0 / math.sqrt(head_dim)
    span = CHUNK * page_len
    for d in range(count):
        pick = goal_mask[d]
        came_all = came[d][...].astype(F32)
        q_rows[...] = jnp.zeros_like(q_rows)
        for h in range(per_kv):
            q_rows[h : h + 1, :] = jnp.sum(
                came_all[:, h * head_dim : (h + 1) * head_dim] * pick, axis=0, keepdims=True
            )
        nk_all = came_all[:, per_kv * head_dim :]
        new_key = jnp.sum(nk_all[:, :head_dim] * pick, axis=0, keepdims=True)
        new_value = jnp.sum(nk_all[:, head_dim:] * pick, axis=0, keepdims=True)
        q = q_rows[...]
        own = jnp.sum(q * new_key, axis=1, keepdims=True) * factor
        q = q.astype(BF16)
        for c in range(max_pages // CHUNK):
            columns = slice(c * span, (c + 1) * span)
            keys = away_kv[d, c * CHUNK : (c + 1) * CHUNK, 0].reshape(span, head_dim)
            raw = dot_keys(q, keys) * away_info[d, 0:1, columns]
            scores[:, columns] = jnp.where(away_info[d, 2:3, columns] > 0, raw, -jnp.inf)
        weights, own_weight, inverse = softmax_parts(scores[...], own)
        total = jnp.zeros((2 * ROWS, head_dim), F32)
        for c in range(max_pages // CHUNK):
            columns = slice(c * span, (c + 1) * span)
            values = away_kv[d, c * CHUNK : (c + 1) * CHUNK, 1].reshape(span, head_dim)
            both = split_scaled(weights[:, columns], inverse, away_info[d, 1:2, columns])
            total = total + jnp.dot(both, values, preferred_element_type=F32)
        own_weight = (own_weight * inverse).astype(BF16).astype(F32)
        mixed = total[:ROWS] + total[ROWS:] + own_weight * new_value
        for h in range(per_kv):
            outs[d][:, h * head_dim : (h + 1) * head_dim] = mixed[h : h + 1, :]


def merge(replicas, attended, here_mask, *refs):
    arrived, out = refs[: replicas - 1], refs[-1]
    head_dim = here_mask.shape[2]
    for h in range(attended.shape[1] // head_dim):
        columns = slice(h * head_dim, (h + 1) * head_dim)
        piece = attended[:, columns]
        for d in range(replicas - 1):
            piece = jnp.where(here_mask[d] > 0, arrived[d][:, columns], piece)
        out[:, columns] = piece.astype(out.dtype)


def on_device(
    kv_pages, page_scale, page_table, lengths, request_moves, queries, new_kv, output_proj, residual
):
    devices = lax.axis_size("replica")
    replicas = devices // KVH
    requests, max_pages = page_table.shape
    pages, _, page_len, head_dim = kv_pages.shape
    per_kv = queries.shape[1] // head_dim
    width = output_proj.shape[1] // KVH
    tokens = max_pages * page_len
    count = replicas - 1

    def toward(value, steps):
        pairs = [(i, (i + steps * KVH) % devices) for i in range(devices)]
        return lax.ppermute(value, "replica", pairs)

    def partner(value, mask):
        return lax.ppermute(value, "replica", [(i, i ^ mask) for i in range(devices)])

    asked = jnp.concatenate([queries, new_kv], axis=1)
    came = [toward(asked, -d) for d in range(1, replicas)]

    def shape(*dims, dtype=F32):
        return jax.ShapeDtypeStruct(dims, dtype)

    in_hbm = functools.partial(pltpu.with_memory_space_constraint, memory_space=pltpu.HBM)
    pool, q_rows, nk_rows, key_scale, value_scale, away_kv, away_info, goal_mask, here_mask = pl.pallas_call(
        functools.partial(bring_pool, replicas, per_kv),
        out_shape=[
            shape(*kv_pages.shape, dtype=BF16),
            shape(requests * ROWS, head_dim),
            shape(requests, 2 * head_dim),
            shape(requests, tokens),
            shape(requests, tokens),
            shape(count, max_pages, 2, page_len, head_dim, dtype=BF16),
            shape(count, 8, tokens),
            shape(count, requests, head_dim),
            shape(count, requests, head_dim),
        ],
        in_specs=[HBM] * 7,
        out_specs=[VMEM] * 9,
        scratch_shapes=[
            pltpu.SMEM(lengths.shape, jnp.int32),
            pltpu.SMEM(request_moves.shape, jnp.int32),
            pltpu.SMEM(page_table.shape, jnp.int32),
            pltpu.VMEM(page_table.shape, jnp.int32),
            pltpu.VMEM((2, pages), BF16),
            pltpu.VMEM(queries.shape, BF16),
            pltpu.VMEM(new_kv.shape, BF16),
            pltpu.SMEM((requests,), jnp.int32),
            pltpu.VMEM((2, requests, max_pages), F32),
            pltpu.SemaphoreType.DMA((7,)),
            pltpu.SemaphoreType.DMA((LOADS,)),
        ],
        compiler_params=pltpu.CompilerParams(vmem_limit_bytes=4 * 2**20),
        cost_estimate=pl.CostEstimate(flops=0, bytes_accessed=4 * kv_pages.size, transcendentals=0),
        name="bring_pool",
    )(*(in_hbm(x) for x in (lengths, request_moves, page_table, page_scale.T, queries, new_kv, kv_pages)))

    rows = pl.pallas_call(
        functools.partial(attend_away, replicas, per_kv),
        out_shape=[shape(1, per_kv * head_dim)] * count,
        in_specs=[VMEM] * (3 + count),
        out_specs=[VMEM] * count,
        scratch_shapes=[pltpu.VMEM((ROWS, head_dim), F32), pltpu.VMEM((ROWS, tokens), F32)],
        compiler_params=pltpu.CompilerParams(vmem_limit_bytes=4 * 2**20),
        name="attend_away",
    )(away_kv, away_info, goal_mask, *came)
    arrived = [toward(rows[d - 1], d) for d in range(1, replicas)]

    half = output_proj.shape[1] // 2
    attended, near, far = pl.pallas_call(
        functools.partial(attend_resident, per_kv),
        out_shape=[shape(requests, per_kv * head_dim)] + [shape(output_proj.shape[0], half, dtype=BF16)] * 2,
        in_specs=[HBM] * 4 + [VMEM] * 5,
        out_specs=[VMEM] * 3,
        scratch_shapes=[
            pltpu.SMEM(lengths.shape, jnp.int32),
            pltpu.SMEM(page_table.shape, jnp.int32),
            pltpu.VMEM((requests * ROWS, tokens), F32),
            pltpu.VMEM((requests * ROWS, head_dim), F32),
            pltpu.SemaphoreType.DMA((2,)),
            pltpu.SemaphoreType.DMA((KVH,)),
        ],
        compiler_params=pltpu.CompilerParams(vmem_limit_bytes=8 * 2**20),
        cost_estimate=pl.CostEstimate(
            flops=4 * per_kv * requests * tokens * head_dim,
            bytes_accessed=4 * output_proj.size,
            transcendentals=requests * ROWS * tokens,
        ),
        name="attend_resident",
    )(
        in_hbm(lengths), in_hbm(page_table), in_hbm(output_proj), rows[0], pool, q_rows, nk_rows, key_scale, value_scale
    )
    mixture = pl.pallas_call(
        functools.partial(merge, replicas),
        out_shape=shape(*attended.shape, dtype=BF16),
        in_specs=[VMEM] * (2 + count),
        out_specs=VMEM,
        compiler_params=pltpu.CompilerParams(vmem_limit_bytes=2**20),
        name="merge",
    )(attended, here_mask, *arrived)

    other = partner(jnp.dot(mixture, far, preferred_element_type=F32), 1)
    chip = lax.optimization_barrier(jnp.dot(mixture, near, preferred_element_type=F32)) + other
    chip = chip.astype(BF16).reshape(requests, KVH // CORES, width).transpose(1, 0, 2)
    groups = [list(range(r * KVH + c, (r + 1) * KVH, CORES)) for r in range(replicas) for c in range(CORES)]
    parts = lax.all_to_all(chip, "replica", 0, 0, axis_index_groups=groups, tiled=True)
    return (residual.astype(F32) + jnp.sum(parts.astype(F32), axis=0)).astype(BF16)


def solution(mesh):
    return jax.shard_map(
        on_device,
        mesh=mesh,
        in_specs=(
            P(("parts", "replica"), None, None, None),
            P(("parts", "replica"), None),
            P(("parts", "replica"), None),
            P("parts"),
            P("parts"),
            P(("parts", "replica"), None),
            P(("parts", "replica"), None),
            P("replica", None),
            P(("parts", "replica"), None),
        ),
        out_specs=P(("parts", "replica"), None),
        check_vma=False,
    )
```

```python
import functools
import math

import jax
import jax.numpy as jnp
from jax import lax
from jax.experimental import pallas as pl
from jax.experimental.pallas import tpu as pltpu
from jax.sharding import PartitionSpec as P

KVH = 8
ORDER = (6, 4, 2, 0)
ROWS = 8
CHUNK = 4
F32 = jnp.float32
BF16 = jnp.bfloat16
VMEM = pl.BlockSpec(memory_space=pltpu.VMEM)
HBM = pl.BlockSpec(memory_space=pltpu.HBM)


def softmax_parts(scores, own):
    highest = jnp.maximum(jnp.max(scores, axis=1, keepdims=True), own)
    weights = jnp.exp(scores - highest)
    own_weight = jnp.exp(own - highest)
    return weights, own_weight, 1.0 / (jnp.sum(weights, axis=1, keepdims=True) + own_weight)


def split_scaled(weights, inverse, value_scale):
    scaled = (weights * inverse).astype(BF16).astype(F32) * value_scale
    high = scaled.astype(BF16)
    low = (scaled - high.astype(F32)).astype(BF16)
    return jnp.concatenate([high, low], axis=0)


def dot_keys(queries, keys):
    return lax.dot_general(queries, keys, (((1,), (1,)), ((), ())), preferred_element_type=F32)


def set_up(
    replicas,
    per_kv,
    lengths_h,
    moves_h,
    table_h,
    scale_h,
    queries_h,
    new_kv_h,
    kv_pages,
    q_rows,
    nk_rows,
    key_scale,
    value_scale,
    away_kv,
    away_info,
    goal_mask,
    here_mask,
    lengths,
    moves,
    table_s,
    table_v,
    scale_v,
    queries,
    new_kv,
    target,
    page_scales,
    small_sem,
    kv_sem,
):
    requests, max_pages = table_h.shape
    pages, _, page_len, head_dim = kv_pages.shape
    tokens = max_pages * page_len
    slots = moves_h.shape[0]
    factor = 1.0 / math.sqrt(head_dim)
    replica = lax.axis_index("replica") // KVH

    small = [
        pltpu.make_async_copy(src, dst, small_sem.at[i])
        for i, (src, dst) in enumerate(
            [
                (moves_h, moves),
                (lengths_h, lengths),
                (table_h, table_s),
                (table_h, table_v),
                (scale_h, scale_v),
                (queries_h, queries),
                (new_kv_h, new_kv),
            ]
        )
    ]
    for copy in small:
        copy.start()
    for copy in small:
        copy.wait()

    def place(g, carry):
        slot = moves[g]

        @pl.when(slot // requests == replica)
        def _():
            target[slot % requests] = g

        return carry

    lax.fori_loop(0, slots, place, 0)
    row_ids = lax.broadcasted_iota(jnp.int32, (requests, head_dim), 0)
    leaver = []
    for d in range(1, replicas):
        out_slot = jnp.int32(0)
        here = jnp.int32(0)
        for j in range(requests):
            away = lax.rem(target[j] // requests - replica + replicas, replicas)
            out_slot = jnp.where(away == d, j, out_slot)
            behind = lax.rem(replica - moves[replica * requests + j] // requests + replicas, replicas)
            here = jnp.where(behind == d, j, here)
        leaver.append(out_slot)

        def fetch(p, carry, d=d, out_slot=out_slot):
            pltpu.make_async_copy(
                kv_pages.at[table_s[out_slot, p]], away_kv.at[d - 1, p], kv_sem.at[d - 1]
            ).start()
            return carry

        lax.fori_loop(0, max_pages, fetch, 0, unroll=4)
        goal_mask[d - 1] = (row_ids == lax.rem(target[out_slot], requests)).astype(F32)
        here_mask[d - 1] = (row_ids == here).astype(F32)

    q_all = queries[...].astype(F32)
    nk_rows[...] = new_kv[...].astype(F32)
    q_rows[...] = jnp.zeros_like(q_rows)
    for h in range(per_kv):
        q_rows[pl.ds(h, requests, stride=ROWS), :] = q_all[:, h * head_dim : (h + 1) * head_dim]

    page_ids = lax.broadcasted_iota(jnp.int32, (pages, max_pages), 0)
    scale_rows = scale_v[...]
    for j in range(requests):
        chosen = (page_ids == table_v[j : j + 1, :]).astype(F32).astype(BF16)
        page_scales[:, j : j + 1, :] = jnp.dot(scale_rows, chosen, preferred_element_type=F32)[:, None, :]
    spread = (
        lax.broadcasted_iota(jnp.int32, (max_pages, tokens), 1) // page_len
        == lax.broadcasted_iota(jnp.int32, (max_pages, tokens), 0)
    ).astype(F32).astype(BF16)
    key_scale[...] = jnp.dot(page_scales[0].astype(BF16), spread, preferred_element_type=F32) * factor
    value_scale[...] = jnp.dot(page_scales[1].astype(BF16), spread, preferred_element_type=F32)
    places = lax.broadcasted_iota(jnp.int32, (1, tokens), 1)
    for d in range(1, replicas):
        out_slot = leaver[d - 1]
        away_info[d - 1, 0:1, :] = key_scale[pl.ds(out_slot, 1), :]
        away_info[d - 1, 1:2, :] = value_scale[pl.ds(out_slot, 1), :]
        away_info[d - 1, 2:3, :] = (places < lengths[replica * requests + out_slot]).astype(F32)

    for d in range(1, replicas):
        pltpu.make_async_copy(kv_pages.at[pl.ds(0, max_pages)], away_kv.at[d - 1], kv_sem.at[d - 1]).wait()


def attend_resident(
    per_kv,
    lengths_h,
    table_h,
    proj,
    after,
    pool,
    q_rows,
    nk_rows,
    key_scale,
    value_scale,
    attended,
    *rest,
):
    blocks = rest[: len(ORDER)]
    lengths, table_s, scores, mixed, small_sem, w_sem = rest[len(ORDER) :]
    del after
    requests, max_pages = table_h.shape
    _, _, page_len, head_dim = pool.shape
    tokens = max_pages * page_len
    factor = 1.0 / math.sqrt(head_dim)
    position = lax.axis_index("replica")
    replica = position // KVH
    shard = position % KVH

    small = [
        pltpu.make_async_copy(lengths_h, lengths, small_sem.at[0]),
        pltpu.make_async_copy(table_h, table_s, small_sem.at[1]),
    ]
    for copy in small:
        copy.start()
    width = proj.shape[1] // KVH
    w_copies = []
    for out, k in zip(blocks, ORDER):
        for mask in range(2):
            column = pl.multiple_of((shard ^ k ^ mask) * width, 128)
            w_copies.append(
                pltpu.make_async_copy(
                    proj.at[:, pl.ds(column, width)], out.at[:, pl.ds(mask * width, width)], w_sem.at[len(w_copies)]
                )
            )
    for copy in w_copies:
        copy.start()
    for copy in small:
        copy.wait()

    def gather(j, c, which):
        return jnp.concatenate([pool[table_s[j, c * CHUNK + i], which] for i in range(CHUNK)], axis=0)

    places = lax.broadcasted_iota(jnp.int32, (1, tokens), 1)
    span = CHUNK * page_len
    own = []
    for j in range(requests):
        rows = slice(j * ROWS, (j + 1) * ROWS)
        q = q_rows[rows, :]
        own.append(jnp.sum(q * nk_rows[j : j + 1, :head_dim], axis=1, keepdims=True) * factor)
        q = q.astype(BF16)
        context = lengths[replica * requests + j]
        for c in range(max_pages // CHUNK):
            columns = slice(c * span, (c + 1) * span)
            raw = dot_keys(q, gather(j, c, 0)) * key_scale[j : j + 1, columns]
            scores[rows, columns] = jnp.where(places[:, columns] < context, raw, -jnp.inf)
    stats = []
    for j in range(requests):
        rows = slice(j * ROWS, (j + 1) * ROWS)
        weights, own_weight, inverse = softmax_parts(scores[rows, :], own[j])
        scores[rows, :] = weights
        stats.append((own_weight, inverse))
    for j in range(requests):
        rows = slice(j * ROWS, (j + 1) * ROWS)
        own_weight, inverse = stats[j]
        total = jnp.zeros((2 * ROWS, head_dim), F32)
        for c in range(max_pages // CHUNK):
            columns = slice(c * span, (c + 1) * span)
            both = split_scaled(scores[rows, columns], inverse, value_scale[j : j + 1, columns])
            total = total + jnp.dot(both, gather(j, c, 1), preferred_element_type=F32)
        own_weight = (own_weight * inverse).astype(BF16).astype(F32)
        mixed[rows, :] = total[:ROWS] + total[ROWS:] + own_weight * nk_rows[j : j + 1, head_dim:]
    for h in range(per_kv):
        attended[:, h * head_dim : (h + 1) * head_dim] = mixed[pl.ds(h, requests, stride=ROWS), :]
    for copy in w_copies:
        copy.wait()


def attend_away(replicas, per_kv, *refs):
    count = replicas - 1
    away_kv, away_info, goal_mask = refs[:3]
    came = refs[3 : 3 + count]
    outs = refs[3 + count : 3 + 2 * count]
    q_rows, scores = refs[3 + 2 * count :]
    max_pages, _, page_len, head_dim = away_kv.shape[1:]
    factor = 1.0 / math.sqrt(head_dim)
    span = CHUNK * page_len
    for d in range(count):
        pick = goal_mask[d]
        came_all = came[d][...].astype(F32)
        q_rows[...] = jnp.zeros_like(q_rows)
        for h in range(per_kv):
            q_rows[h : h + 1, :] = jnp.sum(
                came_all[:, h * head_dim : (h + 1) * head_dim] * pick, axis=0, keepdims=True
            )
        nk_all = came_all[:, per_kv * head_dim :]
        new_key = jnp.sum(nk_all[:, :head_dim] * pick, axis=0, keepdims=True)
        new_value = jnp.sum(nk_all[:, head_dim:] * pick, axis=0, keepdims=True)
        q = q_rows[...]
        own = jnp.sum(q * new_key, axis=1, keepdims=True) * factor
        q = q.astype(BF16)
        for c in range(max_pages // CHUNK):
            columns = slice(c * span, (c + 1) * span)
            keys = away_kv[d, c * CHUNK : (c + 1) * CHUNK, 0].reshape(span, head_dim)
            raw = dot_keys(q, keys) * away_info[d, 0:1, columns]
            scores[:, columns] = jnp.where(away_info[d, 2:3, columns] > 0, raw, -jnp.inf)
        weights, own_weight, inverse = softmax_parts(scores[...], own)
        total = jnp.zeros((2 * ROWS, head_dim), F32)
        for c in range(max_pages // CHUNK):
            columns = slice(c * span, (c + 1) * span)
            values = away_kv[d, c * CHUNK : (c + 1) * CHUNK, 1].reshape(span, head_dim)
            both = split_scaled(weights[:, columns], inverse, away_info[d, 1:2, columns])
            total = total + jnp.dot(both, values, preferred_element_type=F32)
        own_weight = (own_weight * inverse).astype(BF16).astype(F32)
        mixed = total[:ROWS] + total[ROWS:] + own_weight * new_value
        for h in range(per_kv):
            outs[d][:, h * head_dim : (h + 1) * head_dim] = mixed[h : h + 1, :]


def merge(replicas, attended, here_mask, *refs):
    arrived, out = refs[: replicas - 1], refs[-1]
    head_dim = here_mask.shape[2]
    for h in range(attended.shape[1] // head_dim):
        columns = slice(h * head_dim, (h + 1) * head_dim)
        piece = attended[:, columns]
        for d in range(replicas - 1):
            piece = jnp.where(here_mask[d] > 0, arrived[d][:, columns], piece)
        out[:, columns] = piece.astype(out.dtype)


def on_device(
    kv_pages, page_scale, page_table, lengths, request_moves, queries, new_kv, output_proj, residual
):
    devices = lax.axis_size("replica")
    replicas = devices // KVH
    requests, max_pages = page_table.shape
    pages, _, page_len, head_dim = kv_pages.shape
    per_kv = queries.shape[1] // head_dim
    width = output_proj.shape[1] // KVH
    tokens = max_pages * page_len
    count = replicas - 1

    def toward(value, steps):
        pairs = [(i, (i + steps * KVH) % devices) for i in range(devices)]
        return lax.ppermute(value, "replica", pairs)

    def partner(value, mask):
        return lax.ppermute(value, "replica", [(i, i ^ mask) for i in range(devices)])

    asked = jnp.concatenate([queries, new_kv], axis=1)
    came = [toward(asked, -d) for d in range(1, replicas)]

    def shape(*dims, dtype=F32):
        return jax.ShapeDtypeStruct(dims, dtype)

    in_hbm = functools.partial(pltpu.with_memory_space_constraint, memory_space=pltpu.HBM)
    q_rows, nk_rows, key_scale, value_scale, away_kv, away_info, goal_mask, here_mask = pl.pallas_call(
        functools.partial(set_up, replicas, per_kv),
        out_shape=[
            shape(requests * ROWS, head_dim),
            shape(requests, 2 * head_dim),
            shape(requests, tokens),
            shape(requests, tokens),
            shape(count, max_pages, 2, page_len, head_dim, dtype=BF16),
            shape(count, 8, tokens),
            shape(count, requests, head_dim),
            shape(count, requests, head_dim),
        ],
        in_specs=[HBM] * 7,
        out_specs=[VMEM] * 8,
        scratch_shapes=[
            pltpu.SMEM(lengths.shape, jnp.int32),
            pltpu.SMEM(request_moves.shape, jnp.int32),
            pltpu.SMEM(page_table.shape, jnp.int32),
            pltpu.VMEM(page_table.shape, jnp.int32),
            pltpu.VMEM((2, pages), BF16),
            pltpu.VMEM(queries.shape, BF16),
            pltpu.VMEM(new_kv.shape, BF16),
            pltpu.SMEM((requests,), jnp.int32),
            pltpu.VMEM((2, requests, max_pages), F32),
            pltpu.SemaphoreType.DMA((7,)),
            pltpu.SemaphoreType.DMA((count,)),
        ],
        compiler_params=pltpu.CompilerParams(vmem_limit_bytes=4 * 2**20),
        cost_estimate=pl.CostEstimate(flops=0, bytes_accessed=4 * kv_pages.size, transcendentals=0),
        name="set_up",
    )(*(in_hbm(x) for x in (lengths, request_moves, page_table, page_scale.T, queries, new_kv, kv_pages)))

    rows = pl.pallas_call(
        functools.partial(attend_away, replicas, per_kv),
        out_shape=[shape(1, per_kv * head_dim)] * count,
        in_specs=[VMEM] * (3 + count),
        out_specs=[VMEM] * count,
        scratch_shapes=[pltpu.VMEM((ROWS, head_dim), F32), pltpu.VMEM((ROWS, tokens), F32)],
        compiler_params=pltpu.CompilerParams(vmem_limit_bytes=4 * 2**20),
        name="attend_away",
    )(away_kv, away_info, goal_mask, *came)
    arrived = [toward(rows[d - 1], d) for d in range(1, replicas)]

    attended, *blocks = pl.pallas_call(
        functools.partial(attend_resident, per_kv),
        out_shape=[shape(requests, per_kv * head_dim)]
        + [shape(output_proj.shape[0], 2 * width, dtype=BF16)] * len(ORDER),
        in_specs=[HBM] * 4 + [VMEM] * 5,
        out_specs=[VMEM] * (1 + len(ORDER)),
        scratch_shapes=[
            pltpu.SMEM(lengths.shape, jnp.int32),
            pltpu.SMEM(page_table.shape, jnp.int32),
            pltpu.VMEM((requests * ROWS, tokens), F32),
            pltpu.VMEM((requests * ROWS, head_dim), F32),
            pltpu.SemaphoreType.DMA((2,)),
            pltpu.SemaphoreType.DMA((KVH,)),
        ],
        compiler_params=pltpu.CompilerParams(vmem_limit_bytes=8 * 2**20),
        cost_estimate=pl.CostEstimate(
            flops=4 * per_kv * requests * tokens * head_dim,
            bytes_accessed=4 * output_proj.size,
            transcendentals=requests * ROWS * tokens,
        ),
        name="attend_resident",
    )(
        in_hbm(lengths),
        in_hbm(page_table),
        in_hbm(output_proj),
        rows[0],
        pltpu.with_memory_space_constraint(kv_pages, pltpu.VMEM),
        q_rows,
        nk_rows,
        key_scale,
        value_scale,
    )
    mixture = pl.pallas_call(
        functools.partial(merge, replicas),
        out_shape=shape(*attended.shape, dtype=BF16),
        in_specs=[VMEM] * (2 + count),
        out_specs=VMEM,
        compiler_params=pltpu.CompilerParams(vmem_limit_bytes=2**20),
        name="merge",
    )(attended, here_mask, *arrived)

    came = []
    for block, k in zip(blocks[:-1], ORDER):
        came.append(partner(jnp.dot(mixture, block, preferred_element_type=F32).astype(BF16), k))
    own = lax.optimization_barrier(jnp.dot(mixture, blocks[-1], preferred_element_type=F32))
    for part in came:
        own = own + part.astype(F32)
    other = partner(own[:, width:], 1)
    return (residual.astype(F32) + own[:, :width] + other).astype(BF16)


def solution(mesh):
    return jax.shard_map(
        on_device,
        mesh=mesh,
        in_specs=(
            P(("parts", "replica"), None, None, None),
            P(("parts", "replica"), None),
            P(("parts", "replica"), None),
            P("parts"),
            P("parts"),
            P(("parts", "replica"), None),
            P(("parts", "replica"), None),
            P("replica", None),
            P(("parts", "replica"), None),
        ),
        out_specs=P(("parts", "replica"), None),
        check_vma=False,
    )
```

```python
import functools
import math

import jax
import jax.numpy as jnp
from jax import lax
from jax.experimental import pallas as pl
from jax.experimental.pallas import tpu as pltpu
from jax.sharding import PartitionSpec as P

KVH = 8
ORDER = (2, 4, 6, 0)
ROWS = 8
CHUNK = 4
F32 = jnp.float32
BF16 = jnp.bfloat16
VMEM = pl.BlockSpec(memory_space=pltpu.VMEM)
HBM = pl.BlockSpec(memory_space=pltpu.HBM)


def softmax_parts(scores, own):
    highest = jnp.maximum(jnp.max(scores, axis=1, keepdims=True), own)
    weights = jnp.exp(scores - highest)
    own_weight = jnp.exp(own - highest)
    return weights, own_weight, 1.0 / (jnp.sum(weights, axis=1, keepdims=True) + own_weight)


def split_scaled(weights, inverse, value_scale):
    scaled = (weights * inverse).astype(BF16).astype(F32) * value_scale
    high = scaled.astype(BF16)
    low = (scaled - high.astype(F32)).astype(BF16)
    return jnp.concatenate([high, low], axis=0)


def dot_keys(queries, keys):
    return lax.dot_general(queries, keys, (((1,), (1,)), ((), ())), preferred_element_type=F32)


def set_up(
    replicas,
    per_kv,
    lengths_h,
    moves_h,
    table_h,
    scale_h,
    queries_h,
    new_kv_h,
    kv_pages,
    q_rows,
    nk_rows,
    key_scale,
    value_scale,
    away_kv,
    away_info,
    goal_mask,
    here_mask,
    here_own,
    table_out,
    context,
    lengths,
    moves,
    table_s,
    table_v,
    scale_v,
    queries,
    new_kv,
    target,
    page_scales,
    small_sem,
    kv_sem,
):
    requests, max_pages = table_h.shape
    pages, _, page_len, head_dim = kv_pages.shape
    tokens = max_pages * page_len
    slots = moves_h.shape[0]
    factor = 1.0 / math.sqrt(head_dim)
    replica = lax.axis_index("replica") // KVH

    small = [
        pltpu.make_async_copy(src, dst, small_sem.at[i])
        for i, (src, dst) in enumerate(
            [
                (moves_h, moves),
                (lengths_h, lengths),
                (table_h, table_s),
                (table_h, table_v),
                (scale_h, scale_v),
                (queries_h, queries),
                (new_kv_h, new_kv),
            ]
        )
    ]
    for copy in small:
        copy.start()
    for copy in small:
        copy.wait()

    def place(g, carry):
        slot = moves[g]

        @pl.when(slot // requests == replica)
        def _():
            target[slot % requests] = g

        return carry

    lax.fori_loop(0, slots, place, 0)
    row_ids = lax.broadcasted_iota(jnp.int32, (requests, head_dim), 0)
    leaver, arriver = [], []
    for d in range(1, replicas):
        out_slot = jnp.int32(0)
        here = jnp.int32(0)
        for j in range(requests):
            away = lax.rem(target[j] // requests - replica + replicas, replicas)
            out_slot = jnp.where(away == d, j, out_slot)
            behind = lax.rem(replica - moves[replica * requests + j] // requests + replicas, replicas)
            here = jnp.where(behind == d, j, here)
        leaver.append(out_slot)
        arriver.append(here)

        def fetch(p, carry, d=d, out_slot=out_slot):
            pltpu.make_async_copy(
                kv_pages.at[table_s[out_slot, p]], away_kv.at[d - 1, p], kv_sem.at[d - 1]
            ).start()
            return carry

        lax.fori_loop(0, max_pages, fetch, 0, unroll=4)
        goal_mask[d - 1] = (row_ids == lax.rem(target[out_slot], requests)).astype(F32)
        here_mask[d - 1] = (row_ids == here).astype(F32)

    q_all = queries[...].astype(F32)
    nk_rows[...] = new_kv[...].astype(F32)
    q_rows[...] = jnp.zeros_like(q_rows)
    for h in range(per_kv):
        q_rows[pl.ds(h, requests, stride=ROWS), :] = q_all[:, h * head_dim : (h + 1) * head_dim]

    page_ids = lax.broadcasted_iota(jnp.int32, (pages, max_pages), 0)
    scale_rows = scale_v[...]
    for j in range(requests):
        chosen = (page_ids == table_v[j : j + 1, :]).astype(F32).astype(BF16)
        page_scales[:, j : j + 1, :] = jnp.dot(scale_rows, chosen, preferred_element_type=F32)[:, None, :]
    spread = (
        lax.broadcasted_iota(jnp.int32, (max_pages, tokens), 1) // page_len
        == lax.broadcasted_iota(jnp.int32, (max_pages, tokens), 0)
    ).astype(F32).astype(BF16)
    for d in range(1, replicas):
        here = arriver[d - 1]
        own_rows = q_rows[pl.ds(pl.multiple_of(here * ROWS, ROWS), ROWS), :]
        token = nk_rows[pl.ds(here, 1), :]
        score = jnp.sum(own_rows * token[:, :head_dim], axis=1, keepdims=True) * factor
        here_own[d - 1, 0] = jnp.broadcast_to(score, (ROWS, head_dim))
        here_own[d - 1, 1] = jnp.broadcast_to(token[:, head_dim:], (ROWS, head_dim))
    table_out[...] = table_v[...]
    for j in range(requests):
        context[j : j + 1, :] = jnp.full((1, head_dim), lengths[replica * requests + j], jnp.int32)
    key_scale[...] = jnp.dot(page_scales[0].astype(BF16), spread, preferred_element_type=F32) * factor
    value_scale[...] = jnp.dot(page_scales[1].astype(BF16), spread, preferred_element_type=F32)
    places = lax.broadcasted_iota(jnp.int32, (1, tokens), 1)
    for d in range(1, replicas):
        out_slot = leaver[d - 1]
        away_info[d - 1, 0:1, :] = key_scale[pl.ds(out_slot, 1), :]
        away_info[d - 1, 1:2, :] = value_scale[pl.ds(out_slot, 1), :]
        away_info[d - 1, 2:3, :] = (places < lengths[replica * requests + out_slot]).astype(F32)

    for d in range(1, replicas):
        pltpu.make_async_copy(kv_pages.at[pl.ds(0, max_pages)], away_kv.at[d - 1], kv_sem.at[d - 1]).wait()


def attend_resident(
    per_kv,
    after,
    table_v,
    context,
    pool,
    q_rows,
    nk_rows,
    key_scale,
    value_scale,
    attended,
    *rest,
):
    table_s, scores, mixed, table_sem = rest
    del after
    requests, max_pages = table_v.shape
    _, _, page_len, head_dim = pool.shape
    tokens = max_pages * page_len
    factor = 1.0 / math.sqrt(head_dim)
    copy = pltpu.make_async_copy(table_v, table_s, table_sem)
    copy.start()
    copy.wait()

    def gather(j, c, which):
        return jnp.concatenate([pool[table_s[j, c * CHUNK + i], which] for i in range(CHUNK)], axis=0)

    places = lax.broadcasted_iota(jnp.int32, (1, tokens), 1)
    span = CHUNK * page_len
    own = []
    for j in range(requests):
        rows = slice(j * ROWS, (j + 1) * ROWS)
        q = q_rows[rows, :]
        own.append(jnp.sum(q * nk_rows[j : j + 1, :head_dim], axis=1, keepdims=True) * factor)
        q = q.astype(BF16)
        for c in range(max_pages // CHUNK):
            columns = slice(c * span, (c + 1) * span)
            raw = dot_keys(q, gather(j, c, 0)) * key_scale[j : j + 1, columns]
            scores[rows, columns] = jnp.where(places[:, columns] < context[j : j + 1, :1], raw, -jnp.inf)
    stats = []
    for j in range(requests):
        rows = slice(j * ROWS, (j + 1) * ROWS)
        weights, own_weight, inverse = softmax_parts(scores[rows, :], own[j])
        scores[rows, :] = weights
        stats.append((own_weight, inverse))
    for j in range(requests):
        rows = slice(j * ROWS, (j + 1) * ROWS)
        own_weight, inverse = stats[j]
        total = jnp.zeros((2 * ROWS, head_dim), F32)
        for c in range(max_pages // CHUNK):
            columns = slice(c * span, (c + 1) * span)
            both = split_scaled(scores[rows, columns], inverse, value_scale[j : j + 1, columns])
            total = total + jnp.dot(both, gather(j, c, 1), preferred_element_type=F32)
        own_weight = (own_weight * inverse).astype(BF16).astype(F32)
        mixed[rows, :] = total[:ROWS] + total[ROWS:] + own_weight * nk_rows[j : j + 1, head_dim:]
    for h in range(per_kv):
        attended[:, h * head_dim : (h + 1) * head_dim] = mixed[pl.ds(h, requests, stride=ROWS), :]


def attend_away(replicas, per_kv, *refs):
    count = replicas - 1
    away_kv, away_info, goal_mask = refs[:3]
    came = refs[3 : 3 + count]
    outs = refs[3 + count : 3 + 2 * count]
    q_rows, scores = refs[3 + 2 * count :]
    max_pages, _, page_len, head_dim = away_kv.shape[1:]
    span = CHUNK * page_len
    for d in range(count):
        pick = goal_mask[d]
        came_all = came[d][...].astype(F32)
        q_rows[...] = jnp.zeros_like(q_rows)
        for h in range(per_kv):
            q_rows[h : h + 1, :] = jnp.sum(
                came_all[:, h * head_dim : (h + 1) * head_dim] * pick, axis=0, keepdims=True
            )
        q = q_rows[...].astype(BF16)
        for c in range(max_pages // CHUNK):
            columns = slice(c * span, (c + 1) * span)
            keys = away_kv[d, c * CHUNK : (c + 1) * CHUNK, 0].reshape(span, head_dim)
            raw = dot_keys(q, keys) * away_info[d, 0:1, columns]
            scores[:, columns] = jnp.where(away_info[d, 2:3, columns] > 0, raw, -jnp.inf)
        highest = jnp.max(scores[...], axis=1, keepdims=True)
        weights = jnp.exp(scores[...] - highest)
        total = jnp.sum(weights, axis=1, keepdims=True)
        inverse = 1.0 / total
        mixed = jnp.zeros((2 * ROWS, head_dim), F32)
        for c in range(max_pages // CHUNK):
            columns = slice(c * span, (c + 1) * span)
            values = away_kv[d, c * CHUNK : (c + 1) * CHUNK, 1].reshape(span, head_dim)
            both = split_scaled(weights[:, columns], inverse, away_info[d, 1:2, columns])
            mixed = mixed + jnp.dot(both, values, preferred_element_type=F32)
        outs[d][0] = mixed[:ROWS] + mixed[ROWS:]
        outs[d][1] = jnp.broadcast_to(highest, (ROWS, head_dim))
        outs[d][2] = jnp.broadcast_to(total, (ROWS, head_dim))


def merge(replicas, attended, here_mask, here_own, *refs):
    arrived, out = refs[: replicas - 1], refs[-1]
    head_dim = here_mask.shape[2]
    moved = []
    for d in range(replicas - 1):
        own = here_own[d, 0]
        highest = jnp.maximum(arrived[d][1], own)
        cached = arrived[d][2] * jnp.exp(arrived[d][1] - highest)
        own = jnp.exp(own - highest)
        inverse = 1.0 / (cached + own)
        own = (own * inverse).astype(BF16).astype(F32)
        moved.append(arrived[d][0] * (cached * inverse) + own * here_own[d, 1])
    for h in range(attended.shape[1] // head_dim):
        columns = slice(h * head_dim, (h + 1) * head_dim)
        piece = attended[:, columns]
        for d in range(replicas - 1):
            piece = jnp.where(here_mask[d] > 0, moved[d][h : h + 1], piece)
        out[:, columns] = piece.astype(out.dtype)


def on_device(
    kv_pages, page_scale, page_table, lengths, request_moves, queries, new_kv, output_proj, residual
):
    devices = lax.axis_size("replica")
    replicas = devices // KVH
    requests, max_pages = page_table.shape
    pages, _, page_len, head_dim = kv_pages.shape
    per_kv = queries.shape[1] // head_dim
    width = output_proj.shape[1] // KVH
    tokens = max_pages * page_len
    count = replicas - 1

    def toward(value, steps):
        pairs = [(i, (i + steps * KVH) % devices) for i in range(devices)]
        return lax.ppermute(value, "replica", pairs)

    def partner(value, mask):
        return lax.ppermute(value, "replica", [(i, i ^ mask) for i in range(devices)])

    position = lax.axis_index("replica").astype(jnp.uint32)
    offsets = [((position % KVH) >> 1 ^ (k >> 1)) * (2 * width) for k in ORDER]
    queries, start, first, *offsets = lax.optimization_barrier(
        (queries, jnp.uint32(0), position % 2 == 0, *offsets)
    )
    came = [toward(queries, -d) for d in range(1, replicas)]

    def shape(*dims, dtype=F32):
        return jax.ShapeDtypeStruct(dims, dtype)

    in_hbm = functools.partial(pltpu.with_memory_space_constraint, memory_space=pltpu.HBM)
    q_rows, nk_rows, key_scale, value_scale, away_kv, away_info, goal_mask, *home = pl.pallas_call(
        functools.partial(set_up, replicas, per_kv),
        out_shape=[
            shape(requests * ROWS, head_dim),
            shape(requests, 2 * head_dim),
            shape(requests, tokens),
            shape(requests, tokens),
            shape(count, max_pages, 2, page_len, head_dim, dtype=BF16),
            shape(count, 8, tokens),
            shape(count, requests, head_dim),
            shape(count, requests, head_dim),
            shape(count, 2, ROWS, head_dim),
            shape(requests, max_pages, dtype=jnp.int32),
            shape(requests, head_dim, dtype=jnp.int32),
        ],
        in_specs=[HBM] * 7,
        out_specs=[VMEM] * 11,
        scratch_shapes=[
            pltpu.SMEM(lengths.shape, jnp.int32),
            pltpu.SMEM(request_moves.shape, jnp.int32),
            pltpu.SMEM(page_table.shape, jnp.int32),
            pltpu.VMEM(page_table.shape, jnp.int32),
            pltpu.VMEM((2, pages), BF16),
            pltpu.VMEM(queries.shape, BF16),
            pltpu.VMEM(new_kv.shape, BF16),
            pltpu.SMEM((requests,), jnp.int32),
            pltpu.VMEM((2, requests, max_pages), F32),
            pltpu.SemaphoreType.DMA((7,)),
            pltpu.SemaphoreType.DMA((count,)),
        ],
        compiler_params=pltpu.CompilerParams(vmem_limit_bytes=4 * 2**20),
        cost_estimate=pl.CostEstimate(flops=0, bytes_accessed=4 * kv_pages.size, transcendentals=0),
        name="set_up",
    )(*(in_hbm(x) for x in (lengths, request_moves, page_table, page_scale.T, queries, new_kv, kv_pages)))

    here_mask, here_own, table_v, context = home

    rows = pl.pallas_call(
        functools.partial(attend_away, replicas, per_kv),
        out_shape=[shape(3, ROWS, head_dim)] * count,
        in_specs=[VMEM] * (3 + count),
        out_specs=[VMEM] * count,
        scratch_shapes=[pltpu.VMEM((ROWS, head_dim), F32), pltpu.VMEM((ROWS, tokens), F32)],
        compiler_params=pltpu.CompilerParams(vmem_limit_bytes=4 * 2**20),
        name="attend_away",
    )(away_kv, away_info, goal_mask, *came)
    arrived = [toward(rows[d - 1], d) for d in range(1, replicas)]

    attended = pl.pallas_call(
        functools.partial(attend_resident, per_kv),
        out_shape=shape(requests, per_kv * head_dim),
        in_specs=[HBM] + [VMEM] * 7,
        out_specs=VMEM,
        scratch_shapes=[
            pltpu.SMEM(page_table.shape, jnp.int32),
            pltpu.VMEM((requests * ROWS, tokens), F32),
            pltpu.VMEM((requests * ROWS, head_dim), F32),
            pltpu.SemaphoreType.DMA,
        ],
        compiler_params=pltpu.CompilerParams(vmem_limit_bytes=8 * 2**20),
        cost_estimate=pl.CostEstimate(
            flops=4 * per_kv * requests * tokens * head_dim,
            bytes_accessed=4 * output_proj.size,
            transcendentals=requests * ROWS * tokens,
        ),
        name="attend_resident",
    )(
        rows[0],
        table_v,
        context,
        pltpu.with_memory_space_constraint(kv_pages, pltpu.VMEM),
        q_rows,
        nk_rows,
        key_scale,
        value_scale,
    )
    mixture = pl.pallas_call(
        functools.partial(merge, replicas),
        out_shape=shape(*attended.shape, dtype=BF16),
        in_specs=[VMEM] * (3 + count),
        out_specs=VMEM,
        compiler_params=pltpu.CompilerParams(vmem_limit_bytes=2**20),
        name="merge",
    )(attended, here_mask, here_own, *arrived)

    def toward_chip(k):
        block = lax.dynamic_slice(output_proj, (start, offsets[ORDER.index(k)]), (output_proj.shape[0], 2 * width))
        return jnp.dot(mixture, block, preferred_element_type=F32)

    came = []
    for k in ORDER[:-1]:
        came.append(partner(toward_chip(k).astype(BF16), k))
    own = lax.optimization_barrier(toward_chip(0))
    for part in came:
        own = own + part.astype(F32)
    other = partner(jnp.where(first, own[:, width:], own[:, :width]), 1)
    return (residual.astype(F32) + jnp.where(first, own[:, :width], own[:, width:]) + other).astype(BF16)


def solution(mesh):
    return jax.shard_map(
        on_device,
        mesh=mesh,
        in_specs=(
            P(("parts", "replica"), None, None, None),
            P(("parts", "replica"), None),
            P(("parts", "replica"), None),
            P("parts"),
            P("parts"),
            P(("parts", "replica"), None),
            P(("parts", "replica"), None),
            P("replica", None),
            P(("parts", "replica"), None),
        ),
        out_specs=P(("parts", "replica"), None),
        check_vma=False,
    )
```

```python
import functools
import math

import jax
import jax.numpy as jnp
from jax import lax
from jax.experimental import pallas as pl
from jax.experimental.pallas import tpu as pltpu
from jax.sharding import PartitionSpec as P

KVH = 8
ORDER = (2, 6, 4, 0)
EARLY = 2
ROWS = 8
CHUNK = 4
F32 = jnp.float32
BF16 = jnp.bfloat16
VMEM = pl.BlockSpec(memory_space=pltpu.VMEM)
HBM = pl.BlockSpec(memory_space=pltpu.HBM)


def softmax_parts(scores, own):
    highest = jnp.maximum(jnp.max(scores, axis=1, keepdims=True), own)
    weights = jnp.exp(scores - highest)
    own_weight = jnp.exp(own - highest)
    return weights, own_weight, 1.0 / (jnp.sum(weights, axis=1, keepdims=True) + own_weight)


def split_scaled(weights, inverse, value_scale):
    scaled = (weights * inverse).astype(BF16).astype(F32) * value_scale
    high = scaled.astype(BF16)
    low = (scaled - high.astype(F32)).astype(BF16)
    return jnp.concatenate([high, low], axis=0)


def dot_keys(queries, keys):
    return lax.dot_general(queries, keys, (((1,), (1,)), ((), ())), preferred_element_type=F32)


def weight_copies(proj, parts, sem):
    width = proj.shape[1] // KVH
    shard = lax.axis_index("replica") % KVH
    copies = []
    for out, core, distances in parts:
        for i, k in enumerate(distances):
            column = pl.multiple_of((shard ^ k ^ core) * width, 128)
            copies.append(
                pltpu.make_async_copy(
                    proj.at[:, pl.ds(column, width)], out.at[:, pl.ds(i * width, width)], sem.at[len(copies)]
                )
            )
    return copies


def set_up(
    replicas,
    per_kv,
    lengths_h,
    moves_h,
    table_h,
    scale_h,
    queries_h,
    new_kv_h,
    kv_pages,
    proj,
    far_early,
    q_rows,
    nk_rows,
    key_scale,
    value_scale,
    away_kv,
    away_info,
    goal_mask,
    here_mask,
    here_own,
    table_out,
    context,
    lengths,
    moves,
    table_s,
    table_v,
    scale_v,
    queries,
    new_kv,
    target,
    page_scales,
    small_sem,
    kv_sem,
    w_sem,
):
    requests, max_pages = table_h.shape
    pages, _, page_len, head_dim = kv_pages.shape
    tokens = max_pages * page_len
    slots = moves_h.shape[0]
    factor = 1.0 / math.sqrt(head_dim)
    replica = lax.axis_index("replica") // KVH

    small = [
        pltpu.make_async_copy(src, dst, small_sem.at[i])
        for i, (src, dst) in enumerate(
            [
                (moves_h, moves),
                (lengths_h, lengths),
                (table_h, table_s),
                (table_h, table_v),
                (scale_h, scale_v),
                (queries_h, queries),
                (new_kv_h, new_kv),
            ]
        )
    ]
    for copy in small:
        copy.start()
    for copy in small:
        copy.wait()

    def place(g, carry):
        slot = moves[g]

        @pl.when(slot // requests == replica)
        def _():
            target[slot % requests] = g

        return carry

    lax.fori_loop(0, slots, place, 0)
    row_ids = lax.broadcasted_iota(jnp.int32, (requests, head_dim), 0)
    leaver, arriver = [], []
    for d in range(1, replicas):
        out_slot = jnp.int32(0)
        here = jnp.int32(0)
        for j in range(requests):
            away = lax.rem(target[j] // requests - replica + replicas, replicas)
            out_slot = jnp.where(away == d, j, out_slot)
            behind = lax.rem(replica - moves[replica * requests + j] // requests + replicas, replicas)
            here = jnp.where(behind == d, j, here)
        leaver.append(out_slot)
        arriver.append(here)

        def fetch(p, carry, d=d, out_slot=out_slot):
            pltpu.make_async_copy(
                kv_pages.at[table_s[out_slot, p]], away_kv.at[d - 1, p], kv_sem.at[d - 1]
            ).start()
            return carry

        lax.fori_loop(0, max_pages, fetch, 0, unroll=4)
    w_copies = weight_copies(proj, [(far_early, 1, ORDER[:EARLY])], w_sem)
    for copy in w_copies:
        copy.start()
        goal_mask[d - 1] = (row_ids == lax.rem(target[out_slot], requests)).astype(F32)
        here_mask[d - 1] = (row_ids == here).astype(F32)

    q_all = queries[...].astype(F32)
    nk_rows[...] = new_kv[...].astype(F32)
    q_rows[...] = jnp.zeros_like(q_rows)
    for h in range(per_kv):
        q_rows[pl.ds(h, requests, stride=ROWS), :] = q_all[:, h * head_dim : (h + 1) * head_dim]

    page_ids = lax.broadcasted_iota(jnp.int32, (pages, max_pages), 0)
    scale_rows = scale_v[...]
    for j in range(requests):
        chosen = (page_ids == table_v[j : j + 1, :]).astype(F32).astype(BF16)
        page_scales[:, j : j + 1, :] = jnp.dot(scale_rows, chosen, preferred_element_type=F32)[:, None, :]
    spread = (
        lax.broadcasted_iota(jnp.int32, (max_pages, tokens), 1) // page_len
        == lax.broadcasted_iota(jnp.int32, (max_pages, tokens), 0)
    ).astype(F32).astype(BF16)
    for d in range(1, replicas):
        here = arriver[d - 1]
        own_rows = q_rows[pl.ds(pl.multiple_of(here * ROWS, ROWS), ROWS), :]
        token = nk_rows[pl.ds(here, 1), :]
        score = jnp.sum(own_rows * token[:, :head_dim], axis=1, keepdims=True) * factor
        here_own[d - 1, 0] = jnp.broadcast_to(score, (ROWS, head_dim))
        here_own[d - 1, 1] = jnp.broadcast_to(token[:, head_dim:], (ROWS, head_dim))
    table_out[...] = table_v[...]
    for j in range(requests):
        context[j : j + 1, :] = jnp.full((1, head_dim), lengths[replica * requests + j], jnp.int32)
    key_scale[...] = jnp.dot(page_scales[0].astype(BF16), spread, preferred_element_type=F32) * factor
    value_scale[...] = jnp.dot(page_scales[1].astype(BF16), spread, preferred_element_type=F32)
    places = lax.broadcasted_iota(jnp.int32, (1, tokens), 1)
    for d in range(1, replicas):
        out_slot = leaver[d - 1]
        away_info[d - 1, 0:1, :] = key_scale[pl.ds(out_slot, 1), :]
        away_info[d - 1, 1:2, :] = value_scale[pl.ds(out_slot, 1), :]
        away_info[d - 1, 2:3, :] = (places < lengths[replica * requests + out_slot]).astype(F32)

    for d in range(1, replicas):
        pltpu.make_async_copy(kv_pages.at[pl.ds(0, max_pages)], away_kv.at[d - 1], kv_sem.at[d - 1]).wait()
    for copy in w_copies:
        copy.wait()


def attend_resident(
    per_kv,
    proj,
    after,
    table_v,
    context,
    pool,
    q_rows,
    nk_rows,
    key_scale,
    value_scale,
    attended,
    far_late,
    near,
    table_s,
    scores,
    mixed,
    table_sem,
    w_sem,
):
    del after
    requests, max_pages = table_v.shape
    _, _, page_len, head_dim = pool.shape
    tokens = max_pages * page_len
    factor = 1.0 / math.sqrt(head_dim)
    copy = pltpu.make_async_copy(table_v, table_s, table_sem)
    copy.start()
    w_copies = weight_copies(proj, [(far_late, 1, ORDER[EARLY:]), (near, 0, ORDER)], w_sem)
    for w_copy in w_copies:
        w_copy.start()
    copy.wait()

    def gather(j, c, which):
        return jnp.concatenate([pool[table_s[j, c * CHUNK + i], which] for i in range(CHUNK)], axis=0)

    places = lax.broadcasted_iota(jnp.int32, (1, tokens), 1)
    span = CHUNK * page_len
    own = []
    for j in range(requests):
        rows = slice(j * ROWS, (j + 1) * ROWS)
        q = q_rows[rows, :]
        own.append(jnp.sum(q * nk_rows[j : j + 1, :head_dim], axis=1, keepdims=True) * factor)
        q = q.astype(BF16)
        for c in range(max_pages // CHUNK):
            columns = slice(c * span, (c + 1) * span)
            raw = dot_keys(q, gather(j, c, 0)) * key_scale[j : j + 1, columns]
            scores[rows, columns] = jnp.where(places[:, columns] < context[j : j + 1, :1], raw, -jnp.inf)
    stats = []
    for j in range(requests):
        rows = slice(j * ROWS, (j + 1) * ROWS)
        weights, own_weight, inverse = softmax_parts(scores[rows, :], own[j])
        scores[rows, :] = weights
        stats.append((own_weight, inverse))
    for j in range(requests):
        rows = slice(j * ROWS, (j + 1) * ROWS)
        own_weight, inverse = stats[j]
        total = jnp.zeros((2 * ROWS, head_dim), F32)
        for c in range(max_pages // CHUNK):
            columns = slice(c * span, (c + 1) * span)
            both = split_scaled(scores[rows, columns], inverse, value_scale[j : j + 1, columns])
            total = total + jnp.dot(both, gather(j, c, 1), preferred_element_type=F32)
        own_weight = (own_weight * inverse).astype(BF16).astype(F32)
        mixed[rows, :] = total[:ROWS] + total[ROWS:] + own_weight * nk_rows[j : j + 1, head_dim:]
    for h in range(per_kv):
        attended[:, h * head_dim : (h + 1) * head_dim] = mixed[pl.ds(h, requests, stride=ROWS), :]
    for w_copy in w_copies:
        w_copy.wait()


def attend_away(replicas, per_kv, *refs):
    count = replicas - 1
    away_kv, away_info, goal_mask = refs[:3]
    came = refs[3 : 3 + count]
    outs = refs[3 + count : 3 + 2 * count]
    q_rows, scores = refs[3 + 2 * count :]
    max_pages, _, page_len, head_dim = away_kv.shape[1:]
    span = CHUNK * page_len
    for d in range(count):
        pick = goal_mask[d]
        came_all = came[d][...].astype(F32)
        q_rows[...] = jnp.zeros_like(q_rows)
        for h in range(per_kv):
            q_rows[h : h + 1, :] = jnp.sum(
                came_all[:, h * head_dim : (h + 1) * head_dim] * pick, axis=0, keepdims=True
            )
        q = q_rows[...].astype(BF16)
        for c in range(max_pages // CHUNK):
            columns = slice(c * span, (c + 1) * span)
            keys = away_kv[d, c * CHUNK : (c + 1) * CHUNK, 0].reshape(span, head_dim)
            raw = dot_keys(q, keys) * away_info[d, 0:1, columns]
            scores[:, columns] = jnp.where(away_info[d, 2:3, columns] > 0, raw, -jnp.inf)
        highest = jnp.max(scores[...], axis=1, keepdims=True)
        weights = jnp.exp(scores[...] - highest)
        total = jnp.sum(weights, axis=1, keepdims=True)
        inverse = 1.0 / total
        mixed = jnp.zeros((2 * ROWS, head_dim), F32)
        for c in range(max_pages // CHUNK):
            columns = slice(c * span, (c + 1) * span)
            values = away_kv[d, c * CHUNK : (c + 1) * CHUNK, 1].reshape(span, head_dim)
            both = split_scaled(weights[:, columns], inverse, away_info[d, 1:2, columns])
            mixed = mixed + jnp.dot(both, values, preferred_element_type=F32)
        outs[d][0] = mixed[:ROWS] + mixed[ROWS:]
        outs[d][1] = jnp.broadcast_to(highest, (ROWS, head_dim))
        outs[d][2] = jnp.broadcast_to(total, (ROWS, head_dim))


def merge(replicas, attended, here_mask, here_own, *refs):
    arrived, out = refs[: replicas - 1], refs[-1]
    head_dim = here_mask.shape[2]
    moved = []
    for d in range(replicas - 1):
        own = here_own[d, 0]
        highest = jnp.maximum(arrived[d][1], own)
        cached = arrived[d][2] * jnp.exp(arrived[d][1] - highest)
        own = jnp.exp(own - highest)
        inverse = 1.0 / (cached + own)
        own = (own * inverse).astype(BF16).astype(F32)
        moved.append(arrived[d][0] * (cached * inverse) + own * here_own[d, 1])
    for h in range(attended.shape[1] // head_dim):
        columns = slice(h * head_dim, (h + 1) * head_dim)
        piece = attended[:, columns]
        for d in range(replicas - 1):
            piece = jnp.where(here_mask[d] > 0, moved[d][h : h + 1], piece)
        out[:, columns] = piece.astype(out.dtype)


def on_device(
    kv_pages, page_scale, page_table, lengths, request_moves, queries, new_kv, output_proj, residual
):
    devices = lax.axis_size("replica")
    replicas = devices // KVH
    requests, max_pages = page_table.shape
    pages, _, page_len, head_dim = kv_pages.shape
    per_kv = queries.shape[1] // head_dim
    width = output_proj.shape[1] // KVH
    tokens = max_pages * page_len
    count = replicas - 1

    def toward(value, steps):
        pairs = [(i, (i + steps * KVH) % devices) for i in range(devices)]
        return lax.ppermute(value, "replica", pairs)

    def partner(value, mask):
        return lax.ppermute(value, "replica", [(i, i ^ mask) for i in range(devices)])

    came = [toward(queries, -d) for d in range(1, replicas)]

    def shape(*dims, dtype=F32):
        return jax.ShapeDtypeStruct(dims, dtype)

    in_hbm = functools.partial(pltpu.with_memory_space_constraint, memory_space=pltpu.HBM)
    far_early, q_rows, nk_rows, key_scale, value_scale, away_kv, away_info, goal_mask, *home = pl.pallas_call(
        functools.partial(set_up, replicas, per_kv),
        out_shape=[
            shape(output_proj.shape[0], EARLY * width, dtype=BF16),
            shape(requests * ROWS, head_dim),
            shape(requests, 2 * head_dim),
            shape(requests, tokens),
            shape(requests, tokens),
            shape(count, max_pages, 2, page_len, head_dim, dtype=BF16),
            shape(count, 8, tokens),
            shape(count, requests, head_dim),
            shape(count, requests, head_dim),
            shape(count, 2, ROWS, head_dim),
            shape(requests, max_pages, dtype=jnp.int32),
            shape(requests, head_dim, dtype=jnp.int32),
        ],
        in_specs=[HBM] * 8,
        out_specs=[VMEM] * 12,
        scratch_shapes=[
            pltpu.SMEM(lengths.shape, jnp.int32),
            pltpu.SMEM(request_moves.shape, jnp.int32),
            pltpu.SMEM(page_table.shape, jnp.int32),
            pltpu.VMEM(page_table.shape, jnp.int32),
            pltpu.VMEM((2, pages), BF16),
            pltpu.VMEM(queries.shape, BF16),
            pltpu.VMEM(new_kv.shape, BF16),
            pltpu.SMEM((requests,), jnp.int32),
            pltpu.VMEM((2, requests, max_pages), F32),
            pltpu.SemaphoreType.DMA((7,)),
            pltpu.SemaphoreType.DMA((count,)),
            pltpu.SemaphoreType.DMA((EARLY,)),
        ],
        compiler_params=pltpu.CompilerParams(vmem_limit_bytes=4 * 2**20),
        cost_estimate=pl.CostEstimate(flops=0, bytes_accessed=kv_pages.size, transcendentals=0),
        name="set_up",
    )(*(in_hbm(x) for x in (lengths, request_moves, page_table, page_scale.T, queries, new_kv, kv_pages, output_proj)))

    here_mask, here_own, table_v, context = home

    rows = pl.pallas_call(
        functools.partial(attend_away, replicas, per_kv),
        out_shape=[shape(3, ROWS, head_dim)] * count,
        in_specs=[VMEM] * (3 + count),
        out_specs=[VMEM] * count,
        scratch_shapes=[pltpu.VMEM((ROWS, head_dim), F32), pltpu.VMEM((ROWS, tokens), F32)],
        compiler_params=pltpu.CompilerParams(vmem_limit_bytes=4 * 2**20),
        name="attend_away",
    )(away_kv, away_info, goal_mask, *came)
    arrived = [toward(rows[d - 1], d) for d in range(1, replicas)]

    attended, far_late, near = pl.pallas_call(
        functools.partial(attend_resident, per_kv),
        out_shape=[
            shape(requests, per_kv * head_dim),
            shape(output_proj.shape[0], (len(ORDER) - EARLY) * width, dtype=BF16),
            shape(output_proj.shape[0], len(ORDER) * width, dtype=BF16),
        ],
        in_specs=[HBM] * 2 + [VMEM] * 7,
        out_specs=[VMEM] * 3,
        scratch_shapes=[
            pltpu.SMEM(page_table.shape, jnp.int32),
            pltpu.VMEM((requests * ROWS, tokens), F32),
            pltpu.VMEM((requests * ROWS, head_dim), F32),
            pltpu.SemaphoreType.DMA,
            pltpu.SemaphoreType.DMA((2 * len(ORDER) - EARLY,)),
        ],
        compiler_params=pltpu.CompilerParams(vmem_limit_bytes=8 * 2**20),
        cost_estimate=pl.CostEstimate(
            flops=4 * per_kv * requests * tokens * head_dim,
            bytes_accessed=4 * output_proj.size,
            transcendentals=requests * ROWS * tokens,
        ),
        name="attend_resident",
    )(
        in_hbm(output_proj),
        rows[0],
        table_v,
        context,
        pltpu.with_memory_space_constraint(kv_pages, pltpu.VMEM),
        q_rows,
        nk_rows,
        key_scale,
        value_scale,
    )
    mixture = pl.pallas_call(
        functools.partial(merge, replicas),
        out_shape=shape(*attended.shape, dtype=BF16),
        in_specs=[VMEM] * (3 + count),
        out_specs=VMEM,
        compiler_params=pltpu.CompilerParams(vmem_limit_bytes=2**20),
        name="merge",
    )(attended, here_mask, here_own, *arrived)

    other = []
    for weights in (far_early, far_late):
        part = partner(jnp.dot(mixture, weights, preferred_element_type=F32), 1)
        other += [part[:, i * width : (i + 1) * width] for i in range(part.shape[1] // width)]
    own = lax.optimization_barrier(jnp.dot(mixture, near, preferred_element_type=F32))
    chip = [own[:, i * width : (i + 1) * width] + part for i, part in enumerate(other)]
    came = [partner(part.astype(BF16), k) for part, k in zip(chip[:-1], ORDER)]
    total = chip[-1]
    for part in came:
        total = total + part.astype(F32)
    return (residual.astype(F32) + total).astype(BF16)


def solution(mesh):
    return jax.shard_map(
        on_device,
        mesh=mesh,
        in_specs=(
            P(("parts", "replica"), None, None, None),
            P(("parts", "replica"), None),
            P(("parts", "replica"), None),
            P("parts"),
            P("parts"),
            P(("parts", "replica"), None),
            P(("parts", "replica"), None),
            P("replica", None),
            P(("parts", "replica"), None),
        ),
        out_specs=P(("parts", "replica"), None),
        check_vma=False,
    )
```

```python
import functools
import math

import jax
import jax.numpy as jnp
from jax import lax
from jax.experimental import pallas as pl
from jax.experimental.pallas import tpu as pltpu
from jax.sharding import PartitionSpec as P

KVH = 8
ROWS = 8
CHUNK = 4
F32 = jnp.float32
BF16 = jnp.bfloat16
VMEM = pl.BlockSpec(memory_space=pltpu.VMEM)
HBM = pl.BlockSpec(memory_space=pltpu.HBM)


def softmax_parts(scores, own):
    highest = jnp.maximum(jnp.max(scores, axis=1, keepdims=True), own)
    weights = jnp.exp(scores - highest)
    own_weight = jnp.exp(own - highest)
    return weights, own_weight, 1.0 / (jnp.sum(weights, axis=1, keepdims=True) + own_weight)


def split_scaled(weights, inverse, value_scale):
    scaled = (weights * inverse).astype(BF16).astype(F32) * value_scale
    high = scaled.astype(BF16)
    low = (scaled - high.astype(F32)).astype(BF16)
    return jnp.concatenate([high, low], axis=0)


def dot_keys(queries, keys):
    return lax.dot_general(queries, keys, (((1,), (1,)), ((), ())), preferred_element_type=F32)


def set_up(
    replicas,
    per_kv,
    lengths_h,
    moves_h,
    table_h,
    scale_h,
    queries_h,
    new_kv_h,
    kv_pages,
    q_rows,
    nk_rows,
    key_scale,
    value_scale,
    away_kv,
    away_info,
    goal_mask,
    here_mask,
    here_own,
    table_out,
    context,
    lengths,
    moves,
    table_s,
    table_v,
    scale_v,
    queries,
    new_kv,
    target,
    page_scales,
    small_sem,
    kv_sem,
):
    requests, max_pages = table_h.shape
    pages, _, page_len, head_dim = kv_pages.shape
    tokens = max_pages * page_len
    slots = moves_h.shape[0]
    factor = 1.0 / math.sqrt(head_dim)
    replica = lax.axis_index("replica") // KVH

    small = [
        pltpu.make_async_copy(src, dst, small_sem.at[i])
        for i, (src, dst) in enumerate(
            [
                (moves_h, moves),
                (lengths_h, lengths),
                (table_h, table_s),
                (table_h, table_v),
                (scale_h, scale_v),
                (queries_h, queries),
                (new_kv_h, new_kv),
            ]
        )
    ]
    for copy in small:
        copy.start()
    for copy in small:
        copy.wait()

    def place(g, carry):
        slot = moves[g]

        @pl.when(slot // requests == replica)
        def _():
            target[slot % requests] = g

        return carry

    lax.fori_loop(0, slots, place, 0)
    row_ids = lax.broadcasted_iota(jnp.int32, (requests, head_dim), 0)
    leaver, arriver = [], []
    for d in range(1, replicas):
        out_slot = jnp.int32(0)
        here = jnp.int32(0)
        for j in range(requests):
            away = lax.rem(target[j] // requests - replica + replicas, replicas)
            out_slot = jnp.where(away == d, j, out_slot)
            behind = lax.rem(replica - moves[replica * requests + j] // requests + replicas, replicas)
            here = jnp.where(behind == d, j, here)
        leaver.append(out_slot)
        arriver.append(here)

        def fetch(p, carry, d=d, out_slot=out_slot):
            pltpu.make_async_copy(
                kv_pages.at[table_s[out_slot, p]], away_kv.at[d - 1, p], kv_sem.at[d - 1]
            ).start()
            return carry

        lax.fori_loop(0, max_pages, fetch, 0, unroll=4)
        goal_mask[d - 1] = (row_ids == lax.rem(target[out_slot], requests)).astype(F32)
        here_mask[d - 1] = (row_ids == here).astype(F32)

    q_all = queries[...].astype(F32)
    nk_rows[...] = new_kv[...].astype(F32)
    q_rows[...] = jnp.zeros_like(q_rows)
    for h in range(per_kv):
        q_rows[pl.ds(h, requests, stride=ROWS), :] = q_all[:, h * head_dim : (h + 1) * head_dim]

    page_ids = lax.broadcasted_iota(jnp.int32, (pages, max_pages), 0)
    scale_rows = scale_v[...]
    for j in range(requests):
        chosen = (page_ids == table_v[j : j + 1, :]).astype(F32).astype(BF16)
        page_scales[:, j : j + 1, :] = jnp.dot(scale_rows, chosen, preferred_element_type=F32)[:, None, :]
    spread = (
        lax.broadcasted_iota(jnp.int32, (max_pages, tokens), 1) // page_len
        == lax.broadcasted_iota(jnp.int32, (max_pages, tokens), 0)
    ).astype(F32).astype(BF16)
    for d in range(1, replicas):
        here = arriver[d - 1]
        own_rows = q_rows[pl.ds(pl.multiple_of(here * ROWS, ROWS), ROWS), :]
        token = nk_rows[pl.ds(here, 1), :]
        score = jnp.sum(own_rows * token[:, :head_dim], axis=1, keepdims=True) * factor
        here_own[d - 1, 0] = jnp.broadcast_to(score, (ROWS, head_dim))
        here_own[d - 1, 1] = jnp.broadcast_to(token[:, head_dim:], (ROWS, head_dim))
    table_out[...] = table_v[...]
    for j in range(requests):
        context[j : j + 1, :] = jnp.full((1, head_dim), lengths[replica * requests + j], jnp.int32)
    key_scale[...] = jnp.dot(page_scales[0].astype(BF16), spread, preferred_element_type=F32) * factor
    value_scale[...] = jnp.dot(page_scales[1].astype(BF16), spread, preferred_element_type=F32)
    places = lax.broadcasted_iota(jnp.int32, (1, tokens), 1)
    for d in range(1, replicas):
        out_slot = leaver[d - 1]
        away_info[d - 1, 0:1, :] = key_scale[pl.ds(out_slot, 1), :]
        away_info[d - 1, 1:2, :] = value_scale[pl.ds(out_slot, 1), :]
        away_info[d - 1, 2:3, :] = (places < lengths[replica * requests + out_slot]).astype(F32)

    for d in range(1, replicas):
        pltpu.make_async_copy(kv_pages.at[pl.ds(0, max_pages)], away_kv.at[d - 1], kv_sem.at[d - 1]).wait()


def attend_resident(
    per_kv,
    after,
    table_v,
    context,
    pool,
    q_rows,
    nk_rows,
    key_scale,
    value_scale,
    attended,
    *rest,
):
    table_s, scores, mixed, table_sem = rest
    del after
    requests, max_pages = table_v.shape
    _, _, page_len, head_dim = pool.shape
    tokens = max_pages * page_len
    factor = 1.0 / math.sqrt(head_dim)
    copy = pltpu.make_async_copy(table_v, table_s, table_sem)
    copy.start()
    copy.wait()

    def gather(j, c, which):
        return jnp.concatenate([pool[table_s[j, c * CHUNK + i], which] for i in range(CHUNK)], axis=0)

    places = lax.broadcasted_iota(jnp.int32, (1, tokens), 1)
    span = CHUNK * page_len
    own = []
    for j in range(requests):
        rows = slice(j * ROWS, (j + 1) * ROWS)
        q = q_rows[rows, :]
        own.append(jnp.sum(q * nk_rows[j : j + 1, :head_dim], axis=1, keepdims=True) * factor)
        q = q.astype(BF16)
        for c in range(max_pages // CHUNK):
            columns = slice(c * span, (c + 1) * span)
            raw = dot_keys(q, gather(j, c, 0)) * key_scale[j : j + 1, columns]
            scores[rows, columns] = jnp.where(places[:, columns] < context[j : j + 1, :1], raw, -jnp.inf)
    stats = []
    for j in range(requests):
        rows = slice(j * ROWS, (j + 1) * ROWS)
        weights, own_weight, inverse = softmax_parts(scores[rows, :], own[j])
        scores[rows, :] = weights
        stats.append((own_weight, inverse))
    for j in range(requests):
        rows = slice(j * ROWS, (j + 1) * ROWS)
        own_weight, inverse = stats[j]
        total = jnp.zeros((2 * ROWS, head_dim), F32)
        for c in range(max_pages // CHUNK):
            columns = slice(c * span, (c + 1) * span)
            both = split_scaled(scores[rows, columns], inverse, value_scale[j : j + 1, columns])
            total = total + jnp.dot(both, gather(j, c, 1), preferred_element_type=F32)
        own_weight = (own_weight * inverse).astype(BF16).astype(F32)
        mixed[rows, :] = total[:ROWS] + total[ROWS:] + own_weight * nk_rows[j : j + 1, head_dim:]
    for h in range(per_kv):
        attended[:, h * head_dim : (h + 1) * head_dim] = mixed[pl.ds(h, requests, stride=ROWS), :]


def attend_away(replicas, per_kv, *refs):
    count = replicas - 1
    away_kv, away_info, goal_mask = refs[:3]
    came = refs[3 : 3 + count]
    outs = refs[3 + count : 3 + 2 * count]
    q_rows, scores = refs[3 + 2 * count :]
    max_pages, _, page_len, head_dim = away_kv.shape[1:]
    span = CHUNK * page_len
    for d in range(count):
        pick = goal_mask[d]
        came_all = came[d][...].astype(F32)
        q_rows[...] = jnp.zeros_like(q_rows)
        for h in range(per_kv):
            q_rows[h : h + 1, :] = jnp.sum(
                came_all[:, h * head_dim : (h + 1) * head_dim] * pick, axis=0, keepdims=True
            )
        q = q_rows[...].astype(BF16)
        for c in range(max_pages // CHUNK):
            columns = slice(c * span, (c + 1) * span)
            keys = away_kv[d, c * CHUNK : (c + 1) * CHUNK, 0].reshape(span, head_dim)
            raw = dot_keys(q, keys) * away_info[d, 0:1, columns]
            scores[:, columns] = jnp.where(away_info[d, 2:3, columns] > 0, raw, -jnp.inf)
        highest = jnp.max(scores[...], axis=1, keepdims=True)
        weights = jnp.exp(scores[...] - highest)
        total = jnp.sum(weights, axis=1, keepdims=True)
        inverse = 1.0 / total
        mixed = jnp.zeros((2 * ROWS, head_dim), F32)
        for c in range(max_pages // CHUNK):
            columns = slice(c * span, (c + 1) * span)
            values = away_kv[d, c * CHUNK : (c + 1) * CHUNK, 1].reshape(span, head_dim)
            both = split_scaled(weights[:, columns], inverse, away_info[d, 1:2, columns])
            mixed = mixed + jnp.dot(both, values, preferred_element_type=F32)
        outs[d][0] = mixed[:ROWS] + mixed[ROWS:]
        outs[d][1] = jnp.broadcast_to(highest, (ROWS, head_dim))
        outs[d][2] = jnp.broadcast_to(total, (ROWS, head_dim))


def merge(replicas, attended, here_mask, here_own, *refs):
    arrived, out = refs[: replicas - 1], refs[-1]
    head_dim = here_mask.shape[2]
    moved = []
    for d in range(replicas - 1):
        own = here_own[d, 0]
        highest = jnp.maximum(arrived[d][1], own)
        cached = arrived[d][2] * jnp.exp(arrived[d][1] - highest)
        own = jnp.exp(own - highest)
        inverse = 1.0 / (cached + own)
        own = (own * inverse).astype(BF16).astype(F32)
        moved.append(arrived[d][0] * (cached * inverse) + own * here_own[d, 1])
    for h in range(attended.shape[1] // head_dim):
        columns = slice(h * head_dim, (h + 1) * head_dim)
        piece = attended[:, columns]
        for d in range(replicas - 1):
            piece = jnp.where(here_mask[d] > 0, moved[d][h : h + 1], piece)
        out[:, columns] = piece.astype(out.dtype)


def on_device(
    kv_pages, page_scale, page_table, lengths, request_moves, queries, new_kv, output_proj, residual
):
    devices = lax.axis_size("replica")
    replicas = devices // KVH
    requests, max_pages = page_table.shape
    pages, _, page_len, head_dim = kv_pages.shape
    per_kv = queries.shape[1] // head_dim
    width = output_proj.shape[1] // KVH
    tokens = max_pages * page_len
    count = replicas - 1

    def toward(value, steps):
        pairs = [(i, (i + steps * KVH) % devices) for i in range(devices)]
        return lax.ppermute(value, "replica", pairs)

    def partner(value, mask):
        return lax.ppermute(value, "replica", [(i, i ^ mask) for i in range(devices)])

    position = lax.axis_index("replica").astype(jnp.uint32)
    bits = [(position & (1 << i)) != 0 for i in range(KVH.bit_length() - 1)]
    queries, *bits = lax.optimization_barrier((queries, *bits))
    came = [toward(queries, -d) for d in range(1, replicas)]

    def shape(*dims, dtype=F32):
        return jax.ShapeDtypeStruct(dims, dtype)

    in_hbm = functools.partial(pltpu.with_memory_space_constraint, memory_space=pltpu.HBM)
    q_rows, nk_rows, key_scale, value_scale, away_kv, away_info, goal_mask, *home = pl.pallas_call(
        functools.partial(set_up, replicas, per_kv),
        out_shape=[
            shape(requests * ROWS, head_dim),
            shape(requests, 2 * head_dim),
            shape(requests, tokens),
            shape(requests, tokens),
            shape(count, max_pages, 2, page_len, head_dim, dtype=BF16),
            shape(count, 8, tokens),
            shape(count, requests, head_dim),
            shape(count, requests, head_dim),
            shape(count, 2, ROWS, head_dim),
            shape(requests, max_pages, dtype=jnp.int32),
            shape(requests, head_dim, dtype=jnp.int32),
        ],
        in_specs=[HBM] * 7,
        out_specs=[VMEM] * 11,
        scratch_shapes=[
            pltpu.SMEM(lengths.shape, jnp.int32),
            pltpu.SMEM(request_moves.shape, jnp.int32),
            pltpu.SMEM(page_table.shape, jnp.int32),
            pltpu.VMEM(page_table.shape, jnp.int32),
            pltpu.VMEM((2, pages), BF16),
            pltpu.VMEM(queries.shape, BF16),
            pltpu.VMEM(new_kv.shape, BF16),
            pltpu.SMEM((requests,), jnp.int32),
            pltpu.VMEM((2, requests, max_pages), F32),
            pltpu.SemaphoreType.DMA((7,)),
            pltpu.SemaphoreType.DMA((count,)),
        ],
        compiler_params=pltpu.CompilerParams(vmem_limit_bytes=4 * 2**20),
        cost_estimate=pl.CostEstimate(flops=0, bytes_accessed=4 * kv_pages.size, transcendentals=0),
        name="set_up",
    )(*(in_hbm(x) for x in (lengths, request_moves, page_table, page_scale.T, queries, new_kv, kv_pages)))

    here_mask, here_own, table_v, context = home

    rows = pl.pallas_call(
        functools.partial(attend_away, replicas, per_kv),
        out_shape=[shape(3, ROWS, head_dim)] * count,
        in_specs=[VMEM] * (3 + count),
        out_specs=[VMEM] * count,
        scratch_shapes=[pltpu.VMEM((ROWS, head_dim), F32), pltpu.VMEM((ROWS, tokens), F32)],
        compiler_params=pltpu.CompilerParams(vmem_limit_bytes=4 * 2**20),
        name="attend_away",
    )(away_kv, away_info, goal_mask, *came)
    arrived = [toward(rows[d - 1], d) for d in range(1, replicas)]

    attended = pl.pallas_call(
        functools.partial(attend_resident, per_kv),
        out_shape=shape(requests, per_kv * head_dim),
        in_specs=[HBM] + [VMEM] * 7,
        out_specs=VMEM,
        scratch_shapes=[
            pltpu.SMEM(page_table.shape, jnp.int32),
            pltpu.VMEM((requests * ROWS, tokens), F32),
            pltpu.VMEM((requests * ROWS, head_dim), F32),
            pltpu.SemaphoreType.DMA,
        ],
        compiler_params=pltpu.CompilerParams(vmem_limit_bytes=8 * 2**20),
        cost_estimate=pl.CostEstimate(
            flops=4 * per_kv * requests * tokens * head_dim,
            bytes_accessed=4 * output_proj.size,
            transcendentals=requests * ROWS * tokens,
        ),
        name="attend_resident",
    )(
        rows[0],
        table_v,
        context,
        pltpu.with_memory_space_constraint(kv_pages, pltpu.VMEM),
        q_rows,
        nk_rows,
        key_scale,
        value_scale,
    )
    mixture = pl.pallas_call(
        functools.partial(merge, replicas),
        out_shape=shape(*attended.shape, dtype=BF16),
        in_specs=[VMEM] * (3 + count),
        out_specs=VMEM,
        compiler_params=pltpu.CompilerParams(vmem_limit_bytes=2**20),
        name="merge",
    )(attended, here_mask, here_own, *arrived)

    parts = jnp.dot(mixture, output_proj, preferred_element_type=F32)
    parts = [parts[:, i * width : (i + 1) * width] for i in range(KVH)]
    core, y, z = bits

    def split(blocks, bit, step):
        low = [b for i, b in enumerate(blocks) if not i & step]
        high = [b for i, b in enumerate(blocks) if i & step]
        same = [jnp.where(bit, b, a) for a, b in zip(low, high)]
        return same, [jnp.where(bit, a, b) for a, b in zip(low, high)]

    near, far = split(parts, core, 1)
    other = partner(jnp.concatenate(far, axis=1), 1)
    chips = [block + other[:, i * width : (i + 1) * width] for i, block in enumerate(near)]
    same_z, other_z = split(chips, z, 2)
    (own,), (at_y,) = split(same_z, y, 1)
    (at_z,), (at_yz,) = split(other_z, y, 1)
    came = [partner(part.astype(BF16), k) for part, k in ((at_y, 2), (at_yz, 6), (at_z, 4))]
    for part in came:
        own = own + part.astype(F32)
    return (residual.astype(F32) + own).astype(BF16)


def solution(mesh):
    return jax.shard_map(
        on_device,
        mesh=mesh,
        in_specs=(
            P(("parts", "replica"), None, None, None),
            P(("parts", "replica"), None),
            P(("parts", "replica"), None),
            P("parts"),
            P("parts"),
            P(("parts", "replica"), None),
            P(("parts", "replica"), None),
            P("replica", None),
            P(("parts", "replica"), None),
        ),
        out_specs=P(("parts", "replica"), None),
        check_vma=False,
    )
```

```python
import functools
import math

import jax
import jax.numpy as jnp
from jax import lax
from jax.experimental import pallas as pl
from jax.experimental.pallas import tpu as pltpu
from jax.sharding import PartitionSpec as P

KVH = 8
ROWS = 8
CHUNK = 4
F32 = jnp.float32
BF16 = jnp.bfloat16
VMEM = pl.BlockSpec(memory_space=pltpu.VMEM)
HBM = pl.BlockSpec(memory_space=pltpu.HBM)


def softmax_parts(scores, own):
    highest = jnp.maximum(jnp.max(scores, axis=1, keepdims=True), own)
    weights = jnp.exp(scores - highest)
    own_weight = jnp.exp(own - highest)
    return weights, own_weight, 1.0 / (jnp.sum(weights, axis=1, keepdims=True) + own_weight)


def split_scaled(weights, inverse, value_scale):
    scaled = (weights * inverse).astype(BF16).astype(F32) * value_scale
    high = scaled.astype(BF16)
    low = (scaled - high.astype(F32)).astype(BF16)
    return jnp.concatenate([high, low], axis=0)


def dot_keys(queries, keys):
    return lax.dot_general(queries, keys, (((1,), (1,)), ((), ())), preferred_element_type=F32)


def set_up(
    replicas,
    per_kv,
    lengths_h,
    moves_h,
    table_h,
    scale_h,
    queries_h,
    new_kv_h,
    kv_pages,
    q_rows,
    nk_rows,
    key_scale,
    value_scale,
    away_kv,
    away_info,
    goal_mask,
    here_mask,
    here_own,
    table_out,
    context,
    lengths,
    moves,
    table_s,
    table_v,
    scale_v,
    queries,
    new_kv,
    target,
    page_scales,
    small_sem,
    kv_sem,
):
    requests, max_pages = table_h.shape
    pages, _, page_len, head_dim = kv_pages.shape
    tokens = max_pages * page_len
    slots = moves_h.shape[0]
    factor = 1.0 / math.sqrt(head_dim)
    replica = lax.axis_index("replica") // KVH

    small = [
        pltpu.make_async_copy(src, dst, small_sem.at[i])
        for i, (src, dst) in enumerate(
            [
                (moves_h, moves),
                (lengths_h, lengths),
                (table_h, table_s),
                (table_h, table_v),
                (scale_h, scale_v),
                (queries_h, queries),
                (new_kv_h, new_kv),
            ]
        )
    ]
    for copy in small:
        copy.start()
    for copy in small:
        copy.wait()

    def place(g, carry):
        slot = moves[g]

        @pl.when(slot // requests == replica)
        def _():
            target[slot % requests] = g

        return carry

    lax.fori_loop(0, slots, place, 0)
    row_ids = lax.broadcasted_iota(jnp.int32, (requests, head_dim), 0)
    leaver, arriver = [], []
    for d in range(1, replicas):
        out_slot = jnp.int32(0)
        here = jnp.int32(0)
        for j in range(requests):
            away = lax.rem(target[j] // requests - replica + replicas, replicas)
            out_slot = jnp.where(away == d, j, out_slot)
            behind = lax.rem(replica - moves[replica * requests + j] // requests + replicas, replicas)
            here = jnp.where(behind == d, j, here)
        leaver.append(out_slot)
        arriver.append(here)

        def fetch(p, carry, d=d, out_slot=out_slot):
            pltpu.make_async_copy(
                kv_pages.at[table_s[out_slot, p]], away_kv.at[d - 1, p], kv_sem.at[d - 1]
            ).start()
            return carry

        lax.fori_loop(0, max_pages, fetch, 0, unroll=4)
        goal_mask[d - 1] = (row_ids == lax.rem(target[out_slot], requests)).astype(F32)
        here_mask[d - 1] = (row_ids == here).astype(F32)

    q_all = queries[...].astype(F32)
    nk_rows[...] = new_kv[...].astype(F32)
    q_rows[...] = jnp.zeros_like(q_rows)
    for h in range(per_kv):
        q_rows[pl.ds(h, requests, stride=ROWS), :] = q_all[:, h * head_dim : (h + 1) * head_dim]

    page_ids = lax.broadcasted_iota(jnp.int32, (pages, max_pages), 0)
    scale_rows = scale_v[...]
    for j in range(requests):
        chosen = (page_ids == table_v[j : j + 1, :]).astype(F32).astype(BF16)
        page_scales[:, j : j + 1, :] = jnp.dot(scale_rows, chosen, preferred_element_type=F32)[:, None, :]
    spread = (
        lax.broadcasted_iota(jnp.int32, (max_pages, tokens), 1) // page_len
        == lax.broadcasted_iota(jnp.int32, (max_pages, tokens), 0)
    ).astype(F32).astype(BF16)
    for d in range(1, replicas):
        here = arriver[d - 1]
        own_rows = q_rows[pl.ds(pl.multiple_of(here * ROWS, ROWS), ROWS), :]
        token = nk_rows[pl.ds(here, 1), :]
        score = jnp.sum(own_rows * token[:, :head_dim], axis=1, keepdims=True) * factor
        here_own[d - 1, 0] = jnp.broadcast_to(score, (ROWS, head_dim))
        here_own[d - 1, 1] = jnp.broadcast_to(token[:, head_dim:], (ROWS, head_dim))
    table_out[...] = table_v[...]
    for j in range(requests):
        context[j : j + 1, :] = jnp.full((1, head_dim), lengths[replica * requests + j], jnp.int32)
    key_scale[...] = jnp.dot(page_scales[0].astype(BF16), spread, preferred_element_type=F32) * factor
    value_scale[...] = jnp.dot(page_scales[1].astype(BF16), spread, preferred_element_type=F32)
    places = lax.broadcasted_iota(jnp.int32, (1, tokens), 1)
    for d in range(1, replicas):
        out_slot = leaver[d - 1]
        away_info[d - 1, 0:1, :] = key_scale[pl.ds(out_slot, 1), :]
        away_info[d - 1, 1:2, :] = value_scale[pl.ds(out_slot, 1), :]
        away_info[d - 1, 2:3, :] = (places < lengths[replica * requests + out_slot]).astype(F32)

    for d in range(1, replicas):
        pltpu.make_async_copy(kv_pages.at[pl.ds(0, max_pages)], away_kv.at[d - 1], kv_sem.at[d - 1]).wait()


def attend_resident(
    per_kv,
    after,
    table_v,
    context,
    pool,
    q_rows,
    nk_rows,
    key_scale,
    value_scale,
    attended,
    *rest,
):
    table_s, scores, mixed, table_sem = rest
    del after
    requests, max_pages = table_v.shape
    _, _, page_len, head_dim = pool.shape
    tokens = max_pages * page_len
    factor = 1.0 / math.sqrt(head_dim)
    copy = pltpu.make_async_copy(table_v, table_s, table_sem)
    copy.start()
    copy.wait()

    def gather(j, c, which):
        return jnp.concatenate([pool[table_s[j, c * CHUNK + i], which] for i in range(CHUNK)], axis=0)

    places = lax.broadcasted_iota(jnp.int32, (1, tokens), 1)
    span = CHUNK * page_len
    own = []
    for j in range(requests):
        rows = slice(j * ROWS, (j + 1) * ROWS)
        q = q_rows[rows, :]
        own.append(jnp.sum(q * nk_rows[j : j + 1, :head_dim], axis=1, keepdims=True) * factor)
        q = q.astype(BF16)
        for c in range(max_pages // CHUNK):
            columns = slice(c * span, (c + 1) * span)
            raw = dot_keys(q, gather(j, c, 0)) * key_scale[j : j + 1, columns]
            scores[rows, columns] = jnp.where(places[:, columns] < context[j : j + 1, :1], raw, -jnp.inf)
    stats = []
    for j in range(requests):
        rows = slice(j * ROWS, (j + 1) * ROWS)
        weights, own_weight, inverse = softmax_parts(scores[rows, :], own[j])
        scores[rows, :] = weights
        stats.append((own_weight, inverse))
    for j in range(requests):
        rows = slice(j * ROWS, (j + 1) * ROWS)
        own_weight, inverse = stats[j]
        total = jnp.zeros((2 * ROWS, head_dim), F32)
        for c in range(max_pages // CHUNK):
            columns = slice(c * span, (c + 1) * span)
            both = split_scaled(scores[rows, columns], inverse, value_scale[j : j + 1, columns])
            total = total + jnp.dot(both, gather(j, c, 1), preferred_element_type=F32)
        own_weight = (own_weight * inverse).astype(BF16).astype(F32)
        mixed[rows, :] = total[:ROWS] + total[ROWS:] + own_weight * nk_rows[j : j + 1, head_dim:]
    for h in range(per_kv):
        attended[:, h * head_dim : (h + 1) * head_dim] = mixed[pl.ds(h, requests, stride=ROWS), :]


def diagonal(lanes):
    shape = (ROWS, lanes)
    return lax.broadcasted_iota(jnp.int32, shape, 0) == lax.broadcasted_iota(jnp.int32, shape, 1)


def to_lanes(column, lanes):
    return jnp.sum(jnp.where(diagonal(lanes), column, 0.0), axis=0, keepdims=True)


def to_rows(row):
    return jnp.sum(jnp.where(diagonal(row.shape[1]), row, 0.0), axis=1, keepdims=True)


def attend_away(replicas, per_kv, *refs):
    count = replicas - 1
    away_kv, away_info, goal_mask = refs[:3]
    came = refs[3 : 3 + count]
    outs = refs[3 + count : 3 + 2 * count]
    q_rows, scores = refs[3 + 2 * count :]
    max_pages, _, page_len, head_dim = away_kv.shape[1:]
    span = CHUNK * page_len
    for d in range(count):
        pick = goal_mask[d]
        came_all = came[d][...].astype(F32)
        q_rows[...] = jnp.zeros_like(q_rows)
        for h in range(per_kv):
            q_rows[h : h + 1, :] = jnp.sum(
                came_all[:, h * head_dim : (h + 1) * head_dim] * pick, axis=0, keepdims=True
            )
        q = q_rows[...].astype(BF16)
        for c in range(max_pages // CHUNK):
            columns = slice(c * span, (c + 1) * span)
            keys = away_kv[d, c * CHUNK : (c + 1) * CHUNK, 0].reshape(span, head_dim)
            raw = dot_keys(q, keys) * away_info[d, 0:1, columns]
            scores[:, columns] = jnp.where(away_info[d, 2:3, columns] > 0, raw, -jnp.inf)
        highest = jnp.max(scores[...], axis=1, keepdims=True)
        weights = jnp.exp(scores[...] - highest)
        total = jnp.sum(weights, axis=1, keepdims=True)
        inverse = 1.0 / total
        mixed = jnp.zeros((2 * ROWS, head_dim), F32)
        for c in range(max_pages // CHUNK):
            columns = slice(c * span, (c + 1) * span)
            values = away_kv[d, c * CHUNK : (c + 1) * CHUNK, 1].reshape(span, head_dim)
            both = split_scaled(weights[:, columns], inverse, away_info[d, 1:2, columns])
            mixed = mixed + jnp.dot(both, values, preferred_element_type=F32)
        outs[d][...] = mixed[:ROWS] + mixed[ROWS:]
        outs[d][per_kv : per_kv + 1, :] = to_lanes(highest, head_dim)
        outs[d][per_kv + 1 : per_kv + 2, :] = to_lanes(total, head_dim)


def merge(replicas, attended, here_mask, here_own, *refs):
    arrived, out = refs[: replicas - 1], refs[-1]
    head_dim = here_mask.shape[2]
    per_kv = attended.shape[1] // head_dim
    moved = []
    for d in range(replicas - 1):
        own = here_own[d, 0][:, :1]
        cached_highest = to_rows(arrived[d][per_kv : per_kv + 1, :])
        cached = to_rows(arrived[d][per_kv + 1 : per_kv + 2, :])
        highest = jnp.maximum(cached_highest, own)
        cached = cached * jnp.exp(cached_highest - highest)
        own = jnp.exp(own - highest)
        inverse = 1.0 / (cached + own)
        own = (own * inverse).astype(BF16).astype(F32)
        moved.append(arrived[d][...] * (cached * inverse) + own * here_own[d, 1])
    for h in range(per_kv):
        columns = slice(h * head_dim, (h + 1) * head_dim)
        piece = attended[:, columns]
        for d in range(replicas - 1):
            piece = jnp.where(here_mask[d] > 0, moved[d][h : h + 1], piece)
        out[:, columns] = piece.astype(out.dtype)


def on_device(
    kv_pages, page_scale, page_table, lengths, request_moves, queries, new_kv, output_proj, residual
):
    devices = lax.axis_size("replica")
    replicas = devices // KVH
    requests, max_pages = page_table.shape
    pages, _, page_len, head_dim = kv_pages.shape
    per_kv = queries.shape[1] // head_dim
    width = output_proj.shape[1] // KVH
    tokens = max_pages * page_len
    count = replicas - 1

    def toward(value, steps):
        pairs = [(i, (i + steps * KVH) % devices) for i in range(devices)]
        return lax.ppermute(value, "replica", pairs)

    def partner(value, mask):
        return lax.ppermute(value, "replica", [(i, i ^ mask) for i in range(devices)])

    position = lax.axis_index("replica").astype(jnp.uint32)
    bits = [(position & (1 << i)) != 0 for i in range(KVH.bit_length() - 1)]
    queries, *bits = lax.optimization_barrier((queries, *bits))
    came = [toward(queries, -d) for d in range(1, replicas)]

    def shape(*dims, dtype=F32):
        return jax.ShapeDtypeStruct(dims, dtype)

    in_hbm = functools.partial(pltpu.with_memory_space_constraint, memory_space=pltpu.HBM)
    q_rows, nk_rows, key_scale, value_scale, away_kv, away_info, goal_mask, *home = pl.pallas_call(
        functools.partial(set_up, replicas, per_kv),
        out_shape=[
            shape(requests * ROWS, head_dim),
            shape(requests, 2 * head_dim),
            shape(requests, tokens),
            shape(requests, tokens),
            shape(count, max_pages, 2, page_len, head_dim, dtype=BF16),
            shape(count, 8, tokens),
            shape(count, requests, head_dim),
            shape(count, requests, head_dim),
            shape(count, 2, ROWS, head_dim),
            shape(requests, max_pages, dtype=jnp.int32),
            shape(requests, head_dim, dtype=jnp.int32),
        ],
        in_specs=[HBM] * 7,
        out_specs=[VMEM] * 11,
        scratch_shapes=[
            pltpu.SMEM(lengths.shape, jnp.int32),
            pltpu.SMEM(request_moves.shape, jnp.int32),
            pltpu.SMEM(page_table.shape, jnp.int32),
            pltpu.VMEM(page_table.shape, jnp.int32),
            pltpu.VMEM((2, pages), BF16),
            pltpu.VMEM(queries.shape, BF16),
            pltpu.VMEM(new_kv.shape, BF16),
            pltpu.SMEM((requests,), jnp.int32),
            pltpu.VMEM((2, requests, max_pages), F32),
            pltpu.SemaphoreType.DMA((7,)),
            pltpu.SemaphoreType.DMA((count,)),
        ],
        compiler_params=pltpu.CompilerParams(vmem_limit_bytes=4 * 2**20),
        cost_estimate=pl.CostEstimate(flops=0, bytes_accessed=4 * kv_pages.size, transcendentals=0),
        name="set_up",
    )(*(in_hbm(x) for x in (lengths, request_moves, page_table, page_scale.T, queries, new_kv, kv_pages)))

    here_mask, here_own, table_v, context = home

    rows = pl.pallas_call(
        functools.partial(attend_away, replicas, per_kv),
        out_shape=[shape(ROWS, head_dim)] * count,
        in_specs=[VMEM] * (3 + count),
        out_specs=[VMEM] * count,
        scratch_shapes=[pltpu.VMEM((ROWS, head_dim), F32), pltpu.VMEM((ROWS, tokens), F32)],
        compiler_params=pltpu.CompilerParams(vmem_limit_bytes=4 * 2**20),
        name="attend_away",
    )(away_kv, away_info, goal_mask, *came)
    arrived = [toward(rows[d - 1], d) for d in range(1, replicas)]

    attended = pl.pallas_call(
        functools.partial(attend_resident, per_kv),
        out_shape=shape(requests, per_kv * head_dim),
        in_specs=[HBM] + [VMEM] * 7,
        out_specs=VMEM,
        scratch_shapes=[
            pltpu.SMEM(page_table.shape, jnp.int32),
            pltpu.VMEM((requests * ROWS, tokens), F32),
            pltpu.VMEM((requests * ROWS, head_dim), F32),
            pltpu.SemaphoreType.DMA,
        ],
        compiler_params=pltpu.CompilerParams(vmem_limit_bytes=8 * 2**20),
        cost_estimate=pl.CostEstimate(
            flops=4 * per_kv * requests * tokens * head_dim,
            bytes_accessed=4 * output_proj.size,
            transcendentals=requests * ROWS * tokens,
        ),
        name="attend_resident",
    )(
        rows[0],
        table_v,
        context,
        pltpu.with_memory_space_constraint(kv_pages, pltpu.VMEM),
        q_rows,
        nk_rows,
        key_scale,
        value_scale,
    )
    mixture = pl.pallas_call(
        functools.partial(merge, replicas),
        out_shape=shape(*attended.shape, dtype=BF16),
        in_specs=[VMEM] * (3 + count),
        out_specs=VMEM,
        compiler_params=pltpu.CompilerParams(vmem_limit_bytes=2**20),
        name="merge",
    )(attended, here_mask, here_own, *arrived)

    parts = jnp.dot(mixture, output_proj, preferred_element_type=F32)
    parts = [parts[:, i * width : (i + 1) * width] for i in range(KVH)]
    core, y, z = bits

    def split(blocks, bit, step):
        low = [b for i, b in enumerate(blocks) if not i & step]
        high = [b for i, b in enumerate(blocks) if i & step]
        same = [jnp.where(bit, b, a) for a, b in zip(low, high)]
        return same, [jnp.where(bit, a, b) for a, b in zip(low, high)]

    near, far = split(parts, core, 1)
    (near_own, near_z), (near_y, near_yz) = (split(pair, z, 1) for pair in split(near, y, 1))
    (far_own, far_z), (far_y, far_yz) = (split(pair, z, 1) for pair in split(far, y, 1))
    to_y = jnp.concatenate([*near_y, *far_y], axis=1).astype(BF16)
    to_core = jnp.concatenate([*far_yz, *far_z, *far_own], axis=1)
    to_y, to_core, at_yz, at_z, own = lax.optimization_barrier(
        (to_y, to_core, near_yz[0], near_z[0], near_own[0])
    )
    came_y = partner(to_y, 2).astype(F32)
    other = partner(to_core, 1)
    came_yz = partner((at_yz + other[:, :width]).astype(BF16), 6)
    came_z = partner((at_z + other[:, width : 2 * width]).astype(BF16), 4)
    passed_on = partner(came_y[:, width:], 1)
    total = own + other[:, 2 * width :] + came_y[:, :width] + came_yz.astype(F32) + came_z.astype(F32)
    total = lax.optimization_barrier(total) + passed_on
    return (residual.astype(F32) + total).astype(BF16)


def solution(mesh):
    return jax.shard_map(
        on_device,
        mesh=mesh,
        in_specs=(
            P(("parts", "replica"), None, None, None),
            P(("parts", "replica"), None),
            P(("parts", "replica"), None),
            P("parts"),
            P("parts"),
            P(("parts", "replica"), None),
            P(("parts", "replica"), None),
            P("replica", None),
            P(("parts", "replica"), None),
        ),
        out_specs=P(("parts", "replica"), None),
        check_vma=False,
    )
```

```python
import functools
import math

import jax
import jax.numpy as jnp
from jax import lax
from jax.experimental import pallas as pl
from jax.experimental.pallas import tpu as pltpu
from jax.sharding import PartitionSpec as P

KVH = 8
ROWS = 8
CHUNK = 4
F32 = jnp.float32
BF16 = jnp.bfloat16
VMEM = pl.BlockSpec(memory_space=pltpu.VMEM)
HBM = pl.BlockSpec(memory_space=pltpu.HBM)


def softmax_parts(scores, own):
    highest = jnp.maximum(jnp.max(scores, axis=1, keepdims=True), own)
    weights = jnp.exp(scores - highest)
    own_weight = jnp.exp(own - highest)
    return weights, own_weight, 1.0 / (jnp.sum(weights, axis=1, keepdims=True) + own_weight)


def split_scaled(weights, inverse, value_scale):
    scaled = (weights * inverse).astype(BF16).astype(F32) * value_scale
    high = scaled.astype(BF16)
    low = (scaled - high.astype(F32)).astype(BF16)
    return jnp.concatenate([high, low], axis=0)


def dot_keys(queries, keys):
    return lax.dot_general(queries, keys, (((1,), (1,)), ((), ())), preferred_element_type=F32)


def set_up(
    replicas,
    per_kv,
    lengths_h,
    moves_h,
    table_h,
    scale_h,
    queries_h,
    new_kv_h,
    kv_pages,
    q_rows,
    nk_rows,
    key_scale,
    value_scale,
    away_kv,
    away_info,
    goal_mask,
    here_mask,
    here_own,
    table_out,
    context,
    lengths,
    moves,
    table_s,
    table_v,
    scale_v,
    queries,
    new_kv,
    target,
    page_scales,
    small_sem,
    kv_sem,
):
    requests, max_pages = table_h.shape
    pages, _, page_len, head_dim = kv_pages.shape
    tokens = max_pages * page_len
    slots = moves_h.shape[0]
    factor = 1.0 / math.sqrt(head_dim)
    replica = lax.axis_index("replica") // KVH

    small = [
        pltpu.make_async_copy(src, dst, small_sem.at[i])
        for i, (src, dst) in enumerate(
            [
                (moves_h, moves),
                (lengths_h, lengths),
                (table_h, table_s),
                (table_h, table_v),
                (scale_h, scale_v),
                (queries_h, queries),
                (new_kv_h, new_kv),
            ]
        )
    ]
    for copy in small:
        copy.start()
    for copy in small:
        copy.wait()

    def place(g, carry):
        slot = moves[g]

        @pl.when(slot // requests == replica)
        def _():
            target[slot % requests] = g

        return carry

    lax.fori_loop(0, slots, place, 0)
    row_ids = lax.broadcasted_iota(jnp.int32, (requests, head_dim), 0)
    leaver, arriver = [], []
    for d in range(1, replicas):
        out_slot = jnp.int32(0)
        here = jnp.int32(0)
        for j in range(requests):
            away = lax.rem(target[j] // requests - replica + replicas, replicas)
            out_slot = jnp.where(away == d, j, out_slot)
            behind = lax.rem(replica - moves[replica * requests + j] // requests + replicas, replicas)
            here = jnp.where(behind == d, j, here)
        leaver.append(out_slot)
        arriver.append(here)

        def fetch(p, carry, d=d, out_slot=out_slot):
            pltpu.make_async_copy(
                kv_pages.at[table_s[out_slot, p]], away_kv.at[d - 1, p], kv_sem.at[d - 1]
            ).start()
            return carry

        lax.fori_loop(0, max_pages, fetch, 0, unroll=4)
        goal_mask[d - 1] = (row_ids == lax.rem(target[out_slot], requests)).astype(F32)
        here_mask[d - 1] = (row_ids == here).astype(F32)

    q_all = queries[...].astype(F32)
    nk_rows[...] = new_kv[...].astype(F32)
    q_rows[...] = jnp.zeros_like(q_rows)
    for h in range(per_kv):
        q_rows[pl.ds(h, requests, stride=ROWS), :] = q_all[:, h * head_dim : (h + 1) * head_dim]

    page_ids = lax.broadcasted_iota(jnp.int32, (pages, max_pages), 0)
    scale_rows = scale_v[...]
    for j in range(requests):
        chosen = (page_ids == table_v[j : j + 1, :]).astype(F32).astype(BF16)
        page_scales[:, j : j + 1, :] = jnp.dot(scale_rows, chosen, preferred_element_type=F32)[:, None, :]
    spread = (
        lax.broadcasted_iota(jnp.int32, (max_pages, tokens), 1) // page_len
        == lax.broadcasted_iota(jnp.int32, (max_pages, tokens), 0)
    ).astype(F32).astype(BF16)
    for d in range(1, replicas):
        here = arriver[d - 1]
        own_rows = q_rows[pl.ds(pl.multiple_of(here * ROWS, ROWS), ROWS), :]
        token = nk_rows[pl.ds(here, 1), :]
        score = jnp.sum(own_rows * token[:, :head_dim], axis=1, keepdims=True) * factor
        here_own[d - 1, 0] = jnp.broadcast_to(score, (ROWS, head_dim))
        here_own[d - 1, 1] = jnp.broadcast_to(token[:, head_dim:], (ROWS, head_dim))
    table_out[...] = table_v[...]
    for j in range(requests):
        context[j : j + 1, :] = jnp.full((1, head_dim), lengths[replica * requests + j], jnp.int32)
    key_scale[...] = jnp.dot(page_scales[0].astype(BF16), spread, preferred_element_type=F32) * factor
    value_scale[...] = jnp.dot(page_scales[1].astype(BF16), spread, preferred_element_type=F32)
    places = lax.broadcasted_iota(jnp.int32, (1, tokens), 1)
    for d in range(1, replicas):
        out_slot = leaver[d - 1]
        away_info[d - 1, 0:1, :] = key_scale[pl.ds(out_slot, 1), :]
        away_info[d - 1, 1:2, :] = value_scale[pl.ds(out_slot, 1), :]
        away_info[d - 1, 2:3, :] = (places < lengths[replica * requests + out_slot]).astype(F32)

    for d in range(1, replicas):
        pltpu.make_async_copy(kv_pages.at[pl.ds(0, max_pages)], away_kv.at[d - 1], kv_sem.at[d - 1]).wait()


def attend_resident(
    per_kv,
    after,
    table_v,
    context,
    pool,
    q_rows,
    nk_rows,
    key_scale,
    value_scale,
    attended,
    *rest,
):
    table_s, scores, mixed, table_sem = rest
    del after
    requests, max_pages = table_v.shape
    _, _, page_len, head_dim = pool.shape
    tokens = max_pages * page_len
    factor = 1.0 / math.sqrt(head_dim)
    copy = pltpu.make_async_copy(table_v, table_s, table_sem)
    copy.start()
    copy.wait()

    def gather(j, c, which):
        return jnp.concatenate([pool[table_s[j, c * CHUNK + i], which] for i in range(CHUNK)], axis=0)

    places = lax.broadcasted_iota(jnp.int32, (1, tokens), 1)
    span = CHUNK * page_len
    own = []
    for j in range(requests):
        rows = slice(j * ROWS, (j + 1) * ROWS)
        q = q_rows[rows, :]
        own.append(jnp.sum(q * nk_rows[j : j + 1, :head_dim], axis=1, keepdims=True) * factor)
        q = q.astype(BF16)
        for c in range(max_pages // CHUNK):
            columns = slice(c * span, (c + 1) * span)
            raw = dot_keys(q, gather(j, c, 0)) * key_scale[j : j + 1, columns]
            scores[rows, columns] = jnp.where(places[:, columns] < context[j : j + 1, :1], raw, -jnp.inf)
    stats = []
    for j in range(requests):
        rows = slice(j * ROWS, (j + 1) * ROWS)
        weights, own_weight, inverse = softmax_parts(scores[rows, :], own[j])
        scores[rows, :] = weights
        stats.append((own_weight, inverse))
    for j in range(requests):
        rows = slice(j * ROWS, (j + 1) * ROWS)
        own_weight, inverse = stats[j]
        total = jnp.zeros((2 * ROWS, head_dim), F32)
        for c in range(max_pages // CHUNK):
            columns = slice(c * span, (c + 1) * span)
            both = split_scaled(scores[rows, columns], inverse, value_scale[j : j + 1, columns])
            total = total + jnp.dot(both, gather(j, c, 1), preferred_element_type=F32)
        own_weight = (own_weight * inverse).astype(BF16).astype(F32)
        mixed[rows, :] = total[:ROWS] + total[ROWS:] + own_weight * nk_rows[j : j + 1, head_dim:]
    for h in range(per_kv):
        attended[:, h * head_dim : (h + 1) * head_dim] = mixed[pl.ds(h, requests, stride=ROWS), :]


def attend_away(replicas, per_kv, *refs):
    count = replicas - 1
    away_kv, away_info, goal_mask = refs[:3]
    came = refs[3 : 3 + count]
    outs = refs[3 + count : 3 + 2 * count]
    q_rows, scores = refs[3 + 2 * count :]
    max_pages, _, page_len, head_dim = away_kv.shape[1:]
    span = CHUNK * page_len
    for d in range(count):
        pick = goal_mask[d]
        came_all = came[d][...].astype(F32)
        q_rows[...] = jnp.zeros_like(q_rows)
        for h in range(per_kv):
            q_rows[h : h + 1, :] = jnp.sum(
                came_all[:, h * head_dim : (h + 1) * head_dim] * pick, axis=0, keepdims=True
            )
        q = q_rows[...].astype(BF16)
        for c in range(max_pages // CHUNK):
            columns = slice(c * span, (c + 1) * span)
            keys = away_kv[d, c * CHUNK : (c + 1) * CHUNK, 0].reshape(span, head_dim)
            raw = dot_keys(q, keys) * away_info[d, 0:1, columns]
            scores[:, columns] = jnp.where(away_info[d, 2:3, columns] > 0, raw, -jnp.inf)
        highest = jnp.max(scores[...], axis=1, keepdims=True)
        weights = jnp.exp(scores[...] - highest)
        total = jnp.sum(weights, axis=1, keepdims=True)
        inverse = 1.0 / total
        mixed = jnp.zeros((2 * ROWS, head_dim), F32)
        for c in range(max_pages // CHUNK):
            columns = slice(c * span, (c + 1) * span)
            values = away_kv[d, c * CHUNK : (c + 1) * CHUNK, 1].reshape(span, head_dim)
            both = split_scaled(weights[:, columns], inverse, away_info[d, 1:2, columns])
            mixed = mixed + jnp.dot(both, values, preferred_element_type=F32)
        outs[d][0] = mixed[:ROWS] + mixed[ROWS:]
        left = lax.broadcasted_iota(jnp.int32, (ROWS, head_dim), 1) < head_dim // 2
        outs[d][1] = jnp.where(left, highest, total)


def merge(replicas, attended, here_mask, here_own, *refs):
    arrived, out = refs[: replicas - 1], refs[-1]
    head_dim = here_mask.shape[2]
    per_kv = attended.shape[1] // head_dim
    moved = []
    for d in range(replicas - 1):
        own = here_own[d, 0][:, :1]
        cached_highest = arrived[d][1][:, :1]
        cached = arrived[d][1][:, head_dim // 2 : head_dim // 2 + 1]
        highest = jnp.maximum(cached_highest, own)
        cached = cached * jnp.exp(cached_highest - highest)
        own = jnp.exp(own - highest)
        inverse = 1.0 / (cached + own)
        own = (own * inverse).astype(BF16).astype(F32)
        moved.append(arrived[d][0] * (cached * inverse) + own * here_own[d, 1])
    for h in range(per_kv):
        columns = slice(h * head_dim, (h + 1) * head_dim)
        piece = attended[:, columns]
        for d in range(replicas - 1):
            piece = jnp.where(here_mask[d] > 0, moved[d][h : h + 1], piece)
        out[:, columns] = piece.astype(out.dtype)


def on_device(
    kv_pages, page_scale, page_table, lengths, request_moves, queries, new_kv, output_proj, residual
):
    devices = lax.axis_size("replica")
    replicas = devices // KVH
    requests, max_pages = page_table.shape
    pages, _, page_len, head_dim = kv_pages.shape
    per_kv = queries.shape[1] // head_dim
    width = output_proj.shape[1] // KVH
    tokens = max_pages * page_len
    count = replicas - 1

    def toward(value, steps):
        pairs = [(i, (i + steps * KVH) % devices) for i in range(devices)]
        return lax.ppermute(value, "replica", pairs)

    def partner(value, mask):
        return lax.ppermute(value, "replica", [(i, i ^ mask) for i in range(devices)])

    position = lax.axis_index("replica").astype(jnp.uint32)
    bits = [(position & (1 << i)) != 0 for i in range(KVH.bit_length() - 1)]
    queries, *bits = lax.optimization_barrier((queries, *bits))
    came = [toward(queries, -d) for d in range(1, replicas)]

    def shape(*dims, dtype=F32):
        return jax.ShapeDtypeStruct(dims, dtype)

    in_hbm = functools.partial(pltpu.with_memory_space_constraint, memory_space=pltpu.HBM)
    q_rows, nk_rows, key_scale, value_scale, away_kv, away_info, goal_mask, *home = pl.pallas_call(
        functools.partial(set_up, replicas, per_kv),
        out_shape=[
            shape(requests * ROWS, head_dim),
            shape(requests, 2 * head_dim),
            shape(requests, tokens),
            shape(requests, tokens),
            shape(count, max_pages, 2, page_len, head_dim, dtype=BF16),
            shape(count, 8, tokens),
            shape(count, requests, head_dim),
            shape(count, requests, head_dim),
            shape(count, 2, ROWS, head_dim),
            shape(requests, max_pages, dtype=jnp.int32),
            shape(requests, head_dim, dtype=jnp.int32),
        ],
        in_specs=[HBM] * 7,
        out_specs=[VMEM] * 11,
        scratch_shapes=[
            pltpu.SMEM(lengths.shape, jnp.int32),
            pltpu.SMEM(request_moves.shape, jnp.int32),
            pltpu.SMEM(page_table.shape, jnp.int32),
            pltpu.VMEM(page_table.shape, jnp.int32),
            pltpu.VMEM((2, pages), BF16),
            pltpu.VMEM(queries.shape, BF16),
            pltpu.VMEM(new_kv.shape, BF16),
            pltpu.SMEM((requests,), jnp.int32),
            pltpu.VMEM((2, requests, max_pages), F32),
            pltpu.SemaphoreType.DMA((7,)),
            pltpu.SemaphoreType.DMA((count,)),
        ],
        compiler_params=pltpu.CompilerParams(vmem_limit_bytes=4 * 2**20),
        cost_estimate=pl.CostEstimate(flops=0, bytes_accessed=4 * kv_pages.size, transcendentals=0),
        name="set_up",
    )(*(in_hbm(x) for x in (lengths, request_moves, page_table, page_scale.T, queries, new_kv, kv_pages)))

    here_mask, here_own, table_v, context = home

    rows = pl.pallas_call(
        functools.partial(attend_away, replicas, per_kv),
        out_shape=[shape(2, ROWS, head_dim)] * count,
        in_specs=[VMEM] * (3 + count),
        out_specs=[VMEM] * count,
        scratch_shapes=[pltpu.VMEM((ROWS, head_dim), F32), pltpu.VMEM((ROWS, tokens), F32)],
        compiler_params=pltpu.CompilerParams(vmem_limit_bytes=4 * 2**20),
        name="attend_away",
    )(away_kv, away_info, goal_mask, *came)
    arrived = [toward(rows[d - 1], d) for d in range(1, replicas)]

    attended = pl.pallas_call(
        functools.partial(attend_resident, per_kv),
        out_shape=shape(requests, per_kv * head_dim),
        in_specs=[HBM] + [VMEM] * 7,
        out_specs=VMEM,
        scratch_shapes=[
            pltpu.SMEM(page_table.shape, jnp.int32),
            pltpu.VMEM((requests * ROWS, tokens), F32),
            pltpu.VMEM((requests * ROWS, head_dim), F32),
            pltpu.SemaphoreType.DMA,
        ],
        compiler_params=pltpu.CompilerParams(vmem_limit_bytes=8 * 2**20),
        cost_estimate=pl.CostEstimate(
            flops=4 * per_kv * requests * tokens * head_dim,
            bytes_accessed=4 * output_proj.size,
            transcendentals=requests * ROWS * tokens,
        ),
        name="attend_resident",
    )(
        rows[0],
        table_v,
        context,
        pltpu.with_memory_space_constraint(kv_pages, pltpu.VMEM),
        q_rows,
        nk_rows,
        key_scale,
        value_scale,
    )
    mixture = pl.pallas_call(
        functools.partial(merge, replicas),
        out_shape=shape(*attended.shape, dtype=BF16),
        in_specs=[VMEM] * (3 + count),
        out_specs=VMEM,
        compiler_params=pltpu.CompilerParams(vmem_limit_bytes=2**20),
        name="merge",
    )(attended, here_mask, here_own, *arrived)

    parts = jnp.dot(mixture, output_proj, preferred_element_type=F32)
    parts = [parts[:, i * width : (i + 1) * width] for i in range(KVH)]
    core, y, z = bits

    def split(blocks, bit, step):
        low = [b for i, b in enumerate(blocks) if not i & step]
        high = [b for i, b in enumerate(blocks) if i & step]
        same = [jnp.where(bit, b, a) for a, b in zip(low, high)]
        return same, [jnp.where(bit, a, b) for a, b in zip(low, high)]

    near, far = split(parts, core, 1)
    (near_own, near_z), (near_y, near_yz) = (split(pair, z, 1) for pair in split(near, y, 1))
    (far_own, far_z), (far_y, far_yz) = (split(pair, z, 1) for pair in split(far, y, 1))
    to_core, to_y, to_z, at_yz, own = lax.optimization_barrier(
        (
            jnp.concatenate([*far_yz, *far_own], axis=1),
            jnp.concatenate([*near_y, *far_y], axis=1).astype(BF16),
            jnp.concatenate([*near_z, *far_z], axis=1).astype(BF16),
            near_yz[0],
            near_own[0],
        )
    )
    other = partner(to_core, 1)
    came_y = partner(to_y, 2)
    came_z = partner(to_z, 4)
    came_yz = partner((at_yz + other[:, :width]).astype(BF16), 6).astype(F32)
    moving, came_y, came_z = lax.optimization_barrier(
        (came_y[:, width:].astype(F32) + came_z[:, width:].astype(F32), came_y[:, :width], came_z[:, :width])
    )
    passed_on = partner(moving, 1)
    total = own + other[:, width:] + came_y.astype(F32) + came_z.astype(F32) + came_yz
    total = lax.optimization_barrier(total) + passed_on
    return (residual.astype(F32) + total).astype(BF16)


def solution(mesh):
    return jax.shard_map(
        on_device,
        mesh=mesh,
        in_specs=(
            P(("parts", "replica"), None, None, None),
            P(("parts", "replica"), None),
            P(("parts", "replica"), None),
            P("parts"),
            P("parts"),
            P(("parts", "replica"), None),
            P(("parts", "replica"), None),
            P("replica", None),
            P(("parts", "replica"), None),
        ),
        out_specs=P(("parts", "replica"), None),
        check_vma=False,
    )
```

```python
import functools
import math

import jax
import jax.numpy as jnp
from jax import lax
from jax.experimental import pallas as pl
from jax.experimental.pallas import tpu as pltpu
from jax.sharding import PartitionSpec as P

KVH = 8
ROWS = 8
CHUNK = 4
F32 = jnp.float32
BF16 = jnp.bfloat16
VMEM = pl.BlockSpec(memory_space=pltpu.VMEM)
HBM = pl.BlockSpec(memory_space=pltpu.HBM)


def softmax_parts(scores, own):
    highest = jnp.maximum(jnp.max(scores, axis=1, keepdims=True), own)
    weights = jnp.exp(scores - highest)
    own_weight = jnp.exp(own - highest)
    return weights, own_weight, 1.0 / (jnp.sum(weights, axis=1, keepdims=True) + own_weight)


def split_scaled(weights, inverse, value_scale):
    scaled = (weights * inverse).astype(BF16).astype(F32) * value_scale
    high = scaled.astype(BF16)
    low = (scaled - high.astype(F32)).astype(BF16)
    return jnp.concatenate([high, low], axis=0)


def dot_keys(queries, keys):
    return lax.dot_general(queries, keys, (((1,), (1,)), ((), ())), preferred_element_type=F32)


def set_up(
    replicas,
    per_kv,
    lengths_h,
    moves_h,
    table_h,
    scale_h,
    queries_h,
    new_kv_h,
    kv_pages,
    q_rows,
    nk_rows,
    key_scale,
    value_scale,
    away_kv,
    away_info,
    goal_mask,
    here_mask,
    here_own,
    table_out,
    context,
    lengths,
    moves,
    table_s,
    table_v,
    scale_v,
    queries,
    new_kv,
    page_scales,
    small_sem,
    kv_sem,
):
    requests, max_pages = table_h.shape
    pages, _, page_len, head_dim = kv_pages.shape
    tokens = max_pages * page_len
    factor = 1.0 / math.sqrt(head_dim)
    replica = lax.axis_index("replica") // KVH

    small = [
        pltpu.make_async_copy(src, dst, small_sem.at[i])
        for i, (src, dst) in enumerate(
            [
                (moves_h, moves),
                (table_h, table_s),
                (table_h, table_v),
                (lengths_h, lengths),
                (scale_h, scale_v),
                (queries_h, queries),
                (new_kv_h, new_kv),
            ]
        )
    ]
    for copy in small:
        copy.start()
    for copy in small[:2]:
        copy.wait()

    first = replica * requests
    leaver, goal, arriver = [], [], []
    for d in range(1, replicas):
        there = jnp.where(replica + d < replicas, replica + d, replica + d - replicas) * requests
        behind = jnp.where(replica >= d, replica - d, replica - d + replicas) * requests
        out_slot = taken = here = jnp.int32(0)
        for j in range(requests):
            slot = moves[there + j] - first
            ours = (slot >= 0) & (slot < requests)
            out_slot = jnp.where(ours, slot, out_slot)
            taken = jnp.where(ours, j, taken)
            slot = moves[first + j] - behind
            here = jnp.where((slot >= 0) & (slot < requests), j, here)
        leaver.append(out_slot)
        goal.append(taken)
        arriver.append(here)

        def fetch(p, carry, d=d, out_slot=out_slot):
            pltpu.make_async_copy(
                kv_pages.at[table_s[out_slot, p]], away_kv.at[d - 1, p], kv_sem.at[d - 1]
            ).start()
            return carry

        lax.fori_loop(0, max_pages, fetch, 0, unroll=8)
    for copy in small[2:]:
        copy.wait()
    row_ids = lax.broadcasted_iota(jnp.int32, (requests, head_dim), 0)
    for d in range(1, replicas):
        goal_mask[d - 1] = (row_ids == goal[d - 1]).astype(F32)
        here_mask[d - 1] = (row_ids == arriver[d - 1]).astype(F32)

    q_all = queries[...].astype(F32)
    nk_rows[...] = new_kv[...].astype(F32)
    q_rows[...] = jnp.zeros_like(q_rows)
    for h in range(per_kv):
        q_rows[pl.ds(h, requests, stride=ROWS), :] = q_all[:, h * head_dim : (h + 1) * head_dim]

    page_ids = lax.broadcasted_iota(jnp.int32, (pages, max_pages), 0)
    scale_rows = scale_v[...]
    for j in range(requests):
        chosen = (page_ids == table_v[j : j + 1, :]).astype(F32).astype(BF16)
        page_scales[:, j : j + 1, :] = jnp.dot(scale_rows, chosen, preferred_element_type=F32)[:, None, :]
    spread = (
        lax.broadcasted_iota(jnp.int32, (max_pages, tokens), 1) // page_len
        == lax.broadcasted_iota(jnp.int32, (max_pages, tokens), 0)
    ).astype(F32).astype(BF16)
    for d in range(1, replicas):
        here = arriver[d - 1]
        own_rows = q_rows[pl.ds(pl.multiple_of(here * ROWS, ROWS), ROWS), :]
        token = nk_rows[pl.ds(here, 1), :]
        score = jnp.sum(own_rows * token[:, :head_dim], axis=1, keepdims=True) * factor
        here_own[d - 1, 0] = jnp.broadcast_to(score, (ROWS, head_dim))
        here_own[d - 1, 1] = jnp.broadcast_to(token[:, head_dim:], (ROWS, head_dim))
    table_out[...] = table_v[...]
    for j in range(requests):
        context[j : j + 1, :] = jnp.full((1, head_dim), lengths[replica * requests + j], jnp.int32)
    key_scale[...] = jnp.dot(page_scales[0].astype(BF16), spread, preferred_element_type=F32) * factor
    value_scale[...] = jnp.dot(page_scales[1].astype(BF16), spread, preferred_element_type=F32)
    places = lax.broadcasted_iota(jnp.int32, (1, tokens), 1)
    for d in range(1, replicas):
        out_slot = leaver[d - 1]
        away_info[d - 1, 0:1, :] = key_scale[pl.ds(out_slot, 1), :]
        away_info[d - 1, 1:2, :] = value_scale[pl.ds(out_slot, 1), :]
        away_info[d - 1, 2:3, :] = (places < lengths[replica * requests + out_slot]).astype(F32)

    for d in range(1, replicas):
        pltpu.make_async_copy(kv_pages.at[pl.ds(0, max_pages)], away_kv.at[d - 1], kv_sem.at[d - 1]).wait()


def attend_resident(
    per_kv,
    after,
    table_v,
    context,
    pool,
    q_rows,
    nk_rows,
    key_scale,
    value_scale,
    attended,
    *rest,
):
    table_s, scores, mixed, table_sem = rest
    del after
    requests, max_pages = table_v.shape
    _, _, page_len, head_dim = pool.shape
    tokens = max_pages * page_len
    factor = 1.0 / math.sqrt(head_dim)
    copy = pltpu.make_async_copy(table_v, table_s, table_sem)
    copy.start()
    copy.wait()

    def gather(j, c, which):
        return jnp.concatenate([pool[table_s[j, c * CHUNK + i], which] for i in range(CHUNK)], axis=0)

    places = lax.broadcasted_iota(jnp.int32, (1, tokens), 1)
    span = CHUNK * page_len
    own = []
    for j in range(requests):
        rows = slice(j * ROWS, (j + 1) * ROWS)
        q = q_rows[rows, :]
        own.append(jnp.sum(q * nk_rows[j : j + 1, :head_dim], axis=1, keepdims=True) * factor)
        q = q.astype(BF16)
        for c in range(max_pages // CHUNK):
            columns = slice(c * span, (c + 1) * span)
            raw = dot_keys(q, gather(j, c, 0)) * key_scale[j : j + 1, columns]
            scores[rows, columns] = jnp.where(places[:, columns] < context[j : j + 1, :1], raw, -jnp.inf)
    stats = []
    for j in range(requests):
        rows = slice(j * ROWS, (j + 1) * ROWS)
        weights, own_weight, inverse = softmax_parts(scores[rows, :], own[j])
        scores[rows, :] = weights
        stats.append((own_weight, inverse))
    for j in range(requests):
        rows = slice(j * ROWS, (j + 1) * ROWS)
        own_weight, inverse = stats[j]
        total = jnp.zeros((2 * ROWS, head_dim), F32)
        for c in range(max_pages // CHUNK):
            columns = slice(c * span, (c + 1) * span)
            both = split_scaled(scores[rows, columns], inverse, value_scale[j : j + 1, columns])
            total = total + jnp.dot(both, gather(j, c, 1), preferred_element_type=F32)
        own_weight = (own_weight * inverse).astype(BF16).astype(F32)
        mixed[rows, :] = total[:ROWS] + total[ROWS:] + own_weight * nk_rows[j : j + 1, head_dim:]
    for h in range(per_kv):
        attended[:, h * head_dim : (h + 1) * head_dim] = mixed[pl.ds(h, requests, stride=ROWS), :]


def attend_away(replicas, per_kv, *refs):
    count = replicas - 1
    away_kv, away_info, goal_mask = refs[:3]
    came = refs[3 : 3 + count]
    outs = refs[3 + count : 3 + 2 * count]
    q_rows, scores = refs[3 + 2 * count :]
    max_pages, _, page_len, head_dim = away_kv.shape[1:]
    span = CHUNK * page_len
    for d in range(count):
        pick = goal_mask[d]
        came_all = came[d][...].astype(F32)
        q_rows[...] = jnp.zeros_like(q_rows)
        for h in range(per_kv):
            q_rows[h : h + 1, :] = jnp.sum(
                came_all[:, h * head_dim : (h + 1) * head_dim] * pick, axis=0, keepdims=True
            )
        q = q_rows[...].astype(BF16)
        for c in range(max_pages // CHUNK):
            columns = slice(c * span, (c + 1) * span)
            keys = away_kv[d, c * CHUNK : (c + 1) * CHUNK, 0].reshape(span, head_dim)
            raw = dot_keys(q, keys) * away_info[d, 0:1, columns]
            scores[:, columns] = jnp.where(away_info[d, 2:3, columns] > 0, raw, -jnp.inf)
        highest = jnp.max(scores[...], axis=1, keepdims=True)
        weights = jnp.exp(scores[...] - highest)
        total = jnp.sum(weights, axis=1, keepdims=True)
        inverse = 1.0 / total
        mixed = jnp.zeros((2 * ROWS, head_dim), F32)
        for c in range(max_pages // CHUNK):
            columns = slice(c * span, (c + 1) * span)
            values = away_kv[d, c * CHUNK : (c + 1) * CHUNK, 1].reshape(span, head_dim)
            both = split_scaled(weights[:, columns], inverse, away_info[d, 1:2, columns])
            mixed = mixed + jnp.dot(both, values, preferred_element_type=F32)
        outs[d][0] = mixed[:ROWS] + mixed[ROWS:]
        outs[d][1] = jnp.broadcast_to(highest, (ROWS, head_dim))
        outs[d][2] = jnp.broadcast_to(total, (ROWS, head_dim))


def merge(replicas, attended, here_mask, here_own, *refs):
    arrived, out = refs[: replicas - 1], refs[-1]
    head_dim = here_mask.shape[2]
    per_kv = attended.shape[1] // head_dim
    moved = []
    for d in range(replicas - 1):
        own = here_own[d, 0]
        highest = jnp.maximum(arrived[d][1], own)
        cached = arrived[d][2] * jnp.exp(arrived[d][1] - highest)
        own = jnp.exp(own - highest)
        inverse = 1.0 / (cached + own)
        own = (own * inverse).astype(BF16).astype(F32)
        moved.append(arrived[d][0] * (cached * inverse) + own * here_own[d, 1])
    for h in range(per_kv):
        columns = slice(h * head_dim, (h + 1) * head_dim)
        piece = attended[:, columns]
        for d in range(replicas - 1):
            piece = jnp.where(here_mask[d] > 0, moved[d][h : h + 1], piece)
        out[:, columns] = piece.astype(out.dtype)


def on_device(
    kv_pages, page_scale, page_table, lengths, request_moves, queries, new_kv, output_proj, residual
):
    devices = lax.axis_size("replica")
    replicas = devices // KVH
    requests, max_pages = page_table.shape
    pages, _, page_len, head_dim = kv_pages.shape
    per_kv = queries.shape[1] // head_dim
    width = output_proj.shape[1] // KVH
    tokens = max_pages * page_len
    count = replicas - 1

    def toward(value, steps):
        pairs = [(i, (i + steps * KVH) % devices) for i in range(devices)]
        return lax.ppermute(value, "replica", pairs)

    def partner(value, mask):
        return lax.ppermute(value, "replica", [(i, i ^ mask) for i in range(devices)])

    position = lax.axis_index("replica").astype(jnp.uint32)
    bits = [(position & (1 << i)) != 0 for i in range(KVH.bit_length() - 1)]
    queries, *bits = lax.optimization_barrier((queries, *bits))
    came = [toward(queries, -d) for d in range(1, replicas)]

    def shape(*dims, dtype=F32):
        return jax.ShapeDtypeStruct(dims, dtype)

    in_hbm = functools.partial(pltpu.with_memory_space_constraint, memory_space=pltpu.HBM)
    q_rows, nk_rows, key_scale, value_scale, away_kv, away_info, goal_mask, *home = pl.pallas_call(
        functools.partial(set_up, replicas, per_kv),
        out_shape=[
            shape(requests * ROWS, head_dim),
            shape(requests, 2 * head_dim),
            shape(requests, tokens),
            shape(requests, tokens),
            shape(count, max_pages, 2, page_len, head_dim, dtype=BF16),
            shape(count, 8, tokens),
            shape(count, requests, head_dim),
            shape(count, requests, head_dim),
            shape(count, 2, ROWS, head_dim),
            shape(requests, max_pages, dtype=jnp.int32),
            shape(requests, head_dim, dtype=jnp.int32),
        ],
        in_specs=[HBM] * 7,
        out_specs=[VMEM] * 11,
        scratch_shapes=[
            pltpu.SMEM(lengths.shape, jnp.int32),
            pltpu.SMEM(request_moves.shape, jnp.int32),
            pltpu.SMEM(page_table.shape, jnp.int32),
            pltpu.VMEM(page_table.shape, jnp.int32),
            pltpu.VMEM((2, pages), BF16),
            pltpu.VMEM(queries.shape, BF16),
            pltpu.VMEM(new_kv.shape, BF16),
            pltpu.VMEM((2, requests, max_pages), F32),
            pltpu.SemaphoreType.DMA((7,)),
            pltpu.SemaphoreType.DMA((count,)),
        ],
        compiler_params=pltpu.CompilerParams(vmem_limit_bytes=4 * 2**20),
        cost_estimate=pl.CostEstimate(flops=0, bytes_accessed=4 * kv_pages.size, transcendentals=0),
        name="set_up",
    )(*(in_hbm(x) for x in (lengths, request_moves, page_table, page_scale.T, queries, new_kv, kv_pages)))

    here_mask, here_own, table_v, context = home

    rows = pl.pallas_call(
        functools.partial(attend_away, replicas, per_kv),
        out_shape=[shape(3, ROWS, head_dim)] * count,
        in_specs=[VMEM] * (3 + count),
        out_specs=[VMEM] * count,
        scratch_shapes=[pltpu.VMEM((ROWS, head_dim), F32), pltpu.VMEM((ROWS, tokens), F32)],
        compiler_params=pltpu.CompilerParams(vmem_limit_bytes=4 * 2**20),
        name="attend_away",
    )(away_kv, away_info, goal_mask, *came)
    arrived = [toward(rows[d - 1], d) for d in range(1, replicas)]

    attended = pl.pallas_call(
        functools.partial(attend_resident, per_kv),
        out_shape=shape(requests, per_kv * head_dim),
        in_specs=[HBM] + [VMEM] * 7,
        out_specs=VMEM,
        scratch_shapes=[
            pltpu.SMEM(page_table.shape, jnp.int32),
            pltpu.VMEM((requests * ROWS, tokens), F32),
            pltpu.VMEM((requests * ROWS, head_dim), F32),
            pltpu.SemaphoreType.DMA,
        ],
        compiler_params=pltpu.CompilerParams(vmem_limit_bytes=8 * 2**20),
        cost_estimate=pl.CostEstimate(
            flops=4 * per_kv * requests * tokens * head_dim,
            bytes_accessed=4 * output_proj.size,
            transcendentals=requests * ROWS * tokens,
        ),
        name="attend_resident",
    )(
        rows[0],
        table_v,
        context,
        pltpu.with_memory_space_constraint(kv_pages, pltpu.VMEM),
        q_rows,
        nk_rows,
        key_scale,
        value_scale,
    )
    mixture = pl.pallas_call(
        functools.partial(merge, replicas),
        out_shape=shape(*attended.shape, dtype=BF16),
        in_specs=[VMEM] * (3 + count),
        out_specs=VMEM,
        compiler_params=pltpu.CompilerParams(vmem_limit_bytes=2**20),
        name="merge",
    )(attended, here_mask, here_own, *arrived)

    parts = jnp.dot(mixture, output_proj, preferred_element_type=F32)
    parts = [parts[:, i * width : (i + 1) * width] for i in range(KVH)]
    core, y, z = bits

    def split(blocks, bit, step):
        low = [b for i, b in enumerate(blocks) if not i & step]
        high = [b for i, b in enumerate(blocks) if i & step]
        same = [jnp.where(bit, b, a) for a, b in zip(low, high)]
        return same, [jnp.where(bit, a, b) for a, b in zip(low, high)]

    near, far = split(parts, core, 1)
    (near_own, near_z), (near_y, near_yz) = (split(pair, z, 1) for pair in split(near, y, 1))
    (far_own, far_z), (far_y, far_yz) = (split(pair, z, 1) for pair in split(far, y, 1))
    to_yz, to_core, at_y, at_z, own = lax.optimization_barrier(
        (
            jnp.concatenate([*near_yz, *far_yz], axis=1).astype(BF16),
            jnp.concatenate([*far_y, *far_z, *far_own], axis=1),
            near_y[0],
            near_z[0],
            near_own[0],
        )
    )
    came_yz = partner(to_yz, 6).astype(F32)
    other = partner(to_core, 1)
    came_y = partner((at_y + other[:, :width]).astype(BF16), 2)
    came_z = partner((at_z + other[:, width : 2 * width]).astype(BF16), 4)
    passed_on = partner(came_yz[:, width:], 1)
    total = own + other[:, 2 * width :] + came_yz[:, :width] + came_y.astype(F32) + came_z.astype(F32)
    total = lax.optimization_barrier(total) + passed_on
    return (residual.astype(F32) + total).astype(BF16)


def solution(mesh):
    return jax.shard_map(
        on_device,
        mesh=mesh,
        in_specs=(
            P(("parts", "replica"), None, None, None),
            P(("parts", "replica"), None),
            P(("parts", "replica"), None),
            P("parts"),
            P("parts"),
            P(("parts", "replica"), None),
            P(("parts", "replica"), None),
            P("replica", None),
            P(("parts", "replica"), None),
        ),
        out_specs=P(("parts", "replica"), None),
        check_vma=False,
    )
```

```python
import functools
import math

import jax
import jax.numpy as jnp
from jax import lax
from jax.experimental import pallas as pl
from jax.experimental.pallas import tpu as pltpu
from jax.sharding import PartitionSpec as P

KVH = 8
ROWS = 8
CHUNK = 4
F32 = jnp.float32
BF16 = jnp.bfloat16
VMEM = pl.BlockSpec(memory_space=pltpu.VMEM)
HBM = pl.BlockSpec(memory_space=pltpu.HBM)


def softmax_parts(scores, own):
    highest = jnp.maximum(jnp.max(scores, axis=1, keepdims=True), own)
    weights = jnp.exp(scores - highest)
    own_weight = jnp.exp(own - highest)
    return weights, own_weight, 1.0 / (jnp.sum(weights, axis=1, keepdims=True) + own_weight)


def split_scaled(weights, inverse, value_scale):
    scaled = (weights * inverse).astype(BF16).astype(F32) * value_scale
    high = scaled.astype(BF16)
    low = (scaled - high.astype(F32)).astype(BF16)
    return jnp.concatenate([high, low], axis=0)


def dot_keys(queries, keys):
    return lax.dot_general(queries, keys, (((1,), (1,)), ((), ())), preferred_element_type=F32)


def picked_scales(scales, pages):
    ids = lax.broadcasted_iota(jnp.int32, (scales.shape[1], pages.shape[1]), 0)
    return jnp.dot(scales, (ids == pages).astype(F32).astype(BF16), preferred_element_type=F32)


def spread_matrix(max_pages, tokens):
    page_len = tokens // max_pages
    return (
        lax.broadcasted_iota(jnp.int32, (max_pages, tokens), 1) // page_len
        == lax.broadcasted_iota(jnp.int32, (max_pages, tokens), 0)
    ).astype(F32).astype(BF16)


def set_up(
    replicas,
    per_kv,
    lengths_h,
    moves_h,
    table_h,
    scale_h,
    queries_h,
    new_kv_h,
    kv_pages,
    q_rows,
    nk_rows,
    scales,
    away_kv,
    away_info,
    goal_mask,
    here_mask,
    here_own,
    table_out,
    context,
    lengths,
    moves,
    table_s,
    table_v,
    scale_v,
    queries,
    new_kv,
    small_sem,
    kv_sem,
):
    requests, max_pages = table_h.shape
    pages, _, page_len, head_dim = kv_pages.shape
    tokens = max_pages * page_len
    factor = 1.0 / math.sqrt(head_dim)
    replica = lax.axis_index("replica") // KVH

    small = [
        pltpu.make_async_copy(src, dst, small_sem.at[i])
        for i, (src, dst) in enumerate(
            [
                (moves_h, moves),
                (table_h, table_s),
                (table_h, table_v),
                (lengths_h, lengths),
                (scale_h, scale_v),
                (queries_h, queries),
                (new_kv_h, new_kv),
            ]
        )
    ]
    for copy in small:
        copy.start()
    for copy in small[:2]:
        copy.wait()

    first = replica * requests
    leaver, goal, arriver = [], [], []
    for d in range(1, replicas):
        there = jnp.where(replica + d < replicas, replica + d, replica + d - replicas) * requests
        behind = jnp.where(replica >= d, replica - d, replica - d + replicas) * requests
        out_slot = taken = here = jnp.int32(0)
        for j in range(requests):
            slot = moves[there + j] - first
            ours = (slot >= 0) & (slot < requests)
            out_slot = jnp.where(ours, slot, out_slot)
            taken = jnp.where(ours, j, taken)
            slot = moves[first + j] - behind
            here = jnp.where((slot >= 0) & (slot < requests), j, here)
        leaver.append(out_slot)
        goal.append(taken)
        arriver.append(here)

        def fetch(p, carry, d=d, out_slot=out_slot):
            pltpu.make_async_copy(
                kv_pages.at[table_s[out_slot, p]], away_kv.at[d - 1, p], kv_sem.at[d - 1]
            ).start()
            return carry

        lax.fori_loop(0, max_pages, fetch, 0, unroll=8)
    for copy in small[2:]:
        copy.wait()
    row_ids = lax.broadcasted_iota(jnp.int32, (requests, head_dim), 0)
    for d in range(1, replicas):
        goal_mask[d - 1] = (row_ids == goal[d - 1]).astype(F32)
        here_mask[d - 1] = (row_ids == arriver[d - 1]).astype(F32)

    q_all = queries[...].astype(F32)
    nk_rows[...] = new_kv[...].astype(F32)
    q_rows[...] = jnp.zeros_like(q_rows)
    for h in range(per_kv):
        q_rows[pl.ds(h, requests, stride=ROWS), :] = q_all[:, h * head_dim : (h + 1) * head_dim]

    for d in range(1, replicas):
        here = arriver[d - 1]
        own_rows = q_rows[pl.ds(pl.multiple_of(here * ROWS, ROWS), ROWS), :]
        token = nk_rows[pl.ds(here, 1), :]
        score = jnp.sum(own_rows * token[:, :head_dim], axis=1, keepdims=True) * factor
        here_own[d - 1, 0] = jnp.broadcast_to(score, (ROWS, head_dim))
        here_own[d - 1, 1] = jnp.broadcast_to(token[:, head_dim:], (ROWS, head_dim))
    lanes = lax.broadcasted_iota(jnp.int32, (1, max_pages), 1)
    staying = jnp.zeros((1, max_pages), jnp.int32)
    count = jnp.int32(0)
    for j in range(requests):
        stays = jnp.int32(1)
        for out_slot in leaver:
            stays = jnp.where(out_slot == j, 0, stays)
        staying = jnp.where((lanes == count) & (stays == 1), j, staying)
        count = count + stays
    table_out[:requests, :] = table_v[...]
    table_out[requests:, :] = staying
    for j in range(requests):
        context[j : j + 1, :] = jnp.full((1, head_dim), lengths[replica * requests + j], jnp.int32)

    scales[...] = scale_v[...].astype(F32)
    places = lax.broadcasted_iota(jnp.int32, (1, tokens), 1)
    spread = spread_matrix(max_pages, tokens)
    for d in range(1, replicas):
        out_slot = leaver[d - 1]
        picked = picked_scales(scale_v[...], table_v[pl.ds(out_slot, 1), :]).astype(BF16)
        wide = jnp.dot(picked, spread, preferred_element_type=F32)
        away_info[d - 1, 0:1, :] = wide[0:1] * factor
        away_info[d - 1, 1:2, :] = wide[1:2]
        away_info[d - 1, 2:3, :] = (places < lengths[replica * requests + out_slot]).astype(F32)

    for d in range(1, replicas):
        pltpu.make_async_copy(kv_pages.at[pl.ds(0, max_pages)], away_kv.at[d - 1], kv_sem.at[d - 1]).wait()


def attend_resident(
    replicas,
    per_kv,
    after,
    table_v,
    context,
    pool,
    q_rows,
    nk_rows,
    scales,
    attended,
    table_s,
    page_scales,
    key_scale,
    value_scale,
    scores,
    mixed,
    table_sem,
):
    del after
    requests, max_pages = context.shape[0], table_v.shape[1]
    _, _, page_len, head_dim = pool.shape
    tokens = max_pages * page_len
    span = CHUNK * page_len
    factor = 1.0 / math.sqrt(head_dim)
    copy = pltpu.make_async_copy(table_v, table_s, table_sem)
    copy.start()

    scale_rows = scales[...].astype(BF16)
    for j in range(requests):
        page_scales[:, j : j + 1, :] = picked_scales(scale_rows, table_v[j : j + 1, :])[:, None, :]
    spread = spread_matrix(max_pages, tokens)
    key_scale[...] = jnp.dot(page_scales[0].astype(BF16), spread, preferred_element_type=F32) * factor
    value_scale[...] = jnp.dot(page_scales[1].astype(BF16), spread, preferred_element_type=F32)
    places = lax.broadcasted_iota(jnp.int32, (1, tokens), 1)
    copy.wait()

    def gather(j, c, which):
        return jnp.concatenate([pool[table_s[j, c * CHUNK + i], which] for i in range(CHUNK)], axis=0)

    slots = [table_s[requests, i] for i in range(requests - (replicas - 1))]
    own, tokens_new = [], []
    for i, j in enumerate(slots):
        rows = slice(i * ROWS, (i + 1) * ROWS)
        q = q_rows[pl.ds(pl.multiple_of(j * ROWS, ROWS), ROWS), :]
        tokens_new.append(nk_rows[pl.ds(j, 1), :])
        own.append(jnp.sum(q * tokens_new[i][:, :head_dim], axis=1, keepdims=True) * factor)
        q = q.astype(BF16)
        key_row = key_scale[pl.ds(j, 1), :]
        limit = context[pl.ds(j, 1), :][:, :1]
        for c in range(max_pages // CHUNK):
            columns = slice(c * span, (c + 1) * span)
            raw = dot_keys(q, gather(j, c, 0)) * key_row[:, columns]
            scores[rows, columns] = jnp.where(places[:, columns] < limit, raw, -jnp.inf)
    stats = []
    for i in range(len(slots)):
        rows = slice(i * ROWS, (i + 1) * ROWS)
        weights, own_weight, inverse = softmax_parts(scores[rows, :], own[i])
        scores[rows, :] = weights
        stats.append((own_weight, inverse))
    for i, j in enumerate(slots):
        rows = slice(i * ROWS, (i + 1) * ROWS)
        own_weight, inverse = stats[i]
        value_row = value_scale[pl.ds(j, 1), :]
        total = jnp.zeros((2 * ROWS, head_dim), F32)
        for c in range(max_pages // CHUNK):
            columns = slice(c * span, (c + 1) * span)
            both = split_scaled(scores[rows, columns], inverse, value_row[:, columns])
            total = total + jnp.dot(both, gather(j, c, 1), preferred_element_type=F32)
        own_weight = (own_weight * inverse).astype(BF16).astype(F32)
        mixed[pl.ds(pl.multiple_of(j * ROWS, ROWS), ROWS), :] = (
            total[:ROWS] + total[ROWS:] + own_weight * tokens_new[i][:, head_dim:]
        )
    for h in range(per_kv):
        attended[:, h * head_dim : (h + 1) * head_dim] = mixed[pl.ds(h, requests, stride=ROWS), :]


def attend_away(replicas, per_kv, *refs):
    count = replicas - 1
    away_kv, away_info, goal_mask = refs[:3]
    came = refs[3 : 3 + count]
    outs = refs[3 + count : 3 + 2 * count]
    q_rows, scores = refs[3 + 2 * count :]
    max_pages, _, page_len, head_dim = away_kv.shape[1:]
    span = CHUNK * page_len
    for d in range(count):
        pick = goal_mask[d]
        came_all = came[d][...].astype(F32)
        q_rows[...] = jnp.zeros_like(q_rows)
        for h in range(per_kv):
            q_rows[h : h + 1, :] = jnp.sum(
                came_all[:, h * head_dim : (h + 1) * head_dim] * pick, axis=0, keepdims=True
            )
        q = q_rows[...].astype(BF16)
        for c in range(max_pages // CHUNK):
            columns = slice(c * span, (c + 1) * span)
            keys = away_kv[d, c * CHUNK : (c + 1) * CHUNK, 0].reshape(span, head_dim)
            raw = dot_keys(q, keys) * away_info[d, 0:1, columns]
            scores[:, columns] = jnp.where(away_info[d, 2:3, columns] > 0, raw, -jnp.inf)
        highest = jnp.max(scores[...], axis=1, keepdims=True)
        weights = jnp.exp(scores[...] - highest)
        total = jnp.sum(weights, axis=1, keepdims=True)
        inverse = 1.0 / total
        mixed = jnp.zeros((2 * ROWS, head_dim), F32)
        for c in range(max_pages // CHUNK):
            columns = slice(c * span, (c + 1) * span)
            values = away_kv[d, c * CHUNK : (c + 1) * CHUNK, 1].reshape(span, head_dim)
            both = split_scaled(weights[:, columns], inverse, away_info[d, 1:2, columns])
            mixed = mixed + jnp.dot(both, values, preferred_element_type=F32)
        outs[d][0] = mixed[:ROWS] + mixed[ROWS:]
        outs[d][1] = jnp.broadcast_to(highest, (ROWS, head_dim))
        outs[d][2] = jnp.broadcast_to(total, (ROWS, head_dim))


def merge(replicas, attended, here_mask, here_own, *refs):
    arrived, out = refs[: replicas - 1], refs[-1]
    head_dim = here_mask.shape[2]
    per_kv = attended.shape[1] // head_dim
    moved = []
    for d in range(replicas - 1):
        own = here_own[d, 0]
        highest = jnp.maximum(arrived[d][1], own)
        cached = arrived[d][2] * jnp.exp(arrived[d][1] - highest)
        own = jnp.exp(own - highest)
        inverse = 1.0 / (cached + own)
        own = (own * inverse).astype(BF16).astype(F32)
        moved.append(arrived[d][0] * (cached * inverse) + own * here_own[d, 1])
    for h in range(per_kv):
        columns = slice(h * head_dim, (h + 1) * head_dim)
        piece = attended[:, columns]
        for d in range(replicas - 1):
            piece = jnp.where(here_mask[d] > 0, moved[d][h : h + 1], piece)
        out[:, columns] = piece.astype(out.dtype)


def on_device(
    kv_pages, page_scale, page_table, lengths, request_moves, queries, new_kv, output_proj, residual
):
    devices = lax.axis_size("replica")
    replicas = devices // KVH
    requests, max_pages = page_table.shape
    pages, _, page_len, head_dim = kv_pages.shape
    per_kv = queries.shape[1] // head_dim
    width = output_proj.shape[1] // KVH
    tokens = max_pages * page_len
    count = replicas - 1

    def toward(value, steps):
        pairs = [(i, (i + steps * KVH) % devices) for i in range(devices)]
        return lax.ppermute(value, "replica", pairs)

    def partner(value, mask):
        return lax.ppermute(value, "replica", [(i, i ^ mask) for i in range(devices)])

    position = lax.axis_index("replica").astype(jnp.uint32)
    bits = [(position & (1 << i)) != 0 for i in range(KVH.bit_length() - 1)]
    queries, *bits = lax.optimization_barrier((queries, *bits))
    came = [toward(queries, -d) for d in range(1, replicas)]

    def shape(*dims, dtype=F32):
        return jax.ShapeDtypeStruct(dims, dtype)

    in_hbm = functools.partial(pltpu.with_memory_space_constraint, memory_space=pltpu.HBM)
    q_rows, nk_rows, scales, away_kv, away_info, goal_mask, *home = pl.pallas_call(
        functools.partial(set_up, replicas, per_kv),
        out_shape=[
            shape(requests * ROWS, head_dim),
            shape(requests, 2 * head_dim),
            shape(2, pages),
            shape(count, max_pages, 2, page_len, head_dim, dtype=BF16),
            shape(count, 8, tokens),
            shape(count, requests, head_dim),
            shape(count, requests, head_dim),
            shape(count, 2, ROWS, head_dim),
            shape(requests + 1, max_pages, dtype=jnp.int32),
            shape(requests, head_dim, dtype=jnp.int32),
        ],
        in_specs=[HBM] * 7,
        out_specs=[VMEM] * 10,
        scratch_shapes=[
            pltpu.SMEM(lengths.shape, jnp.int32),
            pltpu.SMEM(request_moves.shape, jnp.int32),
            pltpu.SMEM(page_table.shape, jnp.int32),
            pltpu.VMEM(page_table.shape, jnp.int32),
            pltpu.VMEM((2, pages), BF16),
            pltpu.VMEM(queries.shape, BF16),
            pltpu.VMEM(new_kv.shape, BF16),
            pltpu.SemaphoreType.DMA((7,)),
            pltpu.SemaphoreType.DMA((count,)),
        ],
        compiler_params=pltpu.CompilerParams(vmem_limit_bytes=4 * 2**20),
        cost_estimate=pl.CostEstimate(flops=0, bytes_accessed=4 * kv_pages.size, transcendentals=0),
        name="set_up",
    )(*(in_hbm(x) for x in (lengths, request_moves, page_table, page_scale.T, queries, new_kv, kv_pages)))

    here_mask, here_own, table_v, context = home

    rows = pl.pallas_call(
        functools.partial(attend_away, replicas, per_kv),
        out_shape=[shape(3, ROWS, head_dim)] * count,
        in_specs=[VMEM] * (3 + count),
        out_specs=[VMEM] * count,
        scratch_shapes=[pltpu.VMEM((ROWS, head_dim), F32), pltpu.VMEM((ROWS, tokens), F32)],
        compiler_params=pltpu.CompilerParams(vmem_limit_bytes=4 * 2**20),
        name="attend_away",
    )(away_kv, away_info, goal_mask, *came)
    arrived = [toward(rows[d - 1], d) for d in range(1, replicas)]

    attended = pl.pallas_call(
        functools.partial(attend_resident, replicas, per_kv),
        out_shape=shape(requests, per_kv * head_dim),
        in_specs=[HBM] + [VMEM] * 6,
        out_specs=VMEM,
        scratch_shapes=[
            pltpu.SMEM((requests + 1, max_pages), jnp.int32),
            pltpu.VMEM((2, requests, max_pages), F32),
            pltpu.VMEM((requests, tokens), F32),
            pltpu.VMEM((requests, tokens), F32),
            pltpu.VMEM((requests * ROWS, tokens), F32),
            pltpu.VMEM((requests * ROWS, head_dim), F32),
            pltpu.SemaphoreType.DMA,
        ],
        compiler_params=pltpu.CompilerParams(vmem_limit_bytes=8 * 2**20),
        cost_estimate=pl.CostEstimate(
            flops=4 * per_kv * requests * tokens * head_dim,
            bytes_accessed=4 * output_proj.size,
            transcendentals=requests * ROWS * tokens,
        ),
        name="attend_resident",
    )(
        rows[0],
        table_v,
        context,
        pltpu.with_memory_space_constraint(kv_pages, pltpu.VMEM),
        q_rows,
        nk_rows,
        scales,
    )
    mixture = pl.pallas_call(
        functools.partial(merge, replicas),
        out_shape=shape(*attended.shape, dtype=BF16),
        in_specs=[VMEM] * (3 + count),
        out_specs=VMEM,
        compiler_params=pltpu.CompilerParams(vmem_limit_bytes=2**20),
        name="merge",
    )(attended, here_mask, here_own, *arrived)

    parts = jnp.dot(mixture, output_proj, preferred_element_type=F32)
    parts = [parts[:, i * width : (i + 1) * width] for i in range(KVH)]
    core, y, z = bits

    def split(blocks, bit, step):
        low = [b for i, b in enumerate(blocks) if not i & step]
        high = [b for i, b in enumerate(blocks) if i & step]
        same = [jnp.where(bit, b, a) for a, b in zip(low, high)]
        return same, [jnp.where(bit, a, b) for a, b in zip(low, high)]

    near, far = split(parts, core, 1)
    (near_own, near_z), (near_y, near_yz) = (split(pair, z, 1) for pair in split(near, y, 1))
    (far_own, far_z), (far_y, far_yz) = (split(pair, z, 1) for pair in split(far, y, 1))
    to_yz, to_core, at_y, at_z, own = lax.optimization_barrier(
        (
            jnp.concatenate([*near_yz, *far_yz], axis=1).astype(BF16),
            jnp.concatenate([*far_y, *far_z, *far_own], axis=1),
            near_y[0],
            near_z[0],
            near_own[0],
        )
    )
    came_yz = partner(to_yz, 6).astype(F32)
    other = partner(to_core, 1)
    came_y = partner((at_y + other[:, :width]).astype(BF16), 2)
    came_z = partner((at_z + other[:, width : 2 * width]).astype(BF16), 4)
    passed_on = partner(came_yz[:, width:], 1)
    total = own + other[:, 2 * width :] + came_yz[:, :width] + came_y.astype(F32) + came_z.astype(F32)
    total = lax.optimization_barrier(total) + passed_on
    return (residual.astype(F32) + total).astype(BF16)


def solution(mesh):
    return jax.shard_map(
        on_device,
        mesh=mesh,
        in_specs=(
            P(("parts", "replica"), None, None, None),
            P(("parts", "replica"), None),
            P(("parts", "replica"), None),
            P("parts"),
            P("parts"),
            P(("parts", "replica"), None),
            P(("parts", "replica"), None),
            P("replica", None),
            P(("parts", "replica"), None),
        ),
        out_specs=P(("parts", "replica"), None),
        check_vma=False,
    )
```

```python
import functools
import math

import jax
import jax.numpy as jnp
from jax import lax
from jax.experimental import pallas as pl
from jax.experimental.pallas import tpu as pltpu
from jax.sharding import PartitionSpec as P

KVH = 8
ROWS = 8
CHUNK = 4
FETCH = 8
F32 = jnp.float32
BF16 = jnp.bfloat16
VMEM = pl.BlockSpec(memory_space=pltpu.VMEM)
HBM = pl.BlockSpec(memory_space=pltpu.HBM)


def softmax_parts(scores, own):
    highest = jnp.maximum(jnp.max(scores, axis=1, keepdims=True), own)
    weights = jnp.exp(scores - highest)
    own_weight = jnp.exp(own - highest)
    return weights, own_weight, 1.0 / (jnp.sum(weights, axis=1, keepdims=True) + own_weight)


def split_scaled(weights, inverse, value_scale):
    scaled = (weights * inverse).astype(BF16).astype(F32) * value_scale
    high = scaled.astype(BF16)
    low = (scaled - high.astype(F32)).astype(BF16)
    return jnp.concatenate([high, low], axis=0)


def dot_keys(queries, keys):
    return lax.dot_general(queries, keys, (((1,), (1,)), ((), ())), preferred_element_type=F32)


def picked_scales(scales, pages):
    ids = lax.broadcasted_iota(jnp.int32, (scales.shape[1], pages.shape[1]), 0)
    return jnp.dot(scales, (ids == pages).astype(F32).astype(BF16), preferred_element_type=F32)


def spread_matrix(max_pages, tokens):
    page_len = tokens // max_pages
    return (
        lax.broadcasted_iota(jnp.int32, (max_pages, tokens), 1) // page_len
        == lax.broadcasted_iota(jnp.int32, (max_pages, tokens), 0)
    ).astype(F32).astype(BF16)


def set_up(
    replicas,
    per_kv,
    lengths_h,
    moves_h,
    table_h,
    scale_h,
    queries_h,
    new_kv_h,
    kv_pages,
    q_rows,
    nk_rows,
    scales,
    away_kv,
    away_info,
    goal_mask,
    here_mask,
    here_own,
    table_out,
    context,
    lengths,
    moves,
    table_s,
    table_v,
    scale_v,
    queries,
    new_kv,
    small_sem,
    kv_sem,
):
    requests, max_pages = table_h.shape
    pages, _, page_len, head_dim = kv_pages.shape
    tokens = max_pages * page_len
    factor = 1.0 / math.sqrt(head_dim)
    replica = lax.axis_index("replica") // KVH

    small = [
        pltpu.make_async_copy(src, dst, small_sem.at[i])
        for i, (src, dst) in enumerate(
            [
                (moves_h, moves),
                (lengths_h, lengths),
                (table_h, table_s),
                (table_h, table_v),
                (scale_h, scale_v),
                (queries_h, queries),
                (new_kv_h, new_kv),
            ]
        )
    ]
    for copy in small:
        copy.start()
    for copy in small[:3]:
        copy.wait()

    first = replica * requests
    leaver, goal, arriver, groups = [], [], [], []
    for d in range(1, replicas):
        there = jnp.where(replica + d < replicas, replica + d, replica + d - replicas) * requests
        behind = jnp.where(replica >= d, replica - d, replica - d + replicas) * requests
        out_slot = taken = here = jnp.int32(0)
        for j in range(requests):
            slot = moves[there + j] - first
            ours = (slot >= 0) & (slot < requests)
            out_slot = jnp.where(ours, slot, out_slot)
            taken = jnp.where(ours, j, taken)
            slot = moves[first + j] - behind
            here = jnp.where((slot >= 0) & (slot < requests), j, here)
        leaver.append(out_slot)
        goal.append(taken)
        arriver.append(here)

        def fetch(g, carry, d=d, out_slot=out_slot):
            for i in range(FETCH):
                p = g * FETCH + i
                pltpu.make_async_copy(
                    kv_pages.at[table_s[out_slot, p]], away_kv.at[d - 1, p], kv_sem.at[d - 1]
                ).start()
            return carry

        def clear(g, carry, d=d):
            for i in range(FETCH):
                away_kv[d - 1, g * FETCH + i, 1] = jnp.zeros((page_len, head_dim), BF16)
            return carry

        span = FETCH * page_len
        groups.append((lengths[first + out_slot] + span - 1) // span)
        lax.fori_loop(0, groups[-1], fetch, 0)
        lax.fori_loop(groups[-1], max_pages // FETCH, clear, 0)
    for copy in small[3:]:
        copy.wait()
    row_ids = lax.broadcasted_iota(jnp.int32, (requests, head_dim), 0)
    for d in range(1, replicas):
        goal_mask[d - 1] = (row_ids == goal[d - 1]).astype(F32)
        here_mask[d - 1] = (row_ids == arriver[d - 1]).astype(F32)

    q_all = queries[...].astype(F32)
    nk_rows[...] = new_kv[...].astype(F32)
    q_rows[...] = jnp.zeros_like(q_rows)
    for h in range(per_kv):
        q_rows[pl.ds(h, requests, stride=ROWS), :] = q_all[:, h * head_dim : (h + 1) * head_dim]

    for d in range(1, replicas):
        here = arriver[d - 1]
        own_rows = q_rows[pl.ds(pl.multiple_of(here * ROWS, ROWS), ROWS), :]
        token = nk_rows[pl.ds(here, 1), :]
        score = jnp.sum(own_rows * token[:, :head_dim], axis=1, keepdims=True) * factor
        here_own[d - 1, 0] = jnp.broadcast_to(score, (ROWS, head_dim))
        here_own[d - 1, 1] = jnp.broadcast_to(token[:, head_dim:], (ROWS, head_dim))
    lanes = lax.broadcasted_iota(jnp.int32, (1, max_pages), 1)
    staying = jnp.zeros((1, max_pages), jnp.int32)
    count = jnp.int32(0)
    for j in range(requests):
        stays = jnp.int32(1)
        for out_slot in leaver:
            stays = jnp.where(out_slot == j, 0, stays)
        staying = jnp.where((lanes == count) & (stays == 1), j, staying)
        count = count + stays
    table_out[:requests, :] = table_v[...]
    table_out[requests:, :] = staying
    for j in range(requests):
        context[j : j + 1, :] = jnp.full((1, head_dim), lengths[replica * requests + j], jnp.int32)

    scales[...] = scale_v[...].astype(F32)
    places = lax.broadcasted_iota(jnp.int32, (1, tokens), 1)
    spread = spread_matrix(max_pages, tokens)
    for d in range(1, replicas):
        out_slot = leaver[d - 1]
        picked = picked_scales(scale_v[...], table_v[pl.ds(out_slot, 1), :]).astype(BF16)
        wide = jnp.dot(picked, spread, preferred_element_type=F32)
        away_info[d - 1, 0:1, :] = wide[0:1] * factor
        away_info[d - 1, 1:2, :] = wide[1:2]
        away_info[d - 1, 2:3, :] = (places < lengths[replica * requests + out_slot]).astype(F32)

    for d in range(1, replicas):

        def landed(g, carry, d=d):
            pltpu.make_async_copy(
                kv_pages.at[pl.ds(0, FETCH)], away_kv.at[d - 1, pl.ds(0, FETCH)], kv_sem.at[d - 1]
            ).wait()
            return carry

        lax.fori_loop(0, groups[d - 1], landed, 0)


def attend_resident(
    replicas,
    per_kv,
    after,
    table_v,
    context,
    pool,
    q_rows,
    nk_rows,
    scales,
    attended,
    table_s,
    page_scales,
    key_scale,
    value_scale,
    scores,
    mixed,
    table_sem,
):
    del after
    requests, max_pages = context.shape[0], table_v.shape[1]
    _, _, page_len, head_dim = pool.shape
    tokens = max_pages * page_len
    span = CHUNK * page_len
    factor = 1.0 / math.sqrt(head_dim)
    copy = pltpu.make_async_copy(table_v, table_s, table_sem)
    copy.start()

    scale_rows = scales[...].astype(BF16)
    for j in range(requests):
        page_scales[:, j : j + 1, :] = picked_scales(scale_rows, table_v[j : j + 1, :])[:, None, :]
    spread = spread_matrix(max_pages, tokens)
    key_scale[...] = jnp.dot(page_scales[0].astype(BF16), spread, preferred_element_type=F32) * factor
    value_scale[...] = jnp.dot(page_scales[1].astype(BF16), spread, preferred_element_type=F32)
    places = lax.broadcasted_iota(jnp.int32, (1, tokens), 1)
    copy.wait()

    def gather(j, c, which):
        return jnp.concatenate([pool[table_s[j, c * CHUNK + i], which] for i in range(CHUNK)], axis=0)

    slots = [table_s[requests, i] for i in range(requests - (replicas - 1))]
    own, tokens_new = [], []
    for i, j in enumerate(slots):
        rows = slice(i * ROWS, (i + 1) * ROWS)
        q = q_rows[pl.ds(pl.multiple_of(j * ROWS, ROWS), ROWS), :]
        tokens_new.append(nk_rows[pl.ds(j, 1), :])
        own.append(jnp.sum(q * tokens_new[i][:, :head_dim], axis=1, keepdims=True) * factor)
        q = q.astype(BF16)
        key_row = key_scale[pl.ds(j, 1), :]
        limit = context[pl.ds(j, 1), :][:, :1]
        for c in range(max_pages // CHUNK):
            columns = slice(c * span, (c + 1) * span)
            raw = dot_keys(q, gather(j, c, 0)) * key_row[:, columns]
            scores[rows, columns] = jnp.where(places[:, columns] < limit, raw, -jnp.inf)
    stats = []
    for i in range(len(slots)):
        rows = slice(i * ROWS, (i + 1) * ROWS)
        weights, own_weight, inverse = softmax_parts(scores[rows, :], own[i])
        scores[rows, :] = weights
        stats.append((own_weight, inverse))
    for i, j in enumerate(slots):
        rows = slice(i * ROWS, (i + 1) * ROWS)
        own_weight, inverse = stats[i]
        value_row = value_scale[pl.ds(j, 1), :]
        total = jnp.zeros((2 * ROWS, head_dim), F32)
        for c in range(max_pages // CHUNK):
            columns = slice(c * span, (c + 1) * span)
            both = split_scaled(scores[rows, columns], inverse, value_row[:, columns])
            total = total + jnp.dot(both, gather(j, c, 1), preferred_element_type=F32)
        own_weight = (own_weight * inverse).astype(BF16).astype(F32)
        mixed[pl.ds(pl.multiple_of(j * ROWS, ROWS), ROWS), :] = (
            total[:ROWS] + total[ROWS:] + own_weight * tokens_new[i][:, head_dim:]
        )
    for h in range(per_kv):
        attended[:, h * head_dim : (h + 1) * head_dim] = mixed[pl.ds(h, requests, stride=ROWS), :]


def attend_away(replicas, per_kv, *refs):
    count = replicas - 1
    away_kv, away_info, goal_mask = refs[:3]
    came = refs[3 : 3 + count]
    outs = refs[3 + count : 3 + 2 * count]
    (q_rows,) = refs[3 + 2 * count :]
    max_pages, _, page_len, head_dim = away_kv.shape[1:]
    span = CHUNK * page_len
    for d in range(count):
        pick = goal_mask[d]
        came_all = came[d][...].astype(F32)
        q_rows[...] = jnp.zeros_like(q_rows)
        for h in range(per_kv):
            q_rows[h : h + 1, :] = jnp.sum(
                came_all[:, h * head_dim : (h + 1) * head_dim] * pick, axis=0, keepdims=True
            )
        q = q_rows[...].astype(BF16)
        scores = []
        for c in range(max_pages // CHUNK):
            columns = slice(c * span, (c + 1) * span)
            keys = away_kv[d, c * CHUNK : (c + 1) * CHUNK, 0].reshape(span, head_dim)
            raw = dot_keys(q, keys) * away_info[d, 0:1, columns]
            scores.append(jnp.where(away_info[d, 2:3, columns] > 0, raw, -jnp.inf))
        highest = jnp.max(functools.reduce(jnp.maximum, scores), axis=1, keepdims=True)
        weights = [jnp.exp(part - highest) for part in scores]
        total = jnp.sum(functools.reduce(jnp.add, weights), axis=1, keepdims=True)
        inverse = 1.0 / total
        mixed = jnp.zeros((2 * ROWS, head_dim), F32)
        for c in range(max_pages // CHUNK):
            columns = slice(c * span, (c + 1) * span)
            values = away_kv[d, c * CHUNK : (c + 1) * CHUNK, 1].reshape(span, head_dim)
            both = split_scaled(weights[c], inverse, away_info[d, 1:2, columns])
            mixed = mixed + jnp.dot(both, values, preferred_element_type=F32)
        outs[d][0] = mixed[:ROWS] + mixed[ROWS:]
        outs[d][1] = jnp.broadcast_to(highest, (ROWS, head_dim))
        outs[d][2] = jnp.broadcast_to(total, (ROWS, head_dim))


def merge(replicas, attended, here_mask, here_own, *refs):
    arrived, out = refs[: replicas - 1], refs[-1]
    head_dim = here_mask.shape[2]
    per_kv = attended.shape[1] // head_dim
    moved = []
    for d in range(replicas - 1):
        own = here_own[d, 0]
        highest = jnp.maximum(arrived[d][1], own)
        cached = arrived[d][2] * jnp.exp(arrived[d][1] - highest)
        own = jnp.exp(own - highest)
        inverse = 1.0 / (cached + own)
        own = (own * inverse).astype(BF16).astype(F32)
        moved.append(arrived[d][0] * (cached * inverse) + own * here_own[d, 1])
    for h in range(per_kv):
        columns = slice(h * head_dim, (h + 1) * head_dim)
        piece = attended[:, columns]
        for d in range(replicas - 1):
            piece = jnp.where(here_mask[d] > 0, moved[d][h : h + 1], piece)
        out[:, columns] = piece.astype(out.dtype)


def on_device(
    kv_pages, page_scale, page_table, lengths, request_moves, queries, new_kv, output_proj, residual
):
    devices = lax.axis_size("replica")
    replicas = devices // KVH
    requests, max_pages = page_table.shape
    pages, _, page_len, head_dim = kv_pages.shape
    per_kv = queries.shape[1] // head_dim
    width = output_proj.shape[1] // KVH
    tokens = max_pages * page_len
    count = replicas - 1

    def toward(value, steps):
        pairs = [(i, (i + steps * KVH) % devices) for i in range(devices)]
        return lax.ppermute(value, "replica", pairs)

    def partner(value, mask):
        return lax.ppermute(value, "replica", [(i, i ^ mask) for i in range(devices)])

    position = lax.axis_index("replica").astype(jnp.uint32)
    bits = [(position & (1 << i)) != 0 for i in range(KVH.bit_length() - 1)]
    queries, *bits = lax.optimization_barrier((queries, *bits))
    came = [toward(queries, -d) for d in range(1, replicas)]

    def shape(*dims, dtype=F32):
        return jax.ShapeDtypeStruct(dims, dtype)

    in_hbm = functools.partial(pltpu.with_memory_space_constraint, memory_space=pltpu.HBM)
    q_rows, nk_rows, scales, away_kv, away_info, goal_mask, *home = pl.pallas_call(
        functools.partial(set_up, replicas, per_kv),
        out_shape=[
            shape(requests * ROWS, head_dim),
            shape(requests, 2 * head_dim),
            shape(2, pages),
            shape(count, max_pages, 2, page_len, head_dim, dtype=BF16),
            shape(count, 8, tokens),
            shape(count, requests, head_dim),
            shape(count, requests, head_dim),
            shape(count, 2, ROWS, head_dim),
            shape(requests + 1, max_pages, dtype=jnp.int32),
            shape(requests, head_dim, dtype=jnp.int32),
        ],
        in_specs=[HBM] * 7,
        out_specs=[VMEM] * 10,
        scratch_shapes=[
            pltpu.SMEM(lengths.shape, jnp.int32),
            pltpu.SMEM(request_moves.shape, jnp.int32),
            pltpu.SMEM(page_table.shape, jnp.int32),
            pltpu.VMEM(page_table.shape, jnp.int32),
            pltpu.VMEM((2, pages), BF16),
            pltpu.VMEM(queries.shape, BF16),
            pltpu.VMEM(new_kv.shape, BF16),
            pltpu.SemaphoreType.DMA((7,)),
            pltpu.SemaphoreType.DMA((count,)),
        ],
        compiler_params=pltpu.CompilerParams(vmem_limit_bytes=4 * 2**20),
        cost_estimate=pl.CostEstimate(flops=0, bytes_accessed=4 * kv_pages.size, transcendentals=0),
        name="set_up",
    )(*(in_hbm(x) for x in (lengths, request_moves, page_table, page_scale.T, queries, new_kv, kv_pages)))

    here_mask, here_own, table_v, context = home

    rows = pl.pallas_call(
        functools.partial(attend_away, replicas, per_kv),
        out_shape=[shape(3, ROWS, head_dim)] * count,
        in_specs=[VMEM] * (3 + count),
        out_specs=[VMEM] * count,
        scratch_shapes=[pltpu.VMEM((ROWS, head_dim), F32)],
        compiler_params=pltpu.CompilerParams(vmem_limit_bytes=4 * 2**20),
        name="attend_away",
    )(away_kv, away_info, goal_mask, *came)
    arrived = [toward(rows[d - 1], d) for d in range(1, replicas)]

    attended = pl.pallas_call(
        functools.partial(attend_resident, replicas, per_kv),
        out_shape=shape(requests, per_kv * head_dim),
        in_specs=[HBM] + [VMEM] * 6,
        out_specs=VMEM,
        scratch_shapes=[
            pltpu.SMEM((requests + 1, max_pages), jnp.int32),
            pltpu.VMEM((2, requests, max_pages), F32),
            pltpu.VMEM((requests, tokens), F32),
            pltpu.VMEM((requests, tokens), F32),
            pltpu.VMEM((requests * ROWS, tokens), F32),
            pltpu.VMEM((requests * ROWS, head_dim), F32),
            pltpu.SemaphoreType.DMA,
        ],
        compiler_params=pltpu.CompilerParams(vmem_limit_bytes=8 * 2**20),
        cost_estimate=pl.CostEstimate(
            flops=4 * per_kv * requests * tokens * head_dim,
            bytes_accessed=4 * output_proj.size,
            transcendentals=requests * ROWS * tokens,
        ),
        name="attend_resident",
    )(
        rows[0],
        table_v,
        context,
        pltpu.with_memory_space_constraint(kv_pages, pltpu.VMEM),
        q_rows,
        nk_rows,
        scales,
    )
    mixture = pl.pallas_call(
        functools.partial(merge, replicas),
        out_shape=shape(*attended.shape, dtype=BF16),
        in_specs=[VMEM] * (3 + count),
        out_specs=VMEM,
        compiler_params=pltpu.CompilerParams(vmem_limit_bytes=2**20),
        name="merge",
    )(attended, here_mask, here_own, *arrived)

    parts = jnp.dot(mixture, output_proj, preferred_element_type=F32)
    parts = [parts[:, i * width : (i + 1) * width] for i in range(KVH)]
    core, y, z = bits

    def split(blocks, bit, step):
        low = [b for i, b in enumerate(blocks) if not i & step]
        high = [b for i, b in enumerate(blocks) if i & step]
        same = [jnp.where(bit, b, a) for a, b in zip(low, high)]
        return same, [jnp.where(bit, a, b) for a, b in zip(low, high)]

    near, far = split(parts, core, 1)
    (near_own, near_z), (near_y, near_yz) = (split(pair, z, 1) for pair in split(near, y, 1))
    (far_own, far_z), (far_y, far_yz) = (split(pair, z, 1) for pair in split(far, y, 1))
    to_yz, to_core, at_y, at_z, own = lax.optimization_barrier(
        (
            jnp.concatenate([*near_yz, *far_yz], axis=1).astype(BF16),
            jnp.concatenate([*far_y, *far_z, *far_own], axis=1),
            near_y[0],
            near_z[0],
            near_own[0],
        )
    )
    came_yz = partner(to_yz, 6).astype(F32)
    other = partner(to_core, 1)
    came_y = partner((at_y + other[:, :width]).astype(BF16), 2)
    came_z = partner((at_z + other[:, width : 2 * width]).astype(BF16), 4)
    passed_on = partner(came_yz[:, width:], 1)
    total = own + other[:, 2 * width :] + came_yz[:, :width] + came_y.astype(F32) + came_z.astype(F32)
    total = lax.optimization_barrier(total) + passed_on
    return (residual.astype(F32) + total).astype(BF16)


def solution(mesh):
    return jax.shard_map(
        on_device,
        mesh=mesh,
        in_specs=(
            P(("parts", "replica"), None, None, None),
            P(("parts", "replica"), None),
            P(("parts", "replica"), None),
            P("parts"),
            P("parts"),
            P(("parts", "replica"), None),
            P(("parts", "replica"), None),
            P("replica", None),
            P(("parts", "replica"), None),
        ),
        out_specs=P(("parts", "replica"), None),
        check_vma=False,
    )
```

```python
import functools
import math

import jax
import jax.numpy as jnp
from jax import lax
from jax.experimental import pallas as pl
from jax.experimental.pallas import tpu as pltpu
from jax.sharding import PartitionSpec as P

KVH = 8
ROWS = 8
CHUNK = 4
F32 = jnp.float32
BF16 = jnp.bfloat16
VMEM = pl.BlockSpec(memory_space=pltpu.VMEM)
HBM = pl.BlockSpec(memory_space=pltpu.HBM)


def softmax_parts(scores, own):
    highest = jnp.maximum(jnp.max(scores, axis=1, keepdims=True), own)
    weights = jnp.exp(scores - highest)
    own_weight = jnp.exp(own - highest)
    return weights, own_weight, 1.0 / (jnp.sum(weights, axis=1, keepdims=True) + own_weight)


def split_scaled(weights, inverse, value_scale):
    scaled = (weights * inverse).astype(BF16).astype(F32) * value_scale
    high = scaled.astype(BF16)
    low = (scaled - high.astype(F32)).astype(BF16)
    return jnp.concatenate([high, low], axis=0)


def dot_keys(queries, keys):
    return lax.dot_general(queries, keys, (((1,), (1,)), ((), ())), preferred_element_type=F32)


def picked_scales(scales, pages):
    ids = lax.broadcasted_iota(jnp.int32, (scales.shape[1], pages.shape[1]), 0)
    return jnp.dot(scales, (ids == pages).astype(F32).astype(BF16), preferred_element_type=F32)


def spread_matrix(max_pages, tokens):
    page_len = tokens // max_pages
    return (
        lax.broadcasted_iota(jnp.int32, (max_pages, tokens), 1) // page_len
        == lax.broadcasted_iota(jnp.int32, (max_pages, tokens), 0)
    ).astype(F32).astype(BF16)


def set_up(
    replicas,
    per_kv,
    lengths_h,
    moves_h,
    table_h,
    scale_h,
    queries_h,
    new_kv_h,
    kv_pages,
    q_rows,
    nk_rows,
    scales,
    away_kv,
    away_info,
    goal_mask,
    here_mask,
    here_own,
    table_out,
    context,
    lengths,
    moves,
    table_s,
    table_v,
    scale_v,
    queries,
    new_kv,
    small_sem,
    kv_sem,
):
    requests, max_pages = table_h.shape
    pages, _, page_len, head_dim = kv_pages.shape
    tokens = max_pages * page_len
    factor = 1.0 / math.sqrt(head_dim)
    replica = lax.axis_index("replica") // KVH

    small = [
        pltpu.make_async_copy(src, dst, small_sem.at[i])
        for i, (src, dst) in enumerate(
            [
                (moves_h, moves),
                (table_h, table_s),
                (table_h, table_v),
                (lengths_h, lengths),
                (scale_h, scale_v),
                (queries_h, queries),
                (new_kv_h, new_kv),
            ]
        )
    ]
    for copy in small:
        copy.start()
    for copy in small[:2]:
        copy.wait()

    first = replica * requests
    leaver, goal, arriver = [], [], []
    for d in range(1, replicas):
        there = jnp.where(replica + d < replicas, replica + d, replica + d - replicas) * requests
        behind = jnp.where(replica >= d, replica - d, replica - d + replicas) * requests
        out_slot = taken = here = jnp.int32(0)
        for j in range(requests):
            slot = moves[there + j] - first
            ours = (slot >= 0) & (slot < requests)
            out_slot = jnp.where(ours, slot, out_slot)
            taken = jnp.where(ours, j, taken)
            slot = moves[first + j] - behind
            here = jnp.where((slot >= 0) & (slot < requests), j, here)
        leaver.append(out_slot)
        goal.append(taken)
        arriver.append(here)

        def fetch(p, carry, d=d, out_slot=out_slot):
            pltpu.make_async_copy(
                kv_pages.at[table_s[out_slot, p]], away_kv.at[d - 1, p], kv_sem.at[d - 1]
            ).start()
            return carry

        lax.fori_loop(0, max_pages, fetch, 0, unroll=8)
    for copy in small[2:]:
        copy.wait()
    row_ids = lax.broadcasted_iota(jnp.int32, (requests, head_dim), 0)
    for d in range(1, replicas):
        goal_mask[d - 1] = (row_ids == goal[d - 1]).astype(F32)
        here_mask[d - 1] = (row_ids == arriver[d - 1]).astype(F32)

    q_all = queries[...].astype(F32)
    nk_rows[...] = new_kv[...].astype(F32)
    q_rows[...] = jnp.zeros_like(q_rows)
    for h in range(per_kv):
        q_rows[pl.ds(h, requests, stride=ROWS), :] = q_all[:, h * head_dim : (h + 1) * head_dim]

    for d in range(1, replicas):
        here = arriver[d - 1]
        own_rows = q_rows[pl.ds(pl.multiple_of(here * ROWS, ROWS), ROWS), :]
        token = nk_rows[pl.ds(here, 1), :]
        score = jnp.sum(own_rows * token[:, :head_dim], axis=1, keepdims=True) * factor
        here_own[d - 1, 0] = jnp.broadcast_to(score, (ROWS, head_dim))
        here_own[d - 1, 1] = jnp.broadcast_to(token[:, head_dim:], (ROWS, head_dim))
    lanes = lax.broadcasted_iota(jnp.int32, (1, max_pages), 1)
    staying = jnp.zeros((1, max_pages), jnp.int32)
    count = jnp.int32(0)
    for j in range(requests):
        stays = jnp.int32(1)
        for out_slot in leaver:
            stays = jnp.where(out_slot == j, 0, stays)
        staying = jnp.where((lanes == count) & (stays == 1), j, staying)
        count = count + stays
    table_out[:requests, :] = table_v[...]
    table_out[requests:, :] = staying
    for j in range(requests):
        context[j : j + 1, :] = jnp.full((1, head_dim), lengths[replica * requests + j], jnp.int32)

    scales[...] = scale_v[...].astype(F32)
    places = lax.broadcasted_iota(jnp.int32, (1, tokens), 1)
    spread = spread_matrix(max_pages, tokens)
    for d in range(1, replicas):
        out_slot = leaver[d - 1]
        picked = picked_scales(scale_v[...], table_v[pl.ds(out_slot, 1), :]).astype(BF16)
        wide = jnp.dot(picked, spread, preferred_element_type=F32)
        away_info[d - 1, 0:1, :] = wide[0:1] * factor
        away_info[d - 1, 1:2, :] = wide[1:2]
        away_info[d - 1, 2:3, :] = (places < lengths[replica * requests + out_slot]).astype(F32)

    for d in range(1, replicas):
        pltpu.make_async_copy(kv_pages.at[pl.ds(0, max_pages)], away_kv.at[d - 1], kv_sem.at[d - 1]).wait()


def attend_resident(
    replicas,
    per_kv,
    after,
    table_v,
    context,
    pool,
    q_rows,
    nk_rows,
    scales,
    attended,
    table_s,
    page_scales,
    key_scale,
    value_scale,
    scores,
    mixed,
    table_sem,
):
    del after
    requests, max_pages = context.shape[0], table_v.shape[1]
    _, _, page_len, head_dim = pool.shape
    tokens = max_pages * page_len
    span = CHUNK * page_len
    factor = 1.0 / math.sqrt(head_dim)
    copy = pltpu.make_async_copy(table_v, table_s, table_sem)
    copy.start()

    scale_rows = scales[...].astype(BF16)
    for j in range(requests):
        page_scales[:, j : j + 1, :] = picked_scales(scale_rows, table_v[j : j + 1, :])[:, None, :]
    spread = spread_matrix(max_pages, tokens)
    key_scale[...] = jnp.dot(page_scales[0].astype(BF16), spread, preferred_element_type=F32) * factor
    value_scale[...] = jnp.dot(page_scales[1].astype(BF16), spread, preferred_element_type=F32)
    places = lax.broadcasted_iota(jnp.int32, (1, tokens), 1)
    copy.wait()

    def gather(j, c, which):
        return jnp.concatenate([pool[table_s[j, c * CHUNK + i], which] for i in range(CHUNK)], axis=0)

    slots = [table_s[requests, i] for i in range(requests - (replicas - 1))]
    own, tokens_new = [], []
    for i, j in enumerate(slots):
        rows = slice(i * ROWS, (i + 1) * ROWS)
        q = q_rows[pl.ds(pl.multiple_of(j * ROWS, ROWS), ROWS), :]
        tokens_new.append(nk_rows[pl.ds(j, 1), :])
        own.append(jnp.sum(q * tokens_new[i][:, :head_dim], axis=1, keepdims=True) * factor)
        q = q.astype(BF16)
        key_row = key_scale[pl.ds(j, 1), :]
        limit = context[pl.ds(j, 1), :][:, :1]
        for c in range(max_pages // CHUNK):
            columns = slice(c * span, (c + 1) * span)
            raw = dot_keys(q, gather(j, c, 0)) * key_row[:, columns]
            scores[rows, columns] = jnp.where(places[:, columns] < limit, raw, -jnp.inf)
    stats = []
    for i in range(len(slots)):
        rows = slice(i * ROWS, (i + 1) * ROWS)
        weights, own_weight, inverse = softmax_parts(scores[rows, :], own[i])
        scores[rows, :] = weights
        stats.append((own_weight, inverse))
    for i, j in enumerate(slots):
        rows = slice(i * ROWS, (i + 1) * ROWS)
        own_weight, inverse = stats[i]
        value_row = value_scale[pl.ds(j, 1), :]
        total = jnp.zeros((2 * ROWS, head_dim), F32)
        for c in range(max_pages // CHUNK):
            columns = slice(c * span, (c + 1) * span)
            both = split_scaled(scores[rows, columns], inverse, value_row[:, columns])
            total = total + jnp.dot(both, gather(j, c, 1), preferred_element_type=F32)
        own_weight = (own_weight * inverse).astype(BF16).astype(F32)
        mixed[pl.ds(pl.multiple_of(j * ROWS, ROWS), ROWS), :] = (
            total[:ROWS] + total[ROWS:] + own_weight * tokens_new[i][:, head_dim:]
        )
    for h in range(per_kv):
        attended[:, h * head_dim : (h + 1) * head_dim] = mixed[pl.ds(h, requests, stride=ROWS), :]


def attend_away(replicas, per_kv, *refs):
    count = replicas - 1
    away_kv, away_info, goal_mask = refs[:3]
    came = refs[3 : 3 + count]
    outs = refs[3 + count : 3 + 2 * count]
    q_rows, scores = refs[3 + 2 * count :]
    max_pages, _, page_len, head_dim = away_kv.shape[1:]
    span = CHUNK * page_len
    for d in range(count):
        pick = goal_mask[d]
        came_all = came[d][...].astype(F32)
        q_rows[...] = jnp.zeros_like(q_rows)
        for h in range(per_kv):
            q_rows[h : h + 1, :] = jnp.sum(
                came_all[:, h * head_dim : (h + 1) * head_dim] * pick, axis=0, keepdims=True
            )
        q = q_rows[...].astype(BF16)
        for c in range(max_pages // CHUNK):
            columns = slice(c * span, (c + 1) * span)
            keys = away_kv[d, c * CHUNK : (c + 1) * CHUNK, 0].reshape(span, head_dim)
            raw = dot_keys(q, keys) * away_info[d, 0:1, columns]
            scores[:, columns] = jnp.where(away_info[d, 2:3, columns] > 0, raw, -jnp.inf)
        highest = jnp.max(scores[...], axis=1, keepdims=True)
        weights = jnp.exp(scores[...] - highest)
        total = jnp.sum(weights, axis=1, keepdims=True)
        inverse = 1.0 / total
        mixed = jnp.zeros((2 * ROWS, head_dim), F32)
        for c in range(max_pages // CHUNK):
            columns = slice(c * span, (c + 1) * span)
            values = away_kv[d, c * CHUNK : (c + 1) * CHUNK, 1].reshape(span, head_dim)
            both = split_scaled(weights[:, columns], inverse, away_info[d, 1:2, columns])
            mixed = mixed + jnp.dot(both, values, preferred_element_type=F32)
        outs[d][0] = mixed[:ROWS] + mixed[ROWS:]
        outs[d][1] = jnp.broadcast_to(highest, (ROWS, head_dim))
        outs[d][2] = jnp.broadcast_to(total, (ROWS, head_dim))


def merge(replicas, attended, here_mask, here_own, *refs):
    arrived, out = refs[: replicas - 1], refs[-1]
    head_dim = here_mask.shape[2]
    per_kv = attended.shape[1] // head_dim
    moved = []
    for d in range(replicas - 1):
        own = here_own[d, 0]
        highest = jnp.maximum(arrived[d][1], own)
        cached = arrived[d][2] * jnp.exp(arrived[d][1] - highest)
        own = jnp.exp(own - highest)
        inverse = 1.0 / (cached + own)
        own = (own * inverse).astype(BF16).astype(F32)
        moved.append(arrived[d][0] * (cached * inverse) + own * here_own[d, 1])
    for h in range(per_kv):
        columns = slice(h * head_dim, (h + 1) * head_dim)
        piece = attended[:, columns]
        for d in range(replicas - 1):
            piece = jnp.where(here_mask[d] > 0, moved[d][h : h + 1], piece)
        out[:, columns] = piece.astype(out.dtype)


def on_device(
    kv_pages, page_scale, page_table, lengths, request_moves, queries, new_kv, output_proj, residual
):
    devices = lax.axis_size("replica")
    replicas = devices // KVH
    requests, max_pages = page_table.shape
    pages, _, page_len, head_dim = kv_pages.shape
    per_kv = queries.shape[1] // head_dim
    width = output_proj.shape[1] // KVH
    tokens = max_pages * page_len
    count = replicas - 1

    def toward(value, steps):
        pairs = [(i, (i + steps * KVH) % devices) for i in range(devices)]
        return lax.ppermute(value, "replica", pairs)

    def partner(value, mask):
        return lax.ppermute(value, "replica", [(i, i ^ mask) for i in range(devices)])

    position = lax.axis_index("replica").astype(jnp.uint32)
    bits = [(position & (1 << i)) != 0 for i in range(KVH.bit_length() - 1)]
    queries, *bits = lax.optimization_barrier((queries, *bits))
    came = [toward(queries, -d) for d in range(1, replicas)]

    def shape(*dims, dtype=F32):
        return jax.ShapeDtypeStruct(dims, dtype)

    in_hbm = functools.partial(pltpu.with_memory_space_constraint, memory_space=pltpu.HBM)
    q_rows, nk_rows, scales, away_kv, away_info, goal_mask, *home = pl.pallas_call(
        functools.partial(set_up, replicas, per_kv),
        out_shape=[
            shape(requests * ROWS, head_dim),
            shape(requests, 2 * head_dim),
            shape(2, pages),
            shape(count, max_pages, 2, page_len, head_dim, dtype=BF16),
            shape(count, 8, tokens),
            shape(count, requests, head_dim),
            shape(count, requests, head_dim),
            shape(count, 2, ROWS, head_dim),
            shape(requests + 1, max_pages, dtype=jnp.int32),
            shape(requests, head_dim, dtype=jnp.int32),
        ],
        in_specs=[HBM] * 7,
        out_specs=[VMEM] * 10,
        scratch_shapes=[
            pltpu.SMEM(lengths.shape, jnp.int32),
            pltpu.SMEM(request_moves.shape, jnp.int32),
            pltpu.SMEM(page_table.shape, jnp.int32),
            pltpu.VMEM(page_table.shape, jnp.int32),
            pltpu.VMEM((2, pages), BF16),
            pltpu.VMEM(queries.shape, BF16),
            pltpu.VMEM(new_kv.shape, BF16),
            pltpu.SemaphoreType.DMA((7,)),
            pltpu.SemaphoreType.DMA((count,)),
        ],
        compiler_params=pltpu.CompilerParams(vmem_limit_bytes=4 * 2**20),
        cost_estimate=pl.CostEstimate(flops=0, bytes_accessed=4 * kv_pages.size, transcendentals=0),
        name="set_up",
    )(*(in_hbm(x) for x in (lengths, request_moves, page_table, page_scale.T, queries, new_kv, kv_pages)))

    here_mask, here_own, table_v, context = home

    rows = pl.pallas_call(
        functools.partial(attend_away, replicas, per_kv),
        out_shape=[shape(3, ROWS, head_dim)] * count,
        in_specs=[VMEM] * (3 + count),
        out_specs=[VMEM] * count,
        scratch_shapes=[pltpu.VMEM((ROWS, head_dim), F32), pltpu.VMEM((ROWS, tokens), F32)],
        compiler_params=pltpu.CompilerParams(vmem_limit_bytes=4 * 2**20),
        name="attend_away",
    )(away_kv, away_info, goal_mask, *came)
    arrived = [toward(rows[d - 1], d) for d in range(1, replicas)]

    attended = pl.pallas_call(
        functools.partial(attend_resident, replicas, per_kv),
        out_shape=shape(requests, per_kv * head_dim),
        in_specs=[HBM] + [VMEM] * 6,
        out_specs=VMEM,
        scratch_shapes=[
            pltpu.SMEM((requests + 1, max_pages), jnp.int32),
            pltpu.VMEM((2, requests, max_pages), F32),
            pltpu.VMEM((requests, tokens), F32),
            pltpu.VMEM((requests, tokens), F32),
            pltpu.VMEM((requests * ROWS, tokens), F32),
            pltpu.VMEM((requests * ROWS, head_dim), F32),
            pltpu.SemaphoreType.DMA,
        ],
        compiler_params=pltpu.CompilerParams(vmem_limit_bytes=8 * 2**20),
        cost_estimate=pl.CostEstimate(
            flops=4 * per_kv * requests * tokens * head_dim,
            bytes_accessed=4 * output_proj.size,
            transcendentals=requests * ROWS * tokens,
        ),
        name="attend_resident",
    )(
        rows[0],
        table_v,
        context,
        pltpu.with_memory_space_constraint(kv_pages, pltpu.VMEM),
        q_rows,
        nk_rows,
        scales,
    )
    mixture = pl.pallas_call(
        functools.partial(merge, replicas),
        out_shape=shape(*attended.shape, dtype=BF16),
        in_specs=[VMEM] * (3 + count),
        out_specs=VMEM,
        compiler_params=pltpu.CompilerParams(vmem_limit_bytes=2**20),
        name="merge",
    )(attended, here_mask, here_own, *arrived)

    parts = jnp.dot(mixture, output_proj, preferred_element_type=F32)
    parts = [parts[:, i * width : (i + 1) * width] for i in range(KVH)]
    core, y, z = bits

    def split(blocks, bit, step):
        low = [b for i, b in enumerate(blocks) if not i & step]
        high = [b for i, b in enumerate(blocks) if i & step]
        same = [jnp.where(bit, b, a) for a, b in zip(low, high)]
        return same, [jnp.where(bit, a, b) for a, b in zip(low, high)]

    def between(value, one, two):
        pairs = [
            (r * KVH + 2 * source + c, r * KVH + 2 * target + c)
            for r in range(replicas)
            for c in range(2)
            for source, target in ((one, two), (two, one))
        ]
        return lax.ppermute(value, "replica", pairs)

    near, far = split(parts, core, 1)
    (near_own, near_z), (near_y, near_yz) = (split(pair, z, 1) for pair in split(near, y, 1))
    (far_own, far_z), (far_y, far_yz) = (split(pair, z, 1) for pair in split(far, y, 1))
    to_y, to_z, to_yz, to_core, at_y, at_z, at_yz, own = lax.optimization_barrier(
        (
            jnp.concatenate([*near_y, *far_y], axis=1).astype(BF16),
            jnp.concatenate([*near_z, *far_z], axis=1).astype(BF16),
            jnp.concatenate([*near_yz, *far_yz], axis=1).astype(BF16),
            jnp.concatenate([*far_y, *far_z, *far_yz, *far_own], axis=1),
            near_y[0],
            near_z[0],
            near_yz[0],
            near_own[0],
        )
    )
    raw = [between(to_y, 0, 1), between(to_z, 0, 2), between(to_yz, 1, 2)]
    other = partner(to_core, 1)
    other_y, other_z, other_yz, other_own = (other[:, i * width : (i + 1) * width] for i in range(4))
    summed = [
        between((at_yz + other_yz).astype(BF16), 0, 3),
        between((at_z + other_z).astype(BF16), 1, 3),
        between((at_y + other_y).astype(BF16), 2, 3),
    ]
    for_core = sum(part[:, width:].astype(F32) for part in raw)
    for_core, *raw = lax.optimization_barrier((for_core, *(part[:, :width] for part in raw)))
    passed_on = partner(for_core, 1)
    total = own + other_own
    for part in raw + summed:
        total = total + part.astype(F32)
    total = lax.optimization_barrier(total) + passed_on
    return (residual.astype(F32) + total).astype(BF16)


def solution(mesh):
    return jax.shard_map(
        on_device,
        mesh=mesh,
        in_specs=(
            P(("parts", "replica"), None, None, None),
            P(("parts", "replica"), None),
            P(("parts", "replica"), None),
            P("parts"),
            P("parts"),
            P(("parts", "replica"), None),
            P(("parts", "replica"), None),
            P("replica", None),
            P(("parts", "replica"), None),
        ),
        out_specs=P(("parts", "replica"), None),
        check_vma=False,
    )
```

```python
import functools
import math

import jax
import jax.numpy as jnp
from jax import lax
from jax.experimental import pallas as pl
from jax.experimental.pallas import tpu as pltpu
from jax.sharding import PartitionSpec as P

KVH = 8
ROWS = 8
CHUNK = 8
F32 = jnp.float32
BF16 = jnp.bfloat16
VMEM = pl.BlockSpec(memory_space=pltpu.VMEM)
HBM = pl.BlockSpec(memory_space=pltpu.HBM)


def softmax_parts(scores, own):
    highest = jnp.maximum(jnp.max(scores, axis=1, keepdims=True), own)
    weights = jnp.exp(scores - highest)
    own_weight = jnp.exp(own - highest)
    return weights, own_weight, 1.0 / (jnp.sum(weights, axis=1, keepdims=True) + own_weight)


def split_scaled(weights, inverse, value_scale):
    scaled = (weights * inverse).astype(BF16).astype(F32) * value_scale
    high = scaled.astype(BF16)
    low = (scaled - high.astype(F32)).astype(BF16)
    return jnp.concatenate([high, low], axis=0)


def dot_keys(queries, keys):
    return lax.dot_general(queries, keys, (((1,), (1,)), ((), ())), preferred_element_type=F32)


def picked_scales(scales, pages):
    ids = lax.broadcasted_iota(jnp.int32, (scales.shape[1], pages.shape[1]), 0)
    return jnp.dot(scales, (ids == pages).astype(F32).astype(BF16), preferred_element_type=F32)


def spread_matrix(max_pages, tokens):
    page_len = tokens // max_pages
    return (
        lax.broadcasted_iota(jnp.int32, (max_pages, tokens), 1) // page_len
        == lax.broadcasted_iota(jnp.int32, (max_pages, tokens), 0)
    ).astype(F32).astype(BF16)


def set_up(
    replicas,
    per_kv,
    lengths_h,
    moves_h,
    table_h,
    scale_h,
    queries_h,
    new_kv_h,
    kv_pages,
    q_rows,
    nk_rows,
    scales,
    away_kv,
    away_info,
    goal_mask,
    here_mask,
    here_own,
    table_out,
    context,
    lengths,
    moves,
    table_s,
    table_v,
    scale_v,
    queries,
    new_kv,
    small_sem,
    kv_sem,
):
    requests, max_pages = table_h.shape
    pages, _, page_len, head_dim = kv_pages.shape
    tokens = max_pages * page_len
    factor = 1.0 / math.sqrt(head_dim)
    replica = lax.axis_index("replica") // KVH

    small = [
        pltpu.make_async_copy(src, dst, small_sem.at[i])
        for i, (src, dst) in enumerate(
            [
                (moves_h, moves),
                (table_h, table_s),
                (table_h, table_v),
                (lengths_h, lengths),
                (scale_h, scale_v),
                (queries_h, queries),
                (new_kv_h, new_kv),
            ]
        )
    ]
    for copy in small:
        copy.start()
    for copy in small[:2]:
        copy.wait()

    first = replica * requests
    leaver, goal, arriver = [], [], []
    for d in range(1, replicas):
        there = jnp.where(replica + d < replicas, replica + d, replica + d - replicas) * requests
        behind = jnp.where(replica >= d, replica - d, replica - d + replicas) * requests
        out_slot = taken = here = jnp.int32(0)
        for j in range(requests):
            slot = moves[there + j] - first
            ours = (slot >= 0) & (slot < requests)
            out_slot = jnp.where(ours, slot, out_slot)
            taken = jnp.where(ours, j, taken)
            slot = moves[first + j] - behind
            here = jnp.where((slot >= 0) & (slot < requests), j, here)
        leaver.append(out_slot)
        goal.append(taken)
        arriver.append(here)

        def fetch(p, carry, d=d, out_slot=out_slot):
            pltpu.make_async_copy(
                kv_pages.at[table_s[out_slot, p]], away_kv.at[d - 1, p], kv_sem.at[d - 1]
            ).start()
            return carry

        lax.fori_loop(0, max_pages, fetch, 0, unroll=8)
    for copy in small[2:]:
        copy.wait()
    row_ids = lax.broadcasted_iota(jnp.int32, (requests, head_dim), 0)
    for d in range(1, replicas):
        goal_mask[d - 1] = (row_ids == goal[d - 1]).astype(F32)
        here_mask[d - 1] = (row_ids == arriver[d - 1]).astype(F32)

    q_all = queries[...].astype(F32)
    nk_rows[...] = new_kv[...].astype(F32)
    q_rows[...] = jnp.zeros_like(q_rows)
    for h in range(per_kv):
        q_rows[pl.ds(h, requests, stride=ROWS), :] = q_all[:, h * head_dim : (h + 1) * head_dim]

    for d in range(1, replicas):
        here = arriver[d - 1]
        own_rows = q_rows[pl.ds(pl.multiple_of(here * ROWS, ROWS), ROWS), :]
        token = nk_rows[pl.ds(here, 1), :]
        score = jnp.sum(own_rows * token[:, :head_dim], axis=1, keepdims=True) * factor
        here_own[d - 1, 0] = jnp.broadcast_to(score, (ROWS, head_dim))
        here_own[d - 1, 1] = jnp.broadcast_to(token[:, head_dim:], (ROWS, head_dim))
    lanes = lax.broadcasted_iota(jnp.int32, (1, max_pages), 1)
    staying = jnp.zeros((1, max_pages), jnp.int32)
    count = jnp.int32(0)
    for j in range(requests):
        stays = jnp.int32(1)
        for out_slot in leaver:
            stays = jnp.where(out_slot == j, 0, stays)
        staying = jnp.where((lanes == count) & (stays == 1), j, staying)
        count = count + stays
    table_out[:requests, :] = table_v[...]
    table_out[requests:, :] = staying
    for j in range(requests):
        context[j : j + 1, :] = jnp.full((1, head_dim), lengths[replica * requests + j], jnp.int32)

    scales[...] = scale_v[...].astype(F32)
    places = lax.broadcasted_iota(jnp.int32, (1, tokens), 1)
    spread = spread_matrix(max_pages, tokens)
    for d in range(1, replicas):
        out_slot = leaver[d - 1]
        picked = picked_scales(scale_v[...], table_v[pl.ds(out_slot, 1), :]).astype(BF16)
        wide = jnp.dot(picked, spread, preferred_element_type=F32)
        away_info[d - 1, 0:1, :] = wide[0:1] * factor
        away_info[d - 1, 1:2, :] = wide[1:2]
        away_info[d - 1, 2:3, :] = (places < lengths[replica * requests + out_slot]).astype(F32)

    for d in range(1, replicas):
        pltpu.make_async_copy(kv_pages.at[pl.ds(0, max_pages)], away_kv.at[d - 1], kv_sem.at[d - 1]).wait()


def attend_resident(
    replicas,
    per_kv,
    after,
    table_v,
    context,
    pool,
    q_rows,
    nk_rows,
    scales,
    attended,
    table_s,
    page_scales,
    key_scale,
    value_scale,
    scores,
    mixed,
    table_sem,
):
    del after
    requests, max_pages = context.shape[0], table_v.shape[1]
    _, _, page_len, head_dim = pool.shape
    tokens = max_pages * page_len
    span = CHUNK * page_len
    factor = 1.0 / math.sqrt(head_dim)
    copy = pltpu.make_async_copy(table_v, table_s, table_sem)
    copy.start()

    scale_rows = scales[...].astype(BF16)
    for j in range(requests):
        page_scales[:, j : j + 1, :] = picked_scales(scale_rows, table_v[j : j + 1, :])[:, None, :]
    spread = spread_matrix(max_pages, tokens)
    key_scale[...] = jnp.dot(page_scales[0].astype(BF16), spread, preferred_element_type=F32) * factor
    value_scale[...] = jnp.dot(page_scales[1].astype(BF16), spread, preferred_element_type=F32)
    places = lax.broadcasted_iota(jnp.int32, (1, tokens), 1)
    copy.wait()

    def gather(j, c, which):
        return jnp.concatenate([pool[table_s[j, c * CHUNK + i], which] for i in range(CHUNK)], axis=0)

    slots = [table_s[requests, i] for i in range(requests - (replicas - 1))]
    own, tokens_new = [], []
    for i, j in enumerate(slots):
        rows = slice(i * ROWS, (i + 1) * ROWS)
        q = q_rows[pl.ds(pl.multiple_of(j * ROWS, ROWS), ROWS), :]
        tokens_new.append(nk_rows[pl.ds(j, 1), :])
        own.append(jnp.sum(q * tokens_new[i][:, :head_dim], axis=1, keepdims=True) * factor)
        q = q.astype(BF16)
        key_row = key_scale[pl.ds(j, 1), :]
        limit = context[pl.ds(j, 1), :][:, :1]
        for c in range(max_pages // CHUNK):
            columns = slice(c * span, (c + 1) * span)
            raw = dot_keys(q, gather(j, c, 0)) * key_row[:, columns]
            scores[rows, columns] = jnp.where(places[:, columns] < limit, raw, -jnp.inf)
    stats = []
    for i in range(len(slots)):
        rows = slice(i * ROWS, (i + 1) * ROWS)
        weights, own_weight, inverse = softmax_parts(scores[rows, :], own[i])
        scores[rows, :] = weights
        stats.append((own_weight, inverse))
    for i, j in enumerate(slots):
        rows = slice(i * ROWS, (i + 1) * ROWS)
        own_weight, inverse = stats[i]
        value_row = value_scale[pl.ds(j, 1), :]
        total = jnp.zeros((2 * ROWS, head_dim), F32)
        for c in range(max_pages // CHUNK):
            columns = slice(c * span, (c + 1) * span)
            both = split_scaled(scores[rows, columns], inverse, value_row[:, columns])
            total = total + jnp.dot(both, gather(j, c, 1), preferred_element_type=F32)
        own_weight = (own_weight * inverse).astype(BF16).astype(F32)
        mixed[pl.ds(pl.multiple_of(j * ROWS, ROWS), ROWS), :] = (
            total[:ROWS] + total[ROWS:] + own_weight * tokens_new[i][:, head_dim:]
        )
    for h in range(per_kv):
        attended[:, h * head_dim : (h + 1) * head_dim] = mixed[pl.ds(h, requests, stride=ROWS), :]


def attend_away(replicas, per_kv, *refs):
    count = replicas - 1
    away_kv, away_info, goal_mask = refs[:3]
    came = refs[3 : 3 + count]
    outs = refs[3 + count : 3 + 2 * count]
    (q_rows,) = refs[3 + 2 * count :]
    max_pages, _, page_len, head_dim = away_kv.shape[1:]
    tokens = max_pages * page_len
    for d in range(count):
        pick = goal_mask[d]
        came_all = came[d][...].astype(F32)
        q_rows[...] = jnp.zeros_like(q_rows)
        for h in range(per_kv):
            q_rows[h : h + 1, :] = jnp.sum(
                came_all[:, h * head_dim : (h + 1) * head_dim] * pick, axis=0, keepdims=True
            )
        q = q_rows[...].astype(BF16)
        raw = dot_keys(q, away_kv[d, :, 0].reshape(tokens, head_dim)) * away_info[d, 0:1, :]
        scores = jnp.where(away_info[d, 2:3, :] > 0, raw, -jnp.inf)
        highest = jnp.max(scores, axis=1, keepdims=True)
        weights = jnp.exp(scores - highest)
        total = jnp.sum(weights, axis=1, keepdims=True)
        both = split_scaled(weights, 1.0 / total, away_info[d, 1:2, :])
        mixed = jnp.dot(both, away_kv[d, :, 1].reshape(tokens, head_dim), preferred_element_type=F32)
        outs[d][0] = mixed[:ROWS] + mixed[ROWS:]
        outs[d][1] = jnp.broadcast_to(highest, (ROWS, head_dim))
        outs[d][2] = jnp.broadcast_to(total, (ROWS, head_dim))


def merge(replicas, attended, here_mask, here_own, *refs):
    arrived, out = refs[: replicas - 1], refs[-1]
    head_dim = here_mask.shape[2]
    per_kv = attended.shape[1] // head_dim
    moved = []
    for d in range(replicas - 1):
        own = here_own[d, 0]
        highest = jnp.maximum(arrived[d][1], own)
        cached = arrived[d][2] * jnp.exp(arrived[d][1] - highest)
        own = jnp.exp(own - highest)
        inverse = 1.0 / (cached + own)
        own = (own * inverse).astype(BF16).astype(F32)
        moved.append(arrived[d][0] * (cached * inverse) + own * here_own[d, 1])
    for h in range(per_kv):
        columns = slice(h * head_dim, (h + 1) * head_dim)
        piece = attended[:, columns]
        for d in range(replicas - 1):
            piece = jnp.where(here_mask[d] > 0, moved[d][h : h + 1], piece)
        out[:, columns] = piece.astype(out.dtype)


def on_device(
    kv_pages, page_scale, page_table, lengths, request_moves, queries, new_kv, output_proj, residual
):
    devices = lax.axis_size("replica")
    replicas = devices // KVH
    requests, max_pages = page_table.shape
    pages, _, page_len, head_dim = kv_pages.shape
    per_kv = queries.shape[1] // head_dim
    width = output_proj.shape[1] // KVH
    tokens = max_pages * page_len
    count = replicas - 1

    def toward(value, steps):
        pairs = [(i, (i + steps * KVH) % devices) for i in range(devices)]
        return lax.ppermute(value, "replica", pairs)

    def partner(value, mask):
        return lax.ppermute(value, "replica", [(i, i ^ mask) for i in range(devices)])

    position = lax.axis_index("replica").astype(jnp.uint32)
    bits = [(position & (1 << i)) != 0 for i in range(KVH.bit_length() - 1)]
    queries, *bits = lax.optimization_barrier((queries, *bits))
    came = [toward(queries, -d) for d in range(1, replicas)]

    def shape(*dims, dtype=F32):
        return jax.ShapeDtypeStruct(dims, dtype)

    in_hbm = functools.partial(pltpu.with_memory_space_constraint, memory_space=pltpu.HBM)
    q_rows, nk_rows, scales, away_kv, away_info, goal_mask, *home = pl.pallas_call(
        functools.partial(set_up, replicas, per_kv),
        out_shape=[
            shape(requests * ROWS, head_dim),
            shape(requests, 2 * head_dim),
            shape(2, pages),
            shape(count, max_pages, 2, page_len, head_dim, dtype=BF16),
            shape(count, 8, tokens),
            shape(count, requests, head_dim),
            shape(count, requests, head_dim),
            shape(count, 2, ROWS, head_dim),
            shape(requests + 1, max_pages, dtype=jnp.int32),
            shape(requests, head_dim, dtype=jnp.int32),
        ],
        in_specs=[HBM] * 7,
        out_specs=[VMEM] * 10,
        scratch_shapes=[
            pltpu.SMEM(lengths.shape, jnp.int32),
            pltpu.SMEM(request_moves.shape, jnp.int32),
            pltpu.SMEM(page_table.shape, jnp.int32),
            pltpu.VMEM(page_table.shape, jnp.int32),
            pltpu.VMEM((2, pages), BF16),
            pltpu.VMEM(queries.shape, BF16),
            pltpu.VMEM(new_kv.shape, BF16),
            pltpu.SemaphoreType.DMA((7,)),
            pltpu.SemaphoreType.DMA((count,)),
        ],
        compiler_params=pltpu.CompilerParams(vmem_limit_bytes=4 * 2**20),
        cost_estimate=pl.CostEstimate(flops=0, bytes_accessed=4 * kv_pages.size, transcendentals=0),
        name="set_up",
    )(*(in_hbm(x) for x in (lengths, request_moves, page_table, page_scale.T, queries, new_kv, kv_pages)))

    here_mask, here_own, table_v, context = home

    rows = pl.pallas_call(
        functools.partial(attend_away, replicas, per_kv),
        out_shape=[shape(3, ROWS, head_dim)] * count,
        in_specs=[VMEM] * (3 + count),
        out_specs=[VMEM] * count,
        scratch_shapes=[pltpu.VMEM((ROWS, head_dim), F32)],
        compiler_params=pltpu.CompilerParams(vmem_limit_bytes=4 * 2**20),
        name="attend_away",
    )(away_kv, away_info, goal_mask, *came)
    arrived = [toward(rows[d - 1], d) for d in range(1, replicas)]

    attended = pl.pallas_call(
        functools.partial(attend_resident, replicas, per_kv),
        out_shape=shape(requests, per_kv * head_dim),
        in_specs=[HBM] + [VMEM] * 6,
        out_specs=VMEM,
        scratch_shapes=[
            pltpu.SMEM((requests + 1, max_pages), jnp.int32),
            pltpu.VMEM((2, requests, max_pages), F32),
            pltpu.VMEM((requests, tokens), F32),
            pltpu.VMEM((requests, tokens), F32),
            pltpu.VMEM((requests * ROWS, tokens), F32),
            pltpu.VMEM((requests * ROWS, head_dim), F32),
            pltpu.SemaphoreType.DMA,
        ],
        compiler_params=pltpu.CompilerParams(vmem_limit_bytes=8 * 2**20),
        cost_estimate=pl.CostEstimate(
            flops=4 * per_kv * requests * tokens * head_dim,
            bytes_accessed=4 * output_proj.size,
            transcendentals=requests * ROWS * tokens,
        ),
        name="attend_resident",
    )(
        rows[0],
        table_v,
        context,
        pltpu.with_memory_space_constraint(kv_pages, pltpu.VMEM),
        q_rows,
        nk_rows,
        scales,
    )
    mixture = pl.pallas_call(
        functools.partial(merge, replicas),
        out_shape=shape(*attended.shape, dtype=BF16),
        in_specs=[VMEM] * (3 + count),
        out_specs=VMEM,
        compiler_params=pltpu.CompilerParams(vmem_limit_bytes=2**20),
        name="merge",
    )(attended, here_mask, here_own, *arrived)

    parts = jnp.dot(mixture, output_proj, preferred_element_type=F32)
    parts = [parts[:, i * width : (i + 1) * width] for i in range(KVH)]
    core, y, z = bits

    def split(blocks, bit, step):
        low = [b for i, b in enumerate(blocks) if not i & step]
        high = [b for i, b in enumerate(blocks) if i & step]
        same = [jnp.where(bit, b, a) for a, b in zip(low, high)]
        return same, [jnp.where(bit, a, b) for a, b in zip(low, high)]

    near, far = split(parts, core, 1)
    (near_own, near_z), (near_y, near_yz) = (split(pair, z, 1) for pair in split(near, y, 1))
    (far_own, far_z), (far_y, far_yz) = (split(pair, z, 1) for pair in split(far, y, 1))
    to_yz, to_core, at_y, at_z, own = lax.optimization_barrier(
        (
            jnp.concatenate([*near_yz, *far_yz], axis=1).astype(BF16),
            jnp.concatenate([*far_y, *far_z, *far_own], axis=1),
            near_y[0],
            near_z[0],
            near_own[0],
        )
    )
    came_yz = partner(to_yz, 6).astype(F32)
    other = partner(to_core, 1)
    came_y = partner((at_y + other[:, :width]).astype(BF16), 2)
    came_z = partner((at_z + other[:, width : 2 * width]).astype(BF16), 4)
    passed_on = partner(came_yz[:, width:], 1)
    total = own + other[:, 2 * width :] + came_yz[:, :width] + came_y.astype(F32) + came_z.astype(F32)
    total = lax.optimization_barrier(total) + passed_on
    return (residual.astype(F32) + total).astype(BF16)


def solution(mesh):
    return jax.shard_map(
        on_device,
        mesh=mesh,
        in_specs=(
            P(("parts", "replica"), None, None, None),
            P(("parts", "replica"), None),
            P(("parts", "replica"), None),
            P("parts"),
            P("parts"),
            P(("parts", "replica"), None),
            P(("parts", "replica"), None),
            P("replica", None),
            P(("parts", "replica"), None),
        ),
        out_specs=P(("parts", "replica"), None),
        check_vma=False,
    )
```

```python
import functools
import math

import jax
import jax.numpy as jnp
from jax import lax
from jax.experimental import pallas as pl
from jax.experimental.pallas import tpu as pltpu
from jax.sharding import PartitionSpec as P

KVH = 8
ROWS = 8
CHUNK = 4
F32 = jnp.float32
BF16 = jnp.bfloat16
VMEM = pl.BlockSpec(memory_space=pltpu.VMEM)
HBM = pl.BlockSpec(memory_space=pltpu.HBM)


def split_scaled(weights, inverse, value_scale):
    scaled = (weights * inverse).astype(BF16).astype(F32) * value_scale
    high = scaled.astype(BF16)
    low = (scaled - high.astype(F32)).astype(BF16)
    return jnp.concatenate([high, low], axis=0)


def dot_keys(queries, keys):
    return lax.dot_general(queries, keys, (((1,), (1,)), ((), ())), preferred_element_type=F32)


def picked_scales(scales, pages):
    ids = lax.broadcasted_iota(jnp.int32, (scales.shape[1], pages.shape[1]), 0)
    return jnp.dot(scales, (ids == pages).astype(F32).astype(BF16), preferred_element_type=F32)


def spread_matrix(max_pages, tokens):
    page_len = tokens // max_pages
    return (
        lax.broadcasted_iota(jnp.int32, (max_pages, tokens), 1) // page_len
        == lax.broadcasted_iota(jnp.int32, (max_pages, tokens), 0)
    ).astype(F32).astype(BF16)


def set_up(
    replicas,
    per_kv,
    lengths_h,
    moves_h,
    table_h,
    scale_h,
    queries_h,
    new_kv_h,
    kv_pages,
    q_rows,
    nk_rows,
    scales,
    away_kv,
    away_info,
    goal_mask,
    here_mask,
    here_own,
    table_out,
    context,
    lengths,
    moves,
    table_s,
    table_v,
    scale_v,
    queries,
    new_kv,
    small_sem,
    kv_sem,
):
    requests, max_pages = table_h.shape
    pages, _, page_len, head_dim = kv_pages.shape
    tokens = max_pages * page_len
    factor = 1.0 / math.sqrt(head_dim)
    replica = lax.axis_index("replica") // KVH

    small = [
        pltpu.make_async_copy(src, dst, small_sem.at[i])
        for i, (src, dst) in enumerate(
            [
                (moves_h, moves),
                (table_h, table_s),
                (table_h, table_v),
                (lengths_h, lengths),
                (scale_h, scale_v),
                (queries_h, queries),
                (new_kv_h, new_kv),
            ]
        )
    ]
    for copy in small:
        copy.start()
    for copy in small[:2]:
        copy.wait()

    first = replica * requests
    leaver, goal, arriver = [], [], []
    for d in range(1, replicas):
        there = jnp.where(replica + d < replicas, replica + d, replica + d - replicas) * requests
        behind = jnp.where(replica >= d, replica - d, replica - d + replicas) * requests
        out_slot = taken = here = jnp.int32(0)
        for j in range(requests):
            slot = moves[there + j] - first
            ours = (slot >= 0) & (slot < requests)
            out_slot = jnp.where(ours, slot, out_slot)
            taken = jnp.where(ours, j, taken)
            slot = moves[first + j] - behind
            here = jnp.where((slot >= 0) & (slot < requests), j, here)
        leaver.append(out_slot)
        goal.append(taken)
        arriver.append(here)

        def fetch(p, carry, d=d, out_slot=out_slot):
            pltpu.make_async_copy(
                kv_pages.at[table_s[out_slot, p]], away_kv.at[d - 1, p], kv_sem.at[d - 1]
            ).start()
            return carry

        lax.fori_loop(0, max_pages, fetch, 0, unroll=8)
    for copy in small[2:]:
        copy.wait()
    row_ids = lax.broadcasted_iota(jnp.int32, (requests, head_dim), 0)
    for d in range(1, replicas):
        goal_mask[d - 1] = (row_ids == goal[d - 1]).astype(F32)
        here_mask[d - 1] = (row_ids == arriver[d - 1]).astype(F32)

    q_all = queries[...].astype(F32)
    nk_rows[...] = new_kv[...].astype(F32)
    q_rows[...] = jnp.zeros_like(q_rows)
    for h in range(per_kv):
        q_rows[pl.ds(h, requests, stride=ROWS), :] = q_all[:, h * head_dim : (h + 1) * head_dim]

    for d in range(1, replicas):
        here = arriver[d - 1]
        own_rows = q_rows[pl.ds(pl.multiple_of(here * ROWS, ROWS), ROWS), :]
        token = nk_rows[pl.ds(here, 1), :]
        score = jnp.sum(own_rows * token[:, :head_dim], axis=1, keepdims=True) * factor
        here_own[d - 1, 0] = jnp.broadcast_to(score, (ROWS, head_dim))
        here_own[d - 1, 1] = jnp.broadcast_to(token[:, head_dim:], (ROWS, head_dim))
    lanes = lax.broadcasted_iota(jnp.int32, (1, max_pages), 1)
    staying = jnp.zeros((1, max_pages), jnp.int32)
    count = jnp.int32(0)
    for j in range(requests):
        stays = jnp.int32(1)
        for out_slot in leaver:
            stays = jnp.where(out_slot == j, 0, stays)
        staying = jnp.where((lanes == count) & (stays == 1), j, staying)
        count = count + stays
    table_out[:requests, :] = table_v[...]
    table_out[requests:, :] = staying
    for j in range(requests):
        context[j : j + 1, :] = jnp.full((1, head_dim), lengths[replica * requests + j], jnp.int32)

    scales[...] = scale_v[...].astype(F32)
    places = lax.broadcasted_iota(jnp.int32, (1, tokens), 1)
    spread = spread_matrix(max_pages, tokens)
    for d in range(1, replicas):
        out_slot = leaver[d - 1]
        picked = picked_scales(scale_v[...], table_v[pl.ds(out_slot, 1), :]).astype(BF16)
        wide = jnp.dot(picked, spread, preferred_element_type=F32)
        away_info[d - 1, 0:1, :] = wide[0:1] * factor
        away_info[d - 1, 1:2, :] = wide[1:2]
        away_info[d - 1, 2:3, :] = (places < lengths[replica * requests + out_slot]).astype(F32)

    for d in range(1, replicas):
        pltpu.make_async_copy(kv_pages.at[pl.ds(0, max_pages)], away_kv.at[d - 1], kv_sem.at[d - 1]).wait()


def attend_resident(
    replicas,
    per_kv,
    after,
    table_v,
    context,
    pool,
    q_rows,
    nk_rows,
    scales,
    attended,
    table_s,
    page_scales,
    key_scale,
    value_scale,
    mixed,
    table_sem,
):
    del after
    requests, max_pages = context.shape[0], table_v.shape[1]
    _, _, page_len, head_dim = pool.shape
    tokens = max_pages * page_len
    span = CHUNK * page_len
    factor = 1.0 / math.sqrt(head_dim)
    copy = pltpu.make_async_copy(table_v, table_s, table_sem)
    copy.start()

    scale_rows = scales[...].astype(BF16)
    for j in range(requests):
        page_scales[:, j : j + 1, :] = picked_scales(scale_rows, table_v[j : j + 1, :])[:, None, :]
    spread = spread_matrix(max_pages, tokens)
    key_scale[...] = jnp.dot(page_scales[0].astype(BF16), spread, preferred_element_type=F32) * factor
    value_scale[...] = jnp.dot(page_scales[1].astype(BF16), spread, preferred_element_type=F32)
    places = lax.broadcasted_iota(jnp.int32, (1, tokens), 1)
    copy.wait()

    def gather(j, c, which):
        return jnp.concatenate([pool[table_s[j, c * CHUNK + i], which] for i in range(CHUNK)], axis=0)

    slots = [table_s[requests, i] for i in range(requests - (replicas - 1))]
    chunks = [slice(c * span, (c + 1) * span) for c in range(max_pages // CHUNK)]

    def score(j):
        q = q_rows[pl.ds(pl.multiple_of(j * ROWS, ROWS), ROWS), :]
        token = nk_rows[pl.ds(j, 1), :]
        own = jnp.sum(q * token[:, :head_dim], axis=1, keepdims=True) * factor
        q = q.astype(BF16)
        key_row = key_scale[pl.ds(j, 1), :]
        limit = context[pl.ds(j, 1), :][:, :1]
        scores = [
            jnp.where(places[:, columns] < limit, dot_keys(q, gather(j, c, 0)) * key_row[:, columns], -jnp.inf)
            for c, columns in enumerate(chunks)
        ]
        return scores, own, token

    def finish(j, scores, own, token):
        highest = jnp.maximum(jnp.max(functools.reduce(jnp.maximum, scores), axis=1, keepdims=True), own)
        weights = [jnp.exp(part - highest) for part in scores]
        own = jnp.exp(own - highest)
        inverse = 1.0 / (jnp.sum(functools.reduce(jnp.add, weights), axis=1, keepdims=True) + own)
        value_row = value_scale[pl.ds(j, 1), :]
        total = jnp.zeros((2 * ROWS, head_dim), F32)
        for c, columns in enumerate(chunks):
            both = split_scaled(weights[c], inverse, value_row[:, columns])
            total = total + jnp.dot(both, gather(j, c, 1), preferred_element_type=F32)
        own = (own * inverse).astype(BF16).astype(F32)
        mixed[pl.ds(pl.multiple_of(j * ROWS, ROWS), ROWS), :] = (
            total[:ROWS] + total[ROWS:] + own * token[:, head_dim:]
        )

    ready = score(slots[0])
    for i, j in enumerate(slots):
        following = score(slots[i + 1]) if i + 1 < len(slots) else None
        finish(j, *ready)
        ready = following
    for h in range(per_kv):
        attended[:, h * head_dim : (h + 1) * head_dim] = mixed[pl.ds(h, requests, stride=ROWS), :]


def attend_away(replicas, per_kv, *refs):
    count = replicas - 1
    away_kv, away_info, goal_mask = refs[:3]
    came = refs[3 : 3 + count]
    outs = refs[3 + count : 3 + 2 * count]
    q_rows, scores = refs[3 + 2 * count :]
    max_pages, _, page_len, head_dim = away_kv.shape[1:]
    span = CHUNK * page_len
    for d in range(count):
        pick = goal_mask[d]
        came_all = came[d][...].astype(F32)
        q_rows[...] = jnp.zeros_like(q_rows)
        for h in range(per_kv):
            q_rows[h : h + 1, :] = jnp.sum(
                came_all[:, h * head_dim : (h + 1) * head_dim] * pick, axis=0, keepdims=True
            )
        q = q_rows[...].astype(BF16)
        for c in range(max_pages // CHUNK):
            columns = slice(c * span, (c + 1) * span)
            keys = away_kv[d, c * CHUNK : (c + 1) * CHUNK, 0].reshape(span, head_dim)
            raw = dot_keys(q, keys) * away_info[d, 0:1, columns]
            scores[:, columns] = jnp.where(away_info[d, 2:3, columns] > 0, raw, -jnp.inf)
        highest = jnp.max(scores[...], axis=1, keepdims=True)
        weights = jnp.exp(scores[...] - highest)
        total = jnp.sum(weights, axis=1, keepdims=True)
        inverse = 1.0 / total
        mixed = jnp.zeros((2 * ROWS, head_dim), F32)
        for c in range(max_pages // CHUNK):
            columns = slice(c * span, (c + 1) * span)
            values = away_kv[d, c * CHUNK : (c + 1) * CHUNK, 1].reshape(span, head_dim)
            both = split_scaled(weights[:, columns], inverse, away_info[d, 1:2, columns])
            mixed = mixed + jnp.dot(both, values, preferred_element_type=F32)
        outs[d][0] = mixed[:ROWS] + mixed[ROWS:]
        outs[d][1] = jnp.broadcast_to(highest, (ROWS, head_dim))
        outs[d][2] = jnp.broadcast_to(total, (ROWS, head_dim))


def merge(replicas, attended, here_mask, here_own, *refs):
    arrived, out = refs[: replicas - 1], refs[-1]
    head_dim = here_mask.shape[2]
    per_kv = attended.shape[1] // head_dim
    moved = []
    for d in range(replicas - 1):
        own = here_own[d, 0]
        highest = jnp.maximum(arrived[d][1], own)
        cached = arrived[d][2] * jnp.exp(arrived[d][1] - highest)
        own = jnp.exp(own - highest)
        inverse = 1.0 / (cached + own)
        own = (own * inverse).astype(BF16).astype(F32)
        moved.append(arrived[d][0] * (cached * inverse) + own * here_own[d, 1])
    for h in range(per_kv):
        columns = slice(h * head_dim, (h + 1) * head_dim)
        piece = attended[:, columns]
        for d in range(replicas - 1):
            piece = jnp.where(here_mask[d] > 0, moved[d][h : h + 1], piece)
        out[:, columns] = piece.astype(out.dtype)


def on_device(
    kv_pages, page_scale, page_table, lengths, request_moves, queries, new_kv, output_proj, residual
):
    devices = lax.axis_size("replica")
    replicas = devices // KVH
    requests, max_pages = page_table.shape
    pages, _, page_len, head_dim = kv_pages.shape
    per_kv = queries.shape[1] // head_dim
    width = output_proj.shape[1] // KVH
    tokens = max_pages * page_len
    count = replicas - 1

    def toward(value, steps):
        pairs = [(i, (i + steps * KVH) % devices) for i in range(devices)]
        return lax.ppermute(value, "replica", pairs)

    def partner(value, mask):
        return lax.ppermute(value, "replica", [(i, i ^ mask) for i in range(devices)])

    position = lax.axis_index("replica").astype(jnp.uint32)
    bits = [(position & (1 << i)) != 0 for i in range(KVH.bit_length() - 1)]
    queries, *bits = lax.optimization_barrier((queries, *bits))
    came = [toward(queries, -d) for d in range(1, replicas)]

    def shape(*dims, dtype=F32):
        return jax.ShapeDtypeStruct(dims, dtype)

    in_hbm = functools.partial(pltpu.with_memory_space_constraint, memory_space=pltpu.HBM)
    q_rows, nk_rows, scales, away_kv, away_info, goal_mask, *home = pl.pallas_call(
        functools.partial(set_up, replicas, per_kv),
        out_shape=[
            shape(requests * ROWS, head_dim),
            shape(requests, 2 * head_dim),
            shape(2, pages),
            shape(count, max_pages, 2, page_len, head_dim, dtype=BF16),
            shape(count, 8, tokens),
            shape(count, requests, head_dim),
            shape(count, requests, head_dim),
            shape(count, 2, ROWS, head_dim),
            shape(requests + 1, max_pages, dtype=jnp.int32),
            shape(requests, head_dim, dtype=jnp.int32),
        ],
        in_specs=[HBM] * 7,
        out_specs=[VMEM] * 10,
        scratch_shapes=[
            pltpu.SMEM(lengths.shape, jnp.int32),
            pltpu.SMEM(request_moves.shape, jnp.int32),
            pltpu.SMEM(page_table.shape, jnp.int32),
            pltpu.VMEM(page_table.shape, jnp.int32),
            pltpu.VMEM((2, pages), BF16),
            pltpu.VMEM(queries.shape, BF16),
            pltpu.VMEM(new_kv.shape, BF16),
            pltpu.SemaphoreType.DMA((7,)),
            pltpu.SemaphoreType.DMA((count,)),
        ],
        compiler_params=pltpu.CompilerParams(vmem_limit_bytes=4 * 2**20),
        cost_estimate=pl.CostEstimate(flops=0, bytes_accessed=4 * kv_pages.size, transcendentals=0),
        name="set_up",
    )(*(in_hbm(x) for x in (lengths, request_moves, page_table, page_scale.T, queries, new_kv, kv_pages)))

    here_mask, here_own, table_v, context = home

    rows = pl.pallas_call(
        functools.partial(attend_away, replicas, per_kv),
        out_shape=[shape(3, ROWS, head_dim)] * count,
        in_specs=[VMEM] * (3 + count),
        out_specs=[VMEM] * count,
        scratch_shapes=[pltpu.VMEM((ROWS, head_dim), F32), pltpu.VMEM((ROWS, tokens), F32)],
        compiler_params=pltpu.CompilerParams(vmem_limit_bytes=4 * 2**20),
        name="attend_away",
    )(away_kv, away_info, goal_mask, *came)
    arrived = [toward(rows[d - 1], d) for d in range(1, replicas)]

    attended = pl.pallas_call(
        functools.partial(attend_resident, replicas, per_kv),
        out_shape=shape(requests, per_kv * head_dim),
        in_specs=[HBM] + [VMEM] * 6,
        out_specs=VMEM,
        scratch_shapes=[
            pltpu.SMEM((requests + 1, max_pages), jnp.int32),
            pltpu.VMEM((2, requests, max_pages), F32),
            pltpu.VMEM((requests, tokens), F32),
            pltpu.VMEM((requests, tokens), F32),
            pltpu.VMEM((requests * ROWS, head_dim), F32),
            pltpu.SemaphoreType.DMA,
        ],
        compiler_params=pltpu.CompilerParams(vmem_limit_bytes=8 * 2**20),
        cost_estimate=pl.CostEstimate(
            flops=4 * per_kv * requests * tokens * head_dim,
            bytes_accessed=4 * output_proj.size,
            transcendentals=requests * ROWS * tokens,
        ),
        name="attend_resident",
    )(
        rows[0],
        table_v,
        context,
        pltpu.with_memory_space_constraint(kv_pages, pltpu.VMEM),
        q_rows,
        nk_rows,
        scales,
    )
    mixture = pl.pallas_call(
        functools.partial(merge, replicas),
        out_shape=shape(*attended.shape, dtype=BF16),
        in_specs=[VMEM] * (3 + count),
        out_specs=VMEM,
        compiler_params=pltpu.CompilerParams(vmem_limit_bytes=2**20),
        name="merge",
    )(attended, here_mask, here_own, *arrived)

    parts = jnp.dot(mixture, output_proj, preferred_element_type=F32)
    parts = [parts[:, i * width : (i + 1) * width] for i in range(KVH)]
    core, y, z = bits

    def split(blocks, bit, step):
        low = [b for i, b in enumerate(blocks) if not i & step]
        high = [b for i, b in enumerate(blocks) if i & step]
        same = [jnp.where(bit, b, a) for a, b in zip(low, high)]
        return same, [jnp.where(bit, a, b) for a, b in zip(low, high)]

    near, far = split(parts, core, 1)
    (near_own, near_z), (near_y, near_yz) = (split(pair, z, 1) for pair in split(near, y, 1))
    (far_own, far_z), (far_y, far_yz) = (split(pair, z, 1) for pair in split(far, y, 1))
    to_yz, to_core, at_y, at_z, own = lax.optimization_barrier(
        (
            jnp.concatenate([*near_yz, *far_yz], axis=1).astype(BF16),
            jnp.concatenate([*far_y, *far_z, *far_own], axis=1),
            near_y[0],
            near_z[0],
            near_own[0],
        )
    )
    came_yz = partner(to_yz, 6).astype(F32)
    other = partner(to_core, 1)
    came_y = partner((at_y + other[:, :width]).astype(BF16), 2)
    came_z = partner((at_z + other[:, width : 2 * width]).astype(BF16), 4)
    passed_on = partner(came_yz[:, width:], 1)
    total = own + other[:, 2 * width :] + came_yz[:, :width] + came_y.astype(F32) + came_z.astype(F32)
    total = lax.optimization_barrier(total) + passed_on
    return (residual.astype(F32) + total).astype(BF16)


def solution(mesh):
    return jax.shard_map(
        on_device,
        mesh=mesh,
        in_specs=(
            P(("parts", "replica"), None, None, None),
            P(("parts", "replica"), None),
            P(("parts", "replica"), None),
            P("parts"),
            P("parts"),
            P(("parts", "replica"), None),
            P(("parts", "replica"), None),
            P("replica", None),
            P(("parts", "replica"), None),
        ),
        out_specs=P(("parts", "replica"), None),
        check_vma=False,
    )
```

```python
import functools
import math

import jax
import jax.numpy as jnp
from jax import lax
from jax.experimental import pallas as pl
from jax.experimental.pallas import tpu as pltpu
from jax.sharding import PartitionSpec as P

KVH = 8
ROWS = 8
CHUNK = 4
F32 = jnp.float32
BF16 = jnp.bfloat16
VMEM = pl.BlockSpec(memory_space=pltpu.VMEM)
HBM = pl.BlockSpec(memory_space=pltpu.HBM)


def split_scaled(weights, inverse, value_scale):
    scaled = (weights * inverse).astype(BF16).astype(F32) * value_scale
    high = scaled.astype(BF16)
    low = (scaled - high.astype(F32)).astype(BF16)
    return jnp.concatenate([high, low], axis=0)


def dot_keys(queries, keys):
    return lax.dot_general(queries, keys, (((1,), (1,)), ((), ())), preferred_element_type=F32)


def picked_scales(scales, pages):
    ids = lax.broadcasted_iota(jnp.int32, (scales.shape[1], pages.shape[1]), 0)
    return jnp.dot(scales, (ids == pages).astype(F32).astype(BF16), preferred_element_type=F32)


def spread_matrix(max_pages, tokens):
    page_len = tokens // max_pages
    return (
        lax.broadcasted_iota(jnp.int32, (max_pages, tokens), 1) // page_len
        == lax.broadcasted_iota(jnp.int32, (max_pages, tokens), 0)
    ).astype(F32).astype(BF16)


def set_up(
    replicas,
    per_kv,
    lengths_h,
    moves_h,
    table_h,
    scale_h,
    queries_h,
    new_kv_h,
    kv_pages,
    q_rows,
    nk_rows,
    scales,
    away_kv,
    away_info,
    goal_mask,
    here_mask,
    here_own,
    table_out,
    context,
    lengths,
    moves,
    table_s,
    table_v,
    scale_v,
    queries,
    new_kv,
    small_sem,
    kv_sem,
):
    requests, max_pages = table_h.shape
    pages, _, page_len, head_dim = kv_pages.shape
    tokens = max_pages * page_len
    factor = 1.0 / math.sqrt(head_dim)
    replica = lax.axis_index("replica") // KVH

    small = [
        pltpu.make_async_copy(src, dst, small_sem.at[i])
        for i, (src, dst) in enumerate(
            [
                (moves_h, moves),
                (table_h, table_s),
                (table_h, table_v),
                (lengths_h, lengths),
                (scale_h, scale_v),
                (queries_h, queries),
                (new_kv_h, new_kv),
            ]
        )
    ]
    for copy in small:
        copy.start()
    for copy in small[:2]:
        copy.wait()

    first = replica * requests
    leaver, goal, arriver = [], [], []
    for d in range(1, replicas):
        there = jnp.where(replica + d < replicas, replica + d, replica + d - replicas) * requests
        behind = jnp.where(replica >= d, replica - d, replica - d + replicas) * requests
        out_slot = taken = here = jnp.int32(0)
        for j in range(requests):
            slot = moves[there + j] - first
            ours = (slot >= 0) & (slot < requests)
            out_slot = jnp.where(ours, slot, out_slot)
            taken = jnp.where(ours, j, taken)
            slot = moves[first + j] - behind
            here = jnp.where((slot >= 0) & (slot < requests), j, here)
        leaver.append(out_slot)
        goal.append(taken)
        arriver.append(here)

        def fetch(p, carry, d=d, out_slot=out_slot):
            pltpu.make_async_copy(
                kv_pages.at[table_s[out_slot, p]], away_kv.at[d - 1, p], kv_sem.at[d - 1]
            ).start()
            return carry

        lax.fori_loop(0, max_pages, fetch, 0, unroll=8)
    for copy in small[2:]:
        copy.wait()
    row_ids = lax.broadcasted_iota(jnp.int32, (requests, head_dim), 0)
    for d in range(1, replicas):
        goal_mask[d - 1] = (row_ids == goal[d - 1]).astype(F32)
        here_mask[d - 1] = (row_ids == arriver[d - 1]).astype(F32)

    q_all = queries[...].astype(F32)
    nk_rows[...] = new_kv[...].astype(F32)
    q_rows[...] = jnp.zeros_like(q_rows)
    for h in range(per_kv):
        q_rows[pl.ds(h, requests, stride=ROWS), :] = q_all[:, h * head_dim : (h + 1) * head_dim]

    for d in range(1, replicas):
        here = arriver[d - 1]
        own_rows = q_rows[pl.ds(pl.multiple_of(here * ROWS, ROWS), ROWS), :]
        token = nk_rows[pl.ds(here, 1), :]
        score = jnp.sum(own_rows * token[:, :head_dim], axis=1, keepdims=True) * factor
        here_own[d - 1, 0] = jnp.broadcast_to(score, (ROWS, head_dim))
        here_own[d - 1, 1] = jnp.broadcast_to(token[:, head_dim:], (ROWS, head_dim))
    lanes = lax.broadcasted_iota(jnp.int32, (1, max_pages), 1)
    staying = jnp.zeros((1, max_pages), jnp.int32)
    count = jnp.int32(0)
    for j in range(requests):
        stays = jnp.int32(1)
        for out_slot in leaver:
            stays = jnp.where(out_slot == j, 0, stays)
        staying = jnp.where((lanes == count) & (stays == 1), j, staying)
        count = count + stays
    table_out[:requests, :] = table_v[...]
    table_out[requests:, :] = staying
    for j in range(requests):
        context[j : j + 1, :] = jnp.full((1, head_dim), lengths[replica * requests + j], jnp.int32)

    scales[...] = scale_v[...].astype(F32)
    places = lax.broadcasted_iota(jnp.int32, (1, tokens), 1)
    spread = spread_matrix(max_pages, tokens)
    for d in range(1, replicas):
        out_slot = leaver[d - 1]
        picked = picked_scales(scale_v[...], table_v[pl.ds(out_slot, 1), :]).astype(BF16)
        wide = jnp.dot(picked, spread, preferred_element_type=F32)
        away_info[d - 1, 0:1, :] = wide[0:1] * factor
        away_info[d - 1, 1:2, :] = wide[1:2]
        away_info[d - 1, 2:3, :] = (places < lengths[replica * requests + out_slot]).astype(F32)

    for d in range(1, replicas):
        pltpu.make_async_copy(kv_pages.at[pl.ds(0, max_pages)], away_kv.at[d - 1], kv_sem.at[d - 1]).wait()


def attend_resident(
    replicas,
    per_kv,
    after,
    table_v,
    context,
    pool,
    q_rows,
    nk_rows,
    scales,
    attended,
    table_s,
    page_scales,
    key_scale,
    value_scale,
    scores,
    mixed,
    table_sem,
):
    del after
    requests, max_pages = context.shape[0], table_v.shape[1]
    _, _, page_len, head_dim = pool.shape
    tokens = max_pages * page_len
    span = CHUNK * page_len
    factor = 1.0 / math.sqrt(head_dim)
    copy = pltpu.make_async_copy(table_v, table_s, table_sem)
    copy.start()

    scale_rows = scales[...].astype(BF16)
    for j in range(requests):
        page_scales[:, j : j + 1, :] = picked_scales(scale_rows, table_v[j : j + 1, :])[:, None, :]
    spread = spread_matrix(max_pages, tokens)
    key_scale[...] = jnp.dot(page_scales[0].astype(BF16), spread, preferred_element_type=F32) * factor
    value_scale[...] = jnp.dot(page_scales[1].astype(BF16), spread, preferred_element_type=F32)
    places = lax.broadcasted_iota(jnp.int32, (1, tokens), 1)
    copy.wait()

    def gather(j, c, which):
        return jnp.concatenate([pool[table_s[j, c * CHUNK + i], which] for i in range(CHUNK)], axis=0)

    slots = [table_s[requests, i] for i in range(requests - (replicas - 1))]
    chunks = [slice(c * span, (c + 1) * span) for c in range(max_pages // CHUNK)]
    picked = [pl.ds(pl.multiple_of(j * ROWS, ROWS), ROWS) for j in slots]
    queries = [q_rows[rows, :] for rows in picked]
    tokens_new = [nk_rows[pl.ds(j, 1), :] for j in slots]

    def per_head(rows):
        return jnp.concatenate([jnp.broadcast_to(row, (ROWS, row.shape[1])) for row in rows], axis=0)

    limits = per_head([context[pl.ds(j, 1), :] for j in slots])[:, :1]
    key_rows = [key_scale[pl.ds(j, 1), :] for j in slots]
    highest = None
    for c, columns in enumerate(chunks):
        raw = [dot_keys(q.astype(BF16), gather(j, c, 0)) for q, j in zip(queries, slots)]
        part = jnp.concatenate(raw, axis=0) * per_head([row[:, columns] for row in key_rows])
        part = jnp.where(places[:, columns] < limits, part, -jnp.inf)
        scores[:, columns] = part
        highest = part if highest is None else jnp.maximum(highest, part)
    all_queries = jnp.concatenate(queries, axis=0)
    own = jnp.sum(all_queries * per_head([row[:, :head_dim] for row in tokens_new]), axis=1, keepdims=True) * factor
    highest = jnp.maximum(jnp.max(highest, axis=1, keepdims=True), own)
    total = None
    for columns in chunks:
        part = jnp.exp(scores[:, columns] - highest)
        scores[:, columns] = part
        total = part if total is None else total + part
    own = jnp.exp(own - highest)
    inverse = 1.0 / (jnp.sum(total, axis=1, keepdims=True) + own)
    value_rows = [value_scale[pl.ds(j, 1), :] for j in slots]
    sums = [jnp.zeros((2 * ROWS, head_dim), F32) for _ in slots]
    for c, columns in enumerate(chunks):
        scaled = (scores[:, columns] * inverse).astype(BF16).astype(F32) * per_head([row[:, columns] for row in value_rows])
        high = scaled.astype(BF16)
        low = scaled - high.astype(F32)
        for i, j in enumerate(slots):
            rows = slice(i * ROWS, (i + 1) * ROWS)
            both = jnp.concatenate([scaled[rows].astype(BF16), low[rows].astype(BF16)], axis=0)
            sums[i] = sums[i] + jnp.dot(both, gather(j, c, 1), preferred_element_type=F32)
    own = (own * inverse).astype(BF16).astype(F32)
    for i in range(len(slots)):
        rows = slice(i * ROWS, (i + 1) * ROWS)
        mixed[picked[i], :] = sums[i][:ROWS] + sums[i][ROWS:] + own[rows] * tokens_new[i][:, head_dim:]
    for h in range(per_kv):
        attended[:, h * head_dim : (h + 1) * head_dim] = mixed[pl.ds(h, requests, stride=ROWS), :]


def attend_away(replicas, per_kv, *refs):
    count = replicas - 1
    away_kv, away_info, goal_mask = refs[:3]
    came = refs[3 : 3 + count]
    outs = refs[3 + count : 3 + 2 * count]
    q_rows, scores = refs[3 + 2 * count :]
    max_pages, _, page_len, head_dim = away_kv.shape[1:]
    span = CHUNK * page_len
    for d in range(count):
        pick = goal_mask[d]
        came_all = came[d][...].astype(F32)
        q_rows[...] = jnp.zeros_like(q_rows)
        for h in range(per_kv):
            q_rows[h : h + 1, :] = jnp.sum(
                came_all[:, h * head_dim : (h + 1) * head_dim] * pick, axis=0, keepdims=True
            )
        q = q_rows[...].astype(BF16)
        for c in range(max_pages // CHUNK):
            columns = slice(c * span, (c + 1) * span)
            keys = away_kv[d, c * CHUNK : (c + 1) * CHUNK, 0].reshape(span, head_dim)
            raw = dot_keys(q, keys) * away_info[d, 0:1, columns]
            scores[:, columns] = jnp.where(away_info[d, 2:3, columns] > 0, raw, -jnp.inf)
        highest = jnp.max(scores[...], axis=1, keepdims=True)
        weights = jnp.exp(scores[...] - highest)
        total = jnp.sum(weights, axis=1, keepdims=True)
        inverse = 1.0 / total
        mixed = jnp.zeros((2 * ROWS, head_dim), F32)
        for c in range(max_pages // CHUNK):
            columns = slice(c * span, (c + 1) * span)
            values = away_kv[d, c * CHUNK : (c + 1) * CHUNK, 1].reshape(span, head_dim)
            both = split_scaled(weights[:, columns], inverse, away_info[d, 1:2, columns])
            mixed = mixed + jnp.dot(both, values, preferred_element_type=F32)
        outs[d][0] = mixed[:ROWS] + mixed[ROWS:]
        outs[d][1] = jnp.broadcast_to(highest, (ROWS, head_dim))
        outs[d][2] = jnp.broadcast_to(total, (ROWS, head_dim))


def merge(replicas, attended, here_mask, here_own, *refs):
    arrived, out = refs[: replicas - 1], refs[-1]
    head_dim = here_mask.shape[2]
    per_kv = attended.shape[1] // head_dim
    moved = []
    for d in range(replicas - 1):
        own = here_own[d, 0]
        highest = jnp.maximum(arrived[d][1], own)
        cached = arrived[d][2] * jnp.exp(arrived[d][1] - highest)
        own = jnp.exp(own - highest)
        inverse = 1.0 / (cached + own)
        own = (own * inverse).astype(BF16).astype(F32)
        moved.append(arrived[d][0] * (cached * inverse) + own * here_own[d, 1])
    for h in range(per_kv):
        columns = slice(h * head_dim, (h + 1) * head_dim)
        piece = attended[:, columns]
        for d in range(replicas - 1):
            piece = jnp.where(here_mask[d] > 0, moved[d][h : h + 1], piece)
        out[:, columns] = piece.astype(out.dtype)


def on_device(
    kv_pages, page_scale, page_table, lengths, request_moves, queries, new_kv, output_proj, residual
):
    devices = lax.axis_size("replica")
    replicas = devices // KVH
    requests, max_pages = page_table.shape
    pages, _, page_len, head_dim = kv_pages.shape
    per_kv = queries.shape[1] // head_dim
    width = output_proj.shape[1] // KVH
    tokens = max_pages * page_len
    count = replicas - 1

    def toward(value, steps):
        pairs = [(i, (i + steps * KVH) % devices) for i in range(devices)]
        return lax.ppermute(value, "replica", pairs)

    def partner(value, mask):
        return lax.ppermute(value, "replica", [(i, i ^ mask) for i in range(devices)])

    position = lax.axis_index("replica").astype(jnp.uint32)
    bits = [(position & (1 << i)) != 0 for i in range(KVH.bit_length() - 1)]
    queries, *bits = lax.optimization_barrier((queries, *bits))
    came = [toward(queries, -d) for d in range(1, replicas)]

    def shape(*dims, dtype=F32):
        return jax.ShapeDtypeStruct(dims, dtype)

    in_hbm = functools.partial(pltpu.with_memory_space_constraint, memory_space=pltpu.HBM)
    q_rows, nk_rows, scales, away_kv, away_info, goal_mask, *home = pl.pallas_call(
        functools.partial(set_up, replicas, per_kv),
        out_shape=[
            shape(requests * ROWS, head_dim),
            shape(requests, 2 * head_dim),
            shape(2, pages),
            shape(count, max_pages, 2, page_len, head_dim, dtype=BF16),
            shape(count, 8, tokens),
            shape(count, requests, head_dim),
            shape(count, requests, head_dim),
            shape(count, 2, ROWS, head_dim),
            shape(requests + 1, max_pages, dtype=jnp.int32),
            shape(requests, head_dim, dtype=jnp.int32),
        ],
        in_specs=[HBM] * 7,
        out_specs=[VMEM] * 10,
        scratch_shapes=[
            pltpu.SMEM(lengths.shape, jnp.int32),
            pltpu.SMEM(request_moves.shape, jnp.int32),
            pltpu.SMEM(page_table.shape, jnp.int32),
            pltpu.VMEM(page_table.shape, jnp.int32),
            pltpu.VMEM((2, pages), BF16),
            pltpu.VMEM(queries.shape, BF16),
            pltpu.VMEM(new_kv.shape, BF16),
            pltpu.SemaphoreType.DMA((7,)),
            pltpu.SemaphoreType.DMA((count,)),
        ],
        compiler_params=pltpu.CompilerParams(vmem_limit_bytes=4 * 2**20),
        cost_estimate=pl.CostEstimate(flops=0, bytes_accessed=4 * kv_pages.size, transcendentals=0),
        name="set_up",
    )(*(in_hbm(x) for x in (lengths, request_moves, page_table, page_scale.T, queries, new_kv, kv_pages)))

    here_mask, here_own, table_v, context = home

    rows = pl.pallas_call(
        functools.partial(attend_away, replicas, per_kv),
        out_shape=[shape(3, ROWS, head_dim)] * count,
        in_specs=[VMEM] * (3 + count),
        out_specs=[VMEM] * count,
        scratch_shapes=[pltpu.VMEM((ROWS, head_dim), F32), pltpu.VMEM((ROWS, tokens), F32)],
        compiler_params=pltpu.CompilerParams(vmem_limit_bytes=4 * 2**20),
        name="attend_away",
    )(away_kv, away_info, goal_mask, *came)
    arrived = [toward(rows[d - 1], d) for d in range(1, replicas)]

    attended = pl.pallas_call(
        functools.partial(attend_resident, replicas, per_kv),
        out_shape=shape(requests, per_kv * head_dim),
        in_specs=[HBM] + [VMEM] * 6,
        out_specs=VMEM,
        scratch_shapes=[
            pltpu.SMEM((requests + 1, max_pages), jnp.int32),
            pltpu.VMEM((2, requests, max_pages), F32),
            pltpu.VMEM((requests, tokens), F32),
            pltpu.VMEM((requests, tokens), F32),
            pltpu.VMEM(((requests - count) * ROWS, tokens), F32),
            pltpu.VMEM((requests * ROWS, head_dim), F32),
            pltpu.SemaphoreType.DMA,
        ],
        compiler_params=pltpu.CompilerParams(vmem_limit_bytes=8 * 2**20),
        cost_estimate=pl.CostEstimate(
            flops=4 * per_kv * requests * tokens * head_dim,
            bytes_accessed=4 * output_proj.size,
            transcendentals=requests * ROWS * tokens,
        ),
        name="attend_resident",
    )(
        rows[0],
        table_v,
        context,
        pltpu.with_memory_space_constraint(kv_pages, pltpu.VMEM),
        q_rows,
        nk_rows,
        scales,
    )
    mixture = pl.pallas_call(
        functools.partial(merge, replicas),
        out_shape=shape(*attended.shape, dtype=BF16),
        in_specs=[VMEM] * (3 + count),
        out_specs=VMEM,
        compiler_params=pltpu.CompilerParams(vmem_limit_bytes=2**20),
        name="merge",
    )(attended, here_mask, here_own, *arrived)

    parts = jnp.dot(mixture, output_proj, preferred_element_type=F32)
    parts = [parts[:, i * width : (i + 1) * width] for i in range(KVH)]
    core, y, z = bits

    def split(blocks, bit, step):
        low = [b for i, b in enumerate(blocks) if not i & step]
        high = [b for i, b in enumerate(blocks) if i & step]
        same = [jnp.where(bit, b, a) for a, b in zip(low, high)]
        return same, [jnp.where(bit, a, b) for a, b in zip(low, high)]

    near, far = split(parts, core, 1)
    (near_own, near_z), (near_y, near_yz) = (split(pair, z, 1) for pair in split(near, y, 1))
    (far_own, far_z), (far_y, far_yz) = (split(pair, z, 1) for pair in split(far, y, 1))
    to_yz, to_core, at_y, at_z, own = lax.optimization_barrier(
        (
            jnp.concatenate([*near_yz, *far_yz], axis=1).astype(BF16),
            jnp.concatenate([*far_y, *far_z, *far_own], axis=1),
            near_y[0],
            near_z[0],
            near_own[0],
        )
    )
    came_yz = partner(to_yz, 6).astype(F32)
    other = partner(to_core, 1)
    came_y = partner((at_y + other[:, :width]).astype(BF16), 2)
    came_z = partner((at_z + other[:, width : 2 * width]).astype(BF16), 4)
    passed_on = partner(came_yz[:, width:], 1)
    total = own + other[:, 2 * width :] + came_yz[:, :width] + came_y.astype(F32) + came_z.astype(F32)
    total = lax.optimization_barrier(total) + passed_on
    return (residual.astype(F32) + total).astype(BF16)


def solution(mesh):
    return jax.shard_map(
        on_device,
        mesh=mesh,
        in_specs=(
            P(("parts", "replica"), None, None, None),
            P(("parts", "replica"), None),
            P(("parts", "replica"), None),
            P("parts"),
            P("parts"),
            P(("parts", "replica"), None),
            P(("parts", "replica"), None),
            P("replica", None),
            P(("parts", "replica"), None),
        ),
        out_specs=P(("parts", "replica"), None),
        check_vma=False,
    )
```

```python
import functools
import math

import jax
import jax.numpy as jnp
from jax import lax
from jax.experimental import pallas as pl
from jax.experimental.pallas import tpu as pltpu
from jax.sharding import PartitionSpec as P

KVH = 8
ROWS = 8
CHUNK = 4
F32 = jnp.float32
BF16 = jnp.bfloat16
VMEM = pl.BlockSpec(memory_space=pltpu.VMEM)
HBM = pl.BlockSpec(memory_space=pltpu.HBM)


def softmax_parts(scores, own):
    highest = jnp.maximum(jnp.max(scores, axis=1, keepdims=True), own)
    weights = jnp.exp(scores - highest)
    own_weight = jnp.exp(own - highest)
    return weights, own_weight, 1.0 / (jnp.sum(weights, axis=1, keepdims=True) + own_weight)


def split_scaled(weights, inverse, value_scale):
    scaled = (weights * inverse).astype(BF16).astype(F32) * value_scale
    high = scaled.astype(BF16)
    low = (scaled - high.astype(F32)).astype(BF16)
    return jnp.concatenate([high, low], axis=0)


def doubled(queries):
    none = jnp.zeros_like(queries)
    left = jnp.concatenate([queries, none], axis=1)
    right = jnp.concatenate([none, queries], axis=1)
    return jnp.concatenate([left, right], axis=0).astype(BF16)


def dot_keys(queries, one, two):
    keys = jnp.concatenate([one, two], axis=1)
    scores = lax.dot_general(queries, keys, (((1,), (1,)), ((), ())), preferred_element_type=F32)
    return scores[:ROWS], scores[ROWS:]


def dot_values(weights_one, weights_two, one, two):
    weights = jnp.concatenate([weights_one, weights_two], axis=0)
    product = jnp.dot(weights, jnp.concatenate([one, two], axis=1), preferred_element_type=F32)
    rows, columns = weights_one.shape[0], one.shape[1]
    return product[:rows, :columns] + product[rows:, columns:]


def picked_scales(scales, pages):
    ids = lax.broadcasted_iota(jnp.int32, (scales.shape[1], pages.shape[1]), 0)
    return jnp.dot(scales, (ids == pages).astype(F32).astype(BF16), preferred_element_type=F32)


def spread_matrix(max_pages, tokens):
    page_len = tokens // max_pages
    return (
        lax.broadcasted_iota(jnp.int32, (max_pages, tokens), 1) // page_len
        == lax.broadcasted_iota(jnp.int32, (max_pages, tokens), 0)
    ).astype(F32).astype(BF16)


def set_up(
    replicas,
    per_kv,
    lengths_h,
    moves_h,
    table_h,
    scale_h,
    queries_h,
    new_kv_h,
    kv_pages,
    q_rows,
    nk_rows,
    scales,
    away_kv,
    away_info,
    goal_mask,
    here_mask,
    here_own,
    table_out,
    context,
    lengths,
    moves,
    table_s,
    table_v,
    scale_v,
    queries,
    new_kv,
    small_sem,
    kv_sem,
):
    requests, max_pages = table_h.shape
    pages, _, page_len, head_dim = kv_pages.shape
    tokens = max_pages * page_len
    factor = 1.0 / math.sqrt(head_dim)
    replica = lax.axis_index("replica") // KVH

    small = [
        pltpu.make_async_copy(src, dst, small_sem.at[i])
        for i, (src, dst) in enumerate(
            [
                (moves_h, moves),
                (table_h, table_s),
                (table_h, table_v),
                (lengths_h, lengths),
                (scale_h, scale_v),
                (queries_h, queries),
                (new_kv_h, new_kv),
            ]
        )
    ]
    for copy in small:
        copy.start()
    for copy in small[:2]:
        copy.wait()

    first = replica * requests
    leaver, goal, arriver = [], [], []
    for d in range(1, replicas):
        there = jnp.where(replica + d < replicas, replica + d, replica + d - replicas) * requests
        behind = jnp.where(replica >= d, replica - d, replica - d + replicas) * requests
        out_slot = taken = here = jnp.int32(0)
        for j in range(requests):
            slot = moves[there + j] - first
            ours = (slot >= 0) & (slot < requests)
            out_slot = jnp.where(ours, slot, out_slot)
            taken = jnp.where(ours, j, taken)
            slot = moves[first + j] - behind
            here = jnp.where((slot >= 0) & (slot < requests), j, here)
        leaver.append(out_slot)
        goal.append(taken)
        arriver.append(here)

        def fetch(p, carry, d=d, out_slot=out_slot):
            pltpu.make_async_copy(
                kv_pages.at[table_s[out_slot, p]], away_kv.at[d - 1, p], kv_sem.at[d - 1]
            ).start()
            return carry

        lax.fori_loop(0, max_pages, fetch, 0, unroll=8)
    for copy in small[2:]:
        copy.wait()
    row_ids = lax.broadcasted_iota(jnp.int32, (requests, head_dim), 0)
    for d in range(1, replicas):
        goal_mask[d - 1] = (row_ids == goal[d - 1]).astype(F32)
        here_mask[d - 1] = (row_ids == arriver[d - 1]).astype(F32)

    q_all = queries[...].astype(F32)
    nk_rows[...] = new_kv[...].astype(F32)
    q_rows[...] = jnp.zeros_like(q_rows)
    for h in range(per_kv):
        q_rows[pl.ds(h, requests, stride=ROWS), :] = q_all[:, h * head_dim : (h + 1) * head_dim]

    for d in range(1, replicas):
        here = arriver[d - 1]
        own_rows = q_rows[pl.ds(pl.multiple_of(here * ROWS, ROWS), ROWS), :]
        token = nk_rows[pl.ds(here, 1), :]
        score = jnp.sum(own_rows * token[:, :head_dim], axis=1, keepdims=True) * factor
        here_own[d - 1, 0] = jnp.broadcast_to(score, (ROWS, head_dim))
        here_own[d - 1, 1] = jnp.broadcast_to(token[:, head_dim:], (ROWS, head_dim))
    lanes = lax.broadcasted_iota(jnp.int32, (1, max_pages), 1)
    staying = jnp.zeros((1, max_pages), jnp.int32)
    count = jnp.int32(0)
    for j in range(requests):
        stays = jnp.int32(1)
        for out_slot in leaver:
            stays = jnp.where(out_slot == j, 0, stays)
        staying = jnp.where((lanes == count) & (stays == 1), j, staying)
        count = count + stays
    table_out[:requests, :] = table_v[...]
    table_out[requests:, :] = staying
    for j in range(requests):
        context[j : j + 1, :] = jnp.full((1, head_dim), lengths[replica * requests + j], jnp.int32)

    scales[...] = scale_v[...].astype(F32)
    places = lax.broadcasted_iota(jnp.int32, (1, tokens), 1)
    spread = spread_matrix(max_pages, tokens)
    for d in range(1, replicas):
        out_slot = leaver[d - 1]
        picked = picked_scales(scale_v[...], table_v[pl.ds(out_slot, 1), :]).astype(BF16)
        wide = jnp.dot(picked, spread, preferred_element_type=F32)
        away_info[d - 1, 0:1, :] = wide[0:1] * factor
        away_info[d - 1, 1:2, :] = wide[1:2]
        away_info[d - 1, 2:3, :] = (places < lengths[replica * requests + out_slot]).astype(F32)

    for d in range(1, replicas):
        pltpu.make_async_copy(kv_pages.at[pl.ds(0, max_pages)], away_kv.at[d - 1], kv_sem.at[d - 1]).wait()


def attend_resident(
    replicas,
    per_kv,
    after,
    table_v,
    context,
    pool,
    q_rows,
    nk_rows,
    scales,
    attended,
    table_s,
    page_scales,
    key_scale,
    value_scale,
    scores,
    mixed,
    table_sem,
):
    del after
    requests, max_pages = context.shape[0], table_v.shape[1]
    _, _, page_len, head_dim = pool.shape
    tokens = max_pages * page_len
    span = CHUNK * page_len
    factor = 1.0 / math.sqrt(head_dim)
    copy = pltpu.make_async_copy(table_v, table_s, table_sem)
    copy.start()

    scale_rows = scales[...].astype(BF16)
    for j in range(requests):
        page_scales[:, j : j + 1, :] = picked_scales(scale_rows, table_v[j : j + 1, :])[:, None, :]
    spread = spread_matrix(max_pages, tokens)
    key_scale[...] = jnp.dot(page_scales[0].astype(BF16), spread, preferred_element_type=F32) * factor
    value_scale[...] = jnp.dot(page_scales[1].astype(BF16), spread, preferred_element_type=F32)
    places = lax.broadcasted_iota(jnp.int32, (1, tokens), 1)
    copy.wait()

    def gather(j, c, which):
        return jnp.concatenate([pool[table_s[j, c * CHUNK + i], which] for i in range(CHUNK)], axis=0)

    slots = [table_s[requests, i] for i in range(requests - (replicas - 1))]
    own, tokens_new = [], []
    for i, j in enumerate(slots):
        rows = slice(i * ROWS, (i + 1) * ROWS)
        q = q_rows[pl.ds(pl.multiple_of(j * ROWS, ROWS), ROWS), :]
        tokens_new.append(nk_rows[pl.ds(j, 1), :])
        own.append(jnp.sum(q * tokens_new[i][:, :head_dim], axis=1, keepdims=True) * factor)
        q = doubled(q)
        key_row = key_scale[pl.ds(j, 1), :]
        limit = context[pl.ds(j, 1), :][:, :1]
        for c in range(0, max_pages // CHUNK, 2):
            for raw, k in zip(dot_keys(q, gather(j, c, 0), gather(j, c + 1, 0)), (c, c + 1)):
                columns = slice(k * span, (k + 1) * span)
                scores[rows, columns] = jnp.where(places[:, columns] < limit, raw * key_row[:, columns], -jnp.inf)
    stats = []
    for i in range(len(slots)):
        rows = slice(i * ROWS, (i + 1) * ROWS)
        weights, own_weight, inverse = softmax_parts(scores[rows, :], own[i])
        scores[rows, :] = weights
        stats.append((own_weight, inverse))
    for i, j in enumerate(slots):
        rows = slice(i * ROWS, (i + 1) * ROWS)
        own_weight, inverse = stats[i]
        value_row = value_scale[pl.ds(j, 1), :]
        total = jnp.zeros((2 * ROWS, head_dim), F32)
        for c in range(0, max_pages // CHUNK, 2):
            both = []
            for k in (c, c + 1):
                columns = slice(k * span, (k + 1) * span)
                both.append(split_scaled(scores[rows, columns], inverse, value_row[:, columns]))
            total = total + dot_values(*both, gather(j, c, 1), gather(j, c + 1, 1))
        own_weight = (own_weight * inverse).astype(BF16).astype(F32)
        mixed[pl.ds(pl.multiple_of(j * ROWS, ROWS), ROWS), :] = (
            total[:ROWS] + total[ROWS:] + own_weight * tokens_new[i][:, head_dim:]
        )
    for h in range(per_kv):
        attended[:, h * head_dim : (h + 1) * head_dim] = mixed[pl.ds(h, requests, stride=ROWS), :]


def attend_away(replicas, per_kv, *refs):
    count = replicas - 1
    away_kv, away_info, goal_mask = refs[:3]
    came = refs[3 : 3 + count]
    outs = refs[3 + count : 3 + 2 * count]
    q_rows, scores = refs[3 + 2 * count :]
    max_pages, _, page_len, head_dim = away_kv.shape[1:]
    span = CHUNK * page_len
    for d in range(count):
        pick = goal_mask[d]
        came_all = came[d][...].astype(F32)
        q_rows[...] = jnp.zeros_like(q_rows)
        for h in range(per_kv):
            q_rows[h : h + 1, :] = jnp.sum(
                came_all[:, h * head_dim : (h + 1) * head_dim] * pick, axis=0, keepdims=True
            )
        q = doubled(q_rows[...])

        def chunk(c, which, d=d):
            return away_kv[d, c * CHUNK : (c + 1) * CHUNK, which].reshape(span, head_dim)

        for c in range(0, max_pages // CHUNK, 2):
            for raw, k in zip(dot_keys(q, chunk(c, 0), chunk(c + 1, 0)), (c, c + 1)):
                columns = slice(k * span, (k + 1) * span)
                raw = raw * away_info[d, 0:1, columns]
                scores[:, columns] = jnp.where(away_info[d, 2:3, columns] > 0, raw, -jnp.inf)
        highest = jnp.max(scores[...], axis=1, keepdims=True)
        weights = jnp.exp(scores[...] - highest)
        total = jnp.sum(weights, axis=1, keepdims=True)
        inverse = 1.0 / total
        mixed = jnp.zeros((2 * ROWS, head_dim), F32)
        for c in range(0, max_pages // CHUNK, 2):
            both = []
            for k in (c, c + 1):
                columns = slice(k * span, (k + 1) * span)
                both.append(split_scaled(weights[:, columns], inverse, away_info[d, 1:2, columns]))
            mixed = mixed + dot_values(*both, chunk(c, 1), chunk(c + 1, 1))
        outs[d][0] = mixed[:ROWS] + mixed[ROWS:]
        outs[d][1] = jnp.broadcast_to(highest, (ROWS, head_dim))
        outs[d][2] = jnp.broadcast_to(total, (ROWS, head_dim))


def merge(replicas, attended, here_mask, here_own, *refs):
    arrived, out = refs[: replicas - 1], refs[-1]
    head_dim = here_mask.shape[2]
    per_kv = attended.shape[1] // head_dim
    moved = []
    for d in range(replicas - 1):
        own = here_own[d, 0]
        highest = jnp.maximum(arrived[d][1], own)
        cached = arrived[d][2] * jnp.exp(arrived[d][1] - highest)
        own = jnp.exp(own - highest)
        inverse = 1.0 / (cached + own)
        own = (own * inverse).astype(BF16).astype(F32)
        moved.append(arrived[d][0] * (cached * inverse) + own * here_own[d, 1])
    for h in range(per_kv):
        columns = slice(h * head_dim, (h + 1) * head_dim)
        piece = attended[:, columns]
        for d in range(replicas - 1):
            piece = jnp.where(here_mask[d] > 0, moved[d][h : h + 1], piece)
        out[:, columns] = piece.astype(out.dtype)


def on_device(
    kv_pages, page_scale, page_table, lengths, request_moves, queries, new_kv, output_proj, residual
):
    devices = lax.axis_size("replica")
    replicas = devices // KVH
    requests, max_pages = page_table.shape
    pages, _, page_len, head_dim = kv_pages.shape
    per_kv = queries.shape[1] // head_dim
    width = output_proj.shape[1] // KVH
    tokens = max_pages * page_len
    count = replicas - 1

    def toward(value, steps):
        pairs = [(i, (i + steps * KVH) % devices) for i in range(devices)]
        return lax.ppermute(value, "replica", pairs)

    def partner(value, mask):
        return lax.ppermute(value, "replica", [(i, i ^ mask) for i in range(devices)])

    position = lax.axis_index("replica").astype(jnp.uint32)
    bits = [(position & (1 << i)) != 0 for i in range(KVH.bit_length() - 1)]
    queries, *bits = lax.optimization_barrier((queries, *bits))
    came = [toward(queries, -d) for d in range(1, replicas)]

    def shape(*dims, dtype=F32):
        return jax.ShapeDtypeStruct(dims, dtype)

    in_hbm = functools.partial(pltpu.with_memory_space_constraint, memory_space=pltpu.HBM)
    q_rows, nk_rows, scales, away_kv, away_info, goal_mask, *home = pl.pallas_call(
        functools.partial(set_up, replicas, per_kv),
        out_shape=[
            shape(requests * ROWS, head_dim),
            shape(requests, 2 * head_dim),
            shape(2, pages),
            shape(count, max_pages, 2, page_len, head_dim, dtype=BF16),
            shape(count, 8, tokens),
            shape(count, requests, head_dim),
            shape(count, requests, head_dim),
            shape(count, 2, ROWS, head_dim),
            shape(requests + 1, max_pages, dtype=jnp.int32),
            shape(requests, head_dim, dtype=jnp.int32),
        ],
        in_specs=[HBM] * 7,
        out_specs=[VMEM] * 10,
        scratch_shapes=[
            pltpu.SMEM(lengths.shape, jnp.int32),
            pltpu.SMEM(request_moves.shape, jnp.int32),
            pltpu.SMEM(page_table.shape, jnp.int32),
            pltpu.VMEM(page_table.shape, jnp.int32),
            pltpu.VMEM((2, pages), BF16),
            pltpu.VMEM(queries.shape, BF16),
            pltpu.VMEM(new_kv.shape, BF16),
            pltpu.SemaphoreType.DMA((7,)),
            pltpu.SemaphoreType.DMA((count,)),
        ],
        compiler_params=pltpu.CompilerParams(vmem_limit_bytes=4 * 2**20),
        cost_estimate=pl.CostEstimate(flops=0, bytes_accessed=4 * kv_pages.size, transcendentals=0),
        name="set_up",
    )(*(in_hbm(x) for x in (lengths, request_moves, page_table, page_scale.T, queries, new_kv, kv_pages)))

    here_mask, here_own, table_v, context = home

    rows = pl.pallas_call(
        functools.partial(attend_away, replicas, per_kv),
        out_shape=[shape(3, ROWS, head_dim)] * count,
        in_specs=[VMEM] * (3 + count),
        out_specs=[VMEM] * count,
        scratch_shapes=[pltpu.VMEM((ROWS, head_dim), F32), pltpu.VMEM((ROWS, tokens), F32)],
        compiler_params=pltpu.CompilerParams(vmem_limit_bytes=4 * 2**20),
        name="attend_away",
    )(away_kv, away_info, goal_mask, *came)
    arrived = [toward(rows[d - 1], d) for d in range(1, replicas)]

    attended = pl.pallas_call(
        functools.partial(attend_resident, replicas, per_kv),
        out_shape=shape(requests, per_kv * head_dim),
        in_specs=[HBM] + [VMEM] * 6,
        out_specs=VMEM,
        scratch_shapes=[
            pltpu.SMEM((requests + 1, max_pages), jnp.int32),
            pltpu.VMEM((2, requests, max_pages), F32),
            pltpu.VMEM((requests, tokens), F32),
            pltpu.VMEM((requests, tokens), F32),
            pltpu.VMEM((requests * ROWS, tokens), F32),
            pltpu.VMEM((requests * ROWS, head_dim), F32),
            pltpu.SemaphoreType.DMA,
        ],
        compiler_params=pltpu.CompilerParams(vmem_limit_bytes=8 * 2**20),
        cost_estimate=pl.CostEstimate(
            flops=4 * per_kv * requests * tokens * head_dim,
            bytes_accessed=4 * output_proj.size,
            transcendentals=requests * ROWS * tokens,
        ),
        name="attend_resident",
    )(
        rows[0],
        table_v,
        context,
        pltpu.with_memory_space_constraint(kv_pages, pltpu.VMEM),
        q_rows,
        nk_rows,
        scales,
    )
    mixture = pl.pallas_call(
        functools.partial(merge, replicas),
        out_shape=shape(*attended.shape, dtype=BF16),
        in_specs=[VMEM] * (3 + count),
        out_specs=VMEM,
        compiler_params=pltpu.CompilerParams(vmem_limit_bytes=2**20),
        name="merge",
    )(attended, here_mask, here_own, *arrived)

    parts = jnp.dot(mixture, output_proj, preferred_element_type=F32)
    parts = [parts[:, i * width : (i + 1) * width] for i in range(KVH)]
    core, y, z = bits

    def split(blocks, bit, step):
        low = [b for i, b in enumerate(blocks) if not i & step]
        high = [b for i, b in enumerate(blocks) if i & step]
        same = [jnp.where(bit, b, a) for a, b in zip(low, high)]
        return same, [jnp.where(bit, a, b) for a, b in zip(low, high)]

    near, far = split(parts, core, 1)
    (near_own, near_z), (near_y, near_yz) = (split(pair, z, 1) for pair in split(near, y, 1))
    (far_own, far_z), (far_y, far_yz) = (split(pair, z, 1) for pair in split(far, y, 1))
    to_yz, to_core, at_y, at_z, own = lax.optimization_barrier(
        (
            jnp.concatenate([*near_yz, *far_yz], axis=1).astype(BF16),
            jnp.concatenate([*far_y, *far_z, *far_own], axis=1),
            near_y[0],
            near_z[0],
            near_own[0],
        )
    )
    came_yz = partner(to_yz, 6).astype(F32)
    other = partner(to_core, 1)
    came_y = partner((at_y + other[:, :width]).astype(BF16), 2)
    came_z = partner((at_z + other[:, width : 2 * width]).astype(BF16), 4)
    passed_on = partner(came_yz[:, width:], 1)
    total = own + other[:, 2 * width :] + came_yz[:, :width] + came_y.astype(F32) + came_z.astype(F32)
    total = lax.optimization_barrier(total) + passed_on
    return (residual.astype(F32) + total).astype(BF16)


def solution(mesh):
    return jax.shard_map(
        on_device,
        mesh=mesh,
        in_specs=(
            P(("parts", "replica"), None, None, None),
            P(("parts", "replica"), None),
            P(("parts", "replica"), None),
            P("parts"),
            P("parts"),
            P(("parts", "replica"), None),
            P(("parts", "replica"), None),
            P("replica", None),
            P(("parts", "replica"), None),
        ),
        out_specs=P(("parts", "replica"), None),
        check_vma=False,
    )
```

```python
import functools
import math

import jax
import jax.numpy as jnp
from jax import lax
from jax.experimental import pallas as pl
from jax.experimental.pallas import tpu as pltpu
from jax.sharding import PartitionSpec as P

KVH = 8
ROWS = 8
CHUNK = 4
F32 = jnp.float32
BF16 = jnp.bfloat16
VMEM = pl.BlockSpec(memory_space=pltpu.VMEM)
HBM = pl.BlockSpec(memory_space=pltpu.HBM)


def softmax_parts(scores, own):
    highest = jnp.maximum(jnp.max(scores, axis=1, keepdims=True), own)
    weights = jnp.exp(scores - highest)
    own_weight = jnp.exp(own - highest)
    return weights, own_weight, 1.0 / (jnp.sum(weights, axis=1, keepdims=True) + own_weight)


def split_scaled(weights, inverse, value_scale):
    scaled = (weights * inverse).astype(BF16).astype(F32) * value_scale
    high = scaled.astype(BF16)
    low = (scaled - high.astype(F32)).astype(BF16)
    return jnp.concatenate([high, low], axis=0)


def dot_keys(queries, keys):
    return lax.dot_general(queries, keys, (((1,), (1,)), ((), ())), preferred_element_type=F32)


def picked_scales(scales, pages):
    ids = lax.broadcasted_iota(jnp.int32, (scales.shape[1], pages.shape[1]), 0)
    return jnp.dot(scales, (ids == pages).astype(F32).astype(BF16), preferred_element_type=F32)


def spread_matrix(max_pages, tokens):
    page_len = tokens // max_pages
    return (
        lax.broadcasted_iota(jnp.int32, (max_pages, tokens), 1) // page_len
        == lax.broadcasted_iota(jnp.int32, (max_pages, tokens), 0)
    ).astype(F32).astype(BF16)


def set_up(
    replicas,
    per_kv,
    lengths_h,
    moves_h,
    table_h,
    scale_h,
    queries_h,
    new_kv_h,
    kv_pages,
    q_rows,
    nk_rows,
    scales,
    away_kv,
    away_info,
    goal_mask,
    here_mask,
    here_own,
    table_out,
    context,
    lengths,
    moves,
    table_s,
    table_v,
    scale_v,
    queries,
    new_kv,
    small_sem,
    kv_sem,
):
    requests, max_pages = table_h.shape
    pages, _, page_len, head_dim = kv_pages.shape
    tokens = max_pages * page_len
    factor = 1.0 / math.sqrt(head_dim)
    replica = lax.axis_index("replica") // KVH

    small = [
        pltpu.make_async_copy(src, dst, small_sem.at[i])
        for i, (src, dst) in enumerate(
            [
                (moves_h, moves),
                (table_h, table_s),
                (table_h, table_v),
                (lengths_h, lengths),
                (scale_h, scale_v),
                (queries_h, queries),
                (new_kv_h, new_kv),
            ]
        )
    ]
    for copy in small:
        copy.start()
    for copy in small[:2]:
        copy.wait()

    first = replica * requests
    leaver, goal, arriver = [], [], []
    for d in range(1, replicas):
        there = jnp.where(replica + d < replicas, replica + d, replica + d - replicas) * requests
        behind = jnp.where(replica >= d, replica - d, replica - d + replicas) * requests
        out_slot = taken = here = jnp.int32(0)
        for j in range(requests):
            slot = moves[there + j] - first
            ours = (slot >= 0) & (slot < requests)
            out_slot = jnp.where(ours, slot, out_slot)
            taken = jnp.where(ours, j, taken)
            slot = moves[first + j] - behind
            here = jnp.where((slot >= 0) & (slot < requests), j, here)
        leaver.append(out_slot)
        goal.append(taken)
        arriver.append(here)

        def fetch(p, carry, d=d, out_slot=out_slot):
            pltpu.make_async_copy(
                kv_pages.at[table_s[out_slot, p]], away_kv.at[d - 1, p], kv_sem.at[d - 1]
            ).start()
            return carry

        lax.fori_loop(0, max_pages, fetch, 0, unroll=8)
    for copy in small[2:]:
        copy.wait()
    row_ids = lax.broadcasted_iota(jnp.int32, (requests, head_dim), 0)
    for d in range(1, replicas):
        goal_mask[d - 1] = (row_ids == goal[d - 1]).astype(F32)
        here_mask[d - 1] = (row_ids == arriver[d - 1]).astype(F32)

    q_all = queries[...].astype(F32)
    nk_rows[...] = new_kv[...].astype(F32)
    q_rows[...] = jnp.zeros_like(q_rows)
    for h in range(per_kv):
        q_rows[pl.ds(h, requests, stride=ROWS), :] = q_all[:, h * head_dim : (h + 1) * head_dim]

    for d in range(1, replicas):
        here = arriver[d - 1]
        own_rows = q_rows[pl.ds(pl.multiple_of(here * ROWS, ROWS), ROWS), :]
        token = nk_rows[pl.ds(here, 1), :]
        score = jnp.sum(own_rows * token[:, :head_dim], axis=1, keepdims=True) * factor
        here_own[d - 1, 0] = jnp.broadcast_to(score, (ROWS, head_dim))
        here_own[d - 1, 1] = jnp.broadcast_to(token[:, head_dim:], (ROWS, head_dim))
    lanes = lax.broadcasted_iota(jnp.int32, (1, max_pages), 1)
    staying = jnp.zeros((1, max_pages), jnp.int32)
    count = jnp.int32(0)
    for j in range(requests):
        stays = jnp.int32(1)
        for out_slot in leaver:
            stays = jnp.where(out_slot == j, 0, stays)
        staying = jnp.where((lanes == count) & (stays == 1), j, staying)
        count = count + stays
    table_out[:requests, :] = table_v[...]
    table_out[requests:, :] = staying
    for j in range(requests):
        context[j : j + 1, :] = jnp.full((1, head_dim), lengths[replica * requests + j], jnp.int32)

    scales[...] = scale_v[...].astype(F32)
    places = lax.broadcasted_iota(jnp.int32, (1, tokens), 1)
    spread = spread_matrix(max_pages, tokens)
    for d in range(1, replicas):
        out_slot = leaver[d - 1]
        picked = picked_scales(scale_v[...], table_v[pl.ds(out_slot, 1), :]).astype(BF16)
        wide = jnp.dot(picked, spread, preferred_element_type=F32)
        away_info[d - 1, 0:1, :] = wide[0:1] * factor
        away_info[d - 1, 1:2, :] = wide[1:2]
        away_info[d - 1, 2:3, :] = (places < lengths[replica * requests + out_slot]).astype(F32)

    for d in range(1, replicas):
        pltpu.make_async_copy(kv_pages.at[pl.ds(0, max_pages)], away_kv.at[d - 1], kv_sem.at[d - 1]).wait()


def attend_resident(
    replicas,
    per_kv,
    after,
    table_v,
    context,
    pool,
    q_rows,
    nk_rows,
    scales,
    attended,
    table_s,
    page_scales,
    key_scale,
    value_scale,
    scores,
    mixed,
    table_sem,
):
    del after
    requests, max_pages = context.shape[0], table_v.shape[1]
    _, _, page_len, head_dim = pool.shape
    tokens = max_pages * page_len
    span = CHUNK * page_len
    factor = 1.0 / math.sqrt(head_dim)
    copy = pltpu.make_async_copy(table_v, table_s, table_sem)
    copy.start()

    scale_rows = scales[...].astype(BF16)
    for j in range(requests):
        page_scales[:, j : j + 1, :] = picked_scales(scale_rows, table_v[j : j + 1, :])[:, None, :]
    spread = spread_matrix(max_pages, tokens)
    key_scale[...] = jnp.dot(page_scales[0].astype(BF16), spread, preferred_element_type=F32) * factor
    value_scale[...] = jnp.dot(page_scales[1].astype(BF16), spread, preferred_element_type=F32)
    places = lax.broadcasted_iota(jnp.int32, (1, tokens), 1)
    copy.wait()

    def gather(j, c, which):
        return jnp.concatenate([pool[table_s[j, c * CHUNK + i], which] for i in range(CHUNK)], axis=0)

    slots = [table_s[requests, i] for i in range(requests - (replicas - 1))]
    own, tokens_new = [], []
    for i, j in enumerate(slots):
        rows = slice(i * ROWS, (i + 1) * ROWS)
        q = q_rows[pl.ds(pl.multiple_of(j * ROWS, ROWS), ROWS), :]
        tokens_new.append(nk_rows[pl.ds(j, 1), :])
        own.append(jnp.sum(q * tokens_new[i][:, :head_dim], axis=1, keepdims=True) * factor)
        q = q.astype(BF16)
        key_row = key_scale[pl.ds(j, 1), :]
        limit = context[pl.ds(j, 1), :][:, :1]
        for c in range(max_pages // CHUNK):
            columns = slice(c * span, (c + 1) * span)
            raw = dot_keys(q, gather(j, c, 0)) * key_row[:, columns]
            scores[rows, columns] = jnp.where(places[:, columns] < limit, raw, -jnp.inf)
    stats = []
    for i in range(len(slots)):
        rows = slice(i * ROWS, (i + 1) * ROWS)
        weights, own_weight, inverse = softmax_parts(scores[rows, :], own[i])
        scores[rows, :] = weights
        stats.append((own_weight, inverse))
    for i, j in enumerate(slots):
        rows = slice(i * ROWS, (i + 1) * ROWS)
        own_weight, inverse = stats[i]
        value_row = value_scale[pl.ds(j, 1), :]
        total = jnp.zeros((2 * ROWS, head_dim), F32)
        for c in range(max_pages // CHUNK):
            columns = slice(c * span, (c + 1) * span)
            both = split_scaled(scores[rows, columns], inverse, value_row[:, columns])
            total = total + jnp.dot(both, gather(j, c, 1), preferred_element_type=F32)
        own_weight = (own_weight * inverse).astype(BF16).astype(F32)
        mixed[pl.ds(pl.multiple_of(j * ROWS, ROWS), ROWS), :] = (
            total[:ROWS] + total[ROWS:] + own_weight * tokens_new[i][:, head_dim:]
        )
    for h in range(per_kv):
        attended[:, h * head_dim : (h + 1) * head_dim] = mixed[pl.ds(h, requests, stride=ROWS), :]


def attend_away(replicas, per_kv, *refs):
    count = replicas - 1
    away_kv, away_info, goal_mask = refs[:3]
    came = refs[3 : 3 + count]
    outs = refs[3 + count : 3 + 2 * count]
    q_rows, scores = refs[3 + 2 * count :]
    max_pages, _, page_len, head_dim = away_kv.shape[1:]
    span = CHUNK * page_len
    for d in range(count):
        pick = goal_mask[d]
        came_all = came[d][...].astype(F32)
        q_rows[...] = jnp.zeros_like(q_rows)
        for h in range(per_kv):
            q_rows[h : h + 1, :] = jnp.sum(
                came_all[:, h * head_dim : (h + 1) * head_dim] * pick, axis=0, keepdims=True
            )
        q = q_rows[...].astype(BF16)
        for c in range(max_pages // CHUNK):
            columns = slice(c * span, (c + 1) * span)
            keys = away_kv[d, c * CHUNK : (c + 1) * CHUNK, 0].reshape(span, head_dim)
            raw = dot_keys(q, keys) * away_info[d, 0:1, columns]
            scores[:, columns] = jnp.where(away_info[d, 2:3, columns] > 0, raw, -jnp.inf)
        highest = jnp.max(scores[...], axis=1, keepdims=True)
        weights = jnp.exp(scores[...] - highest)
        total = jnp.sum(weights, axis=1, keepdims=True)
        inverse = 1.0 / total
        mixed = jnp.zeros((2 * ROWS, head_dim), F32)
        for c in range(max_pages // CHUNK):
            columns = slice(c * span, (c + 1) * span)
            values = away_kv[d, c * CHUNK : (c + 1) * CHUNK, 1].reshape(span, head_dim)
            both = split_scaled(weights[:, columns], inverse, away_info[d, 1:2, columns])
            mixed = mixed + jnp.dot(both, values, preferred_element_type=F32)
        outs[d][0] = mixed[:ROWS] + mixed[ROWS:]
        outs[d][1] = jnp.broadcast_to(highest, (ROWS, head_dim))
        outs[d][2] = jnp.broadcast_to(total, (ROWS, head_dim))


def merge(replicas, attended, here_mask, here_own, *refs):
    arrived, out = refs[: replicas - 1], refs[-1]
    head_dim = here_mask.shape[2]
    per_kv = attended.shape[1] // head_dim
    moved = []
    for d in range(replicas - 1):
        own = here_own[d, 0]
        highest = jnp.maximum(arrived[d][1], own)
        cached = arrived[d][2] * jnp.exp(arrived[d][1] - highest)
        own = jnp.exp(own - highest)
        inverse = 1.0 / (cached + own)
        own = (own * inverse).astype(BF16).astype(F32)
        moved.append(arrived[d][0] * (cached * inverse) + own * here_own[d, 1])
    for h in range(per_kv):
        columns = slice(h * head_dim, (h + 1) * head_dim)
        piece = attended[:, columns]
        for d in range(replicas - 1):
            piece = jnp.where(here_mask[d] > 0, moved[d][h : h + 1], piece)
        out[:, columns] = piece.astype(out.dtype)


def on_device(
    kv_pages, page_scale, page_table, lengths, request_moves, queries, new_kv, output_proj, residual
):
    devices = lax.axis_size("replica")
    replicas = devices // KVH
    requests, max_pages = page_table.shape
    pages, _, page_len, head_dim = kv_pages.shape
    per_kv = queries.shape[1] // head_dim
    width = output_proj.shape[1] // KVH
    tokens = max_pages * page_len
    count = replicas - 1

    def toward(value, steps):
        pairs = [(i, (i + steps * KVH) % devices) for i in range(devices)]
        return lax.ppermute(value, "replica", pairs)

    def by_core(value, even, odd):
        return lax.ppermute(value, "replica", [(i, i ^ (odd if i % 2 else even)) for i in range(devices)])

    def partner(value, mask):
        return lax.ppermute(value, "replica", [(i, i ^ mask) for i in range(devices)])

    position = lax.axis_index("replica").astype(jnp.uint32)
    bits = [(position & (1 << i)) != 0 for i in range(KVH.bit_length() - 1)]
    queries, *bits = lax.optimization_barrier((queries, *bits))
    came = [toward(queries, -d) for d in range(1, replicas)]

    def shape(*dims, dtype=F32):
        return jax.ShapeDtypeStruct(dims, dtype)

    in_hbm = functools.partial(pltpu.with_memory_space_constraint, memory_space=pltpu.HBM)
    q_rows, nk_rows, scales, away_kv, away_info, goal_mask, *home = pl.pallas_call(
        functools.partial(set_up, replicas, per_kv),
        out_shape=[
            shape(requests * ROWS, head_dim),
            shape(requests, 2 * head_dim),
            shape(2, pages),
            shape(count, max_pages, 2, page_len, head_dim, dtype=BF16),
            shape(count, 8, tokens),
            shape(count, requests, head_dim),
            shape(count, requests, head_dim),
            shape(count, 2, ROWS, head_dim),
            shape(requests + 1, max_pages, dtype=jnp.int32),
            shape(requests, head_dim, dtype=jnp.int32),
        ],
        in_specs=[HBM] * 7,
        out_specs=[VMEM] * 10,
        scratch_shapes=[
            pltpu.SMEM(lengths.shape, jnp.int32),
            pltpu.SMEM(request_moves.shape, jnp.int32),
            pltpu.SMEM(page_table.shape, jnp.int32),
            pltpu.VMEM(page_table.shape, jnp.int32),
            pltpu.VMEM((2, pages), BF16),
            pltpu.VMEM(queries.shape, BF16),
            pltpu.VMEM(new_kv.shape, BF16),
            pltpu.SemaphoreType.DMA((7,)),
            pltpu.SemaphoreType.DMA((count,)),
        ],
        compiler_params=pltpu.CompilerParams(vmem_limit_bytes=4 * 2**20),
        cost_estimate=pl.CostEstimate(flops=0, bytes_accessed=4 * kv_pages.size, transcendentals=0),
        name="set_up",
    )(*(in_hbm(x) for x in (lengths, request_moves, page_table, page_scale.T, queries, new_kv, kv_pages)))

    here_mask, here_own, table_v, context = home

    rows = pl.pallas_call(
        functools.partial(attend_away, replicas, per_kv),
        out_shape=[shape(3, ROWS, head_dim)] * count,
        in_specs=[VMEM] * (3 + count),
        out_specs=[VMEM] * count,
        scratch_shapes=[pltpu.VMEM((ROWS, head_dim), F32), pltpu.VMEM((ROWS, tokens), F32)],
        compiler_params=pltpu.CompilerParams(vmem_limit_bytes=4 * 2**20),
        name="attend_away",
    )(away_kv, away_info, goal_mask, *came)
    arrived = [toward(rows[d - 1], d) for d in range(1, replicas)]

    attended = pl.pallas_call(
        functools.partial(attend_resident, replicas, per_kv),
        out_shape=shape(requests, per_kv * head_dim),
        in_specs=[HBM] + [VMEM] * 6,
        out_specs=VMEM,
        scratch_shapes=[
            pltpu.SMEM((requests + 1, max_pages), jnp.int32),
            pltpu.VMEM((2, requests, max_pages), F32),
            pltpu.VMEM((requests, tokens), F32),
            pltpu.VMEM((requests, tokens), F32),
            pltpu.VMEM((requests * ROWS, tokens), F32),
            pltpu.VMEM((requests * ROWS, head_dim), F32),
            pltpu.SemaphoreType.DMA,
        ],
        compiler_params=pltpu.CompilerParams(vmem_limit_bytes=8 * 2**20),
        cost_estimate=pl.CostEstimate(
            flops=4 * per_kv * requests * tokens * head_dim,
            bytes_accessed=4 * output_proj.size,
            transcendentals=requests * ROWS * tokens,
        ),
        name="attend_resident",
    )(
        rows[0],
        table_v,
        context,
        pltpu.with_memory_space_constraint(kv_pages, pltpu.VMEM),
        q_rows,
        nk_rows,
        scales,
    )
    mixture = pl.pallas_call(
        functools.partial(merge, replicas),
        out_shape=shape(*attended.shape, dtype=BF16),
        in_specs=[VMEM] * (3 + count),
        out_specs=VMEM,
        compiler_params=pltpu.CompilerParams(vmem_limit_bytes=2**20),
        name="merge",
    )(attended, here_mask, here_own, *arrived)

    parts = jnp.dot(mixture, output_proj, preferred_element_type=F32)
    parts = [parts[:, i * width : (i + 1) * width] for i in range(KVH)]
    core, y, z = bits

    def split(blocks, bit, step):
        low = [b for i, b in enumerate(blocks) if not i & step]
        high = [b for i, b in enumerate(blocks) if i & step]
        same = [jnp.where(bit, b, a) for a, b in zip(low, high)]
        return same, [jnp.where(bit, a, b) for a, b in zip(low, high)]

    near, far = split(parts, core, 1)
    (near_own, near_z), (near_y, near_yz) = (split(pair, z, 1) for pair in split(near, y, 1))
    (far_own, far_z), (far_y, far_yz) = (split(pair, z, 1) for pair in split(far, y, 1))
    to_yz, to_core, at_y, at_z, own = lax.optimization_barrier(
        (
            jnp.concatenate([*near_yz, *far_yz], axis=1).astype(BF16),
            jnp.concatenate([*far_y, *far_z, *far_own], axis=1),
            near_y[0],
            near_z[0],
            near_own[0],
        )
    )
    came_yz = partner(to_yz, 6).astype(F32)
    other = partner(to_core, 1)
    at_y, at_z = at_y + other[:, :width], at_z + other[:, width : 2 * width]
    came_one = by_core(jnp.where(core, at_z, at_y).astype(BF16), 2, 4)
    came_two = by_core(jnp.where(core, at_y, at_z).astype(BF16), 4, 2)
    passed_on = partner(came_yz[:, width:], 1)
    total = own + other[:, 2 * width :] + came_yz[:, :width] + came_one.astype(F32) + came_two.astype(F32)
    total = lax.optimization_barrier(total) + passed_on
    return (residual.astype(F32) + total).astype(BF16)


def solution(mesh):
    return jax.shard_map(
        on_device,
        mesh=mesh,
        in_specs=(
            P(("parts", "replica"), None, None, None),
            P(("parts", "replica"), None),
            P(("parts", "replica"), None),
            P("parts"),
            P("parts"),
            P(("parts", "replica"), None),
            P(("parts", "replica"), None),
            P("replica", None),
            P(("parts", "replica"), None),
        ),
        out_specs=P(("parts", "replica"), None),
        check_vma=False,
    )
```

```python
import functools
import math

import jax
import jax.numpy as jnp
from jax import lax
from jax.experimental import pallas as pl
from jax.experimental.pallas import tpu as pltpu
from jax.sharding import PartitionSpec as P

KVH = 8
ROWS = 8
CHUNK = 4
F32 = jnp.float32
BF16 = jnp.bfloat16
VMEM = pl.BlockSpec(memory_space=pltpu.VMEM)
HBM = pl.BlockSpec(memory_space=pltpu.HBM)


def split_scaled(weights, inverse, value_scale):
    scaled = (weights * inverse).astype(BF16).astype(F32) * value_scale
    high = scaled.astype(BF16)
    low = (scaled - high.astype(F32)).astype(BF16)
    return jnp.concatenate([high, low], axis=0)


def dot_keys(queries, keys):
    return lax.dot_general(queries, keys, (((1,), (1,)), ((), ())), preferred_element_type=F32)


def picked_scales(scales, pages):
    ids = lax.broadcasted_iota(jnp.int32, (scales.shape[1], pages.shape[1]), 0)
    return jnp.dot(scales, (ids == pages).astype(F32).astype(BF16), preferred_element_type=F32)


def spread_matrix(max_pages, tokens):
    page_len = tokens // max_pages
    return (
        lax.broadcasted_iota(jnp.int32, (max_pages, tokens), 1) // page_len
        == lax.broadcasted_iota(jnp.int32, (max_pages, tokens), 0)
    ).astype(F32).astype(BF16)


def set_up(
    replicas,
    per_kv,
    lengths_h,
    moves_h,
    table_h,
    scale_h,
    queries_h,
    new_kv_h,
    kv_pages,
    q_rows,
    nk_rows,
    scales,
    away_kv,
    away_info,
    goal_mask,
    here_mask,
    here_own,
    table_out,
    context,
    lengths,
    moves,
    table_s,
    table_v,
    scale_v,
    queries,
    new_kv,
    small_sem,
    kv_sem,
):
    requests, max_pages = table_h.shape
    pages, _, page_len, head_dim = kv_pages.shape
    tokens = max_pages * page_len
    factor = 1.0 / math.sqrt(head_dim)
    replica = lax.axis_index("replica") // KVH

    small = [
        pltpu.make_async_copy(src, dst, small_sem.at[i])
        for i, (src, dst) in enumerate(
            [
                (moves_h, moves),
                (table_h, table_s),
                (table_h, table_v),
                (lengths_h, lengths),
                (scale_h, scale_v),
                (queries_h, queries),
                (new_kv_h, new_kv),
            ]
        )
    ]
    for copy in small:
        copy.start()
    for copy in small[:2]:
        copy.wait()

    first = replica * requests
    leaver, goal, arriver = [], [], []
    for d in range(1, replicas):
        there = jnp.where(replica + d < replicas, replica + d, replica + d - replicas) * requests
        behind = jnp.where(replica >= d, replica - d, replica - d + replicas) * requests
        out_slot = taken = here = jnp.int32(0)
        for j in range(requests):
            slot = moves[there + j] - first
            ours = (slot >= 0) & (slot < requests)
            out_slot = jnp.where(ours, slot, out_slot)
            taken = jnp.where(ours, j, taken)
            slot = moves[first + j] - behind
            here = jnp.where((slot >= 0) & (slot < requests), j, here)
        leaver.append(out_slot)
        goal.append(taken)
        arriver.append(here)

        def fetch(p, carry, d=d, out_slot=out_slot):
            pltpu.make_async_copy(
                kv_pages.at[table_s[out_slot, p]], away_kv.at[d - 1, p], kv_sem.at[d - 1]
            ).start()
            return carry

        lax.fori_loop(0, max_pages, fetch, 0, unroll=8)
    for copy in small[2:]:
        copy.wait()
    row_ids = lax.broadcasted_iota(jnp.int32, (requests, head_dim), 0)
    for d in range(1, replicas):
        goal_mask[d - 1] = (row_ids == goal[d - 1]).astype(F32)
        here_mask[d - 1] = (row_ids == arriver[d - 1]).astype(F32)

    q_all = queries[...].astype(F32)
    nk_rows[...] = new_kv[...].astype(F32)
    q_rows[...] = jnp.zeros_like(q_rows)
    for h in range(per_kv):
        q_rows[pl.ds(h, requests, stride=ROWS), :] = q_all[:, h * head_dim : (h + 1) * head_dim]

    for d in range(1, replicas):
        here = arriver[d - 1]
        own_rows = q_rows[pl.ds(pl.multiple_of(here * ROWS, ROWS), ROWS), :]
        token = nk_rows[pl.ds(here, 1), :]
        score = jnp.sum(own_rows * token[:, :head_dim], axis=1, keepdims=True) * factor
        here_own[d - 1, 0] = jnp.broadcast_to(score, (ROWS, head_dim))
        here_own[d - 1, 1] = jnp.broadcast_to(token[:, head_dim:], (ROWS, head_dim))
    lanes = lax.broadcasted_iota(jnp.int32, (1, max_pages), 1)
    staying = jnp.zeros((1, max_pages), jnp.int32)
    count = jnp.int32(0)
    for j in range(requests):
        stays = jnp.int32(1)
        for out_slot in leaver:
            stays = jnp.where(out_slot == j, 0, stays)
        staying = jnp.where((lanes == count) & (stays == 1), j, staying)
        count = count + stays
    table_out[:requests, :] = table_v[...]
    table_out[requests:, :] = staying
    for j in range(requests):
        context[j : j + 1, :] = jnp.full((1, head_dim), lengths[replica * requests + j], jnp.int32)

    scales[...] = scale_v[...].astype(F32)
    places = lax.broadcasted_iota(jnp.int32, (1, tokens), 1)
    spread = spread_matrix(max_pages, tokens)
    for d in range(1, replicas):
        out_slot = leaver[d - 1]
        picked = picked_scales(scale_v[...], table_v[pl.ds(out_slot, 1), :]).astype(BF16)
        wide = jnp.dot(picked, spread, preferred_element_type=F32)
        away_info[d - 1, 0:1, :] = wide[0:1] * factor
        away_info[d - 1, 1:2, :] = wide[1:2]
        away_info[d - 1, 2:3, :] = (places < lengths[replica * requests + out_slot]).astype(F32)

    for d in range(1, replicas):
        pltpu.make_async_copy(kv_pages.at[pl.ds(0, max_pages)], away_kv.at[d - 1], kv_sem.at[d - 1]).wait()


def attend_resident(
    replicas,
    per_kv,
    after,
    table_v,
    context,
    pool,
    q_rows,
    nk_rows,
    scales,
    attended,
    table_s,
    page_scales,
    key_scale,
    value_scale,
    scores,
    mixed,
    table_sem,
):
    del after
    requests, max_pages = context.shape[0], table_v.shape[1]
    _, _, page_len, head_dim = pool.shape
    tokens = max_pages * page_len
    span = CHUNK * page_len
    factor = 1.0 / math.sqrt(head_dim)
    copy = pltpu.make_async_copy(table_v, table_s, table_sem)
    copy.start()

    scale_rows = scales[...].astype(BF16)
    for j in range(requests):
        page_scales[:, j : j + 1, :] = picked_scales(scale_rows, table_v[j : j + 1, :])[:, None, :]
    spread = spread_matrix(max_pages, tokens)
    key_scale[...] = jnp.dot(page_scales[0].astype(BF16), spread, preferred_element_type=F32) * factor
    value_scale[...] = jnp.dot(page_scales[1].astype(BF16), spread, preferred_element_type=F32)
    places = lax.broadcasted_iota(jnp.int32, (1, tokens), 1)
    copy.wait()

    def gather(j, c, which):
        return jnp.concatenate([pool[table_s[j, c * CHUNK + i], which] for i in range(CHUNK)], axis=0)

    slots = [table_s[requests, i] for i in range(requests - (replicas - 1))]
    own, tokens_new, peaks = [], [], []
    for i, j in enumerate(slots):
        rows = slice(i * ROWS, (i + 1) * ROWS)
        q = q_rows[pl.ds(pl.multiple_of(j * ROWS, ROWS), ROWS), :]
        tokens_new.append(nk_rows[pl.ds(j, 1), :])
        own.append(q * tokens_new[i][:, :head_dim])
        q = q.astype(BF16)
        key_row = key_scale[pl.ds(j, 1), :]
        limit = context[pl.ds(j, 1), :][:, :1]
        peak = None
        for c in range(max_pages // CHUNK):
            columns = slice(c * span, (c + 1) * span)
            part = jnp.where(places[:, columns] < limit, dot_keys(q, gather(j, c, 0)) * key_row[:, columns], -jnp.inf)
            scores[rows, columns] = part
            peak = part if peak is None else jnp.maximum(peak, part)
        peaks.append(peak)
    own = [jnp.sum(product, axis=1, keepdims=True) * factor for product in own]
    peaks = [jnp.maximum(jnp.max(peak, axis=1, keepdims=True), mine) for peak, mine in zip(peaks, own)]
    own = [jnp.exp(mine - peak) for peak, mine in zip(peaks, own)]
    totals = []
    for i, peak in enumerate(peaks):
        rows = slice(i * ROWS, (i + 1) * ROWS)
        total = None
        for c in range(max_pages // CHUNK):
            columns = slice(c * span, (c + 1) * span)
            part = jnp.exp(scores[rows, columns] - peak)
            scores[rows, columns] = part
            total = part if total is None else total + part
        totals.append(total)
    totals = [jnp.sum(total, axis=1, keepdims=True) for total in totals]
    stats = [(mine, 1.0 / (total + mine)) for mine, total in zip(own, totals)]
    for i, j in enumerate(slots):
        rows = slice(i * ROWS, (i + 1) * ROWS)
        own_weight, inverse = stats[i]
        value_row = value_scale[pl.ds(j, 1), :]
        total = jnp.zeros((2 * ROWS, head_dim), F32)
        for c in range(max_pages // CHUNK):
            columns = slice(c * span, (c + 1) * span)
            both = split_scaled(scores[rows, columns], inverse, value_row[:, columns])
            total = total + jnp.dot(both, gather(j, c, 1), preferred_element_type=F32)
        own_weight = (own_weight * inverse).astype(BF16).astype(F32)
        mixed[pl.ds(pl.multiple_of(j * ROWS, ROWS), ROWS), :] = (
            total[:ROWS] + total[ROWS:] + own_weight * tokens_new[i][:, head_dim:]
        )
    for h in range(per_kv):
        attended[:, h * head_dim : (h + 1) * head_dim] = mixed[pl.ds(h, requests, stride=ROWS), :]


def attend_away(replicas, per_kv, *refs):
    count = replicas - 1
    away_kv, away_info, goal_mask = refs[:3]
    came = refs[3 : 3 + count]
    outs = refs[3 + count : 3 + 2 * count]
    q_rows, scores = refs[3 + 2 * count :]
    max_pages, _, page_len, head_dim = away_kv.shape[1:]
    span = CHUNK * page_len
    for d in range(count):
        pick = goal_mask[d]
        came_all = came[d][...].astype(F32)
        q_rows[...] = jnp.zeros_like(q_rows)
        for h in range(per_kv):
            q_rows[h : h + 1, :] = jnp.sum(
                came_all[:, h * head_dim : (h + 1) * head_dim] * pick, axis=0, keepdims=True
            )
        q = q_rows[...].astype(BF16)
        for c in range(max_pages // CHUNK):
            columns = slice(c * span, (c + 1) * span)
            keys = away_kv[d, c * CHUNK : (c + 1) * CHUNK, 0].reshape(span, head_dim)
            raw = dot_keys(q, keys) * away_info[d, 0:1, columns]
            scores[:, columns] = jnp.where(away_info[d, 2:3, columns] > 0, raw, -jnp.inf)
        highest = jnp.max(scores[...], axis=1, keepdims=True)
        weights = jnp.exp(scores[...] - highest)
        total = jnp.sum(weights, axis=1, keepdims=True)
        inverse = 1.0 / total
        mixed = jnp.zeros((2 * ROWS, head_dim), F32)
        for c in range(max_pages // CHUNK):
            columns = slice(c * span, (c + 1) * span)
            values = away_kv[d, c * CHUNK : (c + 1) * CHUNK, 1].reshape(span, head_dim)
            both = split_scaled(weights[:, columns], inverse, away_info[d, 1:2, columns])
            mixed = mixed + jnp.dot(both, values, preferred_element_type=F32)
        outs[d][0] = mixed[:ROWS] + mixed[ROWS:]
        outs[d][1] = jnp.broadcast_to(highest, (ROWS, head_dim))
        outs[d][2] = jnp.broadcast_to(total, (ROWS, head_dim))


def merge(replicas, attended, here_mask, here_own, *refs):
    arrived, out = refs[: replicas - 1], refs[-1]
    head_dim = here_mask.shape[2]
    per_kv = attended.shape[1] // head_dim
    moved = []
    for d in range(replicas - 1):
        own = here_own[d, 0]
        highest = jnp.maximum(arrived[d][1], own)
        cached = arrived[d][2] * jnp.exp(arrived[d][1] - highest)
        own = jnp.exp(own - highest)
        inverse = 1.0 / (cached + own)
        own = (own * inverse).astype(BF16).astype(F32)
        moved.append(arrived[d][0] * (cached * inverse) + own * here_own[d, 1])
    for h in range(per_kv):
        columns = slice(h * head_dim, (h + 1) * head_dim)
        piece = attended[:, columns]
        for d in range(replicas - 1):
            piece = jnp.where(here_mask[d] > 0, moved[d][h : h + 1], piece)
        out[:, columns] = piece.astype(out.dtype)


def on_device(
    kv_pages, page_scale, page_table, lengths, request_moves, queries, new_kv, output_proj, residual
):
    devices = lax.axis_size("replica")
    replicas = devices // KVH
    requests, max_pages = page_table.shape
    pages, _, page_len, head_dim = kv_pages.shape
    per_kv = queries.shape[1] // head_dim
    width = output_proj.shape[1] // KVH
    tokens = max_pages * page_len
    count = replicas - 1

    def toward(value, steps):
        pairs = [(i, (i + steps * KVH) % devices) for i in range(devices)]
        return lax.ppermute(value, "replica", pairs)

    def partner(value, mask):
        return lax.ppermute(value, "replica", [(i, i ^ mask) for i in range(devices)])

    position = lax.axis_index("replica").astype(jnp.uint32)
    bits = [(position & (1 << i)) != 0 for i in range(KVH.bit_length() - 1)]
    queries, *bits = lax.optimization_barrier((queries, *bits))
    came = [toward(queries, -d) for d in range(1, replicas)]

    def shape(*dims, dtype=F32):
        return jax.ShapeDtypeStruct(dims, dtype)

    in_hbm = functools.partial(pltpu.with_memory_space_constraint, memory_space=pltpu.HBM)
    q_rows, nk_rows, scales, away_kv, away_info, goal_mask, *home = pl.pallas_call(
        functools.partial(set_up, replicas, per_kv),
        out_shape=[
            shape(requests * ROWS, head_dim),
            shape(requests, 2 * head_dim),
            shape(2, pages),
            shape(count, max_pages, 2, page_len, head_dim, dtype=BF16),
            shape(count, 8, tokens),
            shape(count, requests, head_dim),
            shape(count, requests, head_dim),
            shape(count, 2, ROWS, head_dim),
            shape(requests + 1, max_pages, dtype=jnp.int32),
            shape(requests, head_dim, dtype=jnp.int32),
        ],
        in_specs=[HBM] * 7,
        out_specs=[VMEM] * 10,
        scratch_shapes=[
            pltpu.SMEM(lengths.shape, jnp.int32),
            pltpu.SMEM(request_moves.shape, jnp.int32),
            pltpu.SMEM(page_table.shape, jnp.int32),
            pltpu.VMEM(page_table.shape, jnp.int32),
            pltpu.VMEM((2, pages), BF16),
            pltpu.VMEM(queries.shape, BF16),
            pltpu.VMEM(new_kv.shape, BF16),
            pltpu.SemaphoreType.DMA((7,)),
            pltpu.SemaphoreType.DMA((count,)),
        ],
        compiler_params=pltpu.CompilerParams(vmem_limit_bytes=4 * 2**20),
        cost_estimate=pl.CostEstimate(flops=0, bytes_accessed=4 * kv_pages.size, transcendentals=0),
        name="set_up",
    )(*(in_hbm(x) for x in (lengths, request_moves, page_table, page_scale.T, queries, new_kv, kv_pages)))

    here_mask, here_own, table_v, context = home

    rows = pl.pallas_call(
        functools.partial(attend_away, replicas, per_kv),
        out_shape=[shape(3, ROWS, head_dim)] * count,
        in_specs=[VMEM] * (3 + count),
        out_specs=[VMEM] * count,
        scratch_shapes=[pltpu.VMEM((ROWS, head_dim), F32), pltpu.VMEM((ROWS, tokens), F32)],
        compiler_params=pltpu.CompilerParams(vmem_limit_bytes=4 * 2**20),
        name="attend_away",
    )(away_kv, away_info, goal_mask, *came)
    arrived = [toward(rows[d - 1], d) for d in range(1, replicas)]

    attended = pl.pallas_call(
        functools.partial(attend_resident, replicas, per_kv),
        out_shape=shape(requests, per_kv * head_dim),
        in_specs=[HBM] + [VMEM] * 6,
        out_specs=VMEM,
        scratch_shapes=[
            pltpu.SMEM((requests + 1, max_pages), jnp.int32),
            pltpu.VMEM((2, requests, max_pages), F32),
            pltpu.VMEM((requests, tokens), F32),
            pltpu.VMEM((requests, tokens), F32),
            pltpu.VMEM((requests * ROWS, tokens), F32),
            pltpu.VMEM((requests * ROWS, head_dim), F32),
            pltpu.SemaphoreType.DMA,
        ],
        compiler_params=pltpu.CompilerParams(vmem_limit_bytes=8 * 2**20),
        cost_estimate=pl.CostEstimate(
            flops=4 * per_kv * requests * tokens * head_dim,
            bytes_accessed=4 * output_proj.size,
            transcendentals=requests * ROWS * tokens,
        ),
        name="attend_resident",
    )(
        rows[0],
        table_v,
        context,
        pltpu.with_memory_space_constraint(kv_pages, pltpu.VMEM),
        q_rows,
        nk_rows,
        scales,
    )
    mixture = pl.pallas_call(
        functools.partial(merge, replicas),
        out_shape=shape(*attended.shape, dtype=BF16),
        in_specs=[VMEM] * (3 + count),
        out_specs=VMEM,
        compiler_params=pltpu.CompilerParams(vmem_limit_bytes=2**20),
        name="merge",
    )(attended, here_mask, here_own, *arrived)

    parts = jnp.dot(mixture, output_proj, preferred_element_type=F32)
    parts = [parts[:, i * width : (i + 1) * width] for i in range(KVH)]
    core, y, z = bits

    def split(blocks, bit, step):
        low = [b for i, b in enumerate(blocks) if not i & step]
        high = [b for i, b in enumerate(blocks) if i & step]
        same = [jnp.where(bit, b, a) for a, b in zip(low, high)]
        return same, [jnp.where(bit, a, b) for a, b in zip(low, high)]

    near, far = split(parts, core, 1)
    (near_own, near_z), (near_y, near_yz) = (split(pair, z, 1) for pair in split(near, y, 1))
    (far_own, far_z), (far_y, far_yz) = (split(pair, z, 1) for pair in split(far, y, 1))
    to_yz, to_core, at_y, at_z, own = lax.optimization_barrier(
        (
            jnp.concatenate([*near_yz, *far_yz], axis=1).astype(BF16),
            jnp.concatenate([*far_y, *far_z, *far_own], axis=1),
            near_y[0],
            near_z[0],
            near_own[0],
        )
    )
    came_yz = partner(to_yz, 6).astype(F32)
    other = partner(to_core, 1)
    came_y = partner((at_y + other[:, :width]).astype(BF16), 2)
    came_z = partner((at_z + other[:, width : 2 * width]).astype(BF16), 4)
    passed_on = partner(came_yz[:, width:], 1)
    total = own + other[:, 2 * width :] + came_yz[:, :width] + came_y.astype(F32) + came_z.astype(F32)
    total = lax.optimization_barrier(total) + passed_on
    return (residual.astype(F32) + total).astype(BF16)


def solution(mesh):
    return jax.shard_map(
        on_device,
        mesh=mesh,
        in_specs=(
            P(("parts", "replica"), None, None, None),
            P(("parts", "replica"), None),
            P(("parts", "replica"), None),
            P("parts"),
            P("parts"),
            P(("parts", "replica"), None),
            P(("parts", "replica"), None),
            P("replica", None),
            P(("parts", "replica"), None),
        ),
        out_specs=P(("parts", "replica"), None),
        check_vma=False,
    )
```

```python
import functools
import math

import jax
import jax.numpy as jnp
from jax import lax
from jax.experimental import pallas as pl
from jax.experimental.pallas import tpu as pltpu
from jax.sharding import PartitionSpec as P

KVH = 8
ROWS = 8
CHUNK = 4
F32 = jnp.float32
BF16 = jnp.bfloat16
VMEM = pl.BlockSpec(memory_space=pltpu.VMEM)
HBM = pl.BlockSpec(memory_space=pltpu.HBM)


def softmax_parts(scores, own):
    highest = jnp.maximum(jnp.max(scores, axis=1, keepdims=True), own)
    weights = jnp.exp(scores - highest)
    own_weight = jnp.exp(own - highest)
    return weights, own_weight, 1.0 / (jnp.sum(weights, axis=1, keepdims=True) + own_weight)


def split_scaled(weights, inverse, value_scale):
    if inverse is not None:
        weights = weights * inverse
    scaled = weights.astype(BF16).astype(F32) * value_scale
    high = scaled.astype(BF16)
    low = (scaled - high.astype(F32)).astype(BF16)
    return jnp.concatenate([high, low], axis=0)


def dot_keys(queries, keys):
    return lax.dot_general(queries, keys, (((1,), (1,)), ((), ())), preferred_element_type=F32)


def picked_scales(scales, pages):
    ids = lax.broadcasted_iota(jnp.int32, (scales.shape[1], pages.shape[1]), 0)
    return jnp.dot(scales, (ids == pages).astype(F32).astype(BF16), preferred_element_type=F32)


def spread_matrix(max_pages, tokens):
    page_len = tokens // max_pages
    return (
        lax.broadcasted_iota(jnp.int32, (max_pages, tokens), 1) // page_len
        == lax.broadcasted_iota(jnp.int32, (max_pages, tokens), 0)
    ).astype(F32).astype(BF16)


def set_up(
    replicas,
    per_kv,
    lengths_h,
    moves_h,
    table_h,
    scale_h,
    queries_h,
    new_kv_h,
    kv_pages,
    q_rows,
    nk_rows,
    scales,
    away_kv,
    away_info,
    goal_mask,
    here_mask,
    here_own,
    table_out,
    context,
    lengths,
    moves,
    table_s,
    table_v,
    scale_v,
    queries,
    new_kv,
    small_sem,
    kv_sem,
):
    requests, max_pages = table_h.shape
    pages, _, page_len, head_dim = kv_pages.shape
    tokens = max_pages * page_len
    factor = 1.0 / math.sqrt(head_dim)
    replica = lax.axis_index("replica") // KVH

    small = [
        pltpu.make_async_copy(src, dst, small_sem.at[i])
        for i, (src, dst) in enumerate(
            [
                (moves_h, moves),
                (table_h, table_s),
                (table_h, table_v),
                (lengths_h, lengths),
                (scale_h, scale_v),
                (queries_h, queries),
                (new_kv_h, new_kv),
            ]
        )
    ]
    for copy in small:
        copy.start()
    for copy in small[:2]:
        copy.wait()

    first = replica * requests
    leaver, goal, arriver = [], [], []
    for d in range(1, replicas):
        there = jnp.where(replica + d < replicas, replica + d, replica + d - replicas) * requests
        behind = jnp.where(replica >= d, replica - d, replica - d + replicas) * requests
        out_slot = taken = here = jnp.int32(0)
        for j in range(requests):
            slot = moves[there + j] - first
            ours = (slot >= 0) & (slot < requests)
            out_slot = jnp.where(ours, slot, out_slot)
            taken = jnp.where(ours, j, taken)
            slot = moves[first + j] - behind
            here = jnp.where((slot >= 0) & (slot < requests), j, here)
        leaver.append(out_slot)
        goal.append(taken)
        arriver.append(here)

        def fetch(p, carry, d=d, out_slot=out_slot):
            pltpu.make_async_copy(
                kv_pages.at[table_s[out_slot, p]], away_kv.at[d - 1, p], kv_sem.at[d - 1]
            ).start()
            return carry

        lax.fori_loop(0, max_pages, fetch, 0, unroll=8)
    for copy in small[2:]:
        copy.wait()
    row_ids = lax.broadcasted_iota(jnp.int32, (requests, head_dim), 0)
    for d in range(1, replicas):
        goal_mask[d - 1] = (row_ids == goal[d - 1]).astype(F32)
        here_mask[d - 1] = (row_ids == arriver[d - 1]).astype(F32)

    q_all = queries[...].astype(F32)
    nk_rows[...] = new_kv[...].astype(F32)
    q_rows[...] = jnp.zeros_like(q_rows)
    for h in range(per_kv):
        q_rows[pl.ds(h, requests, stride=ROWS), :] = q_all[:, h * head_dim : (h + 1) * head_dim]

    for d in range(1, replicas):
        here = arriver[d - 1]
        own_rows = q_rows[pl.ds(pl.multiple_of(here * ROWS, ROWS), ROWS), :]
        token = nk_rows[pl.ds(here, 1), :]
        score = jnp.sum(own_rows * token[:, :head_dim], axis=1, keepdims=True) * factor
        here_own[d - 1, 0] = jnp.broadcast_to(score, (ROWS, head_dim))
        here_own[d - 1, 1] = jnp.broadcast_to(token[:, head_dim:], (ROWS, head_dim))
    lanes = lax.broadcasted_iota(jnp.int32, (1, max_pages), 1)
    staying = jnp.zeros((1, max_pages), jnp.int32)
    count = jnp.int32(0)
    for j in range(requests):
        stays = jnp.int32(1)
        for out_slot in leaver:
            stays = jnp.where(out_slot == j, 0, stays)
        staying = jnp.where((lanes == count) & (stays == 1), j, staying)
        count = count + stays
    table_out[:requests, :] = table_v[...]
    table_out[requests:, :] = staying
    for j in range(requests):
        context[j : j + 1, :] = jnp.full((1, head_dim), lengths[replica * requests + j], jnp.int32)

    scales[...] = scale_v[...].astype(F32)
    places = lax.broadcasted_iota(jnp.int32, (1, tokens), 1)
    spread = spread_matrix(max_pages, tokens)
    for d in range(1, replicas):
        out_slot = leaver[d - 1]
        picked = picked_scales(scale_v[...], table_v[pl.ds(out_slot, 1), :]).astype(BF16)
        wide = jnp.dot(picked, spread, preferred_element_type=F32)
        away_info[d - 1, 0:1, :] = wide[0:1] * factor
        away_info[d - 1, 1:2, :] = wide[1:2]
        away_info[d - 1, 2:3, :] = (places < lengths[replica * requests + out_slot]).astype(F32)

    for d in range(1, replicas):
        pltpu.make_async_copy(kv_pages.at[pl.ds(0, max_pages)], away_kv.at[d - 1], kv_sem.at[d - 1]).wait()


def attend_resident(
    replicas,
    per_kv,
    after,
    table_v,
    context,
    pool,
    q_rows,
    nk_rows,
    scales,
    attended,
    table_s,
    page_scales,
    key_scale,
    value_scale,
    scores,
    mixed,
    table_sem,
):
    del after
    requests, max_pages = context.shape[0], table_v.shape[1]
    _, _, page_len, head_dim = pool.shape
    tokens = max_pages * page_len
    span = CHUNK * page_len
    factor = 1.0 / math.sqrt(head_dim)
    copy = pltpu.make_async_copy(table_v, table_s, table_sem)
    copy.start()

    scale_rows = scales[...].astype(BF16)
    for j in range(requests):
        page_scales[:, j : j + 1, :] = picked_scales(scale_rows, table_v[j : j + 1, :])[:, None, :]
    spread = spread_matrix(max_pages, tokens)
    key_scale[...] = jnp.dot(page_scales[0].astype(BF16), spread, preferred_element_type=F32) * factor
    value_scale[...] = jnp.dot(page_scales[1].astype(BF16), spread, preferred_element_type=F32)
    places = lax.broadcasted_iota(jnp.int32, (1, tokens), 1)
    copy.wait()

    def gather(j, c, which):
        return jnp.concatenate([pool[table_s[j, c * CHUNK + i], which] for i in range(CHUNK)], axis=0)

    slots = [table_s[requests, i] for i in range(requests - (replicas - 1))]
    own, tokens_new = [], []
    for i, j in enumerate(slots):
        rows = slice(i * ROWS, (i + 1) * ROWS)
        q = q_rows[pl.ds(pl.multiple_of(j * ROWS, ROWS), ROWS), :]
        tokens_new.append(nk_rows[pl.ds(j, 1), :])
        own.append(jnp.sum(q * tokens_new[i][:, :head_dim], axis=1, keepdims=True) * factor)
        q = q.astype(BF16)
        key_row = key_scale[pl.ds(j, 1), :]
        limit = context[pl.ds(j, 1), :][:, :1]
        for c in range(max_pages // CHUNK):
            columns = slice(c * span, (c + 1) * span)
            raw = dot_keys(q, gather(j, c, 0)) * key_row[:, columns]
            scores[rows, columns] = jnp.where(places[:, columns] < limit, raw, -jnp.inf)
    stats = []
    for i in range(len(slots)):
        rows = slice(i * ROWS, (i + 1) * ROWS)
        weights, own_weight, inverse = softmax_parts(scores[rows, :], own[i])
        scores[rows, :] = weights
        stats.append((own_weight, inverse))
    for i, j in enumerate(slots):
        rows = slice(i * ROWS, (i + 1) * ROWS)
        own_weight, inverse = stats[i]
        value_row = value_scale[pl.ds(j, 1), :]
        total = jnp.zeros((2 * ROWS, head_dim), F32)
        for c in range(max_pages // CHUNK):
            columns = slice(c * span, (c + 1) * span)
            both = split_scaled(scores[rows, columns], inverse, value_row[:, columns])
            total = total + jnp.dot(both, gather(j, c, 1), preferred_element_type=F32)
        own_weight = (own_weight * inverse).astype(BF16).astype(F32)
        mixed[pl.ds(pl.multiple_of(j * ROWS, ROWS), ROWS), :] = (
            total[:ROWS] + total[ROWS:] + own_weight * tokens_new[i][:, head_dim:]
        )
    for h in range(per_kv):
        attended[:, h * head_dim : (h + 1) * head_dim] = mixed[pl.ds(h, requests, stride=ROWS), :]


def attend_away(replicas, per_kv, *refs):
    count = replicas - 1
    away_kv, away_info, goal_mask = refs[:3]
    came = refs[3 : 3 + count]
    outs = refs[3 + count : 3 + 2 * count]
    q_rows, scores = refs[3 + 2 * count :]
    max_pages, _, page_len, head_dim = away_kv.shape[1:]
    span = CHUNK * page_len
    for d in range(count):
        pick = goal_mask[d]
        came_all = came[d][...].astype(F32)
        q_rows[...] = jnp.zeros_like(q_rows)
        for h in range(per_kv):
            q_rows[h : h + 1, :] = jnp.sum(
                came_all[:, h * head_dim : (h + 1) * head_dim] * pick, axis=0, keepdims=True
            )
        q = q_rows[...].astype(BF16)
        for c in range(max_pages // CHUNK):
            columns = slice(c * span, (c + 1) * span)
            keys = away_kv[d, c * CHUNK : (c + 1) * CHUNK, 0].reshape(span, head_dim)
            raw = dot_keys(q, keys) * away_info[d, 0:1, columns]
            scores[:, columns] = jnp.where(away_info[d, 2:3, columns] > 0, raw, -jnp.inf)
        highest = jnp.max(scores[...], axis=1, keepdims=True)
        weights = jnp.exp(scores[...] - highest)
        total = jnp.sum(weights, axis=1, keepdims=True)
        mixed = jnp.zeros((2 * ROWS, head_dim), F32)
        for c in range(max_pages // CHUNK):
            columns = slice(c * span, (c + 1) * span)
            values = away_kv[d, c * CHUNK : (c + 1) * CHUNK, 1].reshape(span, head_dim)
            both = split_scaled(weights[:, columns], None, away_info[d, 1:2, columns])
            mixed = mixed + jnp.dot(both, values, preferred_element_type=F32)
        outs[d][0] = mixed[:ROWS] + mixed[ROWS:]
        outs[d][1] = jnp.broadcast_to(highest, (ROWS, head_dim))
        outs[d][2] = jnp.broadcast_to(total, (ROWS, head_dim))


def pick(parts, to_yz, to_core, at_y, at_z, own):
    width = own.shape[1]
    shard = lax.axis_index("replica") % KVH

    def block(k):
        return parts[:, pl.ds(pl.multiple_of((shard ^ k) * width, 128), width)]

    for i, k in enumerate((6, 7)):
        to_yz[:, i * width : (i + 1) * width] = block(k).astype(to_yz.dtype)
    for i, k in enumerate((3, 5, 1)):
        to_core[:, i * width : (i + 1) * width] = block(k)
    at_y[...] = block(2)
    at_z[...] = block(4)
    own[...] = block(0)


def merge(replicas, attended, here_mask, here_own, *refs):
    arrived, out = refs[: replicas - 1], refs[-1]
    head_dim = here_mask.shape[2]
    per_kv = attended.shape[1] // head_dim
    moved = []
    for d in range(replicas - 1):
        own = here_own[d, 0]
        highest = jnp.maximum(arrived[d][1], own)
        cached = jnp.exp(arrived[d][1] - highest)
        own = jnp.exp(own - highest)
        inverse = 1.0 / (arrived[d][2] * cached + own)
        own = (own * inverse).astype(BF16).astype(F32)
        moved.append(arrived[d][0] * (cached * inverse) + own * here_own[d, 1])
    for h in range(per_kv):
        columns = slice(h * head_dim, (h + 1) * head_dim)
        piece = attended[:, columns]
        for d in range(replicas - 1):
            piece = jnp.where(here_mask[d] > 0, moved[d][h : h + 1], piece)
        out[:, columns] = piece.astype(out.dtype)


def on_device(
    kv_pages, page_scale, page_table, lengths, request_moves, queries, new_kv, output_proj, residual
):
    devices = lax.axis_size("replica")
    replicas = devices // KVH
    requests, max_pages = page_table.shape
    pages, _, page_len, head_dim = kv_pages.shape
    per_kv = queries.shape[1] // head_dim
    width = output_proj.shape[1] // KVH
    tokens = max_pages * page_len
    count = replicas - 1

    def toward(value, steps):
        pairs = [(i, (i + steps * KVH) % devices) for i in range(devices)]
        return lax.ppermute(value, "replica", pairs)

    def partner(value, mask):
        return lax.ppermute(value, "replica", [(i, i ^ mask) for i in range(devices)])

    came = [toward(queries, -d) for d in range(1, replicas)]

    def shape(*dims, dtype=F32):
        return jax.ShapeDtypeStruct(dims, dtype)

    in_hbm = functools.partial(pltpu.with_memory_space_constraint, memory_space=pltpu.HBM)
    q_rows, nk_rows, scales, away_kv, away_info, goal_mask, *home = pl.pallas_call(
        functools.partial(set_up, replicas, per_kv),
        out_shape=[
            shape(requests * ROWS, head_dim),
            shape(requests, 2 * head_dim),
            shape(2, pages),
            shape(count, max_pages, 2, page_len, head_dim, dtype=BF16),
            shape(count, 8, tokens),
            shape(count, requests, head_dim),
            shape(count, requests, head_dim),
            shape(count, 2, ROWS, head_dim),
            shape(requests + 1, max_pages, dtype=jnp.int32),
            shape(requests, head_dim, dtype=jnp.int32),
        ],
        in_specs=[HBM] * 7,
        out_specs=[VMEM] * 10,
        scratch_shapes=[
            pltpu.SMEM(lengths.shape, jnp.int32),
            pltpu.SMEM(request_moves.shape, jnp.int32),
            pltpu.SMEM(page_table.shape, jnp.int32),
            pltpu.VMEM(page_table.shape, jnp.int32),
            pltpu.VMEM((2, pages), BF16),
            pltpu.VMEM(queries.shape, BF16),
            pltpu.VMEM(new_kv.shape, BF16),
            pltpu.SemaphoreType.DMA((7,)),
            pltpu.SemaphoreType.DMA((count,)),
        ],
        compiler_params=pltpu.CompilerParams(vmem_limit_bytes=4 * 2**20),
        cost_estimate=pl.CostEstimate(flops=0, bytes_accessed=4 * kv_pages.size, transcendentals=0),
        name="set_up",
    )(*(in_hbm(x) for x in (lengths, request_moves, page_table, page_scale.T, queries, new_kv, kv_pages)))

    here_mask, here_own, table_v, context = home

    rows = pl.pallas_call(
        functools.partial(attend_away, replicas, per_kv),
        out_shape=[shape(3, ROWS, head_dim)] * count,
        in_specs=[VMEM] * (3 + count),
        out_specs=[VMEM] * count,
        scratch_shapes=[pltpu.VMEM((ROWS, head_dim), F32), pltpu.VMEM((ROWS, tokens), F32)],
        compiler_params=pltpu.CompilerParams(vmem_limit_bytes=4 * 2**20),
        name="attend_away",
    )(away_kv, away_info, goal_mask, *came)
    arrived = [toward(rows[d - 1], d) for d in range(1, replicas)]

    attended = pl.pallas_call(
        functools.partial(attend_resident, replicas, per_kv),
        out_shape=shape(requests, per_kv * head_dim),
        in_specs=[HBM] + [VMEM] * 6,
        out_specs=VMEM,
        scratch_shapes=[
            pltpu.SMEM((requests + 1, max_pages), jnp.int32),
            pltpu.VMEM((2, requests, max_pages), F32),
            pltpu.VMEM((requests, tokens), F32),
            pltpu.VMEM((requests, tokens), F32),
            pltpu.VMEM((requests * ROWS, tokens), F32),
            pltpu.VMEM((requests * ROWS, head_dim), F32),
            pltpu.SemaphoreType.DMA,
        ],
        compiler_params=pltpu.CompilerParams(vmem_limit_bytes=8 * 2**20),
        cost_estimate=pl.CostEstimate(
            flops=4 * per_kv * requests * tokens * head_dim,
            bytes_accessed=4 * output_proj.size,
            transcendentals=requests * ROWS * tokens,
        ),
        name="attend_resident",
    )(
        rows[0],
        table_v,
        context,
        pltpu.with_memory_space_constraint(kv_pages, pltpu.VMEM),
        q_rows,
        nk_rows,
        scales,
    )
    mixture = pl.pallas_call(
        functools.partial(merge, replicas),
        out_shape=shape(*attended.shape, dtype=BF16),
        in_specs=[VMEM] * (3 + count),
        out_specs=VMEM,
        compiler_params=pltpu.CompilerParams(vmem_limit_bytes=2**20),
        name="merge",
    )(attended, here_mask, here_own, *arrived)

    parts = jnp.dot(mixture, output_proj, preferred_element_type=F32)

    to_yz, to_core, at_y, at_z, own = pl.pallas_call(
        pick,
        out_shape=[shape(requests, 2 * width, dtype=BF16), shape(requests, 3 * width)]
        + [shape(requests, width)] * 3,
        in_specs=[VMEM],
        out_specs=[VMEM] * 5,
        compiler_params=pltpu.CompilerParams(vmem_limit_bytes=2**20),
        name="pick",
    )(parts)
    came_yz = partner(to_yz, 6).astype(F32)
    other = partner(to_core, 1)
    came_y = partner((at_y + other[:, :width]).astype(BF16), 2)
    came_z = partner((at_z + other[:, width : 2 * width]).astype(BF16), 4)
    passed_on = partner(came_yz[:, width:], 1)
    total = own + other[:, 2 * width :] + came_yz[:, :width] + came_y.astype(F32) + came_z.astype(F32)
    total = lax.optimization_barrier(total) + passed_on
    return (residual.astype(F32) + total).astype(BF16)


def solution(mesh):
    return jax.shard_map(
        on_device,
        mesh=mesh,
        in_specs=(
            P(("parts", "replica"), None, None, None),
            P(("parts", "replica"), None),
            P(("parts", "replica"), None),
            P("parts"),
            P("parts"),
            P(("parts", "replica"), None),
            P(("parts", "replica"), None),
            P("replica", None),
            P(("parts", "replica"), None),
        ),
        out_specs=P(("parts", "replica"), None),
        check_vma=False,
    )
```

```python
import functools
import math

import jax
import jax.numpy as jnp
from jax import lax
from jax.experimental import pallas as pl
from jax.experimental.pallas import tpu as pltpu
from jax.sharding import PartitionSpec as P

KVH = 8
ROWS = 8
CHUNK = 4
F32 = jnp.float32
BF16 = jnp.bfloat16
VMEM = pl.BlockSpec(memory_space=pltpu.VMEM)
HBM = pl.BlockSpec(memory_space=pltpu.HBM)


def softmax_parts(scores, own):
    highest = jnp.maximum(jnp.max(scores, axis=1, keepdims=True), own)
    weights = jnp.exp(scores - highest)
    own_weight = jnp.exp(own - highest)
    return weights, own_weight, 1.0 / (jnp.sum(weights, axis=1, keepdims=True) + own_weight)


def split_scaled(weights, inverse, value_scale):
    if inverse is not None:
        weights = weights * inverse
    scaled = weights.astype(BF16).astype(F32) * value_scale
    high = scaled.astype(BF16)
    low = (scaled - high.astype(F32)).astype(BF16)
    return jnp.concatenate([high, low], axis=0)


def dot_keys(queries, keys):
    return lax.dot_general(queries, keys, (((1,), (1,)), ((), ())), preferred_element_type=F32)


def picked_scales(scales, pages):
    ids = lax.broadcasted_iota(jnp.int32, (scales.shape[1], pages.shape[1]), 0)
    return jnp.dot(scales, (ids == pages).astype(F32).astype(BF16), preferred_element_type=F32)


def spread_matrix(max_pages, tokens):
    page_len = tokens // max_pages
    return (
        lax.broadcasted_iota(jnp.int32, (max_pages, tokens), 1) // page_len
        == lax.broadcasted_iota(jnp.int32, (max_pages, tokens), 0)
    ).astype(F32).astype(BF16)


def set_up(
    replicas,
    per_kv,
    lengths_h,
    moves_h,
    table_h,
    scale_h,
    queries_h,
    new_kv_h,
    kv_pages,
    q_rows,
    nk_rows,
    scales,
    away_kv,
    away_info,
    goal_mask,
    here_mask,
    here_own,
    table_out,
    context,
    lengths,
    moves,
    table_s,
    table_v,
    scale_v,
    queries,
    new_kv,
    small_sem,
    kv_sem,
):
    requests, max_pages = table_h.shape
    pages, _, page_len, head_dim = kv_pages.shape
    tokens = max_pages * page_len
    factor = 1.0 / math.sqrt(head_dim)
    replica = lax.axis_index("replica") // KVH

    small = [
        pltpu.make_async_copy(src, dst, small_sem.at[i])
        for i, (src, dst) in enumerate(
            [
                (moves_h, moves),
                (table_h, table_s),
                (table_h, table_v),
                (lengths_h, lengths),
                (scale_h, scale_v),
                (queries_h, queries),
                (new_kv_h, new_kv),
            ]
        )
    ]
    for copy in small:
        copy.start()
    for copy in small[:2]:
        copy.wait()

    first = replica * requests
    leaver, goal, arriver = [], [], []
    for d in range(1, replicas):
        there = jnp.where(replica + d < replicas, replica + d, replica + d - replicas) * requests
        behind = jnp.where(replica >= d, replica - d, replica - d + replicas) * requests
        out_slot = taken = here = jnp.int32(0)
        for j in range(requests):
            slot = moves[there + j] - first
            ours = (slot >= 0) & (slot < requests)
            out_slot = jnp.where(ours, slot, out_slot)
            taken = jnp.where(ours, j, taken)
            slot = moves[first + j] - behind
            here = jnp.where((slot >= 0) & (slot < requests), j, here)
        leaver.append(out_slot)
        goal.append(taken)
        arriver.append(here)

        def fetch(p, carry, d=d, out_slot=out_slot):
            pltpu.make_async_copy(
                kv_pages.at[table_s[out_slot, p]], away_kv.at[d - 1, p], kv_sem.at[d - 1]
            ).start()
            return carry

        lax.fori_loop(0, max_pages, fetch, 0, unroll=True)
    for copy in small[2:]:
        copy.wait()
    row_ids = lax.broadcasted_iota(jnp.int32, (requests, head_dim), 0)
    for d in range(1, replicas):
        goal_mask[d - 1] = (row_ids == goal[d - 1]).astype(F32)
        here_mask[d - 1] = (row_ids == arriver[d - 1]).astype(F32)

    q_all = queries[...].astype(F32)
    nk_rows[...] = new_kv[...].astype(F32)
    q_rows[...] = jnp.zeros_like(q_rows)
    for h in range(per_kv):
        q_rows[pl.ds(h, requests, stride=ROWS), :] = q_all[:, h * head_dim : (h + 1) * head_dim]

    for d in range(1, replicas):
        here = arriver[d - 1]
        own_rows = q_rows[pl.ds(pl.multiple_of(here * ROWS, ROWS), ROWS), :]
        token = nk_rows[pl.ds(here, 1), :]
        score = jnp.sum(own_rows * token[:, :head_dim], axis=1, keepdims=True) * factor
        here_own[d - 1, 0] = jnp.broadcast_to(score, (ROWS, head_dim))
        here_own[d - 1, 1] = jnp.broadcast_to(token[:, head_dim:], (ROWS, head_dim))
    lanes = lax.broadcasted_iota(jnp.int32, (1, max_pages), 1)
    staying = jnp.zeros((1, max_pages), jnp.int32)
    count = jnp.int32(0)
    for j in range(requests):
        stays = jnp.int32(1)
        for out_slot in leaver:
            stays = jnp.where(out_slot == j, 0, stays)
        staying = jnp.where((lanes == count) & (stays == 1), j, staying)
        count = count + stays
    table_out[:requests, :] = table_v[...]
    table_out[requests:, :] = staying
    for j in range(requests):
        context[j : j + 1, :] = jnp.full((1, head_dim), lengths[replica * requests + j], jnp.int32)

    scales[...] = scale_v[...].astype(F32)
    places = lax.broadcasted_iota(jnp.int32, (1, tokens), 1)
    spread = spread_matrix(max_pages, tokens)
    for d in range(1, replicas):
        out_slot = leaver[d - 1]
        picked = picked_scales(scale_v[...], table_v[pl.ds(out_slot, 1), :]).astype(BF16)
        wide = jnp.dot(picked, spread, preferred_element_type=F32)
        away_info[d - 1, 0:1, :] = wide[0:1] * factor
        away_info[d - 1, 1:2, :] = wide[1:2]
        away_info[d - 1, 2:3, :] = (places < lengths[replica * requests + out_slot]).astype(F32)

    for d in range(1, replicas):
        pltpu.make_async_copy(kv_pages.at[pl.ds(0, max_pages)], away_kv.at[d - 1], kv_sem.at[d - 1]).wait()


def attend_resident(
    replicas,
    per_kv,
    after,
    table_v,
    context,
    pool,
    q_rows,
    nk_rows,
    scales,
    attended,
    table_s,
    page_scales,
    key_scale,
    value_scale,
    scores,
    mixed,
    table_sem,
):
    del after
    requests, max_pages = context.shape[0], table_v.shape[1]
    _, _, page_len, head_dim = pool.shape
    tokens = max_pages * page_len
    span = CHUNK * page_len
    factor = 1.0 / math.sqrt(head_dim)
    copy = pltpu.make_async_copy(table_v, table_s, table_sem)
    copy.start()

    scale_rows = scales[...].astype(BF16)
    every_page = jnp.concatenate([table_v[j : j + 1, :] for j in range(requests)], axis=1)
    picked = picked_scales(scale_rows, every_page)
    for j in range(requests):
        page_scales[:, j : j + 1, :] = picked[:, j * max_pages : (j + 1) * max_pages][:, None, :]
    spread = spread_matrix(max_pages, tokens)
    key_scale[...] = jnp.dot(page_scales[0].astype(BF16), spread, preferred_element_type=F32) * factor
    value_scale[...] = jnp.dot(page_scales[1].astype(BF16), spread, preferred_element_type=F32)
    places = lax.broadcasted_iota(jnp.int32, (1, tokens), 1)
    copy.wait()

    def gather(j, c, which):
        return jnp.concatenate([pool[table_s[j, c * CHUNK + i], which] for i in range(CHUNK)], axis=0)

    slots = [table_s[requests, i] for i in range(requests - (replicas - 1))]
    own, tokens_new = [], []
    for i, j in enumerate(slots):
        rows = slice(i * ROWS, (i + 1) * ROWS)
        q = q_rows[pl.ds(pl.multiple_of(j * ROWS, ROWS), ROWS), :]
        tokens_new.append(nk_rows[pl.ds(j, 1), :])
        own.append(jnp.sum(q * tokens_new[i][:, :head_dim], axis=1, keepdims=True) * factor)
        q = q.astype(BF16)
        key_row = key_scale[pl.ds(j, 1), :]
        limit = context[pl.ds(j, 1), :][:, :1]
        for c in range(max_pages // CHUNK):
            columns = slice(c * span, (c + 1) * span)
            raw = dot_keys(q, gather(j, c, 0)) * key_row[:, columns]
            scores[rows, columns] = jnp.where(places[:, columns] < limit, raw, -jnp.inf)
    stats = []
    for i in range(len(slots)):
        rows = slice(i * ROWS, (i + 1) * ROWS)
        weights, own_weight, inverse = softmax_parts(scores[rows, :], own[i])
        scores[rows, :] = weights
        stats.append((own_weight, inverse))
    for i, j in enumerate(slots):
        rows = slice(i * ROWS, (i + 1) * ROWS)
        own_weight, inverse = stats[i]
        value_row = value_scale[pl.ds(j, 1), :]
        total = jnp.zeros((2 * ROWS, head_dim), F32)
        for c in range(max_pages // CHUNK):
            columns = slice(c * span, (c + 1) * span)
            both = split_scaled(scores[rows, columns], inverse, value_row[:, columns])
            total = total + jnp.dot(both, gather(j, c, 1), preferred_element_type=F32)
        own_weight = (own_weight * inverse).astype(BF16).astype(F32)
        mixed[pl.ds(pl.multiple_of(j * ROWS, ROWS), ROWS), :] = (
            total[:ROWS] + total[ROWS:] + own_weight * tokens_new[i][:, head_dim:]
        )
    for h in range(per_kv):
        attended[:, h * head_dim : (h + 1) * head_dim] = mixed[pl.ds(h, requests, stride=ROWS), :]


def attend_away(replicas, per_kv, *refs):
    count = replicas - 1
    away_kv, away_info, goal_mask = refs[:3]
    came = refs[3 : 3 + count]
    outs = refs[3 + count : 3 + 2 * count]
    q_rows, scores = refs[3 + 2 * count :]
    max_pages, _, page_len, head_dim = away_kv.shape[1:]
    span = CHUNK * page_len
    for d in range(count):
        pick = goal_mask[d]
        came_all = came[d][...].astype(F32)
        q_rows[...] = jnp.zeros_like(q_rows)
        for h in range(per_kv):
            q_rows[h : h + 1, :] = jnp.sum(
                came_all[:, h * head_dim : (h + 1) * head_dim] * pick, axis=0, keepdims=True
            )
        q = q_rows[...].astype(BF16)
        for c in range(max_pages // CHUNK):
            columns = slice(c * span, (c + 1) * span)
            keys = away_kv[d, c * CHUNK : (c + 1) * CHUNK, 0].reshape(span, head_dim)
            raw = dot_keys(q, keys) * away_info[d, 0:1, columns]
            scores[:, columns] = jnp.where(away_info[d, 2:3, columns] > 0, raw, -jnp.inf)
        highest = jnp.max(scores[...], axis=1, keepdims=True)
        weights = jnp.exp(scores[...] - highest)
        total = jnp.sum(weights, axis=1, keepdims=True)
        mixed = jnp.zeros((2 * ROWS, head_dim), F32)
        for c in range(max_pages // CHUNK):
            columns = slice(c * span, (c + 1) * span)
            values = away_kv[d, c * CHUNK : (c + 1) * CHUNK, 1].reshape(span, head_dim)
            both = split_scaled(weights[:, columns], None, away_info[d, 1:2, columns])
            mixed = mixed + jnp.dot(both, values, preferred_element_type=F32)
        outs[d][0] = mixed[:ROWS] + mixed[ROWS:]
        outs[d][1] = jnp.broadcast_to(highest, (ROWS, head_dim))
        outs[d][2] = jnp.broadcast_to(total, (ROWS, head_dim))


def pick(parts, to_yz, to_core, at_y, at_z, own):
    width = own.shape[1]
    shard = lax.axis_index("replica") % KVH

    def block(k):
        return parts[:, pl.ds(pl.multiple_of((shard ^ k) * width, 128), width)]

    for i, k in enumerate((6, 7)):
        to_yz[:, i * width : (i + 1) * width] = block(k).astype(to_yz.dtype)
    for i, k in enumerate((3, 5, 1)):
        to_core[:, i * width : (i + 1) * width] = block(k)
    at_y[...] = block(2)
    at_z[...] = block(4)
    own[...] = block(0)


def merge(replicas, attended, here_mask, here_own, *refs):
    arrived, out = refs[: replicas - 1], refs[-1]
    head_dim = here_mask.shape[2]
    per_kv = attended.shape[1] // head_dim
    moved = []
    for d in range(replicas - 1):
        own = here_own[d, 0]
        highest = jnp.maximum(arrived[d][1], own)
        cached = jnp.exp(arrived[d][1] - highest)
        own = jnp.exp(own - highest)
        inverse = 1.0 / (arrived[d][2] * cached + own)
        own = (own * inverse).astype(BF16).astype(F32)
        moved.append(arrived[d][0] * (cached * inverse) + own * here_own[d, 1])
    for h in range(per_kv):
        columns = slice(h * head_dim, (h + 1) * head_dim)
        piece = attended[:, columns]
        for d in range(replicas - 1):
            piece = jnp.where(here_mask[d] > 0, moved[d][h : h + 1], piece)
        out[:, columns] = piece.astype(out.dtype)


def on_device(
    kv_pages, page_scale, page_table, lengths, request_moves, queries, new_kv, output_proj, residual
):
    devices = lax.axis_size("replica")
    replicas = devices // KVH
    requests, max_pages = page_table.shape
    pages, _, page_len, head_dim = kv_pages.shape
    per_kv = queries.shape[1] // head_dim
    width = output_proj.shape[1] // KVH
    tokens = max_pages * page_len
    count = replicas - 1

    def toward(value, steps):
        pairs = [(i, (i + steps * KVH) % devices) for i in range(devices)]
        return lax.ppermute(value, "replica", pairs)

    def partner(value, mask):
        return lax.ppermute(value, "replica", [(i, i ^ mask) for i in range(devices)])

    came = [toward(queries, -d) for d in range(1, replicas)]

    def shape(*dims, dtype=F32):
        return jax.ShapeDtypeStruct(dims, dtype)

    in_hbm = functools.partial(pltpu.with_memory_space_constraint, memory_space=pltpu.HBM)
    q_rows, nk_rows, scales, away_kv, away_info, goal_mask, *home = pl.pallas_call(
        functools.partial(set_up, replicas, per_kv),
        out_shape=[
            shape(requests * ROWS, head_dim),
            shape(requests, 2 * head_dim),
            shape(2, pages),
            shape(count, max_pages, 2, page_len, head_dim, dtype=BF16),
            shape(count, 8, tokens),
            shape(count, requests, head_dim),
            shape(count, requests, head_dim),
            shape(count, 2, ROWS, head_dim),
            shape(requests + 1, max_pages, dtype=jnp.int32),
            shape(requests, head_dim, dtype=jnp.int32),
        ],
        in_specs=[HBM] * 7,
        out_specs=[VMEM] * 10,
        scratch_shapes=[
            pltpu.SMEM(lengths.shape, jnp.int32),
            pltpu.SMEM(request_moves.shape, jnp.int32),
            pltpu.SMEM(page_table.shape, jnp.int32),
            pltpu.VMEM(page_table.shape, jnp.int32),
            pltpu.VMEM((2, pages), BF16),
            pltpu.VMEM(queries.shape, BF16),
            pltpu.VMEM(new_kv.shape, BF16),
            pltpu.SemaphoreType.DMA((7,)),
            pltpu.SemaphoreType.DMA((count,)),
        ],
        compiler_params=pltpu.CompilerParams(vmem_limit_bytes=4 * 2**20),
        cost_estimate=pl.CostEstimate(flops=0, bytes_accessed=4 * kv_pages.size, transcendentals=0),
        name="set_up",
    )(*(in_hbm(x) for x in (lengths, request_moves, page_table, page_scale.T, queries, new_kv, kv_pages)))

    here_mask, here_own, table_v, context = home

    rows = pl.pallas_call(
        functools.partial(attend_away, replicas, per_kv),
        out_shape=[shape(3, ROWS, head_dim)] * count,
        in_specs=[VMEM] * (3 + count),
        out_specs=[VMEM] * count,
        scratch_shapes=[pltpu.VMEM((ROWS, head_dim), F32), pltpu.VMEM((ROWS, tokens), F32)],
        compiler_params=pltpu.CompilerParams(vmem_limit_bytes=4 * 2**20),
        name="attend_away",
    )(away_kv, away_info, goal_mask, *came)
    arrived = [toward(rows[d - 1], d) for d in range(1, replicas)]

    attended = pl.pallas_call(
        functools.partial(attend_resident, replicas, per_kv),
        out_shape=shape(requests, per_kv * head_dim),
        in_specs=[HBM] + [VMEM] * 6,
        out_specs=VMEM,
        scratch_shapes=[
            pltpu.SMEM((requests + 1, max_pages), jnp.int32),
            pltpu.VMEM((2, requests, max_pages), F32),
            pltpu.VMEM((requests, tokens), F32),
            pltpu.VMEM((requests, tokens), F32),
            pltpu.VMEM((requests * ROWS, tokens), F32),
            pltpu.VMEM((requests * ROWS, head_dim), F32),
            pltpu.SemaphoreType.DMA,
        ],
        compiler_params=pltpu.CompilerParams(vmem_limit_bytes=8 * 2**20),
        cost_estimate=pl.CostEstimate(
            flops=4 * per_kv * requests * tokens * head_dim,
            bytes_accessed=4 * output_proj.size,
            transcendentals=requests * ROWS * tokens,
        ),
        name="attend_resident",
    )(
        rows[0],
        table_v,
        context,
        pltpu.with_memory_space_constraint(kv_pages, pltpu.VMEM),
        q_rows,
        nk_rows,
        scales,
    )
    mixture = pl.pallas_call(
        functools.partial(merge, replicas),
        out_shape=shape(*attended.shape, dtype=BF16),
        in_specs=[VMEM] * (3 + count),
        out_specs=VMEM,
        compiler_params=pltpu.CompilerParams(vmem_limit_bytes=2**20),
        name="merge",
    )(attended, here_mask, here_own, *arrived)

    parts = jnp.dot(mixture, output_proj, preferred_element_type=F32)

    to_yz, to_core, at_y, at_z, own = pl.pallas_call(
        pick,
        out_shape=[shape(requests, 2 * width, dtype=BF16), shape(requests, 3 * width)]
        + [shape(requests, width)] * 3,
        in_specs=[VMEM],
        out_specs=[VMEM] * 5,
        compiler_params=pltpu.CompilerParams(vmem_limit_bytes=2**20),
        name="pick",
    )(parts)
    came_yz = partner(to_yz, 6).astype(F32)
    other = partner(to_core, 1)
    came_y = partner((at_y + other[:, :width]).astype(BF16), 2)
    came_z = partner((at_z + other[:, width : 2 * width]).astype(BF16), 4)
    passed_on = partner(came_yz[:, width:], 1)
    total = own + other[:, 2 * width :] + came_yz[:, :width] + came_y.astype(F32) + came_z.astype(F32)
    total = lax.optimization_barrier(total) + passed_on
    return (residual.astype(F32) + total).astype(BF16)


def solution(mesh):
    return jax.shard_map(
        on_device,
        mesh=mesh,
        in_specs=(
            P(("parts", "replica"), None, None, None),
            P(("parts", "replica"), None),
            P(("parts", "replica"), None),
            P("parts"),
            P("parts"),
            P(("parts", "replica"), None),
            P(("parts", "replica"), None),
            P("replica", None),
            P(("parts", "replica"), None),
        ),
        out_specs=P(("parts", "replica"), None),
        check_vma=False,
    )
```

```python
import functools
import math

import jax
import jax.numpy as jnp
from jax import lax
from jax.experimental import pallas as pl
from jax.experimental.pallas import tpu as pltpu
from jax.sharding import PartitionSpec as P

KVH = 8
ROWS = 8
CHUNK = 4
F32 = jnp.float32
BF16 = jnp.bfloat16
VMEM = pl.BlockSpec(memory_space=pltpu.VMEM)
HBM = pl.BlockSpec(memory_space=pltpu.HBM)


def softmax_parts(scores, own):
    highest = jnp.maximum(jnp.max(scores, axis=1, keepdims=True), own)
    weights = jnp.exp(scores - highest)
    own_weight = jnp.exp(own - highest)
    return weights, own_weight, 1.0 / (jnp.sum(weights, axis=1, keepdims=True) + own_weight)


def split_scaled(weights, value_scale):
    scaled = weights.astype(BF16).astype(F32) * value_scale
    high = scaled.astype(BF16)
    low = (scaled - high.astype(F32)).astype(BF16)
    return jnp.concatenate([high, low], axis=0)


def dot_keys(queries, keys):
    return lax.dot_general(queries, keys, (((1,), (1,)), ((), ())), preferred_element_type=F32)


def picked_scales(scales, pages):
    ids = lax.broadcasted_iota(jnp.int32, (scales.shape[1], pages.shape[1]), 0)
    return jnp.dot(scales, (ids == pages).astype(F32).astype(BF16), preferred_element_type=F32)


def spread_matrix(max_pages, tokens):
    page_len = tokens // max_pages
    return (
        lax.broadcasted_iota(jnp.int32, (max_pages, tokens), 1) // page_len
        == lax.broadcasted_iota(jnp.int32, (max_pages, tokens), 0)
    ).astype(F32).astype(BF16)


def set_up(
    replicas,
    per_kv,
    lengths_h,
    moves_h,
    table_h,
    scale_h,
    queries_h,
    new_kv_h,
    kv_pages,
    q_rows,
    nk_rows,
    scales,
    away_kv,
    away_info,
    goal_mask,
    here_mask,
    here_own,
    table_out,
    context,
    lengths,
    moves,
    table_s,
    table_v,
    scale_v,
    queries,
    new_kv,
    small_sem,
    kv_sem,
):
    requests, max_pages = table_h.shape
    pages, _, page_len, head_dim = kv_pages.shape
    tokens = max_pages * page_len
    factor = 1.0 / math.sqrt(head_dim)
    replica = lax.axis_index("replica") // KVH

    small = [
        pltpu.make_async_copy(src, dst, small_sem.at[i])
        for i, (src, dst) in enumerate(
            [
                (moves_h, moves),
                (table_h, table_s),
                (table_h, table_v),
                (lengths_h, lengths),
                (scale_h, scale_v),
                (queries_h, queries),
                (new_kv_h, new_kv),
            ]
        )
    ]
    for copy in small:
        copy.start()
    for copy in small[:2]:
        copy.wait()

    first = replica * requests
    leaver, goal, arriver = [], [], []
    for d in range(1, replicas):
        there = jnp.where(replica + d < replicas, replica + d, replica + d - replicas) * requests
        behind = jnp.where(replica >= d, replica - d, replica - d + replicas) * requests
        out_slot = taken = here = jnp.int32(0)
        for j in range(requests):
            slot = moves[there + j] - first
            ours = (slot >= 0) & (slot < requests)
            out_slot = jnp.where(ours, slot, out_slot)
            taken = jnp.where(ours, j, taken)
            slot = moves[first + j] - behind
            here = jnp.where((slot >= 0) & (slot < requests), j, here)
        leaver.append(out_slot)
        goal.append(taken)
        arriver.append(here)

        def fetch(p, carry, d=d, out_slot=out_slot):
            pltpu.make_async_copy(
                kv_pages.at[table_s[out_slot, p]], away_kv.at[d - 1, p], kv_sem.at[d - 1]
            ).start()
            return carry

        lax.fori_loop(0, max_pages, fetch, 0, unroll=8)
    for copy in small[2:]:
        copy.wait()
    row_ids = lax.broadcasted_iota(jnp.int32, (requests, head_dim), 0)
    for d in range(1, replicas):
        goal_mask[d - 1] = (row_ids == goal[d - 1]).astype(F32)
        here_mask[d - 1] = (row_ids == arriver[d - 1]).astype(F32)

    q_all = queries[...].astype(F32)
    nk_rows[...] = new_kv[...].astype(F32)
    q_rows[...] = jnp.zeros_like(q_rows)
    for h in range(per_kv):
        q_rows[pl.ds(h, requests, stride=ROWS), :] = q_all[:, h * head_dim : (h + 1) * head_dim]

    for d in range(1, replicas):
        here = arriver[d - 1]
        own_rows = q_rows[pl.ds(pl.multiple_of(here * ROWS, ROWS), ROWS), :]
        token = nk_rows[pl.ds(here, 1), :]
        score = jnp.sum(own_rows * token[:, :head_dim], axis=1, keepdims=True) * factor
        here_own[d - 1, 0] = jnp.broadcast_to(score, (ROWS, head_dim))
        here_own[d - 1, 1] = jnp.broadcast_to(token[:, head_dim:], (ROWS, head_dim))
    lanes = lax.broadcasted_iota(jnp.int32, (1, max_pages), 1)
    staying = jnp.zeros((1, max_pages), jnp.int32)
    count = jnp.int32(0)
    for j in range(requests):
        stays = jnp.int32(1)
        for out_slot in leaver:
            stays = jnp.where(out_slot == j, 0, stays)
        staying = jnp.where((lanes == count) & (stays == 1), j, staying)
        count = count + stays
    table_out[:requests, :] = table_v[...]
    table_out[requests:, :] = staying
    for j in range(requests):
        context[j : j + 1, :] = jnp.full((1, head_dim), lengths[replica * requests + j], jnp.int32)

    scales[...] = scale_v[...].astype(F32)
    places = lax.broadcasted_iota(jnp.int32, (1, tokens), 1)
    spread = spread_matrix(max_pages, tokens)
    for d in range(1, replicas):
        out_slot = leaver[d - 1]
        picked = picked_scales(scale_v[...], table_v[pl.ds(out_slot, 1), :]).astype(BF16)
        wide = jnp.dot(picked, spread, preferred_element_type=F32)
        away_info[d - 1, 0:1, :] = wide[0:1] * factor
        away_info[d - 1, 1:2, :] = wide[1:2]
        away_info[d - 1, 2:3, :] = (places < lengths[replica * requests + out_slot]).astype(F32)

    for d in range(1, replicas):
        pltpu.make_async_copy(kv_pages.at[pl.ds(0, max_pages)], away_kv.at[d - 1], kv_sem.at[d - 1]).wait()


def attend_resident(
    replicas,
    per_kv,
    after,
    table_v,
    context,
    pool,
    q_rows,
    nk_rows,
    scales,
    attended,
    table_s,
    page_scales,
    key_scale,
    value_scale,
    scores,
    mixed,
    table_sem,
):
    del after
    requests, max_pages = context.shape[0], table_v.shape[1]
    _, _, page_len, head_dim = pool.shape
    tokens = max_pages * page_len
    span = CHUNK * page_len
    factor = 1.0 / math.sqrt(head_dim)
    copy = pltpu.make_async_copy(table_v, table_s, table_sem)
    copy.start()

    scale_rows = scales[...].astype(BF16)
    for j in range(requests):
        page_scales[:, j : j + 1, :] = picked_scales(scale_rows, table_v[j : j + 1, :])[:, None, :]
    spread = spread_matrix(max_pages, tokens)
    key_scale[...] = jnp.dot(page_scales[0].astype(BF16), spread, preferred_element_type=F32) * factor
    value_scale[...] = jnp.dot(page_scales[1].astype(BF16), spread, preferred_element_type=F32)
    places = lax.broadcasted_iota(jnp.int32, (1, tokens), 1)
    copy.wait()

    def gather(j, c, which):
        return jnp.concatenate([pool[table_s[j, c * CHUNK + i], which] for i in range(CHUNK)], axis=0)

    slots = [table_s[requests, i] for i in range(requests - (replicas - 1))]
    own, tokens_new = [], []
    for i, j in enumerate(slots):
        rows = slice(i * ROWS, (i + 1) * ROWS)
        q = q_rows[pl.ds(pl.multiple_of(j * ROWS, ROWS), ROWS), :]
        tokens_new.append(nk_rows[pl.ds(j, 1), :])
        own.append(jnp.sum(q * tokens_new[i][:, :head_dim], axis=1, keepdims=True) * factor)
        q = q.astype(BF16)
        key_row = key_scale[pl.ds(j, 1), :]
        limit = context[pl.ds(j, 1), :][:, :1]
        for c in range(max_pages // CHUNK):
            columns = slice(c * span, (c + 1) * span)
            raw = dot_keys(q, gather(j, c, 0)) * key_row[:, columns]
            scores[rows, columns] = jnp.where(places[:, columns] < limit, raw, -jnp.inf)
    stats = []
    for i in range(len(slots)):
        rows = slice(i * ROWS, (i + 1) * ROWS)
        weights, own_weight, inverse = softmax_parts(scores[rows, :], own[i])
        scores[rows, :] = weights
        stats.append((own_weight, inverse))
    for i, j in enumerate(slots):
        rows = slice(i * ROWS, (i + 1) * ROWS)
        own_weight, inverse = stats[i]
        value_row = value_scale[pl.ds(j, 1), :]
        total = jnp.zeros((2 * ROWS, head_dim), F32)
        for c in range(max_pages // CHUNK):
            columns = slice(c * span, (c + 1) * span)
            both = split_scaled(scores[rows, columns], value_row[:, columns])
            total = total + jnp.dot(both, gather(j, c, 1), preferred_element_type=F32)
        own_weight = own_weight.astype(BF16).astype(F32)
        mixed[pl.ds(pl.multiple_of(j * ROWS, ROWS), ROWS), :] = (
            total[:ROWS] + total[ROWS:] + own_weight * tokens_new[i][:, head_dim:]
        ) * inverse
    for h in range(per_kv):
        attended[:, h * head_dim : (h + 1) * head_dim] = mixed[pl.ds(h, requests, stride=ROWS), :]


def attend_away(replicas, per_kv, *refs):
    count = replicas - 1
    away_kv, away_info, goal_mask = refs[:3]
    came = refs[3 : 3 + count]
    outs = refs[3 + count : 3 + 2 * count]
    q_rows, scores = refs[3 + 2 * count :]
    max_pages, _, page_len, head_dim = away_kv.shape[1:]
    span = CHUNK * page_len
    for d in range(count):
        pick = goal_mask[d]
        came_all = came[d][...].astype(F32)
        q_rows[...] = jnp.zeros_like(q_rows)
        for h in range(per_kv):
            q_rows[h : h + 1, :] = jnp.sum(
                came_all[:, h * head_dim : (h + 1) * head_dim] * pick, axis=0, keepdims=True
            )
        q = q_rows[...].astype(BF16)
        for c in range(max_pages // CHUNK):
            columns = slice(c * span, (c + 1) * span)
            keys = away_kv[d, c * CHUNK : (c + 1) * CHUNK, 0].reshape(span, head_dim)
            raw = dot_keys(q, keys) * away_info[d, 0:1, columns]
            scores[:, columns] = jnp.where(away_info[d, 2:3, columns] > 0, raw, -jnp.inf)
        highest = jnp.max(scores[...], axis=1, keepdims=True)
        weights = jnp.exp(scores[...] - highest)
        total = jnp.sum(weights, axis=1, keepdims=True)
        mixed = jnp.zeros((2 * ROWS, head_dim), F32)
        for c in range(max_pages // CHUNK):
            columns = slice(c * span, (c + 1) * span)
            values = away_kv[d, c * CHUNK : (c + 1) * CHUNK, 1].reshape(span, head_dim)
            both = split_scaled(weights[:, columns], away_info[d, 1:2, columns])
            mixed = mixed + jnp.dot(both, values, preferred_element_type=F32)
        outs[d][0] = mixed[:ROWS] + mixed[ROWS:]
        outs[d][1] = jnp.broadcast_to(highest, (ROWS, head_dim))
        outs[d][2] = jnp.broadcast_to(total, (ROWS, head_dim))


def pick(parts, to_yz, to_core, at_y, at_z, own):
    width = own.shape[1]
    shard = lax.axis_index("replica") % KVH

    def block(k):
        return parts[:, pl.ds(pl.multiple_of((shard ^ k) * width, 128), width)]

    for i, k in enumerate((6, 7)):
        to_yz[:, i * width : (i + 1) * width] = block(k).astype(to_yz.dtype)
    for i, k in enumerate((3, 5, 1)):
        to_core[:, i * width : (i + 1) * width] = block(k)
    at_y[...] = block(2)
    at_z[...] = block(4)
    own[...] = block(0)


def merge(replicas, attended, here_mask, here_own, *refs):
    arrived, out = refs[: replicas - 1], refs[-1]
    head_dim = here_mask.shape[2]
    per_kv = attended.shape[1] // head_dim
    moved = []
    for d in range(replicas - 1):
        own = here_own[d, 0]
        highest = jnp.maximum(arrived[d][1], own)
        cached = jnp.exp(arrived[d][1] - highest)
        own = jnp.exp(own - highest)
        inverse = 1.0 / (arrived[d][2] * cached + own)
        own = (own * inverse).astype(BF16).astype(F32)
        moved.append(arrived[d][0] * (cached * inverse) + own * here_own[d, 1])
    for h in range(per_kv):
        columns = slice(h * head_dim, (h + 1) * head_dim)
        piece = attended[:, columns]
        for d in range(replicas - 1):
            piece = jnp.where(here_mask[d] > 0, moved[d][h : h + 1], piece)
        out[:, columns] = piece.astype(out.dtype)


def on_device(
    kv_pages, page_scale, page_table, lengths, request_moves, queries, new_kv, output_proj, residual
):
    devices = lax.axis_size("replica")
    replicas = devices // KVH
    requests, max_pages = page_table.shape
    pages, _, page_len, head_dim = kv_pages.shape
    per_kv = queries.shape[1] // head_dim
    width = output_proj.shape[1] // KVH
    tokens = max_pages * page_len
    count = replicas - 1

    def toward(value, steps):
        pairs = [(i, (i + steps * KVH) % devices) for i in range(devices)]
        return lax.ppermute(value, "replica", pairs)

    def partner(value, mask):
        return lax.ppermute(value, "replica", [(i, i ^ mask) for i in range(devices)])

    came = [toward(queries, -d) for d in range(1, replicas)]

    def shape(*dims, dtype=F32):
        return jax.ShapeDtypeStruct(dims, dtype)

    in_hbm = functools.partial(pltpu.with_memory_space_constraint, memory_space=pltpu.HBM)
    q_rows, nk_rows, scales, away_kv, away_info, goal_mask, *home = pl.pallas_call(
        functools.partial(set_up, replicas, per_kv),
        out_shape=[
            shape(requests * ROWS, head_dim),
            shape(requests, 2 * head_dim),
            shape(2, pages),
            shape(count, max_pages, 2, page_len, head_dim, dtype=BF16),
            shape(count, 8, tokens),
            shape(count, requests, head_dim),
            shape(count, requests, head_dim),
            shape(count, 2, ROWS, head_dim),
            shape(requests + 1, max_pages, dtype=jnp.int32),
            shape(requests, head_dim, dtype=jnp.int32),
        ],
        in_specs=[HBM] * 7,
        out_specs=[VMEM] * 10,
        scratch_shapes=[
            pltpu.SMEM(lengths.shape, jnp.int32),
            pltpu.SMEM(request_moves.shape, jnp.int32),
            pltpu.SMEM(page_table.shape, jnp.int32),
            pltpu.VMEM(page_table.shape, jnp.int32),
            pltpu.VMEM((2, pages), BF16),
            pltpu.VMEM(queries.shape, BF16),
            pltpu.VMEM(new_kv.shape, BF16),
            pltpu.SemaphoreType.DMA((7,)),
            pltpu.SemaphoreType.DMA((count,)),
        ],
        compiler_params=pltpu.CompilerParams(vmem_limit_bytes=4 * 2**20),
        cost_estimate=pl.CostEstimate(flops=0, bytes_accessed=4 * kv_pages.size, transcendentals=0),
        name="set_up",
    )(*(in_hbm(x) for x in (lengths, request_moves, page_table, page_scale.T, queries, new_kv, kv_pages)))

    here_mask, here_own, table_v, context = home

    rows = pl.pallas_call(
        functools.partial(attend_away, replicas, per_kv),
        out_shape=[shape(3, ROWS, head_dim)] * count,
        in_specs=[VMEM] * (3 + count),
        out_specs=[VMEM] * count,
        scratch_shapes=[pltpu.VMEM((ROWS, head_dim), F32), pltpu.VMEM((ROWS, tokens), F32)],
        compiler_params=pltpu.CompilerParams(vmem_limit_bytes=4 * 2**20),
        name="attend_away",
    )(away_kv, away_info, goal_mask, *came)
    arrived = [toward(rows[d - 1], d) for d in range(1, replicas)]

    attended = pl.pallas_call(
        functools.partial(attend_resident, replicas, per_kv),
        out_shape=shape(requests, per_kv * head_dim),
        in_specs=[HBM] + [VMEM] * 6,
        out_specs=VMEM,
        scratch_shapes=[
            pltpu.SMEM((requests + 1, max_pages), jnp.int32),
            pltpu.VMEM((2, requests, max_pages), F32),
            pltpu.VMEM((requests, tokens), F32),
            pltpu.VMEM((requests, tokens), F32),
            pltpu.VMEM((requests * ROWS, tokens), F32),
            pltpu.VMEM((requests * ROWS, head_dim), F32),
            pltpu.SemaphoreType.DMA,
        ],
        compiler_params=pltpu.CompilerParams(vmem_limit_bytes=8 * 2**20),
        cost_estimate=pl.CostEstimate(
            flops=4 * per_kv * requests * tokens * head_dim,
            bytes_accessed=4 * output_proj.size,
            transcendentals=requests * ROWS * tokens,
        ),
        name="attend_resident",
    )(
        rows[0],
        table_v,
        context,
        pltpu.with_memory_space_constraint(kv_pages, pltpu.VMEM),
        q_rows,
        nk_rows,
        scales,
    )
    mixture = pl.pallas_call(
        functools.partial(merge, replicas),
        out_shape=shape(*attended.shape, dtype=BF16),
        in_specs=[VMEM] * (3 + count),
        out_specs=VMEM,
        compiler_params=pltpu.CompilerParams(vmem_limit_bytes=2**20),
        name="merge",
    )(attended, here_mask, here_own, *arrived)

    parts = jnp.dot(mixture, output_proj, preferred_element_type=F32)

    to_yz, to_core, at_y, at_z, own = pl.pallas_call(
        pick,
        out_shape=[shape(requests, 2 * width, dtype=BF16), shape(requests, 3 * width)]
        + [shape(requests, width)] * 3,
        in_specs=[VMEM],
        out_specs=[VMEM] * 5,
        compiler_params=pltpu.CompilerParams(vmem_limit_bytes=2**20),
        name="pick",
    )(parts)
    came_yz = partner(to_yz, 6).astype(F32)
    other = partner(to_core, 1)
    came_y = partner((at_y + other[:, :width]).astype(BF16), 2)
    came_z = partner((at_z + other[:, width : 2 * width]).astype(BF16), 4)
    passed_on = partner(came_yz[:, width:], 1)
    total = own + other[:, 2 * width :] + came_yz[:, :width] + came_y.astype(F32) + came_z.astype(F32)
    total = lax.optimization_barrier(total) + passed_on
    return (residual.astype(F32) + total).astype(BF16)


def solution(mesh):
    return jax.shard_map(
        on_device,
        mesh=mesh,
        in_specs=(
            P(("parts", "replica"), None, None, None),
            P(("parts", "replica"), None),
            P(("parts", "replica"), None),
            P("parts"),
            P("parts"),
            P(("parts", "replica"), None),
            P(("parts", "replica"), None),
            P("replica", None),
            P(("parts", "replica"), None),
        ),
        out_specs=P(("parts", "replica"), None),
        check_vma=False,
    )
```
